32 devices in a mesh: gx: 4 (over y, core), gy: 8 (over z, x).
Axes of the slice: x: 2, y: 2, z: 4, core: 2. Of those that a mesh axis runs over, the one named last changes fastest.
Arguments:
- load: float32 [2, 128, 128, 128], P(None, 'gx', 'gy'), may hold values from -8 to 8
- zones: int32 [128, 128, 128], P('gx', 'gy'), may hold values from 0 to 7
- conductance: float32 [2, 8], replicated, may hold values from 0.2 to 1
- capacity: float32 [2, 8], replicated, may hold values from 0.5 to 2
- coupling: float32 [8], replicated, may hold values from 0.2 to 0.8
Outputs:
- solution: float32 [2, 128, 128, 128], P(None, 'gx', 'gy')
- residual: float32 [2, 128, 128, 128], P(None, 'gx', 'gy')
The draws below stay inside these ranges and needn't reach their ends.
All inputs are finite; a program needn't handle non-finite values.
Results may differ from the reference program's by a relative error of at most 0.006.
Values sent between devices are 32-bit elements; how exact they have to be, the bound alone decides.
No kernel may reach another device: no remote copies, remote signals or barrier semaphores. Data moves between devices by JAX's collectives and lax.ppermute only.
A program may use at most 64 MiB of HBM per device.

```python
import math
import jax
import jax.numpy as jnp
from jax import lax

BOX = 16
ZONES = 8
ITERS = 2
NX = 128
NY = 128
NZ = 128


def draw_load(key, part):
    first_key = jax.random.fold_in(key, 0)
    place_x = (jnp.arange(NX, dtype=jnp.float32) + 0.5) / NX
    place_y = (jnp.arange(NY, dtype=jnp.float32) + 0.5) / NY
    scale = jnp.sqrt((1.0 + place_x)[:, None, None] * (1.0 + place_y)[None, :, None])
    values = jax.random.normal(first_key, (2, NX, NY, NZ), jnp.float32) * scale[None]
    return jnp.clip(values, -8.0, 8.0).astype(jnp.float32)


def plant(values, rng, least, high):
    spot = [jax.random.randint(jax.random.fold_in(rng, axis), (), 0, length) for axis, length in enumerate(values.shape)]
    longest = values.shape.index(max(values.shape))
    next_to = spot[:longest] + [(spot[longest] + 1) % values.shape[longest]] + spot[longest + 1:]
    return values.at[tuple(spot)].set(least).at[tuple(next_to)].set(high)


def setup_inputs(seed: int = 0) -> dict:
    key_of = jax.random.split(jax.random.key(seed), 6)
    load = draw_load(jax.random.fold_in(key_of[5], 71), 0)
    zones = plant(jax.random.randint(key_of[1], (NX, NY, NZ), 0, ZONES), jax.random.fold_in(key_of[1], 1), 0, ZONES - 1).astype(jnp.int32)
    conductance = jnp.clip(jnp.exp(jax.random.uniform(key_of[2], (2, ZONES), jnp.float32, math.log(0.2), math.log(1.0))), 0.2, 1.0)
    capacity = jnp.clip(jnp.exp(jax.random.uniform(key_of[3], (2, ZONES), jnp.float32, math.log(0.5), math.log(2.0))), 0.5, 2.0)
    coupling = jnp.clip(jax.random.uniform(key_of[4], (ZONES,), jnp.float32, 0.2, 0.8), 0.2, 0.8)
    return {"load": load, "zones": zones, "conductance": conductance, "capacity": capacity, "coupling": coupling}


NEIGHBOURS = ((1, 0, 0), (-1, 0, 0), (0, 1, 0), (0, -1, 0), (0, 0, 1), (0, 0, -1))

def neighbour(array, offset_x, offset_y, offset_z):
    size_x, size_y, size_z = array.shape[-3:]
    return array[..., 1 + offset_x:size_x - 1 + offset_x, 1 + offset_y:size_y - 1 + offset_y, 1 + offset_z:size_z - 1 + offset_z]

def apply_operator(field, padded, kpadded, inside, mass):
    center = kpadded[:, 1:-1, 1:-1, 1:-1]
    flux = jnp.zeros_like(field)
    for offset_x, offset_y, offset_z in NEIGHBOURS:
        other_k = neighbour(kpadded, offset_x, offset_y, offset_z)
        other_in = neighbour(inside, offset_x, offset_y, offset_z)
        face = 0.5 * (center + jnp.where(other_in[None], other_k, center))
        flux = flux + face * (field - neighbour(padded, offset_x, offset_y, offset_z))
    first = mass[0] * field[0] + mass[2] * field[1] + flux[0]
    second = mass[2] * field[0] + mass[1] * field[1] + flux[1]
    return jnp.stack([first, second])

def box_matrix(cells):
    span = BOX + 2
    count = cells // BOX
    rows = jnp.arange(count * span)
    block_of = rows // span
    mode_of = rows % span
    columns = jnp.arange(cells + 2)
    offset = columns[None, :] - BOX * block_of[:, None]
    valid = (offset >= 0) & (offset < span)
    angle_arg = jnp.pi * (offset + 1).astype(jnp.float32) * (mode_of[:, None] + 1).astype(jnp.float32) / (span + 1)
    basis = jnp.sqrt(2.0 / (span + 1)) * jnp.sin(angle_arg)
    return jnp.where(valid, basis, 0.0).astype(jnp.float32)

def box_eigen():
    span = BOX + 2
    modes = jnp.arange(span).astype(jnp.float32)
    return 4.0 * jnp.sin(jnp.pi * (modes + 1.0) / (2.0 * (span + 1))) ** 2

def box_means(values):
    fields, size_x, size_y, size_z = values.shape
    shaped = values.reshape(fields, size_x // BOX, BOX, size_y // BOX, BOX, size_z // BOX, BOX)
    return lax.optimization_barrier(jnp.mean(shaped, axis=(2, 4, 6)))

def solve_boxes(padded, cbar, kbar):
    highest = lax.Precision.HIGHEST
    fields, length_x, length_y, length_z = padded.shape
    matrix_x = box_matrix(length_x - 2)
    matrix_y = box_matrix(length_y - 2)
    matrix_z = box_matrix(length_z - 2)
    spectral = jnp.einsum('am,fmyz->fayz', matrix_x, padded, precision=highest)
    spectral = jnp.einsum('bn,fanz->fabz', matrix_y, spectral, precision=highest)
    spectral = jnp.einsum('co,fabo->fabc', matrix_z, spectral, precision=highest)
    boxes_x, boxes_y, boxes_z = cbar.shape[1:]
    span = BOX + 2
    eigen = box_eigen()
    summed = eigen[:, None, None] + eigen[None, :, None] + eigen[None, None, :]
    divisor = cbar[:, :, None, :, None, :, None] + kbar[:, :, None, :, None, :, None] * summed[None, None, :, None, :, None, :]
    spectral = spectral.reshape(fields, boxes_x, span, boxes_y, span, boxes_z, span) / divisor
    spectral = spectral.reshape(fields, boxes_x * span, boxes_y * span, boxes_z * span)
    spectral = jnp.einsum('co,fabc->fabo', matrix_z, spectral, precision=highest)
    spectral = jnp.einsum('bn,fabo->fano', matrix_y, spectral, precision=highest)
    return jnp.einsum('am,fano->fmno', matrix_x, spectral, precision=highest)

def reference(load, zones, conductance, capacity, coupling):
    cross = coupling * jnp.sqrt(capacity[0] * capacity[1])
    tables = jnp.concatenate([conductance, capacity, cross[None]], axis=0)
    marks = jnp.pad(zones + 1, 1)
    inside = marks > 0
    safe_marks = jnp.maximum(marks - 1, 0).astype(jnp.int32)
    kpadded = jnp.where(inside[None], jnp.take(tables[0:2], safe_marks, axis=1), 0.0)
    plain = zones.astype(jnp.int32)
    mass = jnp.take(tables[2:5], plain, axis=1)
    cbar = box_means(mass[0:2])
    kbar = box_means(kpadded[:, 1:-1, 1:-1, 1:-1])
    widths = ((0, 0), (1, 1), (1, 1), (1, 1))

    def operate(field):
        return apply_operator(field, jnp.pad(field, widths), kpadded, inside, mass)

    def precondition(vector):
        padded = jnp.pad(vector, widths)
        parts = []
        for field_index in range(2):
            result = solve_boxes(padded[field_index:field_index + 1], cbar[field_index:field_index + 1], kbar[field_index:field_index + 1])
            parts.append(result[0, 1:-1, 1:-1, 1:-1])
        return jnp.stack(parts)
    solution = jnp.zeros_like(load)
    residual = load
    direction = load
    previous = jnp.float32(1.0)
    for iteration in range(ITERS):
        precond = precondition(residual)
        product = jnp.sum(residual * precond)
        if iteration == 0:
            direction = precond
        else:
            direction = precond + product / previous * direction
        image = operate(direction)
        alpha = product / jnp.sum(direction * image)
        solution = solution + alpha * direction
        residual = residual - alpha * image
        previous = product
    return (solution, residual)
```

```python
import functools
import math

import jax
import jax.numpy as jnp
import ml_dtypes
import numpy as np
from jax import lax
from jax.experimental import pallas as pl
from jax.experimental.pallas import tpu as pltpu
from jax.sharding import PartitionSpec as P

BOX = 16
SPAN = BOX + 2
F32 = jnp.float32
BF16 = jnp.bfloat16
AXES = ("gx", "gy")
ROW0 = 4


def split(matrix):
    high = matrix.astype(ml_dtypes.bfloat16)
    low = (matrix - high.astype(np.float64)).astype(ml_dtypes.bfloat16)
    return high, low


def round_up(value, step):
    return (value + step - 1) // step * step


def sine_basis():
    index = np.arange(SPAN)
    angle = np.pi * np.outer(index + 1, index + 1) / (SPAN + 1)
    return np.sqrt(2.0 / (SPAN + 1)) * np.sin(angle)


def eigenvalues():
    return 4.0 * np.sin(np.pi * (np.arange(SPAN) + 1) / (2 * (SPAN + 1))) ** 2


def plane_layout():
    places = [(x, y + 1) for x in range(SPAN) for y in range(BOX)]
    for y in (0, SPAN - 1):
        for position in range(24):
            x = position - (ROW0 - 1)
            places.append((x, y) if 0 <= x < SPAN else None)
    return places


def constants(size_z):
    basis = sine_basis()
    places = plane_layout()
    rows = len(places)
    modes = SPAN * SPAN
    padded_modes = round_up(modes, 16)
    plane = np.zeros((padded_modes, rows))
    for column, place in enumerate(places):
        if place is not None:
            plane[:modes, column] = np.outer(basis[:, place[0]], basis[:, place[1]]).reshape(-1)
    high, low = split(plane)
    forward = np.concatenate([high, high, low], axis=1)
    high, low = split(plane.T)
    inverse = np.concatenate([high, high, low], axis=1)
    boxes = size_z // BOX
    line = np.zeros((size_z, boxes * SPAN))
    means = np.zeros((size_z, boxes * SPAN))
    for box in range(boxes):
        for mode in range(SPAN):
            for offset in range(SPAN):
                cell = box * BOX + offset - 1
                if 0 <= cell < size_z:
                    line[cell, box * SPAN + mode] = basis[mode, offset]
        means[box * BOX : (box + 1) * BOX, box * SPAN : (box + 1) * SPAN] = 1.0 / BOX**3
    high, low = split(line)
    line_forward = np.concatenate([high, high, low], axis=0)
    high, low = split(line.T)
    line_inverse = np.concatenate([high, low], axis=1)
    eigen = eigenvalues()
    pair = np.zeros(padded_modes)
    pair[:modes] = (eigen[:, None] + eigen[None, :]).reshape(-1)
    summed = (pair[:, None] + np.tile(eigen, boxes)[None, :]).astype(np.float32)
    return forward, inverse, line_forward, line_inverse, summed, means.astype(np.float32)


def swap_pairs(mesh, axis, odd):
    sizes = [mesh.shape[name] for name in AXES]
    along = AXES.index(axis)
    pairs = []
    for i in range(sizes[0]):
        for j in range(sizes[1]):
            here = [i, j]
            there = [i, j]
            place = here[along]
            target = place ^ 1 if not odd else (place + 1 if place % 2 else place - 1)
            if 0 <= target < sizes[along]:
                there[along] = target
            elif along == 0:
                there[0] = sizes[0] - 1 - place
            else:
                there[0] = i ^ 1
            pairs.append((here[0] * sizes[1] + here[1], there[0] * sizes[1] + there[1]))
    return pairs


def swap(mesh, axis, even_part, odd_part):
    first = lax.ppermute(even_part, AXES, swap_pairs(mesh, axis, False))
    second = lax.ppermute(odd_part, AXES, swap_pairs(mesh, axis, True))
    return first, second


EVEN_X, EVEN_Y, LOW_X, HIGH_X, LOW_Y, HIGH_Y = range(6)


def chosen(flags, which, yes, no):
    return jnp.where(flags[which] > 0, yes, no)


def keep(flags, which, value):
    return jnp.where(flags[which] > 0, value, jnp.zeros_like(value))


def halves(value):
    high = value.astype(BF16)
    low = (value - high.astype(F32)).astype(BF16)
    return high, low


def dot(left, right):
    return jnp.dot(left, right, preferred_element_type=F32)


def solve(field_ref, rows_ref, inverse_ref, consts, stack_ref, out_ref, out_rows_ref):
    forward_ref, back_ref, line_forward_ref, line_back_ref = consts
    boxes = (field_ref.shape[1] - 2) // BOX
    size_y, size_z = field_ref.shape[2:]
    inner = SPAN * size_y
    rows = inner + 48
    line_rows = line_forward_ref.shape[0] // 3
    for field in range(2):
        for box in range(boxes):
            start = box * BOX
            main = field_ref[field, start : start + SPAN].reshape(inner, size_z)
            lanes = slice(box * size_z, (box + 1) * size_z)
            parts = (
                (0, main),
                (inner, rows_ref[field, 0, start : start + 24]),
                (inner + 24, rows_ref[field, 1, start : start + 24]),
            )
            whole = jnp.concatenate([part for _, part in parts], axis=0)
            high, low = halves(whole)
            stack_ref[0:rows, lanes] = high
            stack_ref[rows : 2 * rows, lanes] = low
            stack_ref[2 * rows : 3 * rows, lanes] = high
        spectral = dot(forward_ref[...], stack_ref[...])
        for box in range(boxes):
            lanes = slice(box * size_z, (box + 1) * size_z)
            high, low = halves(spectral[:, lanes])
            both = jnp.concatenate([high, low], axis=1)
            modes = dot(both, line_forward_ref[0 : 2 * line_rows]) + dot(high, line_forward_ref[2 * line_rows :])
            modes = modes * inverse_ref[field * boxes + box]
            high, low = halves(modes)
            cells = dot(high, line_back_ref[...])
            cells = cells[:, :size_z] + (cells[:, size_z:] + dot(low, line_back_ref[:, :size_z]))
            high, low = halves(cells)
            stack_ref[0:rows, lanes] = high
            stack_ref[rows : 2 * rows, lanes] = low
            stack_ref[2 * rows : 3 * rows, lanes] = high
        result = dot(back_ref[...], stack_ref[...])
        for box in range(boxes):
            lanes = slice(box * size_z, (box + 1) * size_z)
            start = box * BOX
            main = result[:inner, lanes].reshape(SPAN, size_y, size_z)
            if box == 0:
                out_ref[field, 0:SPAN] = main
            else:
                out_ref[field, start : start + 2] = out_ref[field, start : start + 2] + main[0:2]
                out_ref[field, start + 2 : start + SPAN] = main[2:]
            for side in range(2):
                strip = result[inner + 24 * side : inner + 24 * side + 24, lanes]
                if box == 0:
                    out_rows_ref[field, side, 0:24] = strip
                else:
                    out_rows_ref[field, side, start : start + 8] = (
                        out_rows_ref[field, side, start : start + 8] + strip[0:8]
                    )
                    out_rows_ref[field, side, start + 8 : start + 24] = strip[8:]


def pack_x(flags, part_ref, part_rows_ref, even_ref, odd_ref):
    last = part_ref.shape[1] - 1
    size_y = part_ref.shape[2]
    for field in range(2):
        for layer in range(3):
            low, high = layer, last - 2 + layer
            for side, place in ((None, slice(0, size_y)), (0, slice(size_y, size_y + 1)), (1, slice(size_y + 1, size_y + 2))):
                if side is None:
                    to_low, to_high = part_ref[field, low], part_ref[field, high]
                else:
                    shift = ROW0 - 1
                    to_low = part_rows_ref[field, side, low + shift : low + shift + 1]
                    to_high = part_rows_ref[field, side, high + shift : high + shift + 1]
                even_ref[field, layer, place] = chosen(flags, EVEN_X, to_high, to_low)
                odd_ref[field, layer, place] = chosen(flags, EVEN_X, to_low, to_high)
            rest = even_ref.shape[2] - size_y - 2
            blank = jnp.zeros((rest, even_ref.shape[3]), F32)
            even_ref[field, layer, size_y + 2 :] = blank
            odd_ref[field, layer, size_y + 2 :] = blank


def divisor_kernel(table_ref, zones_ref, summed_ref, means_ref, inverse_ref):
    size_x, size_y, size_z = zones_ref.shape
    boxes = size_x // BOX
    lines = []
    for which in (2, 3, 0, 1):
        for box in range(boxes):
            total = jnp.zeros((size_y, size_z), F32)
            for x in range(box * BOX, (box + 1) * BOX):
                zone = zones_ref[x]
                value = jnp.full((size_y, size_z), table_ref[which, 0], F32)
                for label in range(1, table_ref.shape[1]):
                    value = jnp.where(zone == label, table_ref[which, label], value)
                total = total + value
            lines.append(jnp.sum(total, axis=0, keepdims=True))
    sums = jnp.concatenate(lines, axis=0)
    means = jnp.dot(sums, means_ref[...], preferred_element_type=F32, precision=lax.Precision.HIGHEST)
    half = 2 * boxes
    for combo in range(half):
        cbar = means[combo : combo + 1]
        kbar = 2.0 * means[half + combo : half + combo + 1]
        inverse_ref[combo] = 1.0 / (cbar + kbar * summed_ref[...])


def edge_rows_kernel(flags, load_ref, zones_ref, first_ref, second_ref, even_ref, odd_ref):
    size_x, size_y, size_z = zones_ref.shape
    from_low = chosen(flags, EVEN_X, second_ref[...], first_ref[...])
    from_high = chosen(flags, EVEN_X, first_ref[...], second_ref[...])
    blank = jnp.zeros((8, size_z), F32)
    for channel in range(4):
        for ref in (even_ref, odd_ref):
            ref[channel, 0:8] = blank
            ref[channel, size_x : size_x + 8] = blank

    def put(channel, position, count, to_low, to_high):
        place = slice(position, position + count)
        even_ref[channel, place] = chosen(flags, EVEN_Y, to_high, to_low)
        odd_ref[channel, place] = chosen(flags, EVEN_Y, to_low, to_high)

    end = ROW0 + size_x
    for field in range(2):
        put(field, ROW0, size_x, load_ref[field, :, 0], load_ref[field, :, size_y - 1])
        low = keep(flags, LOW_X, from_low[field])
        high = keep(flags, HIGH_X, from_high[field])
        put(field, ROW0 - 1, 1, low[0:1], low[size_y - 1 : size_y])
        put(field, end, 1, high[0:1], high[size_y - 1 : size_y])
    for layer in range(2):
        channel = 2 + layer
        near, far = layer, size_y - 2 + layer
        put(channel, ROW0, size_x, zones_ref[:, near].astype(F32), zones_ref[:, far].astype(F32))
        for depth in range(2):
            low, high = from_low[2 + depth], from_high[2 + depth]
            put(channel, ROW0 - 2 + depth, 1, low[near : near + 1], low[far : far + 1])
            put(channel, end + depth, 1, high[near : near + 1], high[far : far + 1])


def looked_up(table_ref, which, zone):
    value = jnp.full(zone.shape, table_ref[which, 0], F32)
    for label in range(1, table_ref.shape[1]):
        value = jnp.where(zone == float(label), table_ref[which, label], value)
    return value


def coefficient_kernel(
    flags, table_ref, zones_ref, first_x, second_x, first_y, second_y, half_ref, mass_ref, half_rows_ref, mass_rows_ref
):
    size_x, size_y, size_z = zones_ref.shape
    low_x = chosen(flags, EVEN_X, second_x[2:4], first_x[2:4])
    high_x = chosen(flags, EVEN_X, first_x[2:4], second_x[2:4])
    low_y = chosen(flags, EVEN_Y, second_y[2:4], first_y[2:4])
    high_y = chosen(flags, EVEN_Y, first_y[2:4], second_y[2:4])
    inside = slice(8, 8 + size_y)
    for x in range(-2, size_x + 2):
        if x < 0:
            zone = low_x[x + 2]
        elif x >= size_x:
            zone = high_x[x - size_x]
        else:
            zone = zones_ref[x].astype(F32)
        for field in range(2):
            half_ref[field, x + 2, inside] = looked_up(table_ref, field, zone)
        if -1 <= x <= size_x:
            for which in range(3):
                mass_ref[which, x + 1] = looked_up(table_ref, 2 + which, zone)
    for field in range(2):
        for outer in (0, 1):
            half_ref[field, outer, inside] = chosen(
                flags, LOW_X, half_ref[field, outer, inside], half_ref[field, 2, inside]
            )
            place = size_x + 2 + outer
            half_ref[field, place, inside] = chosen(
                flags, HIGH_X, half_ref[field, place, inside], half_ref[field, size_x + 1, inside]
            )
    count = half_rows_ref.shape[2]
    position = lax.broadcasted_iota(jnp.int32, (count, size_z), 0)
    for line, (zone, flag) in enumerate(
        ((low_y[0], LOW_Y), (low_y[1], LOW_Y), (high_y[0], HIGH_Y), (high_y[1], HIGH_Y))
    ):
        for field in range(2):
            value = looked_up(table_ref, field, zone)
            below = value[ROW0 : ROW0 + 1]
            above = value[ROW0 + size_x - 1 : ROW0 + size_x]
            value = jnp.where((position < ROW0) & (flags[LOW_X] == 0), below, value)
            value = jnp.where((position >= ROW0 + size_x) & (flags[HIGH_X] == 0), above, value)
            near = half_ref[field, :, 8 if flag == LOW_Y else 8 + size_y - 1]
            half_rows_ref[field, line] = value
            half_rows_ref[field, line, ROW0 - 2 : ROW0 + size_x + 2] = chosen(
                flags, flag, half_rows_ref[field, line, ROW0 - 2 : ROW0 + size_x + 2], near
            )
            if line in (1, 2):
                row = 7 if line == 1 else 8 + size_y
                half_ref[field, :, row] = half_rows_ref[field, line, ROW0 - 2 : ROW0 + size_x + 2]
        if line in (1, 2):
            for which in range(3):
                mass_rows_ref[which, line - 1] = looked_up(table_ref, 2 + which, zone)
    for field in range(2):
        for line, row in ((4, 8), (5, 8 + size_y - 1)):
            half_rows_ref[field, line] = jnp.zeros((count, size_z), F32)
            half_rows_ref[field, line, ROW0 - 2 : ROW0 + size_x + 2] = half_ref[field, :, row]


def first_solve_kernel(
    flags, load_ref, first_x, second_x, first_y, second_y, inverse_ref, c0, c1, c2, c3,
    part_ref, part_rows_ref, even_ref, odd_ref, field_ref, rows_ref, stack_ref,
):
    size_x = load_ref.shape[1]
    for field in range(2):
        field_ref[field, 1 : 1 + size_x] = load_ref[field]
        field_ref[field, 0] = keep(flags, LOW_X, chosen(flags, EVEN_X, second_x[field], first_x[field]))
        field_ref[field, 1 + size_x] = keep(flags, HIGH_X, chosen(flags, EVEN_X, first_x[field], second_x[field]))
        rows_ref[field, 0] = keep(flags, LOW_Y, chosen(flags, EVEN_Y, second_y[field], first_y[field]))
        rows_ref[field, 1] = keep(flags, HIGH_Y, chosen(flags, EVEN_Y, first_y[field], second_y[field]))
    solve(field_ref, rows_ref, inverse_ref, (c0, c1, c2, c3), stack_ref, part_ref, part_rows_ref)
    pack_x(flags, part_ref, part_rows_ref, even_ref, odd_ref)


def merge_x_kernel(flags, part_ref, part_rows_ref, first_ref, second_ref, whole_ref, whole_rows_ref, even_ref, odd_ref):
    size_x = part_ref.shape[1] - 2
    size_y, size_z = part_ref.shape[2:]
    end = ROW0 + size_x
    for field in range(2):
        low = keep(flags, LOW_X, chosen(flags, EVEN_X, second_ref[field], first_ref[field]))
        high = keep(flags, HIGH_X, chosen(flags, EVEN_X, first_ref[field], second_ref[field]))
        whole_ref[field, 0] = low[0, :size_y]
        whole_ref[field, 1] = keep(flags, LOW_X, part_ref[field, 0]) + low[1, :size_y]
        whole_ref[field, 2] = part_ref[field, 1] + low[2, :size_y]
        whole_ref[field, 3 : size_x + 1] = part_ref[field, 2:size_x]
        whole_ref[field, size_x + 1] = part_ref[field, size_x] + high[0, :size_y]
        whole_ref[field, size_x + 2] = keep(flags, HIGH_X, part_ref[field, size_x + 1]) + high[1, :size_y]
        whole_ref[field, size_x + 3] = high[2, :size_y]
        for side in range(2):
            row = slice(size_y + side, size_y + side + 1)
            whole_rows_ref[field, side] = part_rows_ref[field, side]
            edge = ROW0 - 1
            whole_rows_ref[field, side, edge - 1 : edge] = low[0, row]
            whole_rows_ref[field, side, edge : edge + 1] = (
                keep(flags, LOW_X, part_rows_ref[field, side, edge : edge + 1]) + low[1, row]
            )
            whole_rows_ref[field, side, edge + 1 : edge + 2] = part_rows_ref[field, side, edge + 1 : edge + 2] + low[2, row]
            whole_rows_ref[field, side, end - 1 : end] = part_rows_ref[field, side, end - 1 : end] + high[0, row]
            whole_rows_ref[field, side, end : end + 1] = (
                keep(flags, HIGH_X, part_rows_ref[field, side, end : end + 1]) + high[1, row]
            )
            whole_rows_ref[field, side, end + 1 : end + 2] = high[2, row]
        blank = jnp.zeros((8, size_z), F32)
        spread = slice(ROW0 - 2, end + 2)

        def put(layer, to_low, to_high, place):
            even_ref[field, layer, place] = chosen(flags, EVEN_Y, to_high, to_low)
            odd_ref[field, layer, place] = chosen(flags, EVEN_Y, to_low, to_high)

        for layer in range(3):
            for ref in (even_ref, odd_ref):
                ref[field, layer, 0:8] = blank
                ref[field, layer, size_x : size_x + 8] = blank
        low_rows = whole_rows_ref[field, 0, spread]
        high_rows = whole_rows_ref[field, 1, spread]
        put(0, low_rows, whole_ref[field, :, size_y - 2], spread)
        put(1, whole_ref[field, :, 0], whole_ref[field, :, size_y - 1], spread)
        put(2, whole_ref[field, :, 1], high_rows, spread)


def assemble(flags, whole_ref, whole_rows_ref, first_ref, second_ref, field_ref, lines):
    size_x = whole_ref.shape[1] - 4
    size_y = whole_ref.shape[2]
    spread = slice(ROW0 - 2, ROW0 + size_x + 2)
    for field in range(2):
        low = keep(flags, LOW_Y, chosen(flags, EVEN_Y, second_ref[field], first_ref[field]))
        high = keep(flags, HIGH_Y, chosen(flags, EVEN_Y, first_ref[field], second_ref[field]))
        below = keep(flags, LOW_Y, whole_rows_ref[field, 0]) + low[1]
        above = keep(flags, HIGH_Y, whole_rows_ref[field, 1]) + high[1]
        lines[field, 0] = low[0]
        lines[field, 1] = below
        lines[field, 2] = above
        lines[field, 3] = high[2]
        lines[field, 4] = low[2]
        lines[field, 5] = high[0]
        field_ref[field, :, 8 : 8 + size_y] = whole_ref[field]
        field_ref[field, :, 7] = lines[field, 1, spread]
        field_ref[field, :, 8 + size_y] = lines[field, 2, spread]
        field_ref[field, :, 8] = field_ref[field, :, 8] + lines[field, 4, spread]
        field_ref[field, :, 7 + size_y] = field_ref[field, :, 7 + size_y] + lines[field, 5, spread]


def along_z(value, half):
    size_z = value.shape[-1]
    lane = lax.broadcasted_iota(jnp.int32, value.shape, value.ndim - 1)
    axis = value.ndim - 1
    last = lane == size_z - 1
    beside = jnp.where(last, 0.0, pltpu.roll(value, size_z - 1, axis))
    half_beside = jnp.where(last, half, pltpu.roll(half, size_z - 1, axis))
    upper = (half + half_beside) * (value - beside)
    lower = jnp.where(lane == 0, -2.0 * half * value, pltpu.roll(upper, 1, axis))
    return upper - lower


def operate(field_ref, half_ref, mass_ref, x):
    size_y = mass_ref.shape[2]
    inside = slice(8, 8 + size_y)
    values, images = [], []
    for field in range(2):
        value = field_ref[field, x + 2, inside]
        half = half_ref[field, x + 2, inside]
        flux = along_z(value, half)
        for place in (x + 1, x + 3):
            flux = flux + (half + half_ref[field, place, inside]) * (value - field_ref[field, place, inside])
        for shift in (-1, 1):
            moved = slice(8 + shift, 8 + shift + size_y)
            flux = flux + (half + half_ref[field, x + 2, moved]) * (value - field_ref[field, x + 2, moved])
        values.append(value)
        images.append(flux)
    first = mass_ref[0, x + 1] * values[0] + mass_ref[2, x + 1] * values[1] + images[0]
    second = mass_ref[2, x + 1] * values[0] + mass_ref[1, x + 1] * values[1] + images[1]
    return values, (first, second)


def operate_line(lines, half_lines, mass_lines, side, near):
    outer, center, inner = (0, 1, 4) if side == 0 else (3, 2, 5)
    values, images = [], []
    for field in range(2):
        value = lines[field, center]
        half = half_lines[field, center]
        count = value.shape[0]
        flux = along_z(value, half)
        for turn in (1, count - 1):
            flux = flux + (half + pltpu.roll(half, turn, 0)) * (value - pltpu.roll(value, turn, 0))
        flux = flux + (half + half_lines[field, outer]) * (value - lines[field, outer])
        flux = flux + (half + half_lines[field, inner]) * (value - near[field, side])
        values.append(value)
        images.append(flux)
    first = mass_lines[0, side] * values[0] + mass_lines[2, side] * values[1] + images[0]
    second = mass_lines[2, side] * values[0] + mass_lines[1, side] * values[1] + images[1]
    return first, second


def second_solve_kernel(
    flags, whole_ref, whole_rows_ref, first_ref, second_ref, half_ref, mass_ref, half_lines, mass_lines, load_ref,
    inverse_ref, c0, c1, c2, c3,
    precond_ref, image_ref, sums_ref, part_ref, part_rows_ref, even_ref, odd_ref,
    value_ref, lines, near, field_ref, rows_ref, stack_ref,
):
    size_x, size_y, size_z = load_ref.shape[1:]
    assemble(flags, whole_ref, whole_rows_ref, first_ref, second_ref, value_ref, lines)
    zero = jnp.zeros((size_y, size_z), F32)
    total_a, total_b = zero, zero
    for x in range(-1, size_x + 1):
        values, images = operate(value_ref, half_ref, mass_ref, x)
        for field in range(2):
            image = images[field]
            if x == -1:
                image = keep(flags, LOW_X, image)
            elif x == size_x:
                image = keep(flags, HIGH_X, image)
            else:
                precond_ref[field, x] = values[field]
                image_ref[field, x] = image
                total_a = total_a + load_ref[field, x] * values[field]
                total_b = total_b + image * values[field]
            field_ref[field, x + 1] = image
    sums_ref[0:1] = jnp.sum(total_a, axis=0, keepdims=True)
    sums_ref[1:2] = jnp.sum(total_b, axis=0, keepdims=True)
    sums_ref[2:8] = jnp.zeros((6, size_z), F32)
    count = rows_ref.shape[2]
    position = lax.broadcasted_iota(jnp.int32, (count, size_z), 0)
    begin = jnp.where(flags[LOW_X] > 0, ROW0 - 1, ROW0)
    end = jnp.where(flags[HIGH_X] > 0, ROW0 + size_x + 1, ROW0 + size_x)
    valid = (position >= begin) & (position < end)
    for field in range(2):
        for side, row in ((0, 8), (1, 7 + size_y)):
            near[field, side] = jnp.zeros((count, size_z), F32)
            near[field, side, ROW0 - 2 : ROW0 + size_x + 2] = value_ref[field, :, row]
    for side, flag in ((0, LOW_Y), (1, HIGH_Y)):
        images = operate_line(lines, half_lines, mass_lines, side, near)
        for field in range(2):
            rows_ref[field, side] = keep(flags, flag, jnp.where(valid, images[field], 0.0))
    solve(field_ref, rows_ref, inverse_ref, (c0, c1, c2, c3), stack_ref, part_ref, part_rows_ref)
    pack_x(flags, part_ref, part_rows_ref, even_ref, odd_ref)


def second_image_kernel(
    flags, whole_ref, whole_rows_ref, first_ref, second_ref, half_ref, mass_ref, old_image_ref, old_sums_ref,
    precond_ref, image_ref, sums_ref, value_ref, lines,
):
    size_x, size_y, size_z = old_image_ref.shape[1:]
    assemble(flags, whole_ref, whole_rows_ref, first_ref, second_ref, value_ref, lines)
    zero = jnp.zeros((size_y, size_z), F32)
    total_c, total_d = zero, zero
    for x in range(size_x):
        values, images = operate(value_ref, half_ref, mass_ref, x)
        for field in range(2):
            precond_ref[field, x] = values[field]
            image_ref[field, x] = images[field]
            total_c = total_c + old_image_ref[field, x] * values[field]
            total_d = total_d + images[field] * values[field]
    totals = [
        jnp.sum(old_sums_ref[0:1], axis=1, keepdims=True),
        jnp.sum(old_sums_ref[1:2], axis=1, keepdims=True),
        jnp.sum(jnp.sum(total_c, axis=0, keepdims=True), axis=1, keepdims=True),
        jnp.sum(jnp.sum(total_d, axis=0, keepdims=True), axis=1, keepdims=True),
    ]
    lane = lax.broadcasted_iota(jnp.int32, sums_ref.shape, 1)
    spread = jnp.zeros(sums_ref.shape, F32)
    for place, total in enumerate(totals):
        spread = jnp.where(lane == place, total, spread)
    sums_ref[...] = spread


def finish_kernel(sums_ref, load_ref, z_ref, q_ref, w_ref, s_ref, solution_ref, residual_ref):
    line = jnp.sum(sums_ref[...], axis=0, keepdims=True)
    lane = lax.broadcasted_iota(jnp.int32, line.shape, 1)
    rz, zq, qw, ws = [jnp.sum(jnp.where(lane == place, line, 0.0), axis=1, keepdims=True) for place in range(4)]
    alpha = rz / zq
    rz_next = rz - alpha * (2.0 * zq) + alpha * alpha * qw
    grown = 1.0 + rz_next / rz
    curvature = grown * grown * zq - 2.0 * grown * alpha * qw + alpha * alpha * ws
    alpha_next = rz_next / curvature
    along = alpha + alpha_next * grown
    against = alpha_next * alpha
    for field in range(2):
        for x in range(load_ref.shape[1]):
            solution_ref[field, x] = along * z_ref[field, x] - against * w_ref[field, x]
            residual_ref[field, x] = load_ref[field, x] - along * q_ref[field, x] + against * s_ref[field, x]


SMEM = pl.BlockSpec(memory_space=pltpu.SMEM)
VMEM = pl.BlockSpec(memory_space=pltpu.VMEM)


def call(kernel, scalars, arrays, outs, scratch=(), flops=0, limit=24):
    moved = sum(math.prod(a.shape) * a.dtype.itemsize for a in list(arrays) + list(outs))
    return pl.pallas_call(
        kernel,
        out_shape=tuple(outs),
        in_specs=[SMEM] * len(scalars) + [VMEM] * len(arrays),
        out_specs=tuple([VMEM] * len(outs)),
        scratch_shapes=list(scratch),
        compiler_params=pltpu.CompilerParams(vmem_limit_bytes=limit * 1024 * 1024),
        cost_estimate=pl.CostEstimate(flops=flops, bytes_accessed=moved, transcendentals=0),
    )(*scalars, *arrays)


def shards(mesh, load, zones, conductance, capacity, coupling):
    size_x, size_y, size_z = zones.shape
    assert size_x % BOX == 0 and size_y == BOX and size_z % BOX == 0
    boxes = size_x // BOX
    count = size_x + 8
    sds = lambda *shape: jax.ShapeDtypeStruct(shape, F32)
    forward, back, line_forward, line_back, summed, means = [jnp.asarray(c) for c in constants(size_z)]
    consts = (forward, back, line_forward, line_back)
    modes, lanes = summed.shape
    cross = coupling * jnp.sqrt(capacity[0] * capacity[1])
    table = jnp.concatenate([0.5 * conductance, capacity, cross[None]], axis=0)
    here_x, here_y = lax.axis_index("gx"), lax.axis_index("gy")
    even_x, even_y = here_x % 2 == 0, here_y % 2 == 0
    flags = jnp.stack(
        [even_x, even_y, here_x > 0, here_x < mesh.shape["gx"] - 1, here_y > 0, here_y < mesh.shape["gy"] - 1]
    ).astype(jnp.int32)

    to_low = jnp.concatenate([load[:, 0], zones[:2].astype(F32)], axis=0)
    to_high = jnp.concatenate([load[:, -1], zones[-2:].astype(F32)], axis=0)
    x_halo = swap(mesh, "gx", jnp.where(even_x, to_high, to_low), jnp.where(even_x, to_low, to_high))

    (inverse,) = call(
        divisor_kernel, [table], [zones, summed, means], [sds(2 * boxes, modes, lanes)], flops=40_000_000
    )
    y_halo = swap(
        mesh, "gy", *call(edge_rows_kernel, [flags], [load, zones, *x_halo], [sds(4, count, size_z)] * 2)
    )
    half, mass, half_lines, mass_lines = call(
        coefficient_kernel,
        [flags, table],
        [zones, *x_halo, *y_halo],
        [
            sds(2, size_x + 4, size_y + 16, size_z),
            sds(3, size_x + 2, size_y, size_z),
            sds(2, 6, count, size_z),
            sds(3, 2, count, size_z),
        ],
        flops=20_000_000,
    )
    parts = [sds(2, size_x + 2, size_y, size_z), sds(2, 2, count, size_z)]
    packed_x = [sds(2, 3, size_y + 8, size_z)] * 2
    wholes = [sds(2, size_x + 4, size_y, size_z), sds(2, 2, count, size_z)]
    packed_y = [sds(2, 3, count, size_z)] * 2
    rows = SPAN * size_y + 48
    work = [
        pltpu.VMEM((2, size_x + 2, size_y, size_z), F32),
        pltpu.VMEM((2, 2, count, size_z), F32),
        pltpu.VMEM((3 * rows, boxes * size_z), BF16),
    ]
    padded = [
        pltpu.VMEM((2, size_x + 4, size_y + 16, size_z), F32),
        pltpu.VMEM((2, 6, count, size_z), F32),
    ]
    own = sds(2, size_x, size_y, size_z)

    part, part_rows, *packed = call(
        first_solve_kernel, [flags], [load, *x_halo, *y_halo, inverse, *consts], parts + packed_x, work, 3_000_000_000
    )
    received = swap(mesh, "gx", *packed)
    whole, whole_rows, *packed = call(merge_x_kernel, [flags], [part, part_rows, *received], wholes + packed_y)
    received = swap(mesh, "gy", *packed)
    precond, image, sums, part, part_rows, *packed = call(
        second_solve_kernel,
        [flags],
        [whole, whole_rows, *received, half, mass, half_lines, mass_lines, load, inverse, *consts],
        [own, own, sds(8, size_z)] + parts + packed_x,
        padded + [pltpu.VMEM((2, 2, count, size_z), F32)] + work,
        3_000_000_000,
    )
    received = swap(mesh, "gx", *packed)
    whole, whole_rows, *packed = call(merge_x_kernel, [flags], [part, part_rows, *received], wholes + packed_y)
    received = swap(mesh, "gy", *packed)
    devices = mesh.shape["gx"] * mesh.shape["gy"]
    last_precond, last_image, sums = call(
        second_image_kernel,
        [flags],
        [whole, whole_rows, *received, half, mass, image, sums],
        [own, own, sds(devices, size_z)],
        padded,
        10_000_000,
    )
    sums = lax.all_to_all(sums, AXES, 0, 0, tiled=True)
    return call(finish_kernel, [], [sums, load, precond, image, last_precond, last_image], [own, own])


def solution(mesh):
    in_specs = (P(None, "gx", "gy", None), P("gx", "gy", None), P(), P(), P())
    out_specs = (P(None, "gx", "gy", None), P(None, "gx", "gy", None))
    return jax.shard_map(
        functools.partial(shards, mesh), mesh=mesh, in_specs=in_specs, out_specs=out_specs, check_vma=False
    )
```

```python
import functools
import math

import jax
import jax.numpy as jnp
import ml_dtypes
import numpy as np
from jax import lax
from jax.experimental import pallas as pl
from jax.experimental.pallas import tpu as pltpu
from jax.sharding import PartitionSpec as P

BOX = 16
SPAN = BOX + 2
F32 = jnp.float32
BF16 = jnp.bfloat16
AXES = ("gx", "gy")
ROW0 = 4
CHUNK = 4


def split(matrix):
    high = matrix.astype(ml_dtypes.bfloat16)
    low = (matrix - high.astype(np.float64)).astype(ml_dtypes.bfloat16)
    return high, low


def round_up(value, step):
    return (value + step - 1) // step * step


def sine_basis():
    index = np.arange(SPAN)
    angle = np.pi * np.outer(index + 1, index + 1) / (SPAN + 1)
    return np.sqrt(2.0 / (SPAN + 1)) * np.sin(angle)


def eigenvalues():
    return 4.0 * np.sin(np.pi * (np.arange(SPAN) + 1) / (2 * (SPAN + 1))) ** 2


def plane_layout():
    places = [(x, y + 1) for x in range(SPAN) for y in range(BOX)]
    for y in (0, SPAN - 1):
        for position in range(24):
            x = position - (ROW0 - 1)
            places.append((x, y) if 0 <= x < SPAN else None)
    return places


def constants(size_z):
    basis = sine_basis()
    places = plane_layout()
    rows = len(places)
    modes = SPAN * SPAN
    padded_modes = round_up(modes, 16)
    plane = np.zeros((padded_modes, rows))
    for column, place in enumerate(places):
        if place is not None:
            plane[:modes, column] = np.outer(basis[:, place[0]], basis[:, place[1]]).reshape(-1)
    high, low = split(plane)
    forward = np.concatenate([high, high, low], axis=1)
    high, low = split(plane.T)
    inverse = np.concatenate([high, high, low], axis=1)
    boxes = size_z // BOX
    line = np.zeros((size_z, boxes * SPAN))
    means = np.zeros((size_z, boxes * SPAN))
    for box in range(boxes):
        for mode in range(SPAN):
            for offset in range(SPAN):
                cell = box * BOX + offset - 1
                if 0 <= cell < size_z:
                    line[cell, box * SPAN + mode] = basis[mode, offset]
        means[box * BOX : (box + 1) * BOX, box * SPAN : (box + 1) * SPAN] = 1.0 / BOX**3
    high, low = split(line)
    line_forward = np.concatenate([high, high, low], axis=0)
    high, low = split(line.T)
    line_inverse = np.concatenate([high, low], axis=1)
    eigen = eigenvalues()
    pair = np.zeros(padded_modes)
    pair[:modes] = (eigen[:, None] + eigen[None, :]).reshape(-1)
    summed = (pair[:, None] + np.tile(eigen, boxes)[None, :]).astype(np.float32)
    return forward, inverse, line_forward, line_inverse, summed, means.astype(np.float32)


def swap_pairs(mesh, axis, odd):
    sizes = [mesh.shape[name] for name in AXES]
    along = AXES.index(axis)
    pairs = []
    for i in range(sizes[0]):
        for j in range(sizes[1]):
            here = [i, j]
            there = [i, j]
            place = here[along]
            target = place ^ 1 if not odd else (place + 1 if place % 2 else place - 1)
            if 0 <= target < sizes[along]:
                there[along] = target
            elif along == 0:
                there[0] = sizes[0] - 1 - place
            else:
                there[0] = i ^ 1
            pairs.append((here[0] * sizes[1] + here[1], there[0] * sizes[1] + there[1]))
    return pairs


def swap(mesh, axis, even_part, odd_part):
    if axis == "gx":
        first = lax.ppermute(even_part, AXES, swap_pairs(mesh, axis, False))
        second = lax.ppermute(odd_part, AXES, swap_pairs(mesh, axis, True))
    else:
        second = lax.ppermute(odd_part, AXES, swap_pairs(mesh, axis, True))
        first = lax.ppermute(even_part, AXES, swap_pairs(mesh, axis, False))
    return first, second


EVEN_X, EVEN_Y, LOW_X, HIGH_X, LOW_Y, HIGH_Y = range(6)


def chosen(flags, which, yes, no):
    return jnp.where(flags[which] > 0, yes, no)


def keep(flags, which, value):
    return jnp.where(flags[which] > 0, value, jnp.zeros_like(value))


def halves(value):
    high = value.astype(BF16)
    low = (value - high.astype(F32)).astype(BF16)
    return high, low


def dot(left, right):
    return jnp.dot(left, right, preferred_element_type=F32)


def solve(field_ref, rows_ref, inverse_ref, consts, stack_ref, out_ref, out_rows_ref):
    forward_ref, back_ref, line_forward_ref, line_back_ref = consts
    boxes = (field_ref.shape[1] - 2) // BOX
    size_y, size_z = field_ref.shape[2:]
    inner = SPAN * size_y
    rows = inner + 48
    line_rows = line_forward_ref.shape[0] // 3
    for field in range(2):
        for box in range(boxes):
            start = box * BOX
            main = field_ref[field, start : start + SPAN].reshape(inner, size_z)
            lanes = slice(box * size_z, (box + 1) * size_z)
            parts = (
                (0, main),
                (inner, rows_ref[field, 0, start : start + 24]),
                (inner + 24, rows_ref[field, 1, start : start + 24]),
            )
            whole = jnp.concatenate([part for _, part in parts], axis=0)
            high, low = halves(whole)
            stack_ref[0:rows, lanes] = high
            stack_ref[rows : 2 * rows, lanes] = low
            stack_ref[2 * rows : 3 * rows, lanes] = high
        spectral = dot(forward_ref[...], stack_ref[...])
        for box in range(boxes):
            lanes = slice(box * size_z, (box + 1) * size_z)
            high, low = halves(spectral[:, lanes])
            both = jnp.concatenate([high, low], axis=1)
            modes = dot(both, line_forward_ref[0 : 2 * line_rows]) + dot(high, line_forward_ref[2 * line_rows :])
            modes = modes * inverse_ref[field * boxes + box]
            high, low = halves(modes)
            cells = dot(high, line_back_ref[...])
            cells = cells[:, :size_z] + (cells[:, size_z:] + dot(low, line_back_ref[:, :size_z]))
            high, low = halves(cells)
            stack_ref[0:rows, lanes] = high
            stack_ref[rows : 2 * rows, lanes] = low
            stack_ref[2 * rows : 3 * rows, lanes] = high
        result = dot(back_ref[...], stack_ref[...])
        for box in range(boxes):
            lanes = slice(box * size_z, (box + 1) * size_z)
            start = box * BOX
            main = result[:inner, lanes].reshape(SPAN, size_y, size_z)
            if box == 0:
                out_ref[field, 0:SPAN] = main
            else:
                out_ref[field, start : start + 2] = out_ref[field, start : start + 2] + main[0:2]
                out_ref[field, start + 2 : start + SPAN] = main[2:]
            for side in range(2):
                strip = result[inner + 24 * side : inner + 24 * side + 24, lanes]
                if box == 0:
                    out_rows_ref[field, side, 0:24] = strip
                else:
                    out_rows_ref[field, side, start : start + 8] = (
                        out_rows_ref[field, side, start : start + 8] + strip[0:8]
                    )
                    out_rows_ref[field, side, start + 8 : start + 24] = strip[8:]


def pack_x(flags, part_ref, part_rows_ref, even_ref, odd_ref):
    last = part_ref.shape[1] - 1
    depth = even_ref.shape[1]
    size_y = part_ref.shape[2]
    for field in range(2):
        for layer in range(depth):
            low, high = layer, last + 1 - depth + layer
            for side, place in ((None, slice(0, size_y)), (0, slice(size_y, size_y + 1)), (1, slice(size_y + 1, size_y + 2))):
                if side is None:
                    to_low, to_high = part_ref[field, low], part_ref[field, high]
                else:
                    shift = ROW0 - 1
                    to_low = part_rows_ref[field, side, low + shift : low + shift + 1]
                    to_high = part_rows_ref[field, side, high + shift : high + shift + 1]
                even_ref[field, layer, place] = chosen(flags, EVEN_X, to_high, to_low)
                odd_ref[field, layer, place] = chosen(flags, EVEN_X, to_low, to_high)
            rest = even_ref.shape[2] - size_y - 2
            blank = jnp.zeros((rest, even_ref.shape[3]), F32)
            even_ref[field, layer, size_y + 2 :] = blank
            odd_ref[field, layer, size_y + 2 :] = blank


def divisor_kernel(table_ref, zones_ref, summed_ref, means_ref, inverse_ref):
    size_x, size_y, size_z = zones_ref.shape
    boxes = size_x // BOX
    lines = []
    for which in (2, 3, 0, 1):
        for box in range(boxes):
            total = jnp.zeros((size_y, size_z), F32)
            for x in range(box * BOX, (box + 1) * BOX):
                zone = zones_ref[x]
                value = jnp.full((size_y, size_z), table_ref[which, 0], F32)
                for label in range(1, table_ref.shape[1]):
                    value = jnp.where(zone == label, table_ref[which, label], value)
                total = total + value
            lines.append(jnp.sum(total, axis=0, keepdims=True))
    sums = jnp.concatenate(lines, axis=0)
    means = jnp.dot(sums, means_ref[...], preferred_element_type=F32, precision=lax.Precision.HIGHEST)
    half = 2 * boxes
    for combo in range(half):
        cbar = means[combo : combo + 1]
        kbar = 2.0 * means[half + combo : half + combo + 1]
        inverse_ref[combo] = 1.0 / (cbar + kbar * summed_ref[...])


def edge_rows_kernel(flags, load_ref, zones_ref, first_ref, second_ref, even_ref, odd_ref):
    size_x, size_y, size_z = zones_ref.shape
    from_low = chosen(flags, EVEN_X, second_ref[...], first_ref[...])
    from_high = chosen(flags, EVEN_X, first_ref[...], second_ref[...])
    blank = jnp.zeros((8, size_z), F32)
    for channel in range(4):
        for ref in (even_ref, odd_ref):
            ref[channel, 0:8] = blank
            ref[channel, size_x : size_x + 8] = blank

    def put(channel, position, count, to_low, to_high):
        place = slice(position, position + count)
        even_ref[channel, place] = chosen(flags, EVEN_Y, to_high, to_low)
        odd_ref[channel, place] = chosen(flags, EVEN_Y, to_low, to_high)

    end = ROW0 + size_x
    for field in range(2):
        put(field, ROW0, size_x, load_ref[field, :, 0], load_ref[field, :, size_y - 1])
        low = keep(flags, LOW_X, from_low[field])
        high = keep(flags, HIGH_X, from_high[field])
        put(field, ROW0 - 1, 1, low[0:1], low[size_y - 1 : size_y])
        put(field, end, 1, high[0:1], high[size_y - 1 : size_y])
    for layer in range(2):
        channel = 2 + layer
        near, far = layer, size_y - 2 + layer
        put(channel, ROW0, size_x, zones_ref[:, near].astype(F32), zones_ref[:, far].astype(F32))
        for depth in range(2):
            low, high = from_low[2 + depth], from_high[2 + depth]
            put(channel, ROW0 - 2 + depth, 1, low[near : near + 1], low[far : far + 1])
            put(channel, end + depth, 1, high[near : near + 1], high[far : far + 1])


def looked_up(table_ref, which, zone):
    value = jnp.full(zone.shape, table_ref[which, 0], F32)
    for label in range(1, table_ref.shape[1]):
        value = jnp.where(zone == float(label), table_ref[which, label], value)
    return value


def coefficient_kernel(
    flags, table_ref, zones_ref, first_x, second_x, first_y, second_y,
    half_ref, mass_ref, face_ref, half_rows_ref, mass_rows_ref, face_rows_ref,
):
    size_x, size_y, size_z = zones_ref.shape
    low_x = chosen(flags, EVEN_X, second_x[2:4], first_x[2:4])
    high_x = chosen(flags, EVEN_X, first_x[2:4], second_x[2:4])
    low_y = chosen(flags, EVEN_Y, second_y[2:4], first_y[2:4])
    high_y = chosen(flags, EVEN_Y, first_y[2:4], second_y[2:4])
    inside = slice(8, 8 + size_y)
    for x in range(-2, size_x + 2):
        if x < 0:
            zone = low_x[x + 2]
        elif x >= size_x:
            zone = high_x[x - size_x]
        else:
            zone = zones_ref[x].astype(F32)
        for field in range(2):
            half_ref[field, x + 2, inside] = looked_up(table_ref, field, zone)
        if -1 <= x <= size_x:
            for which in range(3):
                mass_ref[which, x + 1] = looked_up(table_ref, 2 + which, zone)
    for field in range(2):
        for outer in (0, 1):
            half_ref[field, outer, inside] = chosen(
                flags, LOW_X, half_ref[field, outer, inside], half_ref[field, 2, inside]
            )
            place = size_x + 2 + outer
            half_ref[field, place, inside] = chosen(
                flags, HIGH_X, half_ref[field, place, inside], half_ref[field, size_x + 1, inside]
            )
    count = half_rows_ref.shape[2]
    position = lax.broadcasted_iota(jnp.int32, (count, size_z), 0)
    for line, (zone, flag) in enumerate(
        ((low_y[0], LOW_Y), (low_y[1], LOW_Y), (high_y[0], HIGH_Y), (high_y[1], HIGH_Y))
    ):
        for field in range(2):
            value = looked_up(table_ref, field, zone)
            below = value[ROW0 : ROW0 + 1]
            above = value[ROW0 + size_x - 1 : ROW0 + size_x]
            value = jnp.where((position < ROW0) & (flags[LOW_X] == 0), below, value)
            value = jnp.where((position >= ROW0 + size_x) & (flags[HIGH_X] == 0), above, value)
            near = half_ref[field, :, 8 if flag == LOW_Y else 8 + size_y - 1]
            half_rows_ref[field, line] = value
            half_rows_ref[field, line, ROW0 - 2 : ROW0 + size_x + 2] = chosen(
                flags, flag, half_rows_ref[field, line, ROW0 - 2 : ROW0 + size_x + 2], near
            )
            if line in (1, 2):
                row = 7 if line == 1 else 8 + size_y
                half_ref[field, :, row] = half_rows_ref[field, line, ROW0 - 2 : ROW0 + size_x + 2]
        if line in (1, 2):
            for which in range(3):
                mass_rows_ref[which, line - 1] = looked_up(table_ref, 2 + which, zone)
    for field in range(2):
        for x in range(0, size_x + 2, 2):
            faces = faces_z(half_ref[field, x + 1 : x + 3, inside])
            for way in range(2):
                face_ref[field, way, x : x + 2] = faces[way]
        for side in range(2):
            faces = faces_z(half_rows_ref[field, side + 1])
            for way in range(2):
                face_rows_ref[field, way, side] = faces[way]
        for line, row in ((4, 8), (5, 8 + size_y - 1)):
            half_rows_ref[field, line] = jnp.zeros((count, size_z), F32)
            half_rows_ref[field, line, ROW0 - 2 : ROW0 + size_x + 2] = half_ref[field, :, row]


def first_solve_kernel(
    flags, load_ref, first_x, second_x, first_y, second_y, inverse_ref, c0, c1, c2, c3,
    part_ref, part_rows_ref, even_ref, odd_ref, field_ref, rows_ref, stack_ref,
):
    size_x = load_ref.shape[1]
    for field in range(2):
        field_ref[field, 1 : 1 + size_x] = load_ref[field]
        field_ref[field, 0] = keep(flags, LOW_X, chosen(flags, EVEN_X, second_x[field], first_x[field]))
        field_ref[field, 1 + size_x] = keep(flags, HIGH_X, chosen(flags, EVEN_X, first_x[field], second_x[field]))
        rows_ref[field, 0] = keep(flags, LOW_Y, chosen(flags, EVEN_Y, second_y[field], first_y[field]))
        rows_ref[field, 1] = keep(flags, HIGH_Y, chosen(flags, EVEN_Y, first_y[field], second_y[field]))
    solve(field_ref, rows_ref, inverse_ref, (c0, c1, c2, c3), stack_ref, part_ref, part_rows_ref)
    pack_x(flags, part_ref, part_rows_ref, even_ref, odd_ref)


def merge_x_kernel(flags, part_ref, part_rows_ref, first_ref, second_ref, whole_ref, whole_rows_ref, even_ref, odd_ref):
    size_x = part_ref.shape[1] - 2
    size_y, size_z = part_ref.shape[2:]
    depth = first_ref.shape[1]
    count = part_rows_ref.shape[2]
    end = ROW0 + size_x
    for field in range(2):
        low = keep(flags, LOW_X, chosen(flags, EVEN_X, second_ref[field], first_ref[field]))
        high = keep(flags, HIGH_X, chosen(flags, EVEN_X, first_ref[field], second_ref[field]))
        whole_ref[field, 1] = keep(flags, LOW_X, part_ref[field, 0]) + low[depth - 2, :size_y]
        whole_ref[field, 2] = part_ref[field, 1] + low[depth - 1, :size_y]
        whole_ref[field, 3 : size_x + 1] = part_ref[field, 2:size_x]
        whole_ref[field, size_x + 1] = part_ref[field, size_x] + high[0, :size_y]
        whole_ref[field, size_x + 2] = keep(flags, HIGH_X, part_ref[field, size_x + 1]) + high[1, :size_y]
        if depth == 3:
            whole_ref[field, 0] = low[0, :size_y]
            whole_ref[field, size_x + 3] = high[2, :size_y]
        for side in range(2):
            row = slice(size_y + side, size_y + side + 1)
            edge = ROW0 - 1
            whole_rows_ref[field, side] = part_rows_ref[field, side]
            whole_rows_ref[field, side, edge : edge + 1] = (
                keep(flags, LOW_X, part_rows_ref[field, side, edge : edge + 1]) + low[depth - 2, row]
            )
            whole_rows_ref[field, side, edge + 1 : edge + 2] = (
                part_rows_ref[field, side, edge + 1 : edge + 2] + low[depth - 1, row]
            )
            whole_rows_ref[field, side, end - 1 : end] = part_rows_ref[field, side, end - 1 : end] + high[0, row]
            whole_rows_ref[field, side, end : end + 1] = (
                keep(flags, HIGH_X, part_rows_ref[field, side, end : end + 1]) + high[1, row]
            )
            if depth == 3:
                whole_rows_ref[field, side, edge - 1 : edge] = low[0, row]
                whole_rows_ref[field, side, end + 1 : end + 2] = high[2, row]

        def put(at, to_low, to_high):
            even_ref[(field, *at)] = chosen(flags, EVEN_Y, to_high, to_low)
            odd_ref[(field, *at)] = chosen(flags, EVEN_Y, to_low, to_high)

        if depth == 3:
            blank = jnp.zeros((8, size_z), F32)
            for layer in range(3):
                for ref in (even_ref, odd_ref):
                    ref[field, layer, 0:8] = blank
                    ref[field, layer, count - 8 : count] = blank
            rows = slice(ROW0 - 2, end + 2)
            low_rows = whole_rows_ref[field, 0, rows]
            high_rows = whole_rows_ref[field, 1, rows]
            put((0, rows), low_rows, whole_ref[field, :, size_y - 2])
            put((1, rows), whole_ref[field, :, 0], whole_ref[field, :, size_y - 1])
            put((2, rows), whole_ref[field, :, 1], high_rows)
        else:
            own = slice(2, size_x + 2)
            put((slice(0, size_x),), whole_ref[field, own, 0], whole_ref[field, own, size_y - 1])
            put((slice(size_x, None),), whole_rows_ref[field, 0], whole_rows_ref[field, 1])


def assemble(flags, whole_ref, whole_rows_ref, first_ref, second_ref, field_ref, lines):
    size_x = whole_ref.shape[1] - 4
    size_y = whole_ref.shape[2]
    spread = slice(ROW0 - 2, ROW0 + size_x + 2)
    for field in range(2):
        low = keep(flags, LOW_Y, chosen(flags, EVEN_Y, second_ref[field], first_ref[field]))
        high = keep(flags, HIGH_Y, chosen(flags, EVEN_Y, first_ref[field], second_ref[field]))
        below = keep(flags, LOW_Y, whole_rows_ref[field, 0]) + low[1]
        above = keep(flags, HIGH_Y, whole_rows_ref[field, 1]) + high[1]
        lines[field, 0] = low[0]
        lines[field, 1] = below
        lines[field, 2] = above
        lines[field, 3] = high[2]
        lines[field, 4] = low[2]
        lines[field, 5] = high[0]
        field_ref[field, :, 8 : 8 + size_y] = whole_ref[field]
        field_ref[field, :, 7] = lines[field, 1, spread]
        field_ref[field, :, 8 + size_y] = lines[field, 2, spread]
        field_ref[field, :, 8] = field_ref[field, :, 8] + lines[field, 4, spread]
        field_ref[field, :, 7 + size_y] = field_ref[field, :, 7 + size_y] + lines[field, 5, spread]


def faces_z(half):
    size_z, axis = half.shape[-1], half.ndim - 1
    lane = lax.broadcasted_iota(jnp.int32, half.shape, axis)
    upper = half + jnp.where(lane == size_z - 1, half, pltpu.roll(half, size_z - 1, axis))
    lower = half + jnp.where(lane == 0, half, pltpu.roll(half, 1, axis))
    return upper, lower


def along_z(value, upper, lower):
    size_z, axis = value.shape[-1], value.ndim - 1
    lane = lax.broadcasted_iota(jnp.int32, value.shape, axis)
    above = jnp.where(lane == size_z - 1, 0.0, pltpu.roll(value, size_z - 1, axis))
    below = jnp.where(lane == 0, 0.0, pltpu.roll(value, 1, axis))
    return upper * (value - above) + lower * (value - below)


def operate(field_ref, half_ref, mass_ref, face_ref, x, count):
    size_y = mass_ref.shape[2]
    inside = slice(8, 8 + size_y)
    masses = slice(x + 1, x + 1 + count)
    here = slice(x + 2, x + 2 + count)
    values, images = [], []
    for field in range(2):
        value = field_ref[field, here, inside]
        half = half_ref[field, here, inside]
        flux = along_z(value, face_ref[field, 0, masses], face_ref[field, 1, masses])
        for start in (x + 1, x + 3):
            place = slice(start, start + count)
            flux = flux + (half + half_ref[field, place, inside]) * (value - field_ref[field, place, inside])
        for shift in (-1, 1):
            moved = slice(8 + shift, 8 + shift + size_y)
            flux = flux + (half + half_ref[field, here, moved]) * (value - field_ref[field, here, moved])
        values.append(value)
        images.append(flux)
    first = mass_ref[0, masses] * values[0] + mass_ref[2, masses] * values[1] + images[0]
    second = mass_ref[2, masses] * values[0] + mass_ref[1, masses] * values[1] + images[1]
    return values, (first, second)


def operate_line(lines, half_lines, mass_lines, face_lines, side, near):
    outer, center, inner = (0, 1, 4) if side == 0 else (3, 2, 5)
    values, images = [], []
    for field in range(2):
        value = lines[field, center]
        half = half_lines[field, center]
        count = value.shape[0]
        flux = along_z(value, face_lines[field, 0, side], face_lines[field, 1, side])
        for turn in (1, count - 1):
            flux = flux + (half + pltpu.roll(half, turn, 0)) * (value - pltpu.roll(value, turn, 0))
        flux = flux + (half + half_lines[field, outer]) * (value - lines[field, outer])
        flux = flux + (half + half_lines[field, inner]) * (value - near[field, side])
        values.append(value)
        images.append(flux)
    first = mass_lines[0, side] * values[0] + mass_lines[2, side] * values[1] + images[0]
    second = mass_lines[2, side] * values[0] + mass_lines[1, side] * values[1] + images[1]
    return first, second


def second_solve_kernel(
    flags, whole_ref, whole_rows_ref, first_ref, second_ref,
    half_ref, mass_ref, face_ref, half_lines, mass_lines, face_lines, load_ref, inverse_ref, c0, c1, c2, c3,
    precond_ref, image_ref, sums_ref, part_ref, part_rows_ref, even_ref, odd_ref,
    value_ref, lines, near, field_ref, rows_ref, stack_ref,
):
    size_x, size_y, size_z = load_ref.shape[1:]
    assemble(flags, whole_ref, whole_rows_ref, first_ref, second_ref, value_ref, lines)
    for x, flag in ((-1, LOW_X), (size_x, HIGH_X)):
        _, images = operate(value_ref, half_ref, mass_ref, face_ref, x, 1)
        for field in range(2):
            field_ref[field, x + 1 : x + 2] = keep(flags, flag, images[field])
    total_a = total_b = jnp.zeros((CHUNK, size_y, size_z), F32)
    for x in range(0, size_x, CHUNK):
        chunk = slice(x, x + CHUNK)
        values, images = operate(value_ref, half_ref, mass_ref, face_ref, x, CHUNK)
        for field in range(2):
            precond_ref[field, chunk] = values[field]
            image_ref[field, chunk] = images[field]
            field_ref[field, x + 1 : x + 1 + CHUNK] = images[field]
            total_a = total_a + load_ref[field, chunk] * values[field]
            total_b = total_b + images[field] * values[field]
    sums_ref[0:1] = jnp.sum(jnp.sum(total_a, axis=0), axis=0, keepdims=True)
    sums_ref[1:2] = jnp.sum(jnp.sum(total_b, axis=0), axis=0, keepdims=True)
    sums_ref[2:8] = jnp.zeros((6, size_z), F32)
    count = rows_ref.shape[2]
    position = lax.broadcasted_iota(jnp.int32, (count, size_z), 0)
    begin = jnp.where(flags[LOW_X] > 0, ROW0 - 1, ROW0)
    end = jnp.where(flags[HIGH_X] > 0, ROW0 + size_x + 1, ROW0 + size_x)
    valid = (position >= begin) & (position < end)
    for field in range(2):
        for side, row in ((0, 8), (1, 7 + size_y)):
            near[field, side] = jnp.zeros((count, size_z), F32)
            near[field, side, ROW0 - 2 : ROW0 + size_x + 2] = value_ref[field, :, row]
    for side, flag in ((0, LOW_Y), (1, HIGH_Y)):
        images = operate_line(lines, half_lines, mass_lines, face_lines, side, near)
        for field in range(2):
            rows_ref[field, side] = keep(flags, flag, jnp.where(valid, images[field], 0.0))
    solve(field_ref, rows_ref, inverse_ref, (c0, c1, c2, c3), stack_ref, part_ref, part_rows_ref)
    pack_x(flags, part_ref, part_rows_ref, even_ref, odd_ref)


def second_image_kernel(
    flags, whole_ref, whole_rows_ref, first_ref, second_ref, half_ref, mass_ref, face_ref, old_image_ref, old_sums_ref,
    precond_ref, image_ref, sums_ref, value_ref,
):
    size_x, size_y, size_z = old_image_ref.shape[1:]
    own, wide = slice(2, size_x + 2), slice(1, size_x + 3)
    rows, margins = slice(ROW0, ROW0 + size_x), slice(size_x + ROW0 - 1, 2 * size_x + ROW0 + 1)
    for field in range(2):
        low = keep(flags, LOW_Y, chosen(flags, EVEN_Y, second_ref[field], first_ref[field]))
        high = keep(flags, HIGH_Y, chosen(flags, EVEN_Y, first_ref[field], second_ref[field]))
        value_ref[field, wide, 8 : 8 + size_y] = whole_ref[field, wide]
        value_ref[field, own, 7] = keep(flags, LOW_Y, whole_rows_ref[field, 0, rows]) + low[:size_x]
        value_ref[field, wide, 8] = whole_ref[field, wide, 0] + low[margins]
        value_ref[field, wide, 7 + size_y] = whole_ref[field, wide, size_y - 1] + high[margins]
        value_ref[field, own, 8 + size_y] = keep(flags, HIGH_Y, whole_rows_ref[field, 1, rows]) + high[:size_x]
    total_c = total_d = jnp.zeros((CHUNK, size_y, size_z), F32)
    for x in range(0, size_x, CHUNK):
        chunk = slice(x, x + CHUNK)
        values, images = operate(value_ref, half_ref, mass_ref, face_ref, x, CHUNK)
        for field in range(2):
            precond_ref[field, chunk] = values[field]
            image_ref[field, chunk] = images[field]
            total_c = total_c + old_image_ref[field, chunk] * values[field]
            total_d = total_d + images[field] * values[field]
    total_c, total_d = jnp.sum(total_c, axis=0), jnp.sum(total_d, axis=0)
    totals = [
        jnp.sum(old_sums_ref[0:1], axis=1, keepdims=True),
        jnp.sum(old_sums_ref[1:2], axis=1, keepdims=True),
        jnp.sum(jnp.sum(total_c, axis=0, keepdims=True), axis=1, keepdims=True),
        jnp.sum(jnp.sum(total_d, axis=0, keepdims=True), axis=1, keepdims=True),
    ]
    lane = lax.broadcasted_iota(jnp.int32, sums_ref.shape, 1)
    spread = jnp.zeros(sums_ref.shape, F32)
    for place, total in enumerate(totals):
        spread = jnp.where(lane == place, total, spread)
    sums_ref[...] = spread


def finish_kernel(sums_ref, load_ref, z_ref, q_ref, w_ref, s_ref, solution_ref, residual_ref):
    line = jnp.sum(sums_ref[...], axis=0, keepdims=True)
    lane = lax.broadcasted_iota(jnp.int32, line.shape, 1)
    rz, zq, qw, ws = [jnp.sum(jnp.where(lane == place, line, 0.0), axis=1, keepdims=True) for place in range(4)]
    alpha = rz / zq
    rz_next = rz - alpha * (2.0 * zq) + alpha * alpha * qw
    grown = 1.0 + rz_next / rz
    curvature = grown * grown * zq - 2.0 * grown * alpha * qw + alpha * alpha * ws
    alpha_next = rz_next / curvature
    along = alpha + alpha_next * grown
    against = alpha_next * alpha
    for field in range(2):
        for x in range(load_ref.shape[1]):
            solution_ref[field, x] = along * z_ref[field, x] - against * w_ref[field, x]
            residual_ref[field, x] = load_ref[field, x] - along * q_ref[field, x] + against * s_ref[field, x]


SMEM = pl.BlockSpec(memory_space=pltpu.SMEM)
VMEM = pl.BlockSpec(memory_space=pltpu.VMEM)


def call(kernel, scalars, arrays, outs, scratch=(), flops=0, limit=24):
    moved = sum(math.prod(a.shape) * a.dtype.itemsize for a in list(arrays) + list(outs))
    return pl.pallas_call(
        kernel,
        out_shape=tuple(outs),
        in_specs=[SMEM] * len(scalars) + [VMEM] * len(arrays),
        out_specs=tuple([VMEM] * len(outs)),
        scratch_shapes=list(scratch),
        compiler_params=pltpu.CompilerParams(vmem_limit_bytes=limit * 1024 * 1024),
        cost_estimate=pl.CostEstimate(flops=flops, bytes_accessed=moved, transcendentals=0),
    )(*scalars, *arrays)


def shards(mesh, load, zones, conductance, capacity, coupling):
    size_x, size_y, size_z = zones.shape
    assert size_x % BOX == 0 and size_y == BOX and size_z % BOX == 0
    boxes = size_x // BOX
    count = size_x + 8
    sds = lambda *shape: jax.ShapeDtypeStruct(shape, F32)
    forward, back, line_forward, line_back, summed, means = [jnp.asarray(c) for c in constants(size_z)]
    consts = (forward, back, line_forward, line_back)
    modes, lanes = summed.shape
    cross = coupling * jnp.sqrt(capacity[0] * capacity[1])
    table = jnp.concatenate([0.5 * conductance, capacity, cross[None]], axis=0)
    here_x, here_y = lax.axis_index("gx"), lax.axis_index("gy")
    even_x, even_y = here_x % 2 == 0, here_y % 2 == 0
    flags = jnp.stack(
        [even_x, even_y, here_x > 0, here_x < mesh.shape["gx"] - 1, here_y > 0, here_y < mesh.shape["gy"] - 1]
    ).astype(jnp.int32)

    to_low = jnp.concatenate([load[:, 0], zones[:2].astype(F32)], axis=0)
    to_high = jnp.concatenate([load[:, -1], zones[-2:].astype(F32)], axis=0)
    x_halo = swap(mesh, "gx", jnp.where(even_x, to_high, to_low), jnp.where(even_x, to_low, to_high))

    (inverse,) = call(
        divisor_kernel, [table], [zones, summed, means], [sds(2 * boxes, modes, lanes)], flops=40_000_000
    )
    y_halo = swap(
        mesh, "gy", *call(edge_rows_kernel, [flags], [load, zones, *x_halo], [sds(4, count, size_z)] * 2)
    )
    half, mass, face, half_lines, mass_lines, face_lines = call(
        coefficient_kernel,
        [flags, table],
        [zones, *x_halo, *y_halo],
        [
            sds(2, size_x + 4, size_y + 16, size_z),
            sds(3, size_x + 2, size_y, size_z),
            sds(2, 2, size_x + 2, size_y, size_z),
            sds(2, 6, count, size_z),
            sds(3, 2, count, size_z),
            sds(2, 2, 2, count, size_z),
        ],
        flops=20_000_000,
    )
    parts = [sds(2, size_x + 2, size_y, size_z), sds(2, 2, count, size_z)]
    packed_x = [[sds(2, depth, size_y + 8, size_z)] * 2 for depth in (3, 2)]
    wholes = [sds(2, size_x + 4, size_y, size_z), sds(2, 2, count, size_z)]
    packed_y = [[sds(2, 3, count, size_z)] * 2, [sds(2, size_x + count, size_z)] * 2]
    rows = SPAN * size_y + 48
    work = [
        pltpu.VMEM((2, size_x + 2, size_y, size_z), F32),
        pltpu.VMEM((2, 2, count, size_z), F32),
        pltpu.VMEM((3 * rows, boxes * size_z), BF16),
    ]
    padded = [
        pltpu.VMEM((2, size_x + 4, size_y + 16, size_z), F32),
        pltpu.VMEM((2, 6, count, size_z), F32),
    ]
    own = sds(2, size_x, size_y, size_z)

    part, part_rows, *packed = call(
        first_solve_kernel, [flags], [load, *x_halo, *y_halo, inverse, *consts], parts + packed_x[0], work, 3_000_000_000
    )
    received = swap(mesh, "gx", *packed)
    whole, whole_rows, *packed = call(merge_x_kernel, [flags], [part, part_rows, *received], wholes + packed_y[0])
    received = swap(mesh, "gy", *packed)
    precond, image, sums, part, part_rows, *packed = call(
        second_solve_kernel,
        [flags],
        [whole, whole_rows, *received, half, mass, face, half_lines, mass_lines, face_lines, load, inverse, *consts],
        [own, own, sds(8, size_z)] + parts + packed_x[1],
        padded + [pltpu.VMEM((2, 2, count, size_z), F32)] + work,
        3_000_000_000,
    )
    received = swap(mesh, "gx", *packed)
    whole, whole_rows, *packed = call(merge_x_kernel, [flags], [part, part_rows, *received], wholes + packed_y[1])
    received = swap(mesh, "gy", *packed)
    devices = mesh.shape["gx"] * mesh.shape["gy"]
    last_precond, last_image, sums = call(
        second_image_kernel,
        [flags],
        [whole, whole_rows, *received, half, mass, face, image, sums],
        [own, own, sds(devices, size_z)],
        padded[:1],
        10_000_000,
    )
    sums = lax.all_to_all(sums, AXES, 0, 0, tiled=True)
    return call(finish_kernel, [], [sums, load, precond, image, last_precond, last_image], [own, own])


def solution(mesh):
    in_specs = (P(None, "gx", "gy", None), P("gx", "gy", None), P(), P(), P())
    out_specs = (P(None, "gx", "gy", None), P(None, "gx", "gy", None))
    return jax.shard_map(
        functools.partial(shards, mesh), mesh=mesh, in_specs=in_specs, out_specs=out_specs, check_vma=False
    )
```

```python
import functools
import math

import jax
import jax.numpy as jnp
import ml_dtypes
import numpy as np
from jax import lax
from jax.experimental import pallas as pl
from jax.experimental.pallas import tpu as pltpu
from jax.sharding import PartitionSpec as P

BOX = 16
SPAN = BOX + 2
F32 = jnp.float32
BF16 = jnp.bfloat16
AXES = ("gx", "gy")
ROW0 = 4
CHUNK = 4


def split(matrix):
    high = matrix.astype(ml_dtypes.bfloat16)
    low = (matrix - high.astype(np.float64)).astype(ml_dtypes.bfloat16)
    return high, low


def round_up(value, step):
    return (value + step - 1) // step * step


def sine_basis():
    index = np.arange(SPAN)
    angle = np.pi * np.outer(index + 1, index + 1) / (SPAN + 1)
    return np.sqrt(2.0 / (SPAN + 1)) * np.sin(angle)


def eigenvalues():
    return 4.0 * np.sin(np.pi * (np.arange(SPAN) + 1) / (2 * (SPAN + 1))) ** 2


def plane_layout():
    places = [(x, y + 1) for x in range(SPAN) for y in range(BOX)]
    for y in (0, SPAN - 1):
        for position in range(24):
            x = position - (ROW0 - 1)
            places.append((x, y) if 0 <= x < SPAN else None)
    return places


def constants(size_z):
    basis = sine_basis()
    places = plane_layout()
    rows = len(places)
    modes = SPAN * SPAN
    padded_modes = round_up(modes, 16)
    plane = np.zeros((padded_modes, rows))
    for column, place in enumerate(places):
        if place is not None:
            plane[:modes, column] = np.outer(basis[:, place[0]], basis[:, place[1]]).reshape(-1)
    high, low = split(plane)
    forward = np.concatenate([high, high, low], axis=1)
    high, low = split(plane.T)
    inverse = np.concatenate([high, high, low], axis=1)
    boxes = size_z // BOX
    line = np.zeros((size_z, boxes * SPAN))
    means = np.zeros((size_z, boxes * SPAN))
    for box in range(boxes):
        for mode in range(SPAN):
            for offset in range(SPAN):
                cell = box * BOX + offset - 1
                if 0 <= cell < size_z:
                    line[cell, box * SPAN + mode] = basis[mode, offset]
        means[box * BOX : (box + 1) * BOX, box * SPAN : (box + 1) * SPAN] = 1.0 / BOX**3
    high, low = split(line)
    line_forward = np.concatenate([high, high, low], axis=0)
    high, low = split(line.T)
    line_inverse = np.concatenate([high, low], axis=1)
    eigen = eigenvalues()
    pair = np.zeros(padded_modes)
    pair[:modes] = (eigen[:, None] + eigen[None, :]).reshape(-1)
    summed = (pair[:, None] + np.tile(eigen, boxes)[None, :]).astype(np.float32)
    return forward, inverse, line_forward, line_inverse, summed, means.astype(np.float32)


def swap_pairs(mesh, axis, odd):
    sizes = [mesh.shape[name] for name in AXES]
    along = AXES.index(axis)
    pairs = []
    for i in range(sizes[0]):
        for j in range(sizes[1]):
            here = [i, j]
            there = [i, j]
            place = here[along]
            target = place ^ 1 if not odd else (place + 1 if place % 2 else place - 1)
            if 0 <= target < sizes[along]:
                there[along] = target
            elif along == 0:
                there[0] = sizes[0] - 1 - place
            else:
                there[0] = i ^ 1
            pairs.append((here[0] * sizes[1] + here[1], there[0] * sizes[1] + there[1]))
    return pairs


def swap(mesh, axis, even_part, odd_part):
    if axis == "gx":
        first = lax.ppermute(even_part, AXES, swap_pairs(mesh, axis, False))
        second = lax.ppermute(odd_part, AXES, swap_pairs(mesh, axis, True))
    else:
        second = lax.ppermute(odd_part, AXES, swap_pairs(mesh, axis, True))
        first = lax.ppermute(even_part, AXES, swap_pairs(mesh, axis, False))
    return first, second


EVEN_X, EVEN_Y, LOW_X, HIGH_X, LOW_Y, HIGH_Y = range(6)


def standing(mesh):
    here_x, here_y = lax.axis_index("gx"), lax.axis_index("gy")
    facts = (
        lax.rem(here_x, 2) == 0,
        lax.rem(here_y, 2) == 0,
        here_x > 0,
        here_x < mesh.shape["gx"] - 1,
        here_y > 0,
        here_y < mesh.shape["gy"] - 1,
    )
    return [fact.astype(jnp.int32) for fact in facts]


def chosen(flags, which, yes, no):
    return jnp.where(flags[which] > 0, yes, no)


def keep(flags, which, value):
    return jnp.where(flags[which] > 0, value, jnp.zeros_like(value))


def halves(value):
    high = value.astype(BF16)
    low = (value - high.astype(F32)).astype(BF16)
    return high, low


def dot(left, right):
    return jnp.dot(left, right, preferred_element_type=F32)


def solve(field_ref, rows_ref, inverse_ref, consts, stack_ref, out_ref, out_rows_ref):
    forward_ref, back_ref, line_forward_ref, line_back_ref = consts
    boxes = (field_ref.shape[1] - 2) // BOX
    size_y, size_z = field_ref.shape[2:]
    inner = SPAN * size_y
    rows = inner + 48
    line_rows = line_forward_ref.shape[0] // 3
    for field in range(2):
        for box in range(boxes):
            start = box * BOX
            main = field_ref[field, start : start + SPAN].reshape(inner, size_z)
            lanes = slice(box * size_z, (box + 1) * size_z)
            parts = (
                (0, main),
                (inner, rows_ref[field, 0, start : start + 24]),
                (inner + 24, rows_ref[field, 1, start : start + 24]),
            )
            whole = jnp.concatenate([part for _, part in parts], axis=0)
            high, low = halves(whole)
            stack_ref[0:rows, lanes] = high
            stack_ref[rows : 2 * rows, lanes] = low
            stack_ref[2 * rows : 3 * rows, lanes] = high
        spectral = dot(forward_ref[...], stack_ref[...])
        for box in range(boxes):
            lanes = slice(box * size_z, (box + 1) * size_z)
            high, low = halves(spectral[:, lanes])
            both = jnp.concatenate([high, low], axis=1)
            modes = dot(both, line_forward_ref[0 : 2 * line_rows]) + dot(high, line_forward_ref[2 * line_rows :])
            modes = modes * inverse_ref[field * boxes + box]
            high, low = halves(modes)
            cells = dot(high, line_back_ref[...])
            cells = cells[:, :size_z] + (cells[:, size_z:] + dot(low, line_back_ref[:, :size_z]))
            high, low = halves(cells)
            stack_ref[0:rows, lanes] = high
            stack_ref[rows : 2 * rows, lanes] = low
            stack_ref[2 * rows : 3 * rows, lanes] = high
        result = dot(back_ref[...], stack_ref[...])
        for box in range(boxes):
            lanes = slice(box * size_z, (box + 1) * size_z)
            start = box * BOX
            main = result[:inner, lanes].reshape(SPAN, size_y, size_z)
            if box == 0:
                out_ref[field, 0:SPAN] = main
            else:
                out_ref[field, start : start + 2] = out_ref[field, start : start + 2] + main[0:2]
                out_ref[field, start + 2 : start + SPAN] = main[2:]
            for side in range(2):
                strip = result[inner + 24 * side : inner + 24 * side + 24, lanes]
                if box == 0:
                    out_rows_ref[field, side, 0:24] = strip
                else:
                    out_rows_ref[field, side, start : start + 8] = (
                        out_rows_ref[field, side, start : start + 8] + strip[0:8]
                    )
                    out_rows_ref[field, side, start + 8 : start + 24] = strip[8:]


def pack_x(flags, part_ref, part_rows_ref, even_ref, odd_ref):
    last = part_ref.shape[1] - 1
    depth = even_ref.shape[1]
    size_y = part_ref.shape[2]
    for field in range(2):
        for layer in range(depth):
            low, high = layer, last + 1 - depth + layer
            for side, place in ((None, slice(0, size_y)), (0, slice(size_y, size_y + 1)), (1, slice(size_y + 1, size_y + 2))):
                if side is None:
                    to_low, to_high = part_ref[field, low], part_ref[field, high]
                else:
                    shift = ROW0 - 1
                    to_low = part_rows_ref[field, side, low + shift : low + shift + 1]
                    to_high = part_rows_ref[field, side, high + shift : high + shift + 1]
                even_ref[field, layer, place] = chosen(flags, EVEN_X, to_high, to_low)
                odd_ref[field, layer, place] = chosen(flags, EVEN_X, to_low, to_high)
            rest = even_ref.shape[2] - size_y - 2
            blank = jnp.zeros((rest, even_ref.shape[3]), F32)
            even_ref[field, layer, size_y + 2 :] = blank
            odd_ref[field, layer, size_y + 2 :] = blank


def divisor_kernel(conductance_ref, capacity_ref, zones_ref, summed_ref, means_ref, inverse_ref):
    size_x, size_y, size_z = zones_ref.shape
    boxes = size_x // BOX
    lines = []
    for table_ref, which in ((capacity_ref, 0), (capacity_ref, 1), (conductance_ref, 0), (conductance_ref, 1)):
        for box in range(boxes):
            total = jnp.zeros((size_y, size_z), F32)
            for x in range(box * BOX, (box + 1) * BOX):
                zone = zones_ref[x]
                value = jnp.full((size_y, size_z), table_ref[which, 0], F32)
                for label in range(1, table_ref.shape[1]):
                    value = jnp.where(zone == label, table_ref[which, label], value)
                total = total + value
            lines.append(jnp.sum(total, axis=0, keepdims=True))
    sums = jnp.concatenate(lines, axis=0)
    means = jnp.dot(sums, means_ref[...], preferred_element_type=F32, precision=lax.Precision.HIGHEST)
    half = 2 * boxes
    for combo in range(half):
        cbar = means[combo : combo + 1]
        kbar = means[half + combo : half + combo + 1]
        inverse_ref[combo] = 1.0 / (cbar + kbar * summed_ref[...])


def edge_layers_kernel(mesh, load_ref, zones_ref, even_ref, odd_ref):
    flags = standing(mesh)
    last = zones_ref.shape[0] - 1
    for channel in range(4):
        if channel < 2:
            low, high = load_ref[channel, 0], load_ref[channel, last]
        else:
            low, high = zones_ref[channel - 2].astype(F32), zones_ref[last - 3 + channel].astype(F32)
        even_ref[channel] = chosen(flags, EVEN_X, high, low)
        odd_ref[channel] = chosen(flags, EVEN_X, low, high)


def edge_rows_kernel(mesh, load_ref, zones_ref, first_ref, second_ref, even_ref, odd_ref):
    flags = standing(mesh)
    size_x, size_y, size_z = zones_ref.shape
    from_low = chosen(flags, EVEN_X, second_ref[...], first_ref[...])
    from_high = chosen(flags, EVEN_X, first_ref[...], second_ref[...])
    blank = jnp.zeros((8, size_z), F32)
    for channel in range(4):
        for ref in (even_ref, odd_ref):
            ref[channel, 0:8] = blank
            ref[channel, size_x : size_x + 8] = blank

    def put(channel, position, count, to_low, to_high):
        place = slice(position, position + count)
        even_ref[channel, place] = chosen(flags, EVEN_Y, to_high, to_low)
        odd_ref[channel, place] = chosen(flags, EVEN_Y, to_low, to_high)

    end = ROW0 + size_x
    for field in range(2):
        put(field, ROW0, size_x, load_ref[field, :, 0], load_ref[field, :, size_y - 1])
        low = keep(flags, LOW_X, from_low[field])
        high = keep(flags, HIGH_X, from_high[field])
        put(field, ROW0 - 1, 1, low[0:1], low[size_y - 1 : size_y])
        put(field, end, 1, high[0:1], high[size_y - 1 : size_y])
    for layer in range(2):
        channel = 2 + layer
        near, far = layer, size_y - 2 + layer
        put(channel, ROW0, size_x, zones_ref[:, near].astype(F32), zones_ref[:, far].astype(F32))
        for depth in range(2):
            low, high = from_low[2 + depth], from_high[2 + depth]
            put(channel, ROW0 - 2 + depth, 1, low[near : near + 1], low[far : far + 1])
            put(channel, end + depth, 1, high[near : near + 1], high[far : far + 1])


def looked_up(entries, zone):
    value = jnp.full(zone.shape, entries[0], F32)
    for label in range(1, len(entries)):
        value = jnp.where(zone == float(label), entries[label], value)
    return value


def coefficient_kernel(
    mesh, conductance_ref, capacity_ref, coupling_ref, zones_ref, first_x, second_x, first_y, second_y,
    half_ref, mass_ref, face_ref, half_rows_ref, mass_rows_ref, face_rows_ref,
):
    flags = standing(mesh)
    labels = range(coupling_ref.shape[0])
    halves_of = [[0.5 * conductance_ref[field, label] for label in labels] for field in range(2)]
    masses = [[capacity_ref[field, label] for label in labels] for field in range(2)]
    line = zones_ref.shape[2:]
    roots = [jnp.sqrt(jnp.full((8, *line), capacity_ref[0, label] * capacity_ref[1, label], F32)) for label in labels]
    masses.append([coupling_ref[label] * roots[label][0:1] for label in labels])
    size_x, size_y, size_z = zones_ref.shape
    low_x = chosen(flags, EVEN_X, second_x[2:4], first_x[2:4])
    high_x = chosen(flags, EVEN_X, first_x[2:4], second_x[2:4])
    low_y = chosen(flags, EVEN_Y, second_y[2:4], first_y[2:4])
    high_y = chosen(flags, EVEN_Y, first_y[2:4], second_y[2:4])
    inside = slice(8, 8 + size_y)
    for x in range(-2, size_x + 2):
        if x < 0:
            zone = low_x[x + 2]
        elif x >= size_x:
            zone = high_x[x - size_x]
        else:
            zone = zones_ref[x].astype(F32)
        for field in range(2):
            half_ref[field, x + 2, inside] = looked_up(halves_of[field], zone)
        if -1 <= x <= size_x:
            for which in range(3):
                mass_ref[which, x + 1] = looked_up(masses[which], zone)
    for field in range(2):
        for outer in (0, 1):
            half_ref[field, outer, inside] = chosen(
                flags, LOW_X, half_ref[field, outer, inside], half_ref[field, 2, inside]
            )
            place = size_x + 2 + outer
            half_ref[field, place, inside] = chosen(
                flags, HIGH_X, half_ref[field, place, inside], half_ref[field, size_x + 1, inside]
            )
    count = half_rows_ref.shape[2]
    position = lax.broadcasted_iota(jnp.int32, (count, size_z), 0)
    for line, (zone, flag) in enumerate(
        ((low_y[0], LOW_Y), (low_y[1], LOW_Y), (high_y[0], HIGH_Y), (high_y[1], HIGH_Y))
    ):
        for field in range(2):
            value = looked_up(halves_of[field], zone)
            below = value[ROW0 : ROW0 + 1]
            above = value[ROW0 + size_x - 1 : ROW0 + size_x]
            value = jnp.where((position < ROW0) & (flags[LOW_X] == 0), below, value)
            value = jnp.where((position >= ROW0 + size_x) & (flags[HIGH_X] == 0), above, value)
            near = half_ref[field, :, 8 if flag == LOW_Y else 8 + size_y - 1]
            half_rows_ref[field, line] = value
            half_rows_ref[field, line, ROW0 - 2 : ROW0 + size_x + 2] = chosen(
                flags, flag, half_rows_ref[field, line, ROW0 - 2 : ROW0 + size_x + 2], near
            )
            if line in (1, 2):
                row = 7 if line == 1 else 8 + size_y
                half_ref[field, :, row] = half_rows_ref[field, line, ROW0 - 2 : ROW0 + size_x + 2]
        if line in (1, 2):
            for which in range(3):
                mass_rows_ref[which, line - 1] = looked_up(masses[which], zone)
    for field in range(2):
        for x in range(0, size_x + 2, 2):
            faces = faces_z(half_ref[field, x + 1 : x + 3, inside])
            for way in range(2):
                face_ref[field, way, x : x + 2] = faces[way]
        for side in range(2):
            faces = faces_z(half_rows_ref[field, side + 1])
            for way in range(2):
                face_rows_ref[field, way, side] = faces[way]
        for line, row in ((4, 8), (5, 8 + size_y - 1)):
            half_rows_ref[field, line] = jnp.zeros((count, size_z), F32)
            half_rows_ref[field, line, ROW0 - 2 : ROW0 + size_x + 2] = half_ref[field, :, row]


def first_solve_kernel(
    mesh, load_ref, first_x, second_x, first_y, second_y, inverse_ref, c0, c1, c2, c3,
    part_ref, part_rows_ref, even_ref, odd_ref, field_ref, rows_ref, stack_ref,
):
    flags = standing(mesh)
    size_x = load_ref.shape[1]
    for field in range(2):
        field_ref[field, 1 : 1 + size_x] = load_ref[field]
        field_ref[field, 0] = keep(flags, LOW_X, chosen(flags, EVEN_X, second_x[field], first_x[field]))
        field_ref[field, 1 + size_x] = keep(flags, HIGH_X, chosen(flags, EVEN_X, first_x[field], second_x[field]))
        rows_ref[field, 0] = keep(flags, LOW_Y, chosen(flags, EVEN_Y, second_y[field], first_y[field]))
        rows_ref[field, 1] = keep(flags, HIGH_Y, chosen(flags, EVEN_Y, first_y[field], second_y[field]))
    solve(field_ref, rows_ref, inverse_ref, (c0, c1, c2, c3), stack_ref, part_ref, part_rows_ref)
    pack_x(flags, part_ref, part_rows_ref, even_ref, odd_ref)


def merge_x_kernel(mesh, part_ref, part_rows_ref, first_ref, second_ref, whole_ref, whole_rows_ref, even_ref, odd_ref):
    flags = standing(mesh)
    size_x = part_ref.shape[1] - 2
    size_y, size_z = part_ref.shape[2:]
    depth = first_ref.shape[1]
    count = part_rows_ref.shape[2]
    end = ROW0 + size_x
    for field in range(2):
        low = keep(flags, LOW_X, chosen(flags, EVEN_X, second_ref[field], first_ref[field]))
        high = keep(flags, HIGH_X, chosen(flags, EVEN_X, first_ref[field], second_ref[field]))
        whole_ref[field, 1] = keep(flags, LOW_X, part_ref[field, 0]) + low[depth - 2, :size_y]
        whole_ref[field, 2] = part_ref[field, 1] + low[depth - 1, :size_y]
        whole_ref[field, 3 : size_x + 1] = part_ref[field, 2:size_x]
        whole_ref[field, size_x + 1] = part_ref[field, size_x] + high[0, :size_y]
        whole_ref[field, size_x + 2] = keep(flags, HIGH_X, part_ref[field, size_x + 1]) + high[1, :size_y]
        if depth == 3:
            whole_ref[field, 0] = low[0, :size_y]
            whole_ref[field, size_x + 3] = high[2, :size_y]
        for side in range(2):
            row = slice(size_y + side, size_y + side + 1)
            edge = ROW0 - 1
            whole_rows_ref[field, side] = part_rows_ref[field, side]
            whole_rows_ref[field, side, edge : edge + 1] = (
                keep(flags, LOW_X, part_rows_ref[field, side, edge : edge + 1]) + low[depth - 2, row]
            )
            whole_rows_ref[field, side, edge + 1 : edge + 2] = (
                part_rows_ref[field, side, edge + 1 : edge + 2] + low[depth - 1, row]
            )
            whole_rows_ref[field, side, end - 1 : end] = part_rows_ref[field, side, end - 1 : end] + high[0, row]
            whole_rows_ref[field, side, end : end + 1] = (
                keep(flags, HIGH_X, part_rows_ref[field, side, end : end + 1]) + high[1, row]
            )
            if depth == 3:
                whole_rows_ref[field, side, edge - 1 : edge] = low[0, row]
                whole_rows_ref[field, side, end + 1 : end + 2] = high[2, row]

        def put(at, to_low, to_high):
            even_ref[(field, *at)] = chosen(flags, EVEN_Y, to_high, to_low)
            odd_ref[(field, *at)] = chosen(flags, EVEN_Y, to_low, to_high)

        if depth == 3:
            blank = jnp.zeros((8, size_z), F32)
            for layer in range(3):
                for ref in (even_ref, odd_ref):
                    ref[field, layer, 0:8] = blank
                    ref[field, layer, count - 8 : count] = blank
            rows = slice(ROW0 - 2, end + 2)
            low_rows = whole_rows_ref[field, 0, rows]
            high_rows = whole_rows_ref[field, 1, rows]
            put((0, rows), low_rows, whole_ref[field, :, size_y - 2])
            put((1, rows), whole_ref[field, :, 0], whole_ref[field, :, size_y - 1])
            put((2, rows), whole_ref[field, :, 1], high_rows)
        else:
            own = slice(2, size_x + 2)
            put((slice(0, size_x),), whole_ref[field, own, 0], whole_ref[field, own, size_y - 1])
            put((slice(size_x, None),), whole_rows_ref[field, 0], whole_rows_ref[field, 1])


def assemble(flags, whole_ref, whole_rows_ref, first_ref, second_ref, field_ref, lines):
    size_x = whole_ref.shape[1] - 4
    size_y = whole_ref.shape[2]
    spread = slice(ROW0 - 2, ROW0 + size_x + 2)
    for field in range(2):
        low = keep(flags, LOW_Y, chosen(flags, EVEN_Y, second_ref[field], first_ref[field]))
        high = keep(flags, HIGH_Y, chosen(flags, EVEN_Y, first_ref[field], second_ref[field]))
        below = keep(flags, LOW_Y, whole_rows_ref[field, 0]) + low[1]
        above = keep(flags, HIGH_Y, whole_rows_ref[field, 1]) + high[1]
        lines[field, 0] = low[0]
        lines[field, 1] = below
        lines[field, 2] = above
        lines[field, 3] = high[2]
        lines[field, 4] = low[2]
        lines[field, 5] = high[0]
        field_ref[field, :, 8 : 8 + size_y] = whole_ref[field]
        field_ref[field, :, 7] = lines[field, 1, spread]
        field_ref[field, :, 8 + size_y] = lines[field, 2, spread]
        field_ref[field, :, 8] = field_ref[field, :, 8] + lines[field, 4, spread]
        field_ref[field, :, 7 + size_y] = field_ref[field, :, 7 + size_y] + lines[field, 5, spread]


def faces_z(half):
    size_z, axis = half.shape[-1], half.ndim - 1
    lane = lax.broadcasted_iota(jnp.int32, half.shape, axis)
    upper = half + jnp.where(lane == size_z - 1, half, pltpu.roll(half, size_z - 1, axis))
    lower = half + jnp.where(lane == 0, half, pltpu.roll(half, 1, axis))
    return upper, lower


def along_z(value, upper, lower):
    size_z, axis = value.shape[-1], value.ndim - 1
    lane = lax.broadcasted_iota(jnp.int32, value.shape, axis)
    above = jnp.where(lane == size_z - 1, 0.0, pltpu.roll(value, size_z - 1, axis))
    below = jnp.where(lane == 0, 0.0, pltpu.roll(value, 1, axis))
    return upper * (value - above) + lower * (value - below)


def operate(field_ref, half_ref, mass_ref, face_ref, x, count):
    size_y = mass_ref.shape[2]
    inside = slice(8, 8 + size_y)
    masses = slice(x + 1, x + 1 + count)
    here = slice(x + 2, x + 2 + count)
    values, images = [], []
    for field in range(2):
        value = field_ref[field, here, inside]
        half = half_ref[field, here, inside]
        flux = along_z(value, face_ref[field, 0, masses], face_ref[field, 1, masses])
        for start in (x + 1, x + 3):
            place = slice(start, start + count)
            flux = flux + (half + half_ref[field, place, inside]) * (value - field_ref[field, place, inside])
        for shift in (-1, 1):
            moved = slice(8 + shift, 8 + shift + size_y)
            flux = flux + (half + half_ref[field, here, moved]) * (value - field_ref[field, here, moved])
        values.append(value)
        images.append(flux)
    first = mass_ref[0, masses] * values[0] + mass_ref[2, masses] * values[1] + images[0]
    second = mass_ref[2, masses] * values[0] + mass_ref[1, masses] * values[1] + images[1]
    return values, (first, second)


def operate_line(lines, half_lines, mass_lines, face_lines, side, near):
    outer, center, inner = (0, 1, 4) if side == 0 else (3, 2, 5)
    values, images = [], []
    for field in range(2):
        value = lines[field, center]
        half = half_lines[field, center]
        count = value.shape[0]
        flux = along_z(value, face_lines[field, 0, side], face_lines[field, 1, side])
        for turn in (1, count - 1):
            flux = flux + (half + pltpu.roll(half, turn, 0)) * (value - pltpu.roll(value, turn, 0))
        flux = flux + (half + half_lines[field, outer]) * (value - lines[field, outer])
        flux = flux + (half + half_lines[field, inner]) * (value - near[field, side])
        values.append(value)
        images.append(flux)
    first = mass_lines[0, side] * values[0] + mass_lines[2, side] * values[1] + images[0]
    second = mass_lines[2, side] * values[0] + mass_lines[1, side] * values[1] + images[1]
    return first, second


def second_solve_kernel(
    mesh, whole_ref, whole_rows_ref, first_ref, second_ref,
    half_ref, mass_ref, face_ref, half_lines, mass_lines, face_lines, load_ref, inverse_ref, c0, c1, c2, c3,
    precond_ref, image_ref, sums_ref, part_ref, part_rows_ref, even_ref, odd_ref,
    value_ref, lines, near, field_ref, rows_ref, stack_ref,
):
    flags = standing(mesh)
    size_x, size_y, size_z = load_ref.shape[1:]
    assemble(flags, whole_ref, whole_rows_ref, first_ref, second_ref, value_ref, lines)
    for x, flag in ((-1, LOW_X), (size_x, HIGH_X)):
        _, images = operate(value_ref, half_ref, mass_ref, face_ref, x, 1)
        for field in range(2):
            field_ref[field, x + 1 : x + 2] = keep(flags, flag, images[field])
    total_a = total_b = jnp.zeros((CHUNK, size_y, size_z), F32)
    for x in range(0, size_x, CHUNK):
        chunk = slice(x, x + CHUNK)
        values, images = operate(value_ref, half_ref, mass_ref, face_ref, x, CHUNK)
        for field in range(2):
            precond_ref[field, chunk] = values[field]
            image_ref[field, chunk] = images[field]
            field_ref[field, x + 1 : x + 1 + CHUNK] = images[field]
            total_a = total_a + load_ref[field, chunk] * values[field]
            total_b = total_b + images[field] * values[field]
    sums_ref[0:1] = jnp.sum(jnp.sum(total_a, axis=0), axis=0, keepdims=True)
    sums_ref[1:2] = jnp.sum(jnp.sum(total_b, axis=0), axis=0, keepdims=True)
    sums_ref[2:8] = jnp.zeros((6, size_z), F32)
    count = rows_ref.shape[2]
    position = lax.broadcasted_iota(jnp.int32, (count, size_z), 0)
    begin = jnp.where(flags[LOW_X] > 0, ROW0 - 1, ROW0)
    end = jnp.where(flags[HIGH_X] > 0, ROW0 + size_x + 1, ROW0 + size_x)
    valid = (position >= begin) & (position < end)
    for field in range(2):
        for side, row in ((0, 8), (1, 7 + size_y)):
            near[field, side] = jnp.zeros((count, size_z), F32)
            near[field, side, ROW0 - 2 : ROW0 + size_x + 2] = value_ref[field, :, row]
    for side, flag in ((0, LOW_Y), (1, HIGH_Y)):
        images = operate_line(lines, half_lines, mass_lines, face_lines, side, near)
        for field in range(2):
            rows_ref[field, side] = keep(flags, flag, jnp.where(valid, images[field], 0.0))
    solve(field_ref, rows_ref, inverse_ref, (c0, c1, c2, c3), stack_ref, part_ref, part_rows_ref)
    pack_x(flags, part_ref, part_rows_ref, even_ref, odd_ref)


def second_image_kernel(
    mesh, whole_ref, whole_rows_ref, first_ref, second_ref, half_ref, mass_ref, face_ref, old_image_ref, old_sums_ref,
    precond_ref, image_ref, sums_ref, value_ref,
):
    flags = standing(mesh)
    size_x, size_y, size_z = old_image_ref.shape[1:]
    own, wide = slice(2, size_x + 2), slice(1, size_x + 3)
    rows, margins = slice(ROW0, ROW0 + size_x), slice(size_x + ROW0 - 1, 2 * size_x + ROW0 + 1)
    for field in range(2):
        low = keep(flags, LOW_Y, chosen(flags, EVEN_Y, second_ref[field], first_ref[field]))
        high = keep(flags, HIGH_Y, chosen(flags, EVEN_Y, first_ref[field], second_ref[field]))
        value_ref[field, wide, 8 : 8 + size_y] = whole_ref[field, wide]
        value_ref[field, own, 7] = keep(flags, LOW_Y, whole_rows_ref[field, 0, rows]) + low[:size_x]
        value_ref[field, wide, 8] = whole_ref[field, wide, 0] + low[margins]
        value_ref[field, wide, 7 + size_y] = whole_ref[field, wide, size_y - 1] + high[margins]
        value_ref[field, own, 8 + size_y] = keep(flags, HIGH_Y, whole_rows_ref[field, 1, rows]) + high[:size_x]
    total_c = total_d = jnp.zeros((CHUNK, size_y, size_z), F32)
    for x in range(0, size_x, CHUNK):
        chunk = slice(x, x + CHUNK)
        values, images = operate(value_ref, half_ref, mass_ref, face_ref, x, CHUNK)
        for field in range(2):
            precond_ref[field, chunk] = values[field]
            image_ref[field, chunk] = images[field]
            total_c = total_c + old_image_ref[field, chunk] * values[field]
            total_d = total_d + images[field] * values[field]
    total_c, total_d = jnp.sum(total_c, axis=0), jnp.sum(total_d, axis=0)
    totals = [
        jnp.sum(old_sums_ref[0:1], axis=1, keepdims=True),
        jnp.sum(old_sums_ref[1:2], axis=1, keepdims=True),
        jnp.sum(jnp.sum(total_c, axis=0, keepdims=True), axis=1, keepdims=True),
        jnp.sum(jnp.sum(total_d, axis=0, keepdims=True), axis=1, keepdims=True),
    ]
    lane = lax.broadcasted_iota(jnp.int32, sums_ref.shape, 1)
    spread = jnp.zeros(sums_ref.shape, F32)
    for place, total in enumerate(totals):
        spread = jnp.where(lane == place, total, spread)
    sums_ref[...] = spread


def finish_kernel(sums_ref, load_ref, z_ref, q_ref, w_ref, s_ref, solution_ref, residual_ref):
    line = jnp.sum(sums_ref[...], axis=0, keepdims=True)
    lane = lax.broadcasted_iota(jnp.int32, line.shape, 1)
    rz, zq, qw, ws = [jnp.sum(jnp.where(lane == place, line, 0.0), axis=1, keepdims=True) for place in range(4)]
    alpha = rz / zq
    rz_next = rz - alpha * (2.0 * zq) + alpha * alpha * qw
    grown = 1.0 + rz_next / rz
    curvature = grown * grown * zq - 2.0 * grown * alpha * qw + alpha * alpha * ws
    alpha_next = rz_next / curvature
    along = alpha + alpha_next * grown
    against = alpha_next * alpha
    for field in range(2):
        for x in range(load_ref.shape[1]):
            solution_ref[field, x] = along * z_ref[field, x] - against * w_ref[field, x]
            residual_ref[field, x] = load_ref[field, x] - along * q_ref[field, x] + against * s_ref[field, x]


SMEM = pl.BlockSpec(memory_space=pltpu.SMEM)
VMEM = pl.BlockSpec(memory_space=pltpu.VMEM)


def call(mesh, kernel, scalars, arrays, outs, scratch=(), flops=0, limit=24):
    moved = sum(math.prod(a.shape) * a.dtype.itemsize for a in list(arrays) + list(outs))
    return pl.pallas_call(
        kernel if mesh is None else functools.partial(kernel, mesh),
        out_shape=tuple(outs),
        in_specs=[SMEM] * len(scalars) + [VMEM] * len(arrays),
        out_specs=tuple([VMEM] * len(outs)),
        scratch_shapes=list(scratch),
        compiler_params=pltpu.CompilerParams(vmem_limit_bytes=limit * 1024 * 1024),
        cost_estimate=pl.CostEstimate(flops=flops, bytes_accessed=moved, transcendentals=0),
    )(*scalars, *arrays)


def shards(mesh, load, zones, conductance, capacity, coupling):
    size_x, size_y, size_z = zones.shape
    assert size_x % BOX == 0 and size_y == BOX and size_z % BOX == 0
    boxes = size_x // BOX
    count = size_x + 8
    sds = lambda *shape: jax.ShapeDtypeStruct(shape, F32)
    forward, back, line_forward, line_back, summed, means = [jnp.asarray(c) for c in constants(size_z)]
    consts = (forward, back, line_forward, line_back)
    modes, lanes = summed.shape
    packed = call(
        mesh, edge_layers_kernel, [], [load, zones], [sds(4, size_y, size_z)] * 2
    )
    x_halo = swap(mesh, "gx", *packed)
    (inverse,) = call(
        None,
        divisor_kernel,
        [conductance, capacity],
        [zones, summed, means],
        [sds(2 * boxes, modes, lanes)],
        flops=40_000_000,
    )
    packed = call(mesh, edge_rows_kernel, [], [load, zones, *x_halo], [sds(4, count, size_z)] * 2)
    y_halo = swap(mesh, "gy", *packed)
    half, mass, face, half_lines, mass_lines, face_lines = call(
        mesh,
        coefficient_kernel,
        [conductance, capacity, coupling],
        [zones, *x_halo, *y_halo],
        [
            sds(2, size_x + 4, size_y + 16, size_z),
            sds(3, size_x + 2, size_y, size_z),
            sds(2, 2, size_x + 2, size_y, size_z),
            sds(2, 6, count, size_z),
            sds(3, 2, count, size_z),
            sds(2, 2, 2, count, size_z),
        ],
        flops=20_000_000,
    )
    parts = [sds(2, size_x + 2, size_y, size_z), sds(2, 2, count, size_z)]
    packed_x = [[sds(2, depth, size_y + 8, size_z)] * 2 for depth in (3, 2)]
    wholes = [sds(2, size_x + 4, size_y, size_z), sds(2, 2, count, size_z)]
    packed_y = [[sds(2, 3, count, size_z)] * 2, [sds(2, size_x + count, size_z)] * 2]
    rows = SPAN * size_y + 48
    work = [
        pltpu.VMEM((2, size_x + 2, size_y, size_z), F32),
        pltpu.VMEM((2, 2, count, size_z), F32),
        pltpu.VMEM((3 * rows, boxes * size_z), BF16),
    ]
    padded = [
        pltpu.VMEM((2, size_x + 4, size_y + 16, size_z), F32),
        pltpu.VMEM((2, 6, count, size_z), F32),
    ]
    own = sds(2, size_x, size_y, size_z)

    part, part_rows, *packed = call(
        mesh, first_solve_kernel, [], [load, *x_halo, *y_halo, inverse, *consts], parts + packed_x[0], work, 3_000_000_000
    )
    received = swap(mesh, "gx", *packed)
    whole, whole_rows, *packed = call(mesh, merge_x_kernel, [], [part, part_rows, *received], wholes + packed_y[0])
    received = swap(mesh, "gy", *packed)
    precond, image, sums, part, part_rows, *packed = call(
        mesh,
        second_solve_kernel,
        [],
        [whole, whole_rows, *received, half, mass, face, half_lines, mass_lines, face_lines, load, inverse, *consts],
        [own, own, sds(8, size_z)] + parts + packed_x[1],
        padded + [pltpu.VMEM((2, 2, count, size_z), F32)] + work,
        3_000_000_000,
    )
    received = swap(mesh, "gx", *packed)
    whole, whole_rows, *packed = call(mesh, merge_x_kernel, [], [part, part_rows, *received], wholes + packed_y[1])
    received = swap(mesh, "gy", *packed)
    devices = mesh.shape["gx"] * mesh.shape["gy"]
    last_precond, last_image, sums = call(
        mesh,
        second_image_kernel,
        [],
        [whole, whole_rows, *received, half, mass, face, image, sums],
        [own, own, sds(devices, size_z)],
        padded[:1],
        10_000_000,
    )
    sums = lax.all_to_all(sums, AXES, 0, 0, tiled=True)
    return call(None, finish_kernel, [], [sums, load, precond, image, last_precond, last_image], [own, own])


def solution(mesh):
    in_specs = (P(None, "gx", "gy", None), P("gx", "gy", None), P(), P(), P())
    out_specs = (P(None, "gx", "gy", None), P(None, "gx", "gy", None))
    return jax.shard_map(
        functools.partial(shards, mesh), mesh=mesh, in_specs=in_specs, out_specs=out_specs, check_vma=False
    )
```

```python
import functools
import math

import jax
import jax.numpy as jnp
import ml_dtypes
import numpy as np
from jax import lax
from jax.experimental import pallas as pl
from jax.experimental.pallas import tpu as pltpu
from jax.sharding import PartitionSpec as P

BOX = 16
SPAN = BOX + 2
F32 = jnp.float32
BF16 = jnp.bfloat16
AXES = ("gx", "gy")
ROW0 = 4
CHUNK = 4


def split(matrix):
    high = matrix.astype(ml_dtypes.bfloat16)
    low = (matrix - high.astype(np.float64)).astype(ml_dtypes.bfloat16)
    return high, low


def round_up(value, step):
    return (value + step - 1) // step * step


def sine_basis():
    index = np.arange(SPAN)
    angle = np.pi * np.outer(index + 1, index + 1) / (SPAN + 1)
    return np.sqrt(2.0 / (SPAN + 1)) * np.sin(angle)


def eigenvalues():
    return 4.0 * np.sin(np.pi * (np.arange(SPAN) + 1) / (2 * (SPAN + 1))) ** 2


def plane_layout():
    places = [(x, y + 1) for x in range(SPAN) for y in range(BOX)]
    for y in (0, SPAN - 1):
        for position in range(24):
            x = position - (ROW0 - 1)
            places.append((x, y) if 0 <= x < SPAN else None)
    return places


def constants(size_z):
    basis = sine_basis()
    places = plane_layout()
    rows = len(places)
    modes = SPAN * SPAN
    padded_modes = round_up(modes, 16)
    plane = np.zeros((padded_modes, rows))
    for column, place in enumerate(places):
        if place is not None:
            plane[:modes, column] = np.outer(basis[:, place[0]], basis[:, place[1]]).reshape(-1)
    high, low = split(plane)
    forward = np.concatenate([high, high, low], axis=1)
    high, low = split(plane.T)
    inverse = np.concatenate([high, high, low], axis=1)
    boxes = size_z // BOX
    line = np.zeros((size_z, boxes * SPAN))
    means = np.zeros((size_z, boxes * SPAN))
    for box in range(boxes):
        for mode in range(SPAN):
            for offset in range(SPAN):
                cell = box * BOX + offset - 1
                if 0 <= cell < size_z:
                    line[cell, box * SPAN + mode] = basis[mode, offset]
        means[box * BOX : (box + 1) * BOX, box * SPAN : (box + 1) * SPAN] = 1.0 / BOX**3
    high, low = split(line)
    line_forward = np.concatenate([high, high, low], axis=0)
    high, low = split(line.T)
    line_inverse = np.concatenate([high, low], axis=1)
    eigen = eigenvalues()
    pair = np.zeros(padded_modes)
    pair[:modes] = (eigen[:, None] + eigen[None, :]).reshape(-1)
    summed = (pair[:, None] + np.tile(eigen, boxes)[None, :]).astype(np.float32)
    return forward, inverse, line_forward, line_inverse, summed, means.astype(np.float32)


def swap_pairs(mesh, axis, odd):
    sizes = [mesh.shape[name] for name in AXES]
    along = AXES.index(axis)
    pairs = []
    for i in range(sizes[0]):
        for j in range(sizes[1]):
            here = [i, j]
            there = [i, j]
            place = here[along]
            target = place ^ 1 if not odd else (place + 1 if place % 2 else place - 1)
            if 0 <= target < sizes[along]:
                there[along] = target
            elif along == 0:
                there[0] = sizes[0] - 1 - place
            else:
                there[0] = i ^ 1
            pairs.append((here[0] * sizes[1] + here[1], there[0] * sizes[1] + there[1]))
    return pairs


def swap(mesh, axis, even_part, odd_part):
    if axis == "gx":
        first = lax.ppermute(even_part, AXES, swap_pairs(mesh, axis, False))
        second = lax.ppermute(odd_part, AXES, swap_pairs(mesh, axis, True))
    else:
        second = lax.ppermute(odd_part, AXES, swap_pairs(mesh, axis, True))
        first = lax.ppermute(even_part, AXES, swap_pairs(mesh, axis, False))
    return first, second


EVEN_X, EVEN_Y, LOW_X, HIGH_X, LOW_Y, HIGH_Y = range(6)


def standing(mesh):
    here_x, here_y = lax.axis_index("gx"), lax.axis_index("gy")
    facts = (
        lax.rem(here_x, 2) == 0,
        lax.rem(here_y, 2) == 0,
        here_x > 0,
        here_x < mesh.shape["gx"] - 1,
        here_y > 0,
        here_y < mesh.shape["gy"] - 1,
    )
    return [fact.astype(jnp.int32) for fact in facts]


def chosen(flags, which, yes, no):
    return jnp.where(flags[which] > 0, yes, no)


def keep(flags, which, value):
    return jnp.where(flags[which] > 0, value, jnp.zeros_like(value))


def halves(value):
    high = value.astype(BF16)
    low = (value - high.astype(F32)).astype(BF16)
    return high, low


def dot(left, right):
    return jnp.dot(left, right, preferred_element_type=F32)


def store_split(stack_ref, lanes, value):
    rows = value.shape[0]
    high, low = halves(value)
    stack_ref[0:rows, lanes] = high
    stack_ref[rows : 2 * rows, lanes] = low
    stack_ref[2 * rows : 3 * rows, lanes] = high


def solve(field_ref, rows_ref, inverse_ref, consts, before_ref, after_ref, out_ref, out_rows_ref):
    forward_ref, back_ref, line_forward_ref, line_back_ref = consts
    boxes = (field_ref.shape[1] - 2) // BOX
    size_y, size_z = field_ref.shape[2:]
    inner = SPAN * size_y
    line_rows = line_forward_ref.shape[0] // 3
    lanes = [slice(box * size_z, (box + 1) * size_z) for box in range(boxes)]
    for field in range(2):
        for box in range(boxes):
            start = box * BOX
            main = field_ref[field, start : start + SPAN].reshape(inner, size_z)
            strips = [rows_ref[field, side, start : start + 24] for side in range(2)]
            store_split(before_ref.at[field], lanes[box], jnp.concatenate([main, *strips], axis=0))
    spectral = [dot(forward_ref[...], before_ref[field]) for field in range(2)]
    for field in range(2):
        for box in range(boxes):
            high, low = halves(spectral[field][:, lanes[box]])
            both = jnp.concatenate([high, low], axis=1)
            modes = dot(both, line_forward_ref[0 : 2 * line_rows]) + dot(high, line_forward_ref[2 * line_rows :])
            modes = modes * inverse_ref[field * boxes + box]
            high, low = halves(modes)
            cells = dot(high, line_back_ref[...])
            cells = cells[:, :size_z] + (cells[:, size_z:] + dot(low, line_back_ref[:, :size_z]))
            store_split(after_ref.at[field], lanes[box], cells)
    for field in range(2):
        result = dot(back_ref[...], after_ref[field])
        for box in range(boxes):
            start = box * BOX
            main = result[:inner, lanes[box]].reshape(SPAN, size_y, size_z)
            if box == 0:
                out_ref[field, 0:SPAN] = main
            else:
                out_ref[field, start : start + 2] = out_ref[field, start : start + 2] + main[0:2]
                out_ref[field, start + 2 : start + SPAN] = main[2:]
            for side in range(2):
                strip = result[inner + 24 * side : inner + 24 * side + 24, lanes[box]]
                if box == 0:
                    out_rows_ref[field, side, 0:24] = strip
                else:
                    out_rows_ref[field, side, start : start + 8] = (
                        out_rows_ref[field, side, start : start + 8] + strip[0:8]
                    )
                    out_rows_ref[field, side, start + 8 : start + 24] = strip[8:]


def pack_x(flags, part_ref, part_rows_ref, even_ref, odd_ref):
    last = part_ref.shape[1] - 1
    depth = even_ref.shape[1]
    size_y = part_ref.shape[2]
    for field in range(2):
        for layer in range(depth):
            low, high = layer, last + 1 - depth + layer
            for side, place in ((None, slice(0, size_y)), (0, slice(size_y, size_y + 1)), (1, slice(size_y + 1, size_y + 2))):
                if side is None:
                    to_low, to_high = part_ref[field, low], part_ref[field, high]
                else:
                    shift = ROW0 - 1
                    to_low = part_rows_ref[field, side, low + shift : low + shift + 1]
                    to_high = part_rows_ref[field, side, high + shift : high + shift + 1]
                even_ref[field, layer, place] = chosen(flags, EVEN_X, to_high, to_low)
                odd_ref[field, layer, place] = chosen(flags, EVEN_X, to_low, to_high)
            rest = even_ref.shape[2] - size_y - 2
            blank = jnp.zeros((rest, even_ref.shape[3]), F32)
            even_ref[field, layer, size_y + 2 :] = blank
            odd_ref[field, layer, size_y + 2 :] = blank


def divisor_kernel(conductance_ref, capacity_ref, zones_ref, summed_ref, means_ref, inverse_ref):
    size_x, size_y, size_z = zones_ref.shape
    boxes = size_x // BOX
    lines = []
    for table_ref, which in ((capacity_ref, 0), (capacity_ref, 1), (conductance_ref, 0), (conductance_ref, 1)):
        for box in range(boxes):
            total = jnp.zeros((size_y, size_z), F32)
            for x in range(box * BOX, (box + 1) * BOX):
                zone = zones_ref[x]
                value = jnp.full((size_y, size_z), table_ref[which, 0], F32)
                for label in range(1, table_ref.shape[1]):
                    value = jnp.where(zone == label, table_ref[which, label], value)
                total = total + value
            lines.append(jnp.sum(total, axis=0, keepdims=True))
    sums = jnp.concatenate(lines, axis=0)
    means = jnp.dot(sums, means_ref[...], preferred_element_type=F32, precision=lax.Precision.HIGHEST)
    half = 2 * boxes
    for combo in range(half):
        cbar = means[combo : combo + 1]
        kbar = means[half + combo : half + combo + 1]
        inverse_ref[combo] = 1.0 / (cbar + kbar * summed_ref[...])


def edge_layers_kernel(mesh, load_hbm, zones_hbm, load_ref, zones_ref, even_ref, odd_ref, sems):
    copies = [
        pltpu.make_async_copy(load_hbm.at[0], load_ref.at[0], sems.at[0]),
        pltpu.make_async_copy(load_hbm.at[1], load_ref.at[1], sems.at[1]),
        pltpu.make_async_copy(zones_hbm, zones_ref, sems.at[2]),
    ]
    for copy in copies:
        copy.start()
    flags = standing(mesh)
    last = zones_ref.shape[0] - 1
    for channel in range(4):
        if channel < 3:
            copies[channel].wait()
        if channel < 2:
            low, high = load_ref[channel, 0], load_ref[channel, last]
        else:
            low, high = zones_ref[channel - 2].astype(F32), zones_ref[last - 3 + channel].astype(F32)
        even_ref[channel] = chosen(flags, EVEN_X, high, low)
        odd_ref[channel] = chosen(flags, EVEN_X, low, high)


def edge_rows_kernel(mesh, load_ref, zones_ref, first_ref, second_ref, even_ref, odd_ref):
    flags = standing(mesh)
    size_x, size_y, size_z = zones_ref.shape
    from_low = chosen(flags, EVEN_X, second_ref[...], first_ref[...])
    from_high = chosen(flags, EVEN_X, first_ref[...], second_ref[...])
    blank = jnp.zeros((8, size_z), F32)
    for ref in (even_ref, odd_ref):
        for channel in range(4):
            ref[channel, 0:8] = blank
            ref[channel, size_x : size_x + 8] = blank

    def put(channel, position, count, to_low, to_high):
        place = slice(position, position + count)
        even_ref[channel, place] = chosen(flags, EVEN_Y, to_high, to_low)
        odd_ref[channel, place] = chosen(flags, EVEN_Y, to_low, to_high)

    end = ROW0 + size_x
    for field in range(2):
        put(field, ROW0, size_x, load_ref[field, :, 0], load_ref[field, :, size_y - 1])
        low = keep(flags, LOW_X, from_low[field])
        high = keep(flags, HIGH_X, from_high[field])
        put(field, ROW0 - 1, 1, low[0:1], low[size_y - 1 : size_y])
        put(field, end, 1, high[0:1], high[size_y - 1 : size_y])
    for layer in range(2):
        channel = 2 + layer
        near, far = layer, size_y - 2 + layer
        put(channel, ROW0, size_x, zones_ref[:, near].astype(F32), zones_ref[:, far].astype(F32))
        for depth in range(2):
            low, high = from_low[2 + depth], from_high[2 + depth]
            put(channel, ROW0 - 2 + depth, 1, low[near : near + 1], low[far : far + 1])
            put(channel, end + depth, 1, high[near : near + 1], high[far : far + 1])


def looked_up(entries, zone):
    value = jnp.full(zone.shape, entries[0], F32)
    for label in range(1, len(entries)):
        value = jnp.where(zone == float(label), entries[label], value)
    return value


def coefficient_kernel(
    mesh, conductance_ref, capacity_ref, coupling_ref, zones_ref, first_x, second_x, first_y, second_y,
    half_ref, mass_ref, face_ref, half_rows_ref, mass_rows_ref, face_rows_ref,
):
    flags = standing(mesh)
    labels = range(coupling_ref.shape[0])
    halves_of = [[0.5 * conductance_ref[field, label] for label in labels] for field in range(2)]
    masses = [[capacity_ref[field, label] for label in labels] for field in range(2)]
    line = zones_ref.shape[2:]
    roots = [jnp.sqrt(jnp.full((8, *line), capacity_ref[0, label] * capacity_ref[1, label], F32)) for label in labels]
    masses.append([coupling_ref[label] * roots[label][0:1] for label in labels])
    size_x, size_y, size_z = zones_ref.shape
    low_x = chosen(flags, EVEN_X, second_x[2:4], first_x[2:4])
    high_x = chosen(flags, EVEN_X, first_x[2:4], second_x[2:4])
    low_y = chosen(flags, EVEN_Y, second_y[2:4], first_y[2:4])
    high_y = chosen(flags, EVEN_Y, first_y[2:4], second_y[2:4])
    inside = slice(8, 8 + size_y)
    for x in range(-2, size_x + 2):
        if x < 0:
            zone = low_x[x + 2]
        elif x >= size_x:
            zone = high_x[x - size_x]
        else:
            zone = zones_ref[x].astype(F32)
        for field in range(2):
            half_ref[field, x + 2, inside] = looked_up(halves_of[field], zone)
        if -1 <= x <= size_x:
            for which in range(3):
                mass_ref[which, x + 1] = looked_up(masses[which], zone)
    for field in range(2):
        for outer in (0, 1):
            half_ref[field, outer, inside] = chosen(
                flags, LOW_X, half_ref[field, outer, inside], half_ref[field, 2, inside]
            )
            place = size_x + 2 + outer
            half_ref[field, place, inside] = chosen(
                flags, HIGH_X, half_ref[field, place, inside], half_ref[field, size_x + 1, inside]
            )
    count = half_rows_ref.shape[2]
    position = lax.broadcasted_iota(jnp.int32, (count, size_z), 0)
    for line, (zone, flag) in enumerate(
        ((low_y[0], LOW_Y), (low_y[1], LOW_Y), (high_y[0], HIGH_Y), (high_y[1], HIGH_Y))
    ):
        for field in range(2):
            value = looked_up(halves_of[field], zone)
            below = value[ROW0 : ROW0 + 1]
            above = value[ROW0 + size_x - 1 : ROW0 + size_x]
            value = jnp.where((position < ROW0) & (flags[LOW_X] == 0), below, value)
            value = jnp.where((position >= ROW0 + size_x) & (flags[HIGH_X] == 0), above, value)
            near = half_ref[field, :, 8 if flag == LOW_Y else 8 + size_y - 1]
            half_rows_ref[field, line] = value
            half_rows_ref[field, line, ROW0 - 2 : ROW0 + size_x + 2] = chosen(
                flags, flag, half_rows_ref[field, line, ROW0 - 2 : ROW0 + size_x + 2], near
            )
            if line in (1, 2):
                row = 7 if line == 1 else 8 + size_y
                half_ref[field, :, row] = half_rows_ref[field, line, ROW0 - 2 : ROW0 + size_x + 2]
        if line in (1, 2):
            for which in range(3):
                mass_rows_ref[which, line - 1] = looked_up(masses[which], zone)
    for field in range(2):
        for x in range(0, size_x + 2, 2):
            faces = faces_z(half_ref[field, x + 1 : x + 3, inside])
            for way in range(2):
                face_ref[field, way, x : x + 2] = faces[way]
        for side in range(2):
            faces = faces_z(half_rows_ref[field, side + 1])
            for way in range(2):
                face_rows_ref[field, way, side] = faces[way]
        for line, row in ((4, 8), (5, 8 + size_y - 1)):
            half_rows_ref[field, line] = jnp.zeros((count, size_z), F32)
            half_rows_ref[field, line, ROW0 - 2 : ROW0 + size_x + 2] = half_ref[field, :, row]


def first_solve_kernel(
    mesh, load_ref, first_x, second_x, first_y, second_y, inverse_ref, c0, c1, c2, c3,
    part_ref, part_rows_ref, even_ref, odd_ref, field_ref, rows_ref, before_ref, after_ref,
):
    flags = standing(mesh)
    size_x = load_ref.shape[1]
    for field in range(2):
        field_ref[field, 1 : 1 + size_x] = load_ref[field]
        field_ref[field, 0] = keep(flags, LOW_X, chosen(flags, EVEN_X, second_x[field], first_x[field]))
        field_ref[field, 1 + size_x] = keep(flags, HIGH_X, chosen(flags, EVEN_X, first_x[field], second_x[field]))
        rows_ref[field, 0] = keep(flags, LOW_Y, chosen(flags, EVEN_Y, second_y[field], first_y[field]))
        rows_ref[field, 1] = keep(flags, HIGH_Y, chosen(flags, EVEN_Y, first_y[field], second_y[field]))
    solve(field_ref, rows_ref, inverse_ref, (c0, c1, c2, c3), before_ref, after_ref, part_ref, part_rows_ref)
    pack_x(flags, part_ref, part_rows_ref, even_ref, odd_ref)


def merge_x_kernel(mesh, part_ref, part_rows_ref, first_ref, second_ref, whole_ref, whole_rows_ref, even_ref, odd_ref):
    flags = standing(mesh)
    size_x = part_ref.shape[1] - 2
    size_y, size_z = part_ref.shape[2:]
    depth = first_ref.shape[1]
    count = part_rows_ref.shape[2]
    end = ROW0 + size_x
    for field in range(2):
        low = keep(flags, LOW_X, chosen(flags, EVEN_X, second_ref[field], first_ref[field]))
        high = keep(flags, HIGH_X, chosen(flags, EVEN_X, first_ref[field], second_ref[field]))
        whole_ref[field, 1] = keep(flags, LOW_X, part_ref[field, 0]) + low[depth - 2, :size_y]
        whole_ref[field, 2] = part_ref[field, 1] + low[depth - 1, :size_y]
        whole_ref[field, 3 : size_x + 1] = part_ref[field, 2:size_x]
        whole_ref[field, size_x + 1] = part_ref[field, size_x] + high[0, :size_y]
        whole_ref[field, size_x + 2] = keep(flags, HIGH_X, part_ref[field, size_x + 1]) + high[1, :size_y]
        if depth == 3:
            whole_ref[field, 0] = low[0, :size_y]
            whole_ref[field, size_x + 3] = high[2, :size_y]
        for side in range(2):
            row = slice(size_y + side, size_y + side + 1)
            edge = ROW0 - 1
            whole_rows_ref[field, side] = part_rows_ref[field, side]
            whole_rows_ref[field, side, edge : edge + 1] = (
                keep(flags, LOW_X, part_rows_ref[field, side, edge : edge + 1]) + low[depth - 2, row]
            )
            whole_rows_ref[field, side, edge + 1 : edge + 2] = (
                part_rows_ref[field, side, edge + 1 : edge + 2] + low[depth - 1, row]
            )
            whole_rows_ref[field, side, end - 1 : end] = part_rows_ref[field, side, end - 1 : end] + high[0, row]
            whole_rows_ref[field, side, end : end + 1] = (
                keep(flags, HIGH_X, part_rows_ref[field, side, end : end + 1]) + high[1, row]
            )
            if depth == 3:
                whole_rows_ref[field, side, edge - 1 : edge] = low[0, row]
                whole_rows_ref[field, side, end + 1 : end + 2] = high[2, row]

        def put(at, to_low, to_high):
            even_ref[(field, *at)] = chosen(flags, EVEN_Y, to_high, to_low)
            odd_ref[(field, *at)] = chosen(flags, EVEN_Y, to_low, to_high)

        if depth == 3:
            blank = jnp.zeros((8, size_z), F32)
            for layer in range(3):
                for ref in (even_ref, odd_ref):
                    ref[field, layer, 0:8] = blank
                    ref[field, layer, count - 8 : count] = blank
            rows = slice(ROW0 - 2, end + 2)
            low_rows = whole_rows_ref[field, 0, rows]
            high_rows = whole_rows_ref[field, 1, rows]
            put((0, rows), low_rows, whole_ref[field, :, size_y - 2])
            put((1, rows), whole_ref[field, :, 0], whole_ref[field, :, size_y - 1])
            put((2, rows), whole_ref[field, :, 1], high_rows)
        else:
            own = slice(2, size_x + 2)
            put((slice(0, size_x),), whole_ref[field, own, 0], whole_ref[field, own, size_y - 1])
            put((slice(size_x, None),), whole_rows_ref[field, 0], whole_rows_ref[field, 1])


def assemble(flags, whole_ref, whole_rows_ref, first_ref, second_ref, field_ref, lines):
    size_x = whole_ref.shape[1] - 4
    size_y = whole_ref.shape[2]
    spread = slice(ROW0 - 2, ROW0 + size_x + 2)
    for field in range(2):
        low = keep(flags, LOW_Y, chosen(flags, EVEN_Y, second_ref[field], first_ref[field]))
        high = keep(flags, HIGH_Y, chosen(flags, EVEN_Y, first_ref[field], second_ref[field]))
        below = keep(flags, LOW_Y, whole_rows_ref[field, 0]) + low[1]
        above = keep(flags, HIGH_Y, whole_rows_ref[field, 1]) + high[1]
        lines[field, 0] = low[0]
        lines[field, 1] = below
        lines[field, 2] = above
        lines[field, 3] = high[2]
        lines[field, 4] = low[2]
        lines[field, 5] = high[0]
        field_ref[field, :, 8 : 8 + size_y] = whole_ref[field]
        field_ref[field, :, 7] = lines[field, 1, spread]
        field_ref[field, :, 8 + size_y] = lines[field, 2, spread]
        field_ref[field, :, 8] = field_ref[field, :, 8] + lines[field, 4, spread]
        field_ref[field, :, 7 + size_y] = field_ref[field, :, 7 + size_y] + lines[field, 5, spread]


def faces_z(half):
    size_z, axis = half.shape[-1], half.ndim - 1
    lane = lax.broadcasted_iota(jnp.int32, half.shape, axis)
    upper = half + jnp.where(lane == size_z - 1, half, pltpu.roll(half, size_z - 1, axis))
    lower = half + jnp.where(lane == 0, half, pltpu.roll(half, 1, axis))
    return upper, lower


def along_z(value, upper, lower):
    size_z, axis = value.shape[-1], value.ndim - 1
    lane = lax.broadcasted_iota(jnp.int32, value.shape, axis)
    above = jnp.where(lane == size_z - 1, 0.0, pltpu.roll(value, size_z - 1, axis))
    below = jnp.where(lane == 0, 0.0, pltpu.roll(value, 1, axis))
    return upper * (value - above) + lower * (value - below)


def operate(field_ref, half_ref, mass_ref, face_ref, x, count):
    size_y = mass_ref.shape[2]
    inside = slice(8, 8 + size_y)
    masses = slice(x + 1, x + 1 + count)
    here = slice(x + 2, x + 2 + count)
    values, images = [], []
    for field in range(2):
        value = field_ref[field, here, inside]
        half = half_ref[field, here, inside]
        flux = along_z(value, face_ref[field, 0, masses], face_ref[field, 1, masses])
        for start in (x + 1, x + 3):
            place = slice(start, start + count)
            flux = flux + (half + half_ref[field, place, inside]) * (value - field_ref[field, place, inside])
        for shift in (-1, 1):
            moved = slice(8 + shift, 8 + shift + size_y)
            flux = flux + (half + half_ref[field, here, moved]) * (value - field_ref[field, here, moved])
        values.append(value)
        images.append(flux)
    first = mass_ref[0, masses] * values[0] + mass_ref[2, masses] * values[1] + images[0]
    second = mass_ref[2, masses] * values[0] + mass_ref[1, masses] * values[1] + images[1]
    return values, (first, second)


def operate_line(lines, half_lines, mass_lines, face_lines, side, near):
    outer, center, inner = (0, 1, 4) if side == 0 else (3, 2, 5)
    values, images = [], []
    for field in range(2):
        value = lines[field, center]
        half = half_lines[field, center]
        count = value.shape[0]
        flux = along_z(value, face_lines[field, 0, side], face_lines[field, 1, side])
        for turn in (1, count - 1):
            flux = flux + (half + pltpu.roll(half, turn, 0)) * (value - pltpu.roll(value, turn, 0))
        flux = flux + (half + half_lines[field, outer]) * (value - lines[field, outer])
        flux = flux + (half + half_lines[field, inner]) * (value - near[field, side])
        values.append(value)
        images.append(flux)
    first = mass_lines[0, side] * values[0] + mass_lines[2, side] * values[1] + images[0]
    second = mass_lines[2, side] * values[0] + mass_lines[1, side] * values[1] + images[1]
    return first, second


def second_solve_kernel(
    mesh, whole_ref, whole_rows_ref, first_ref, second_ref,
    half_ref, mass_ref, face_ref, half_lines, mass_lines, face_lines, load_ref, inverse_ref, c0, c1, c2, c3,
    precond_ref, image_ref, sums_ref, part_ref, part_rows_ref, even_ref, odd_ref,
    value_ref, lines, near, field_ref, rows_ref, before_ref, after_ref,
):
    flags = standing(mesh)
    size_x, size_y, size_z = load_ref.shape[1:]
    assemble(flags, whole_ref, whole_rows_ref, first_ref, second_ref, value_ref, lines)
    for x, flag in ((-1, LOW_X), (size_x, HIGH_X)):
        _, images = operate(value_ref, half_ref, mass_ref, face_ref, x, 1)
        for field in range(2):
            field_ref[field, x + 1 : x + 2] = keep(flags, flag, images[field])
    total_a = total_b = jnp.zeros((CHUNK, size_y, size_z), F32)
    for x in range(0, size_x, CHUNK):
        chunk = slice(x, x + CHUNK)
        values, images = operate(value_ref, half_ref, mass_ref, face_ref, x, CHUNK)
        for field in range(2):
            precond_ref[field, chunk] = values[field]
            image_ref[field, chunk] = images[field]
            field_ref[field, x + 1 : x + 1 + CHUNK] = images[field]
            total_a = total_a + load_ref[field, chunk] * values[field]
            total_b = total_b + images[field] * values[field]
    sums_ref[0:1] = jnp.sum(jnp.sum(total_a, axis=0), axis=0, keepdims=True)
    sums_ref[1:2] = jnp.sum(jnp.sum(total_b, axis=0), axis=0, keepdims=True)
    sums_ref[2:8] = jnp.zeros((6, size_z), F32)
    count = rows_ref.shape[2]
    position = lax.broadcasted_iota(jnp.int32, (count, size_z), 0)
    begin = jnp.where(flags[LOW_X] > 0, ROW0 - 1, ROW0)
    end = jnp.where(flags[HIGH_X] > 0, ROW0 + size_x + 1, ROW0 + size_x)
    valid = (position >= begin) & (position < end)
    for field in range(2):
        for side, row in ((0, 8), (1, 7 + size_y)):
            near[field, side] = jnp.zeros((count, size_z), F32)
            near[field, side, ROW0 - 2 : ROW0 + size_x + 2] = value_ref[field, :, row]
    for side, flag in ((0, LOW_Y), (1, HIGH_Y)):
        images = operate_line(lines, half_lines, mass_lines, face_lines, side, near)
        for field in range(2):
            rows_ref[field, side] = keep(flags, flag, jnp.where(valid, images[field], 0.0))
    solve(field_ref, rows_ref, inverse_ref, (c0, c1, c2, c3), before_ref, after_ref, part_ref, part_rows_ref)
    pack_x(flags, part_ref, part_rows_ref, even_ref, odd_ref)


def second_image_kernel(
    mesh, whole_ref, whole_rows_ref, first_ref, second_ref, half_ref, mass_ref, face_ref, old_image_ref, old_sums_ref,
    precond_ref, image_ref, sums_ref, value_ref,
):
    flags = standing(mesh)
    size_x, size_y, size_z = old_image_ref.shape[1:]
    own, wide = slice(2, size_x + 2), slice(1, size_x + 3)
    rows, margins = slice(ROW0, ROW0 + size_x), slice(size_x + ROW0 - 1, 2 * size_x + ROW0 + 1)
    for field in range(2):
        low = keep(flags, LOW_Y, chosen(flags, EVEN_Y, second_ref[field], first_ref[field]))
        high = keep(flags, HIGH_Y, chosen(flags, EVEN_Y, first_ref[field], second_ref[field]))
        value_ref[field, wide, 8 : 8 + size_y] = whole_ref[field, wide]
        value_ref[field, own, 7] = keep(flags, LOW_Y, whole_rows_ref[field, 0, rows]) + low[:size_x]
        value_ref[field, wide, 8] = whole_ref[field, wide, 0] + low[margins]
        value_ref[field, wide, 7 + size_y] = whole_ref[field, wide, size_y - 1] + high[margins]
        value_ref[field, own, 8 + size_y] = keep(flags, HIGH_Y, whole_rows_ref[field, 1, rows]) + high[:size_x]
    total_c = total_d = jnp.zeros((CHUNK, size_y, size_z), F32)
    for x in range(0, size_x, CHUNK):
        chunk = slice(x, x + CHUNK)
        values, images = operate(value_ref, half_ref, mass_ref, face_ref, x, CHUNK)
        for field in range(2):
            precond_ref[field, chunk] = values[field]
            image_ref[field, chunk] = images[field]
            total_c = total_c + old_image_ref[field, chunk] * values[field]
            total_d = total_d + images[field] * values[field]
    total_c, total_d = jnp.sum(total_c, axis=0), jnp.sum(total_d, axis=0)
    totals = [
        jnp.sum(old_sums_ref[0:1], axis=1, keepdims=True),
        jnp.sum(old_sums_ref[1:2], axis=1, keepdims=True),
        jnp.sum(jnp.sum(total_c, axis=0, keepdims=True), axis=1, keepdims=True),
        jnp.sum(jnp.sum(total_d, axis=0, keepdims=True), axis=1, keepdims=True),
    ]
    lane = lax.broadcasted_iota(jnp.int32, sums_ref.shape, 1)
    spread = jnp.zeros(sums_ref.shape, F32)
    for place, total in enumerate(totals):
        spread = jnp.where(lane == place, total, spread)
    sums_ref[...] = spread


def finish_kernel(
    sums_ref, load_ref, z_ref, q_ref, w_ref, s_ref, solution_hbm, residual_hbm, solution_ref, residual_ref, sems
):
    line = jnp.sum(sums_ref[...], axis=0, keepdims=True)
    lane = lax.broadcasted_iota(jnp.int32, line.shape, 1)
    rz, zq, qw, ws = [jnp.sum(jnp.where(lane == place, line, 0.0), axis=1, keepdims=True) for place in range(4)]
    alpha = rz / zq
    rz_next = rz - alpha * (2.0 * zq) + alpha * alpha * qw
    grown = 1.0 + rz_next / rz
    curvature = grown * grown * zq - 2.0 * grown * alpha * qw + alpha * alpha * ws
    alpha_next = rz_next / curvature
    along = alpha + alpha_next * grown
    against = alpha_next * alpha
    copies = []
    step = load_ref.shape[1] // 2
    for field in range(2):
        for start in range(0, 2 * step, step):
            part = pl.ds(start, step)
            for x in range(start, start + step):
                solution_ref[field, x] = along * z_ref[field, x] - against * w_ref[field, x]
                residual_ref[field, x] = load_ref[field, x] - along * q_ref[field, x] + against * s_ref[field, x]
            for here, there in ((solution_ref, solution_hbm), (residual_ref, residual_hbm)):
                copies.append(
                    pltpu.make_async_copy(here.at[field, part], there.at[field, part], sems.at[len(copies)])
                )
                copies[-1].start()
    for copy in copies:
        copy.wait()


SMEM = pl.BlockSpec(memory_space=pltpu.SMEM)
VMEM = pl.BlockSpec(memory_space=pltpu.VMEM)
HBM = pl.BlockSpec(memory_space=pltpu.HBM)


def call(mesh, kernel, scalars, arrays, outs, scratch=(), flops=0, limit=24, in_hbm=False, outs_in_hbm=False):
    moved = sum(math.prod(a.shape) * a.dtype.itemsize for a in list(arrays) + list(outs))
    return pl.pallas_call(
        kernel if mesh is None else functools.partial(kernel, mesh),
        out_shape=tuple(outs),
        in_specs=[SMEM] * len(scalars) + [HBM if in_hbm else VMEM] * len(arrays),
        out_specs=tuple([HBM if outs_in_hbm else VMEM] * len(outs)),
        scratch_shapes=list(scratch),
        compiler_params=pltpu.CompilerParams(vmem_limit_bytes=limit * 1024 * 1024),
        cost_estimate=pl.CostEstimate(flops=flops, bytes_accessed=moved, transcendentals=0),
    )(*scalars, *arrays)


def shards(mesh, load, zones, conductance, capacity, coupling):
    size_x, size_y, size_z = zones.shape
    assert size_x % BOX == 0 and size_y == BOX and size_z % BOX == 0
    boxes = size_x // BOX
    count = size_x + 8
    sds = lambda *shape: jax.ShapeDtypeStruct(shape, F32)
    forward, back, line_forward, line_back, summed, means = [jnp.asarray(c) for c in constants(size_z)]
    consts = (forward, back, line_forward, line_back)
    modes, lanes = summed.shape
    load, zones, *packed = call(
        mesh,
        edge_layers_kernel,
        [],
        [load, zones],
        [sds(*load.shape), jax.ShapeDtypeStruct(zones.shape, zones.dtype)] + [sds(4, size_y, size_z)] * 2,
        [pltpu.SemaphoreType.DMA((3,))],
        in_hbm=True,
    )
    x_halo = swap(mesh, "gx", *packed)
    (inverse,) = call(
        None,
        divisor_kernel,
        [conductance, capacity],
        [zones, summed, means],
        [sds(2 * boxes, modes, lanes)],
        flops=40_000_000,
    )
    packed = call(mesh, edge_rows_kernel, [], [load, zones, *x_halo], [sds(4, count, size_z)] * 2)
    y_halo = swap(mesh, "gy", *packed)
    half, mass, face, half_lines, mass_lines, face_lines = call(
        mesh,
        coefficient_kernel,
        [conductance, capacity, coupling],
        [zones, *x_halo, *y_halo],
        [
            sds(2, size_x + 4, size_y + 16, size_z),
            sds(3, size_x + 2, size_y, size_z),
            sds(2, 2, size_x + 2, size_y, size_z),
            sds(2, 6, count, size_z),
            sds(3, 2, count, size_z),
            sds(2, 2, 2, count, size_z),
        ],
        flops=20_000_000,
    )
    parts = [sds(2, size_x + 2, size_y, size_z), sds(2, 2, count, size_z)]
    packed_x = [[sds(2, depth, size_y + 8, size_z)] * 2 for depth in (3, 2)]
    wholes = [sds(2, size_x + 4, size_y, size_z), sds(2, 2, count, size_z)]
    packed_y = [[sds(2, 3, count, size_z)] * 2, [sds(2, size_x + count, size_z)] * 2]
    rows = SPAN * size_y + 48
    work = [
        pltpu.VMEM((2, size_x + 2, size_y, size_z), F32),
        pltpu.VMEM((2, 2, count, size_z), F32),
        pltpu.VMEM((2, 3 * rows, boxes * size_z), BF16),
        pltpu.VMEM((2, 3 * rows, boxes * size_z), BF16),
    ]
    padded = [
        pltpu.VMEM((2, size_x + 4, size_y + 16, size_z), F32),
        pltpu.VMEM((2, 6, count, size_z), F32),
    ]
    own = sds(2, size_x, size_y, size_z)

    part, part_rows, *packed = call(
        mesh, first_solve_kernel, [], [load, *x_halo, *y_halo, inverse, *consts], parts + packed_x[0], work, 3_000_000_000
    )
    received = swap(mesh, "gx", *packed)
    whole, whole_rows, *packed = call(mesh, merge_x_kernel, [], [part, part_rows, *received], wholes + packed_y[0])
    received = swap(mesh, "gy", *packed)
    precond, image, sums, part, part_rows, *packed = call(
        mesh,
        second_solve_kernel,
        [],
        [whole, whole_rows, *received, half, mass, face, half_lines, mass_lines, face_lines, load, inverse, *consts],
        [own, own, sds(8, size_z)] + parts + packed_x[1],
        padded + [pltpu.VMEM((2, 2, count, size_z), F32)] + work,
        3_000_000_000,
    )
    received = swap(mesh, "gx", *packed)
    whole, whole_rows, *packed = call(mesh, merge_x_kernel, [], [part, part_rows, *received], wholes + packed_y[1])
    received = swap(mesh, "gy", *packed)
    devices = mesh.shape["gx"] * mesh.shape["gy"]
    last_precond, last_image, sums = call(
        mesh,
        second_image_kernel,
        [],
        [whole, whole_rows, *received, half, mass, face, image, sums],
        [own, own, sds(devices, size_z)],
        padded[:1],
        10_000_000,
    )
    sums = lax.all_to_all(sums, AXES, 0, 0, tiled=True)
    whole_block = pltpu.VMEM((2, size_x, size_y, size_z), F32)
    return call(
        None,
        finish_kernel,
        [],
        [sums, load, precond, image, last_precond, last_image],
        [own, own],
        [whole_block, whole_block, pltpu.SemaphoreType.DMA((8,))],
        outs_in_hbm=True,
    )


def solution(mesh):
    in_specs = (P(None, "gx", "gy", None), P("gx", "gy", None), P(), P(), P())
    out_specs = (P(None, "gx", "gy", None), P(None, "gx", "gy", None))
    return jax.shard_map(
        functools.partial(shards, mesh), mesh=mesh, in_specs=in_specs, out_specs=out_specs, check_vma=False
    )
```

```python
import functools
import math

import jax
import jax.numpy as jnp
import ml_dtypes
import numpy as np
from jax import lax
from jax.experimental import pallas as pl
from jax.experimental.pallas import tpu as pltpu
from jax.sharding import PartitionSpec as P

BOX = 16
SPAN = BOX + 2
F32 = jnp.float32
BF16 = jnp.bfloat16
AXES = ("gx", "gy")
ROW0 = 4
CHUNK = 4


def split(matrix):
    high = matrix.astype(ml_dtypes.bfloat16)
    low = (matrix - high.astype(np.float64)).astype(ml_dtypes.bfloat16)
    return high, low


def round_up(value, step):
    return (value + step - 1) // step * step


def sine_basis():
    index = np.arange(SPAN)
    angle = np.pi * np.outer(index + 1, index + 1) / (SPAN + 1)
    return np.sqrt(2.0 / (SPAN + 1)) * np.sin(angle)


def eigenvalues():
    return 4.0 * np.sin(np.pi * (np.arange(SPAN) + 1) / (2 * (SPAN + 1))) ** 2


def plane_layout():
    places = [(x, y + 1) for x in range(SPAN) for y in range(BOX)]
    for y in (0, SPAN - 1):
        for position in range(24):
            x = position - (ROW0 - 1)
            places.append((x, y) if 0 <= x < SPAN else None)
    return places


def constants(size_z):
    basis = sine_basis()
    places = plane_layout()
    rows = len(places)
    modes = SPAN * SPAN
    padded_modes = round_up(modes, 16)
    plane = np.zeros((padded_modes, rows))
    for column, place in enumerate(places):
        if place is not None:
            plane[:modes, column] = np.outer(basis[:, place[0]], basis[:, place[1]]).reshape(-1)
    high, low = split(plane)
    forward = np.concatenate([high, high, low], axis=1)
    high, low = split(plane.T)
    inverse = np.concatenate([high, high, low], axis=1)
    boxes = size_z // BOX
    line = np.zeros((size_z, boxes * SPAN))
    for box in range(boxes):
        for mode in range(SPAN):
            for offset in range(SPAN):
                cell = box * BOX + offset - 1
                if 0 <= cell < size_z:
                    line[cell, box * SPAN + mode] = basis[mode, offset]
    high, low = split(line)
    line_forward = np.concatenate([high, high, low], axis=0)
    high, low = split(line.T)
    line_inverse = np.concatenate([high, low], axis=1)
    return forward, inverse, line_forward, line_inverse


def swap_pairs(mesh, axis, odd):
    sizes = [mesh.shape[name] for name in AXES]
    along = AXES.index(axis)
    pairs = []
    for i in range(sizes[0]):
        for j in range(sizes[1]):
            here = [i, j]
            there = [i, j]
            place = here[along]
            target = place ^ 1 if not odd else (place + 1 if place % 2 else place - 1)
            if 0 <= target < sizes[along]:
                there[along] = target
            elif along == 0:
                there[0] = sizes[0] - 1 - place
            else:
                there[0] = i ^ 1
            pairs.append((here[0] * sizes[1] + here[1], there[0] * sizes[1] + there[1]))
    return pairs


def swap(mesh, axis, even_part, odd_part):
    if axis == "gx":
        first = lax.ppermute(even_part, AXES, swap_pairs(mesh, axis, False))
        second = lax.ppermute(odd_part, AXES, swap_pairs(mesh, axis, True))
    else:
        second = lax.ppermute(odd_part, AXES, swap_pairs(mesh, axis, True))
        first = lax.ppermute(even_part, AXES, swap_pairs(mesh, axis, False))
    return first, second


EVEN_X, EVEN_Y, LOW_X, HIGH_X, LOW_Y, HIGH_Y = range(6)


def standing(mesh):
    here_x, here_y = lax.axis_index("gx"), lax.axis_index("gy")
    facts = (
        lax.rem(here_x, 2) == 0,
        lax.rem(here_y, 2) == 0,
        here_x > 0,
        here_x < mesh.shape["gx"] - 1,
        here_y > 0,
        here_y < mesh.shape["gy"] - 1,
    )
    return [fact.astype(jnp.int32) for fact in facts]


def chosen(flags, which, yes, no):
    return jnp.where(flags[which] > 0, yes, no)


def keep(flags, which, value):
    return jnp.where(flags[which] > 0, value, jnp.zeros_like(value))


def halves(value):
    high = value.astype(BF16)
    low = (value - high.astype(F32)).astype(BF16)
    return high, low


def dot(left, right):
    return jnp.dot(left, right, preferred_element_type=F32)


def store_split(stack_ref, lanes, value):
    rows = value.shape[0]
    high, low = halves(value)
    stack_ref[0:rows, lanes] = high
    stack_ref[rows : 2 * rows, lanes] = low
    stack_ref[2 * rows : 3 * rows, lanes] = high


def solve(field_ref, rows_ref, inverse_ref, consts, before_ref, after_ref, out_ref, out_rows_ref):
    forward_ref, back_ref, line_forward_ref, line_back_ref = consts
    boxes = (field_ref.shape[1] - 2) // BOX
    size_y, size_z = field_ref.shape[2:]
    inner = SPAN * size_y
    line_rows = line_forward_ref.shape[0] // 3
    lanes = [slice(box * size_z, (box + 1) * size_z) for box in range(boxes)]
    for field in range(2):
        for box in range(boxes):
            start = box * BOX
            main = field_ref[field, start : start + SPAN].reshape(inner, size_z)
            strips = [rows_ref[field, side, start : start + 24] for side in range(2)]
            store_split(before_ref.at[field], lanes[box], jnp.concatenate([main, *strips], axis=0))
    spectral = [dot(forward_ref[...], before_ref[field]) for field in range(2)]
    for field in range(2):
        for box in range(boxes):
            high, low = halves(spectral[field][:, lanes[box]])
            both = jnp.concatenate([high, low], axis=1)
            modes = dot(both, line_forward_ref[0 : 2 * line_rows]) + dot(high, line_forward_ref[2 * line_rows :])
            modes = modes * inverse_ref[field * boxes + box]
            high, low = halves(modes)
            cells = dot(high, line_back_ref[...])
            cells = cells[:, :size_z] + (cells[:, size_z:] + dot(low, line_back_ref[:, :size_z]))
            store_split(after_ref.at[field], lanes[box], cells)
    for field in range(2):
        result = dot(back_ref[...], after_ref[field])
        for box in range(boxes):
            start = box * BOX
            main = result[:inner, lanes[box]].reshape(SPAN, size_y, size_z)
            if box == 0:
                out_ref[field, 0:SPAN] = main
            else:
                out_ref[field, start : start + 2] = out_ref[field, start : start + 2] + main[0:2]
                out_ref[field, start + 2 : start + SPAN] = main[2:]
            for side in range(2):
                strip = result[inner + 24 * side : inner + 24 * side + 24, lanes[box]]
                if box == 0:
                    out_rows_ref[field, side, 0:24] = strip
                else:
                    out_rows_ref[field, side, start : start + 8] = (
                        out_rows_ref[field, side, start : start + 8] + strip[0:8]
                    )
                    out_rows_ref[field, side, start + 8 : start + 24] = strip[8:]


def pack_x(flags, part_ref, part_rows_ref, even_ref, odd_ref):
    last = part_ref.shape[1] - 1
    depth = even_ref.shape[1]
    size_y = part_ref.shape[2]
    for field in range(2):
        for layer in range(depth):
            low, high = layer, last + 1 - depth + layer
            for side, place in ((None, slice(0, size_y)), (0, slice(size_y, size_y + 1)), (1, slice(size_y + 1, size_y + 2))):
                if side is None:
                    to_low, to_high = part_ref[field, low], part_ref[field, high]
                else:
                    shift = ROW0 - 1
                    to_low = part_rows_ref[field, side, low + shift : low + shift + 1]
                    to_high = part_rows_ref[field, side, high + shift : high + shift + 1]
                even_ref[field, layer, place] = chosen(flags, EVEN_X, to_high, to_low)
                odd_ref[field, layer, place] = chosen(flags, EVEN_X, to_low, to_high)
            rest = even_ref.shape[2] - size_y - 2
            blank = jnp.zeros((rest, even_ref.shape[3]), F32)
            even_ref[field, layer, size_y + 2 :] = blank
            odd_ref[field, layer, size_y + 2 :] = blank


def line_pairs(whole_ref, whole_rows_ref, field, layers, rows, depth):
    size_y = whole_ref.shape[2]
    if depth == 3:
        return (
            (whole_rows_ref[field, 0, rows], whole_ref[field, layers, size_y - 2]),
            (whole_ref[field, layers, 0], whole_ref[field, layers, size_y - 1]),
            (whole_ref[field, layers, 1], whole_rows_ref[field, 1, rows]),
        )
    return (
        (whole_ref[field, layers, 0], whole_ref[field, layers, size_y - 1]),
        (whole_rows_ref[field, 0, rows], whole_rows_ref[field, 1, rows]),
    )


def pack_lines(flags, part_ref, part_rows_ref, even_ref, odd_ref):
    size_x = part_ref.shape[1] - 2
    depth = even_ref.shape[1] // size_x
    for field in range(2):
        pairs = line_pairs(
            part_ref, part_rows_ref, field, slice(1, size_x + 1), slice(ROW0, ROW0 + size_x), depth
        )
        for line, (to_low, to_high) in enumerate(pairs):
            place = slice(line * size_x, (line + 1) * size_x)
            even_ref[field, place] = chosen(flags, EVEN_Y, to_high, to_low)
            odd_ref[field, place] = chosen(flags, EVEN_Y, to_low, to_high)


def unpack_lines(flags, lines_refs, ends_refs, out_ref, field):
    size_x = out_ref.shape[2] - 8
    depth = lines_refs[0].shape[1] // size_x
    blank = jnp.zeros((8, out_ref.shape[3]), F32)
    for side, flag, (even, odd) in ((0, LOW_Y, (1, 0)), (1, HIGH_Y, (0, 1))):
        lines = keep(flags, flag, chosen(flags, EVEN_Y, lines_refs[even][field], lines_refs[odd][field]))
        ends = keep(flags, flag, chosen(flags, EVEN_Y, ends_refs[even][field], ends_refs[odd][field]))
        for line in range(depth):
            out_ref[side, line, 0:8] = blank
            out_ref[side, line, size_x : size_x + 8] = blank
            out_ref[side, line, ROW0 : ROW0 + size_x] = lines[line * size_x : (line + 1) * size_x]
            out_ref[side, line, ROW0 - 2 : ROW0 + 1] = ends[8 * line : 8 * line + 3]
            out_ref[side, line, ROW0 + size_x - 1 : ROW0 + size_x + 2] = ends[8 * line + 3 : 8 * line + 6]


def divisor_kernel(conductance_ref, capacity_ref, zones_ref, inverse_ref):
    size_x, size_y, size_z = zones_ref.shape
    boxes = size_x // BOX
    lines = []
    for table_ref, which in ((capacity_ref, 0), (capacity_ref, 1), (conductance_ref, 0), (conductance_ref, 1)):
        for box in range(boxes):
            total = jnp.zeros((size_y, size_z), F32)
            for x in range(box * BOX, (box + 1) * BOX):
                zone = zones_ref[x]
                value = jnp.full((size_y, size_z), table_ref[which, 0], F32)
                for label in range(1, table_ref.shape[1]):
                    value = jnp.where(zone == label, table_ref[which, label], value)
                total = total + value
            lines.append(jnp.sum(total, axis=0, keepdims=True))
    sums = jnp.concatenate(lines, axis=0)
    modes, lanes = inverse_ref.shape[1:]
    cell = lax.broadcasted_iota(jnp.int32, (size_z, lanes), 0)
    lane = lax.broadcasted_iota(jnp.int32, (size_z, lanes), 1)
    spread = jnp.zeros((size_z, lanes), F32)
    for box in range(size_z // BOX):
        here = (cell >= box * BOX) & (cell < (box + 1) * BOX) & (lane >= box * SPAN) & (lane < (box + 1) * SPAN)
        spread = jnp.where(here, 1.0 / BOX**3, spread)
    means = jnp.dot(sums, spread, preferred_element_type=F32, precision=lax.Precision.HIGHEST)
    eigen = [float(value) for value in eigenvalues()]
    row = lax.broadcasted_iota(jnp.int32, (modes, 128), 0)
    first = jnp.zeros(row.shape, jnp.int32)
    for mode in range(1, SPAN):
        first = first + (row >= mode * SPAN).astype(jnp.int32)
    second = row - SPAN * first
    pair = jnp.zeros(row.shape, F32)
    for mode in range(SPAN):
        pair = pair + jnp.where(first == mode, eigen[mode], 0.0) + jnp.where(second == mode, eigen[mode], 0.0)
    lane = lax.broadcasted_iota(jnp.int32, (8, lanes), 1)
    for box in range(1, size_z // BOX):
        lane = lane - SPAN * (lax.broadcasted_iota(jnp.int32, (8, lanes), 1) >= box * SPAN).astype(jnp.int32)
    third = jnp.zeros(lane.shape, F32)
    for mode in range(SPAN):
        third = jnp.where(lane == mode, eigen[mode], third)
    summed = jnp.concatenate([pair, pair[:, : lanes - 128]], axis=1) + third[0:1]
    half = 2 * boxes
    for combo in range(half):
        cbar = means[combo : combo + 1]
        kbar = means[half + combo : half + combo + 1]
        inverse_ref[combo] = 1.0 / (cbar + kbar * summed)


def edge_layers_kernel(
    mesh, load_hbm, zones_hbm, load_ref, zones_ref, even_ref, odd_ref, even_lines, odd_lines, sems
):
    copies = [
        pltpu.make_async_copy(load_hbm.at[0], load_ref.at[0], sems.at[0]),
        pltpu.make_async_copy(load_hbm.at[1], load_ref.at[1], sems.at[1]),
        pltpu.make_async_copy(zones_hbm, zones_ref, sems.at[2]),
    ]
    for copy in copies:
        copy.start()
    flags = standing(mesh)
    last = zones_ref.shape[0] - 1
    size_y = zones_ref.shape[1]
    for channel in range(4):
        if channel < 3:
            copies[channel].wait()
        if channel < 2:
            low, high = load_ref[channel, 0], load_ref[channel, last]
            low_line, high_line = load_ref[channel, :, 0], load_ref[channel, :, size_y - 1]
        else:
            low, high = zones_ref[channel - 2].astype(F32), zones_ref[last - 3 + channel].astype(F32)
            low_line = zones_ref[:, channel - 2].astype(F32)
            high_line = zones_ref[:, size_y - 4 + channel].astype(F32)
        even_ref[channel] = chosen(flags, EVEN_X, high, low)
        odd_ref[channel] = chosen(flags, EVEN_X, low, high)
        even_lines[channel] = chosen(flags, EVEN_Y, high_line, low_line)
        odd_lines[channel] = chosen(flags, EVEN_Y, low_line, high_line)


def edge_ends_kernel(mesh, first_ref, second_ref, inverse_ref, even_ref, odd_ref):
    flags = standing(mesh)
    size_y = first_ref.shape[1]
    from_low = chosen(flags, EVEN_X, second_ref[...], first_ref[...])
    from_high = chosen(flags, EVEN_X, first_ref[...], second_ref[...])

    def put(row, layer, near, far):
        to_low, to_high = layer[near : near + 1], layer[far : far + 1]
        even_ref[row : row + 1] = chosen(flags, EVEN_Y, to_high, to_low)
        odd_ref[row : row + 1] = chosen(flags, EVEN_Y, to_low, to_high)

    for ref in (even_ref, odd_ref):
        ref[8:16] = jnp.zeros((8, ref.shape[1]), F32)
    for field in range(2):
        put(2 * field, keep(flags, LOW_X, from_low[field]), 0, size_y - 1)
        put(2 * field + 1, keep(flags, HIGH_X, from_high[field]), 0, size_y - 1)
    for line in range(2):
        for depth in range(2):
            put(4 + 4 * line + depth, from_low[2 + depth], line, size_y - 2 + line)
            put(6 + 4 * line + depth, from_high[2 + depth], line, size_y - 2 + line)


def looked_up(entries, zone):
    value = jnp.full(zone.shape, entries[0], F32)
    for label in range(1, len(entries)):
        value = jnp.where(zone == float(label), entries[label], value)
    return value


def coefficient_kernel(
    mesh, conductance_ref, capacity_ref, coupling_ref, zones_ref, first_x, second_x, first_y, second_y,
    first_end, second_end,
    half_ref, mass_ref, face_ref, half_rows_ref, mass_rows_ref, face_rows_ref, line_ref,
):
    flags = standing(mesh)
    labels = range(coupling_ref.shape[0])
    halves_of = [[0.5 * conductance_ref[field, label] for label in labels] for field in range(2)]
    masses = [[capacity_ref[field, label] for label in labels] for field in range(2)]
    line = zones_ref.shape[2:]
    roots = [jnp.sqrt(jnp.full((8, *line), capacity_ref[0, label] * capacity_ref[1, label], F32)) for label in labels]
    masses.append([coupling_ref[label] * roots[label][0:1] for label in labels])
    size_x, size_y, size_z = zones_ref.shape
    low_x = chosen(flags, EVEN_X, second_x[2:4], first_x[2:4])
    high_x = chosen(flags, EVEN_X, first_x[2:4], second_x[2:4])
    for side, (lines, ends) in enumerate(
        (
            (chosen(flags, EVEN_Y, second_y[2:4], first_y[2:4]), chosen(flags, EVEN_Y, second_end[...], first_end[...])),
            (chosen(flags, EVEN_Y, first_y[2:4], second_y[2:4]), chosen(flags, EVEN_Y, first_end[...], second_end[...])),
        )
    ):
        for line in range(2):
            place = 2 * side + line
            line_ref[place, 0:8] = jnp.zeros((8, size_z), F32)
            line_ref[place, size_x : size_x + 8] = jnp.zeros((8, size_z), F32)
            line_ref[place, ROW0 - 2 : ROW0] = ends[4 + 4 * line : 6 + 4 * line]
            line_ref[place, ROW0 : ROW0 + size_x] = lines[line]
            line_ref[place, ROW0 + size_x : ROW0 + size_x + 2] = ends[6 + 4 * line : 8 + 4 * line]
    inside = slice(8, 8 + size_y)
    for x in range(-2, size_x + 2):
        if x < 0:
            zone = low_x[x + 2]
        elif x >= size_x:
            zone = high_x[x - size_x]
        else:
            zone = zones_ref[x].astype(F32)
        for field in range(2):
            half_ref[field, x + 2, inside] = looked_up(halves_of[field], zone)
        if -1 <= x <= size_x:
            for which in range(3):
                mass_ref[which, x + 1] = looked_up(masses[which], zone)
    for field in range(2):
        for outer in (0, 1):
            half_ref[field, outer, inside] = chosen(
                flags, LOW_X, half_ref[field, outer, inside], half_ref[field, 2, inside]
            )
            place = size_x + 2 + outer
            half_ref[field, place, inside] = chosen(
                flags, HIGH_X, half_ref[field, place, inside], half_ref[field, size_x + 1, inside]
            )
    count = half_rows_ref.shape[2]
    position = lax.broadcasted_iota(jnp.int32, (count, size_z), 0)
    for line, flag in enumerate((LOW_Y, LOW_Y, HIGH_Y, HIGH_Y)):
        zone = line_ref[line]
        for field in range(2):
            value = looked_up(halves_of[field], zone)
            below = value[ROW0 : ROW0 + 1]
            above = value[ROW0 + size_x - 1 : ROW0 + size_x]
            value = jnp.where((position < ROW0) & (flags[LOW_X] == 0), below, value)
            value = jnp.where((position >= ROW0 + size_x) & (flags[HIGH_X] == 0), above, value)
            near = half_ref[field, :, 8 if flag == LOW_Y else 8 + size_y - 1]
            half_rows_ref[field, line] = value
            half_rows_ref[field, line, ROW0 - 2 : ROW0 + size_x + 2] = chosen(
                flags, flag, half_rows_ref[field, line, ROW0 - 2 : ROW0 + size_x + 2], near
            )
            if line in (1, 2):
                row = 7 if line == 1 else 8 + size_y
                half_ref[field, :, row] = half_rows_ref[field, line, ROW0 - 2 : ROW0 + size_x + 2]
        if line in (1, 2):
            for which in range(3):
                mass_rows_ref[which, line - 1] = looked_up(masses[which], zone)
    for field in range(2):
        for x in range(0, size_x + 2, 2):
            faces = faces_z(half_ref[field, x + 1 : x + 3, inside])
            for way in range(2):
                face_ref[field, way, x : x + 2] = faces[way]
        for side in range(2):
            faces = faces_z(half_rows_ref[field, side + 1])
            for way in range(2):
                face_rows_ref[field, way, side] = faces[way]
        for line, row in ((4, 8), (5, 8 + size_y - 1)):
            half_rows_ref[field, line] = jnp.zeros((count, size_z), F32)
            half_rows_ref[field, line, ROW0 - 2 : ROW0 + size_x + 2] = half_ref[field, :, row]


def first_solve_kernel(
    mesh, load_ref, first_x, second_x, first_y, second_y, first_end, second_end, inverse_ref, c0, c1, c2, c3,
    part_ref, part_rows_ref, even_ref, odd_ref, even_lines, odd_lines, field_ref, rows_ref, before_ref, after_ref,
):
    flags = standing(mesh)
    size_x = load_ref.shape[1]
    for field in range(2):
        field_ref[field, 1 : 1 + size_x] = load_ref[field]
        field_ref[field, 0] = keep(flags, LOW_X, chosen(flags, EVEN_X, second_x[field], first_x[field]))
        field_ref[field, 1 + size_x] = keep(flags, HIGH_X, chosen(flags, EVEN_X, first_x[field], second_x[field]))
        for side, flag, (even, odd), (even_end, odd_end) in (
            (0, LOW_Y, (second_y, first_y), (second_end, first_end)),
            (1, HIGH_Y, (first_y, second_y), (first_end, second_end)),
        ):
            line = keep(flags, flag, chosen(flags, EVEN_Y, even[field], odd[field]))
            ends = keep(flags, flag, chosen(flags, EVEN_Y, even_end[0:8], odd_end[0:8]))
            rows_ref[field, side, 0:8] = jnp.zeros((8, line.shape[1]), F32)
            rows_ref[field, side, size_x : size_x + 8] = jnp.zeros((8, line.shape[1]), F32)
            rows_ref[field, side, ROW0 - 1 : ROW0] = ends[2 * field : 2 * field + 1]
            rows_ref[field, side, ROW0 : ROW0 + size_x] = line
            rows_ref[field, side, ROW0 + size_x : ROW0 + size_x + 1] = ends[2 * field + 1 : 2 * field + 2]
    solve(field_ref, rows_ref, inverse_ref, (c0, c1, c2, c3), before_ref, after_ref, part_ref, part_rows_ref)
    pack_x(flags, part_ref, part_rows_ref, even_ref, odd_ref)
    pack_lines(flags, part_ref, part_rows_ref, even_lines, odd_lines)


def merge_x_kernel(mesh, part_ref, part_rows_ref, first_ref, second_ref, whole_ref, whole_rows_ref, even_ref, odd_ref):
    flags = standing(mesh)
    size_x = part_ref.shape[1] - 2
    size_y, size_z = part_ref.shape[2:]
    depth = first_ref.shape[1]
    end = ROW0 + size_x
    for field in range(2):
        low = keep(flags, LOW_X, chosen(flags, EVEN_X, second_ref[field], first_ref[field]))
        high = keep(flags, HIGH_X, chosen(flags, EVEN_X, first_ref[field], second_ref[field]))
        whole_ref[field, 1] = keep(flags, LOW_X, part_ref[field, 0]) + low[depth - 2, :size_y]
        whole_ref[field, 2] = part_ref[field, 1] + low[depth - 1, :size_y]
        whole_ref[field, 3 : size_x + 1] = part_ref[field, 2:size_x]
        whole_ref[field, size_x + 1] = part_ref[field, size_x] + high[0, :size_y]
        whole_ref[field, size_x + 2] = keep(flags, HIGH_X, part_ref[field, size_x + 1]) + high[1, :size_y]
        whole_ref[field, 0] = low[0, :size_y] if depth == 3 else jnp.zeros((size_y, size_z), F32)
        whole_ref[field, size_x + 3] = high[2, :size_y] if depth == 3 else jnp.zeros((size_y, size_z), F32)
        for side in range(2):
            row = slice(size_y + side, size_y + side + 1)
            edge = ROW0 - 1
            whole_rows_ref[field, side] = part_rows_ref[field, side]
            whole_rows_ref[field, side, edge : edge + 1] = (
                keep(flags, LOW_X, part_rows_ref[field, side, edge : edge + 1]) + low[depth - 2, row]
            )
            whole_rows_ref[field, side, edge + 1 : edge + 2] = (
                part_rows_ref[field, side, edge + 1 : edge + 2] + low[depth - 1, row]
            )
            whole_rows_ref[field, side, end - 1 : end] = part_rows_ref[field, side, end - 1 : end] + high[0, row]
            whole_rows_ref[field, side, end : end + 1] = (
                keep(flags, HIGH_X, part_rows_ref[field, side, end : end + 1]) + high[1, row]
            )
            if depth == 3:
                whole_rows_ref[field, side, edge - 1 : edge] = low[0, row]
                whole_rows_ref[field, side, end + 1 : end + 2] = high[2, row]

        for line in range(depth):
            for ref in (even_ref, odd_ref):
                ref[field, 8 * line : 8 * line + 8] = jnp.zeros((8, size_z), F32)
        for start, x in ((0, -2), (3, size_x - 1)):
            layers, rows = slice(x + 2, x + 5), slice(x + ROW0, x + ROW0 + 3)
            pairs = line_pairs(whole_ref, whole_rows_ref, field, layers, rows, depth)
            for line, (to_low, to_high) in enumerate(pairs):
                place = slice(8 * line + start, 8 * line + start + 3)
                even_ref[field, place] = chosen(flags, EVEN_Y, to_high, to_low)
                odd_ref[field, place] = chosen(flags, EVEN_Y, to_low, to_high)


def assemble(flags, whole_ref, whole_rows_ref, lines_refs, ends_refs, came_ref, field_ref, lines):
    size_x = whole_ref.shape[1] - 4
    size_y = whole_ref.shape[2]
    spread = slice(ROW0 - 2, ROW0 + size_x + 2)
    for field in range(2):
        unpack_lines(flags, lines_refs, ends_refs, came_ref, field)
        low, high = came_ref[0], came_ref[1]
        below = keep(flags, LOW_Y, whole_rows_ref[field, 0]) + low[1]
        above = keep(flags, HIGH_Y, whole_rows_ref[field, 1]) + high[1]
        lines[field, 0] = low[0]
        lines[field, 1] = below
        lines[field, 2] = above
        lines[field, 3] = high[2]
        lines[field, 4] = low[2]
        lines[field, 5] = high[0]
        field_ref[field, :, 8 : 8 + size_y] = whole_ref[field]
        field_ref[field, :, 7] = lines[field, 1, spread]
        field_ref[field, :, 8 + size_y] = lines[field, 2, spread]
        field_ref[field, :, 8] = field_ref[field, :, 8] + lines[field, 4, spread]
        field_ref[field, :, 7 + size_y] = field_ref[field, :, 7 + size_y] + lines[field, 5, spread]


def faces_z(half):
    size_z, axis = half.shape[-1], half.ndim - 1
    lane = lax.broadcasted_iota(jnp.int32, half.shape, axis)
    upper = half + jnp.where(lane == size_z - 1, half, pltpu.roll(half, size_z - 1, axis))
    lower = half + jnp.where(lane == 0, half, pltpu.roll(half, 1, axis))
    return upper, lower


def along_z(value, upper, lower):
    size_z, axis = value.shape[-1], value.ndim - 1
    lane = lax.broadcasted_iota(jnp.int32, value.shape, axis)
    above = jnp.where(lane == size_z - 1, 0.0, pltpu.roll(value, size_z - 1, axis))
    below = jnp.where(lane == 0, 0.0, pltpu.roll(value, 1, axis))
    return upper * (value - above) + lower * (value - below)


def operate(field_ref, half_ref, mass_ref, face_ref, x, count):
    size_y = mass_ref.shape[2]
    inside = slice(8, 8 + size_y)
    masses = slice(x + 1, x + 1 + count)
    here = slice(x + 2, x + 2 + count)
    values, images = [], []
    for field in range(2):
        value = field_ref[field, here, inside]
        half = half_ref[field, here, inside]
        flux = along_z(value, face_ref[field, 0, masses], face_ref[field, 1, masses])
        for start in (x + 1, x + 3):
            place = slice(start, start + count)
            flux = flux + (half + half_ref[field, place, inside]) * (value - field_ref[field, place, inside])
        for shift in (-1, 1):
            moved = slice(8 + shift, 8 + shift + size_y)
            flux = flux + (half + half_ref[field, here, moved]) * (value - field_ref[field, here, moved])
        values.append(value)
        images.append(flux)
    first = mass_ref[0, masses] * values[0] + mass_ref[2, masses] * values[1] + images[0]
    second = mass_ref[2, masses] * values[0] + mass_ref[1, masses] * values[1] + images[1]
    return values, (first, second)


def operate_line(lines, half_lines, mass_lines, face_lines, side, near):
    outer, center, inner = (0, 1, 4) if side == 0 else (3, 2, 5)
    values, images = [], []
    for field in range(2):
        value = lines[field, center]
        half = half_lines[field, center]
        count = value.shape[0]
        flux = along_z(value, face_lines[field, 0, side], face_lines[field, 1, side])
        for turn in (1, count - 1):
            flux = flux + (half + pltpu.roll(half, turn, 0)) * (value - pltpu.roll(value, turn, 0))
        flux = flux + (half + half_lines[field, outer]) * (value - lines[field, outer])
        flux = flux + (half + half_lines[field, inner]) * (value - near[field, side])
        values.append(value)
        images.append(flux)
    first = mass_lines[0, side] * values[0] + mass_lines[2, side] * values[1] + images[0]
    second = mass_lines[2, side] * values[0] + mass_lines[1, side] * values[1] + images[1]
    return first, second


def second_solve_kernel(
    mesh, whole_ref, whole_rows_ref, first_lines, second_lines, first_ends, second_ends,
    half_ref, mass_ref, face_ref, half_lines, mass_lines, face_lines, load_ref, inverse_ref, c0, c1, c2, c3,
    precond_ref, image_ref, sums_ref, part_ref, part_rows_ref, even_ref, odd_ref, even_lines, odd_lines,
    came_ref, value_ref, lines, near, field_ref, rows_ref, before_ref, after_ref,
):
    flags = standing(mesh)
    size_x, size_y, size_z = load_ref.shape[1:]
    lines_refs, ends_refs = (first_lines, second_lines), (first_ends, second_ends)
    assemble(flags, whole_ref, whole_rows_ref, lines_refs, ends_refs, came_ref, value_ref, lines)
    for x, flag in ((-1, LOW_X), (size_x, HIGH_X)):
        _, images = operate(value_ref, half_ref, mass_ref, face_ref, x, 1)
        for field in range(2):
            field_ref[field, x + 1 : x + 2] = keep(flags, flag, images[field])
    total_a = total_b = jnp.zeros((CHUNK, size_y, size_z), F32)
    for x in range(0, size_x, CHUNK):
        chunk = slice(x, x + CHUNK)
        values, images = operate(value_ref, half_ref, mass_ref, face_ref, x, CHUNK)
        for field in range(2):
            precond_ref[field, chunk] = values[field]
            image_ref[field, chunk] = images[field]
            field_ref[field, x + 1 : x + 1 + CHUNK] = images[field]
            total_a = total_a + load_ref[field, chunk] * values[field]
            total_b = total_b + images[field] * values[field]
    sums_ref[0:1] = jnp.sum(jnp.sum(total_a, axis=0), axis=0, keepdims=True)
    sums_ref[1:2] = jnp.sum(jnp.sum(total_b, axis=0), axis=0, keepdims=True)
    sums_ref[2:8] = jnp.zeros((6, size_z), F32)
    count = rows_ref.shape[2]
    position = lax.broadcasted_iota(jnp.int32, (count, size_z), 0)
    begin = jnp.where(flags[LOW_X] > 0, ROW0 - 1, ROW0)
    end = jnp.where(flags[HIGH_X] > 0, ROW0 + size_x + 1, ROW0 + size_x)
    valid = (position >= begin) & (position < end)
    for field in range(2):
        for side, row in ((0, 8), (1, 7 + size_y)):
            near[field, side] = jnp.zeros((count, size_z), F32)
            near[field, side, ROW0 - 2 : ROW0 + size_x + 2] = value_ref[field, :, row]
    for side, flag in ((0, LOW_Y), (1, HIGH_Y)):
        images = operate_line(lines, half_lines, mass_lines, face_lines, side, near)
        for field in range(2):
            rows_ref[field, side] = keep(flags, flag, jnp.where(valid, images[field], 0.0))
    solve(field_ref, rows_ref, inverse_ref, (c0, c1, c2, c3), before_ref, after_ref, part_ref, part_rows_ref)
    pack_x(flags, part_ref, part_rows_ref, even_ref, odd_ref)
    pack_lines(flags, part_ref, part_rows_ref, even_lines, odd_lines)


def second_image_kernel(
    mesh, whole_ref, whole_rows_ref, first_lines, second_lines, first_ends, second_ends,
    half_ref, mass_ref, face_ref, old_image_ref, old_sums_ref,
    precond_ref, image_ref, sums_ref, came_ref, value_ref,
):
    flags = standing(mesh)
    size_x, size_y, size_z = old_image_ref.shape[1:]
    own, wide = slice(2, size_x + 2), slice(1, size_x + 3)
    rows, margins = slice(ROW0, ROW0 + size_x), slice(ROW0 - 1, ROW0 + size_x + 1)
    for field in range(2):
        unpack_lines(flags, (first_lines, second_lines), (first_ends, second_ends), came_ref, field)
        value_ref[field, wide, 8 : 8 + size_y] = whole_ref[field, wide]
        value_ref[field, own, 7] = keep(flags, LOW_Y, whole_rows_ref[field, 0, rows]) + came_ref[0, 0, rows]
        value_ref[field, wide, 8] = whole_ref[field, wide, 0] + came_ref[0, 1, margins]
        value_ref[field, wide, 7 + size_y] = whole_ref[field, wide, size_y - 1] + came_ref[1, 1, margins]
        value_ref[field, own, 8 + size_y] = keep(flags, HIGH_Y, whole_rows_ref[field, 1, rows]) + came_ref[1, 0, rows]
    total_c = total_d = jnp.zeros((CHUNK, size_y, size_z), F32)
    for x in range(0, size_x, CHUNK):
        chunk = slice(x, x + CHUNK)
        values, images = operate(value_ref, half_ref, mass_ref, face_ref, x, CHUNK)
        for field in range(2):
            precond_ref[field, chunk] = values[field]
            image_ref[field, chunk] = images[field]
            total_c = total_c + old_image_ref[field, chunk] * values[field]
            total_d = total_d + images[field] * values[field]
    total_c, total_d = jnp.sum(total_c, axis=0), jnp.sum(total_d, axis=0)
    totals = [
        jnp.sum(old_sums_ref[0:1], axis=1, keepdims=True),
        jnp.sum(old_sums_ref[1:2], axis=1, keepdims=True),
        jnp.sum(jnp.sum(total_c, axis=0, keepdims=True), axis=1, keepdims=True),
        jnp.sum(jnp.sum(total_d, axis=0, keepdims=True), axis=1, keepdims=True),
    ]
    lane = lax.broadcasted_iota(jnp.int32, sums_ref.shape, 1)
    spread = jnp.zeros(sums_ref.shape, F32)
    for place, total in enumerate(totals):
        spread = jnp.where(lane == place, total, spread)
    sums_ref[...] = spread


def finish_kernel(
    sums_ref, load_ref, z_ref, q_ref, w_ref, s_ref, solution_hbm, residual_hbm, solution_ref, residual_ref, sems
):
    line = jnp.sum(sums_ref[...], axis=0, keepdims=True)
    lane = lax.broadcasted_iota(jnp.int32, line.shape, 1)
    rz, zq, qw, ws = [jnp.sum(jnp.where(lane == place, line, 0.0), axis=1, keepdims=True) for place in range(4)]
    alpha = rz / zq
    rz_next = rz - alpha * (2.0 * zq) + alpha * alpha * qw
    grown = 1.0 + rz_next / rz
    curvature = grown * grown * zq - 2.0 * grown * alpha * qw + alpha * alpha * ws
    alpha_next = rz_next / curvature
    along = alpha + alpha_next * grown
    against = alpha_next * alpha
    copies = []
    step = load_ref.shape[1] // 2
    for field in range(2):
        for start in range(0, 2 * step, step):
            part = pl.ds(start, step)
            for x in range(start, start + step):
                solution_ref[field, x] = along * z_ref[field, x] - against * w_ref[field, x]
                residual_ref[field, x] = load_ref[field, x] - along * q_ref[field, x] + against * s_ref[field, x]
            for here, there in ((solution_ref, solution_hbm), (residual_ref, residual_hbm)):
                copies.append(
                    pltpu.make_async_copy(here.at[field, part], there.at[field, part], sems.at[len(copies)])
                )
                copies[-1].start()
    for copy in copies:
        copy.wait()


SMEM = pl.BlockSpec(memory_space=pltpu.SMEM)
VMEM = pl.BlockSpec(memory_space=pltpu.VMEM)
HBM = pl.BlockSpec(memory_space=pltpu.HBM)


def call(mesh, kernel, scalars, arrays, outs, scratch=(), flops=0, limit=24, in_hbm=False, outs_in_hbm=False):
    moved = sum(math.prod(a.shape) * a.dtype.itemsize for a in list(arrays) + list(outs))
    return pl.pallas_call(
        kernel if mesh is None else functools.partial(kernel, mesh),
        out_shape=tuple(outs),
        in_specs=[SMEM] * len(scalars) + [HBM if in_hbm else VMEM] * len(arrays),
        out_specs=tuple([HBM if outs_in_hbm else VMEM] * len(outs)),
        scratch_shapes=list(scratch),
        compiler_params=pltpu.CompilerParams(vmem_limit_bytes=limit * 1024 * 1024),
        cost_estimate=pl.CostEstimate(flops=flops, bytes_accessed=moved, transcendentals=0),
    )(*scalars, *arrays)


def shards(mesh, load, zones, conductance, capacity, coupling):
    size_x, size_y, size_z = zones.shape
    assert size_x % BOX == 0 and size_y == BOX and size_z % BOX == 0
    boxes = size_x // BOX
    count = size_x + 8
    sds = lambda *shape: jax.ShapeDtypeStruct(shape, F32)
    consts = [jnp.asarray(c) for c in constants(size_z)]
    modes, lanes = consts[0].shape[0], size_z // BOX * SPAN
    assert size_z == 128
    load, zones, *packed = call(
        mesh,
        edge_layers_kernel,
        [],
        [load, zones],
        [sds(*load.shape), jax.ShapeDtypeStruct(zones.shape, zones.dtype)] + [sds(4, size_y, size_z)] * 2 + [sds(4, size_x, size_z)] * 2,
        [pltpu.SemaphoreType.DMA((3,))],
        in_hbm=True,
    )
    x_halo = swap(mesh, "gx", *packed[:2])
    y_halo = swap(mesh, "gy", *packed[2:])
    (inverse,) = call(
        None,
        divisor_kernel,
        [conductance, capacity],
        [zones],
        [sds(2 * boxes, modes, lanes)],
        flops=40_000_000,
    )
    packed = call(mesh, edge_ends_kernel, [], [*x_halo, inverse], [sds(16, size_z)] * 2)
    y_ends = swap(mesh, "gy", *packed)
    half, mass, face, half_lines, mass_lines, face_lines = call(
        mesh,
        coefficient_kernel,
        [conductance, capacity, coupling],
        [zones, *x_halo, *y_halo, *y_ends],
        [
            sds(2, size_x + 4, size_y + 16, size_z),
            sds(3, size_x + 2, size_y, size_z),
            sds(2, 2, size_x + 2, size_y, size_z),
            sds(2, 6, count, size_z),
            sds(3, 2, count, size_z),
            sds(2, 2, 2, count, size_z),
        ],
        [pltpu.VMEM((4, count, size_z), F32)],
        flops=20_000_000,
    )
    parts = [sds(2, size_x + 2, size_y, size_z), sds(2, 2, count, size_z)]
    packed_x = [[sds(2, depth, size_y + 8, size_z)] * 2 for depth in (3, 2)]
    wholes = [sds(2, size_x + 4, size_y, size_z), sds(2, 2, count, size_z)]
    packed_lines = [[sds(2, depth * size_x, size_z)] * 2 for depth in (3, 2)]
    packed_ends = [[sds(2, depth * 8, size_z)] * 2 for depth in (3, 2)]
    rows = SPAN * size_y + 48
    work = [
        pltpu.VMEM((2, size_x + 2, size_y, size_z), F32),
        pltpu.VMEM((2, 2, count, size_z), F32),
        pltpu.VMEM((2, 3 * rows, boxes * size_z), BF16),
        pltpu.VMEM((2, 3 * rows, boxes * size_z), BF16),
    ]
    padded = [
        pltpu.VMEM((2, size_x + 4, size_y + 16, size_z), F32),
        pltpu.VMEM((2, 6, count, size_z), F32),
    ]
    own = sds(2, size_x, size_y, size_z)

    part, part_rows, *packed = call(
        mesh,
        first_solve_kernel,
        [],
        [load, *x_halo, *y_halo, *y_ends, inverse, *consts],
        parts + packed_x[0] + packed_lines[0],
        work,
        3_000_000_000,
    )
    lines = swap(mesh, "gy", *packed[2:])
    received = swap(mesh, "gx", *packed[:2])
    whole, whole_rows, *packed = call(mesh, merge_x_kernel, [], [part, part_rows, *received], wholes + packed_ends[0])
    ends = swap(mesh, "gy", *packed)
    precond, image, sums, part, part_rows, *packed = call(
        mesh,
        second_solve_kernel,
        [],
        [whole, whole_rows, *lines, *ends, half, mass, face, half_lines, mass_lines, face_lines, load, inverse, *consts],
        [own, own, sds(8, size_z)] + parts + packed_x[1] + packed_lines[1],
        [pltpu.VMEM((2, 3, count, size_z), F32)] + padded + [pltpu.VMEM((2, 2, count, size_z), F32)] + work,
        3_000_000_000,
    )
    lines = swap(mesh, "gy", *packed[2:])
    received = swap(mesh, "gx", *packed[:2])
    whole, whole_rows, *packed = call(mesh, merge_x_kernel, [], [part, part_rows, *received], wholes + packed_ends[1])
    ends = swap(mesh, "gy", *packed)
    devices = mesh.shape["gx"] * mesh.shape["gy"]
    last_precond, last_image, sums = call(
        mesh,
        second_image_kernel,
        [],
        [whole, whole_rows, *lines, *ends, half, mass, face, image, sums],
        [own, own, sds(devices, size_z)],
        [pltpu.VMEM((2, 2, count, size_z), F32), padded[0]],
        10_000_000,
    )
    sums = lax.all_to_all(sums, AXES, 0, 0, tiled=True)
    whole_block = pltpu.VMEM((2, size_x, size_y, size_z), F32)
    return call(
        None,
        finish_kernel,
        [],
        [sums, load, precond, image, last_precond, last_image],
        [own, own],
        [whole_block, whole_block, pltpu.SemaphoreType.DMA((8,))],
        outs_in_hbm=True,
    )


def solution(mesh):
    in_specs = (P(None, "gx", "gy", None), P("gx", "gy", None), P(), P(), P())
    out_specs = (P(None, "gx", "gy", None), P(None, "gx", "gy", None))
    return jax.shard_map(
        functools.partial(shards, mesh), mesh=mesh, in_specs=in_specs, out_specs=out_specs, check_vma=False
    )
```

```python
import functools
import math

import jax
import jax.numpy as jnp
import ml_dtypes
import numpy as np
from jax import lax
from jax.experimental import pallas as pl
from jax.experimental.pallas import tpu as pltpu
from jax.sharding import PartitionSpec as P

BOX = 16
SPAN = BOX + 2
F32 = jnp.float32
BF16 = jnp.bfloat16
AXES = ("gx", "gy")
ROW0 = 4
CHUNK = 4


def split(matrix):
    high = matrix.astype(ml_dtypes.bfloat16)
    low = (matrix - high.astype(np.float64)).astype(ml_dtypes.bfloat16)
    return high, low


def round_up(value, step):
    return (value + step - 1) // step * step


def sine_basis():
    index = np.arange(SPAN)
    angle = np.pi * np.outer(index + 1, index + 1) / (SPAN + 1)
    return np.sqrt(2.0 / (SPAN + 1)) * np.sin(angle)


def eigenvalues():
    return 4.0 * np.sin(np.pi * (np.arange(SPAN) + 1) / (2 * (SPAN + 1))) ** 2


def plane_layout():
    places = [(x, y + 1) for x in range(SPAN) for y in range(BOX)]
    for y in (0, SPAN - 1):
        for position in range(24):
            x = position - (ROW0 - 1)
            places.append((x, y) if 0 <= x < SPAN else None)
    return places


def constants(size_z):
    basis = sine_basis()
    places = plane_layout()
    rows = len(places)
    modes = SPAN * SPAN
    padded_modes = round_up(modes, 16)
    plane = np.zeros((padded_modes, rows))
    for column, place in enumerate(places):
        if place is not None:
            plane[:modes, column] = np.outer(basis[:, place[0]], basis[:, place[1]]).reshape(-1)
    high, low = split(plane)
    forward = np.concatenate([high, high, low], axis=1)
    high, low = split(plane.T)
    inverse = np.concatenate([high, high, low], axis=1)
    boxes = size_z // BOX
    line = np.zeros((size_z, boxes * SPAN))
    for box in range(boxes):
        for mode in range(SPAN):
            for offset in range(SPAN):
                cell = box * BOX + offset - 1
                if 0 <= cell < size_z:
                    line[cell, box * SPAN + mode] = basis[mode, offset]
    high, low = split(line)
    line_forward = np.concatenate([high, high, low], axis=0)
    high, low = split(line.T)
    line_inverse = np.concatenate([high, low], axis=1)
    return forward, inverse, line_forward, line_inverse


def swap_pairs(mesh, axis, odd):
    sizes = [mesh.shape[name] for name in AXES]
    along = AXES.index(axis)
    pairs = []
    for i in range(sizes[0]):
        for j in range(sizes[1]):
            here = [i, j]
            there = [i, j]
            place = here[along]
            target = place ^ 1 if not odd else (place + 1 if place % 2 else place - 1)
            if 0 <= target < sizes[along]:
                there[along] = target
            elif along == 0:
                there[0] = sizes[0] - 1 - place
            else:
                there[0] = i ^ 1
            pairs.append((here[0] * sizes[1] + here[1], there[0] * sizes[1] + there[1]))
    return pairs


def swap(mesh, axis, even_part, odd_part):
    if axis == "gx":
        first = lax.ppermute(even_part, AXES, swap_pairs(mesh, axis, False))
        second = lax.ppermute(odd_part, AXES, swap_pairs(mesh, axis, True))
    else:
        second = lax.ppermute(odd_part, AXES, swap_pairs(mesh, axis, True))
        first = lax.ppermute(even_part, AXES, swap_pairs(mesh, axis, False))
    return first, second


EVEN_X, EVEN_Y, LOW_X, HIGH_X, LOW_Y, HIGH_Y = range(6)


def standing(mesh):
    here_x, here_y = lax.axis_index("gx"), lax.axis_index("gy")
    facts = (
        lax.rem(here_x, 2) == 0,
        lax.rem(here_y, 2) == 0,
        here_x > 0,
        here_x < mesh.shape["gx"] - 1,
        here_y > 0,
        here_y < mesh.shape["gy"] - 1,
    )
    return [fact.astype(jnp.int32) for fact in facts]


def chosen(flags, which, yes, no):
    return jnp.where(flags[which] > 0, yes, no)


def keep(flags, which, value):
    return jnp.where(flags[which] > 0, value, jnp.zeros_like(value))


def halves(value):
    high = value.astype(BF16)
    low = (value - high.astype(F32)).astype(BF16)
    return high, low


def dot(left, right):
    return jnp.dot(left, right, preferred_element_type=F32)


def store_split(stack_ref, lanes, value):
    rows = value.shape[0]
    high, low = halves(value)
    stack_ref[0:rows, lanes] = high
    stack_ref[rows : 2 * rows, lanes] = low
    stack_ref[2 * rows : 3 * rows, lanes] = high


def solve(field_ref, rows_ref, inverse_ref, consts, before_ref, after_ref, out_ref, out_rows_ref):
    forward_ref, back_ref, line_forward_ref, line_back_ref = consts
    boxes = (field_ref.shape[1] - 2) // BOX
    size_y, size_z = field_ref.shape[2:]
    inner = SPAN * size_y
    line_rows = line_forward_ref.shape[0] // 3
    lanes = [slice(box * size_z, (box + 1) * size_z) for box in range(boxes)]
    for field in range(2):
        for box in range(boxes):
            start = box * BOX
            main = field_ref[field, start : start + SPAN].reshape(inner, size_z)
            strips = [rows_ref[field, side, start : start + 24] for side in range(2)]
            store_split(before_ref.at[field], lanes[box], jnp.concatenate([main, *strips], axis=0))
    spectral = [dot(forward_ref[...], before_ref[field]) for field in range(2)]
    for field in range(2):
        for box in range(boxes):
            high, low = halves(spectral[field][:, lanes[box]])
            both = jnp.concatenate([high, low], axis=1)
            modes = dot(both, line_forward_ref[0 : 2 * line_rows]) + dot(high, line_forward_ref[2 * line_rows :])
            modes = modes * inverse_ref[field * boxes + box]
            high, low = halves(modes)
            cells = dot(high, line_back_ref[...])
            cells = cells[:, :size_z] + (cells[:, size_z:] + dot(low, line_back_ref[:, :size_z]))
            store_split(after_ref.at[field], lanes[box], cells)
    for field in range(2):
        result = dot(back_ref[...], after_ref[field])
        for box in range(boxes):
            start = box * BOX
            main = result[:inner, lanes[box]].reshape(SPAN, size_y, size_z)
            if box == 0:
                out_ref[field, 0:SPAN] = main
            else:
                out_ref[field, start : start + 2] = out_ref[field, start : start + 2] + main[0:2]
                out_ref[field, start + 2 : start + SPAN] = main[2:]
            for side in range(2):
                strip = result[inner + 24 * side : inner + 24 * side + 24, lanes[box]]
                if box == 0:
                    out_rows_ref[field, side, 0:24] = strip
                else:
                    out_rows_ref[field, side, start : start + 8] = (
                        out_rows_ref[field, side, start : start + 8] + strip[0:8]
                    )
                    out_rows_ref[field, side, start + 8 : start + 24] = strip[8:]


def pack_x(flags, part_ref, part_rows_ref, even_ref, odd_ref):
    last = part_ref.shape[1] - 1
    depth = even_ref.shape[1]
    size_y = part_ref.shape[2]
    for field in range(2):
        for layer in range(depth):
            low, high = layer, last + 1 - depth + layer
            for side, place in ((None, slice(0, size_y)), (0, slice(size_y, size_y + 1)), (1, slice(size_y + 1, size_y + 2))):
                if side is None:
                    to_low, to_high = part_ref[field, low], part_ref[field, high]
                else:
                    shift = ROW0 - 1
                    to_low = part_rows_ref[field, side, low + shift : low + shift + 1]
                    to_high = part_rows_ref[field, side, high + shift : high + shift + 1]
                even_ref[field, layer, place] = chosen(flags, EVEN_X, to_high, to_low)
                odd_ref[field, layer, place] = chosen(flags, EVEN_X, to_low, to_high)
            rest = even_ref.shape[2] - size_y - 2
            blank = jnp.zeros((rest, even_ref.shape[3]), F32)
            even_ref[field, layer, size_y + 2 :] = blank
            odd_ref[field, layer, size_y + 2 :] = blank


def line_pairs(whole_ref, whole_rows_ref, field, layers, rows, depth):
    size_y = whole_ref.shape[2]
    if depth == 3:
        return (
            (whole_rows_ref[field, 0, rows], whole_ref[field, layers, size_y - 2]),
            (whole_ref[field, layers, 0], whole_ref[field, layers, size_y - 1]),
            (whole_ref[field, layers, 1], whole_rows_ref[field, 1, rows]),
        )
    return (
        (whole_ref[field, layers, 0], whole_ref[field, layers, size_y - 1]),
        (whole_rows_ref[field, 0, rows], whole_rows_ref[field, 1, rows]),
    )


def pack_lines(flags, part_ref, part_rows_ref, even_ref, odd_ref):
    size_x = part_ref.shape[1] - 2
    depth = even_ref.shape[1] // size_x
    for field in range(2):
        pairs = line_pairs(
            part_ref, part_rows_ref, field, slice(1, size_x + 1), slice(ROW0, ROW0 + size_x), depth
        )
        for line, (to_low, to_high) in enumerate(pairs):
            place = slice(line * size_x, (line + 1) * size_x)
            even_ref[field, place] = chosen(flags, EVEN_Y, to_high, to_low)
            odd_ref[field, place] = chosen(flags, EVEN_Y, to_low, to_high)


def unpack_lines(flags, lines_refs, ends_refs, out_ref, field):
    size_x = out_ref.shape[2] - 8
    depth = lines_refs[0].shape[1] // size_x
    blank = jnp.zeros((8, out_ref.shape[3]), F32)
    for side, flag, (even, odd) in ((0, LOW_Y, (1, 0)), (1, HIGH_Y, (0, 1))):
        lines = keep(flags, flag, chosen(flags, EVEN_Y, lines_refs[even][field], lines_refs[odd][field]))
        ends = keep(flags, flag, chosen(flags, EVEN_Y, ends_refs[even][field], ends_refs[odd][field]))
        for line in range(depth):
            out_ref[side, line, 0:8] = blank
            out_ref[side, line, size_x : size_x + 8] = blank
            out_ref[side, line, ROW0 : ROW0 + size_x] = lines[line * size_x : (line + 1) * size_x]
            out_ref[side, line, ROW0 - 2 : ROW0 + 1] = ends[8 * line : 8 * line + 3]
            out_ref[side, line, ROW0 + size_x - 1 : ROW0 + size_x + 2] = ends[8 * line + 3 : 8 * line + 6]


def divisor_kernel(conductance_ref, capacity_ref, zones_ref, inverse_ref):
    size_x, size_y, size_z = zones_ref.shape
    boxes = size_x // BOX
    lines = []
    for table_ref, which in ((capacity_ref, 0), (capacity_ref, 1), (conductance_ref, 0), (conductance_ref, 1)):
        for box in range(boxes):
            total = jnp.zeros((size_y, size_z), F32)
            for x in range(box * BOX, (box + 1) * BOX):
                zone = zones_ref[x]
                value = jnp.full((size_y, size_z), table_ref[which, 0], F32)
                for label in range(1, table_ref.shape[1]):
                    value = jnp.where(zone == label, table_ref[which, label], value)
                total = total + value
            lines.append(jnp.sum(total, axis=0, keepdims=True))
    sums = jnp.concatenate(lines, axis=0)
    modes, lanes = inverse_ref.shape[1:]
    cell = lax.broadcasted_iota(jnp.int32, (size_z, lanes), 0)
    lane = lax.broadcasted_iota(jnp.int32, (size_z, lanes), 1)
    spread = jnp.zeros((size_z, lanes), F32)
    for box in range(size_z // BOX):
        here = (cell >= box * BOX) & (cell < (box + 1) * BOX) & (lane >= box * SPAN) & (lane < (box + 1) * SPAN)
        spread = jnp.where(here, 1.0 / BOX**3, spread)
    means = jnp.dot(sums, spread, preferred_element_type=F32, precision=lax.Precision.HIGHEST)
    eigen = [float(value) for value in eigenvalues()]
    row = lax.broadcasted_iota(jnp.int32, (modes, 128), 0)
    first = jnp.zeros(row.shape, jnp.int32)
    for mode in range(1, SPAN):
        first = first + (row >= mode * SPAN).astype(jnp.int32)
    second = row - SPAN * first
    pair = jnp.zeros(row.shape, F32)
    for mode in range(SPAN):
        pair = pair + jnp.where(first == mode, eigen[mode], 0.0) + jnp.where(second == mode, eigen[mode], 0.0)
    lane = lax.broadcasted_iota(jnp.int32, (8, lanes), 1)
    for box in range(1, size_z // BOX):
        lane = lane - SPAN * (lax.broadcasted_iota(jnp.int32, (8, lanes), 1) >= box * SPAN).astype(jnp.int32)
    third = jnp.zeros(lane.shape, F32)
    for mode in range(SPAN):
        third = jnp.where(lane == mode, eigen[mode], third)
    summed = jnp.concatenate([pair, pair[:, : lanes - 128]], axis=1) + third[0:1]
    half = 2 * boxes
    for combo in range(half):
        cbar = means[combo : combo + 1]
        kbar = means[half + combo : half + combo + 1]
        inverse_ref[combo] = 1.0 / (cbar + kbar * summed)


def edge_layers_kernel(mesh, load_hbm, zones_hbm, load_ref, zones_ref, even_ref, odd_ref, sems):
    copies = [
        pltpu.make_async_copy(load_hbm.at[0], load_ref.at[0], sems.at[0]),
        pltpu.make_async_copy(load_hbm.at[1], load_ref.at[1], sems.at[1]),
        pltpu.make_async_copy(zones_hbm, zones_ref, sems.at[2]),
    ]
    for copy in copies:
        copy.start()
    flags = standing(mesh)
    last = zones_ref.shape[0] - 1
    for channel in range(4):
        if channel < 3:
            copies[channel].wait()
        if channel < 2:
            low, high = load_ref[channel, 0], load_ref[channel, last]
        else:
            low, high = zones_ref[channel - 2].astype(F32), zones_ref[last - 3 + channel].astype(F32)
        even_ref[channel] = chosen(flags, EVEN_X, high, low)
        odd_ref[channel] = chosen(flags, EVEN_X, low, high)


def edge_lines_kernel(mesh, load_ref, zones_ref, first_ref, second_ref, even_ref, odd_ref):
    flags = standing(mesh)
    size_x, size_y = zones_ref.shape[:2]
    from_low = chosen(flags, EVEN_X, second_ref[...], first_ref[...])
    from_high = chosen(flags, EVEN_X, first_ref[...], second_ref[...])

    def put(row, to_low, to_high):
        place = slice(row, row + to_low.shape[0])
        even_ref[place] = chosen(flags, EVEN_Y, to_high, to_low)
        odd_ref[place] = chosen(flags, EVEN_Y, to_low, to_high)

    def put_end(row, layer, near, far):
        put(4 * size_x + row, layer[near : near + 1], layer[far : far + 1])

    blank = jnp.zeros((8, even_ref.shape[1]), F32)
    put(4 * size_x + 8, blank, blank)
    for field in range(2):
        put(field * size_x, load_ref[field, :, 0], load_ref[field, :, size_y - 1])
        put_end(2 * field, keep(flags, LOW_X, from_low[field]), 0, size_y - 1)
        put_end(2 * field + 1, keep(flags, HIGH_X, from_high[field]), 0, size_y - 1)
    for line in range(2):
        far = size_y - 2 + line
        put((2 + line) * size_x, zones_ref[:, line].astype(F32), zones_ref[:, far].astype(F32))
        for depth in range(2):
            put_end(4 + 4 * line + depth, from_low[2 + depth], line, far)
            put_end(6 + 4 * line + depth, from_high[2 + depth], line, far)


def looked_up(entries, zone):
    value = jnp.full(zone.shape, entries[0], F32)
    for label in range(1, len(entries)):
        value = jnp.where(zone == float(label), entries[label], value)
    return value


def coefficient_kernel(
    mesh, conductance_ref, capacity_ref, coupling_ref, zones_ref, first_x, second_x, first_y, second_y,
    half_ref, mass_ref, face_ref, half_rows_ref, mass_rows_ref, face_rows_ref, line_ref,
):
    flags = standing(mesh)
    labels = range(coupling_ref.shape[0])
    halves_of = [[0.5 * conductance_ref[field, label] for label in labels] for field in range(2)]
    masses = [[capacity_ref[field, label] for label in labels] for field in range(2)]
    line = zones_ref.shape[2:]
    roots = [jnp.sqrt(jnp.full((8, *line), capacity_ref[0, label] * capacity_ref[1, label], F32)) for label in labels]
    masses.append([coupling_ref[label] * roots[label][0:1] for label in labels])
    size_x, size_y, size_z = zones_ref.shape
    low_x = chosen(flags, EVEN_X, second_x[2:4], first_x[2:4])
    high_x = chosen(flags, EVEN_X, first_x[2:4], second_x[2:4])
    for side, (even, odd) in enumerate(((second_y, first_y), (first_y, second_y))):
        came = chosen(flags, EVEN_Y, even[2 * size_x :], odd[2 * size_x :])
        lines, ends = (came[:size_x], came[size_x : 2 * size_x]), came[2 * size_x :]
        for line in range(2):
            place = 2 * side + line
            line_ref[place, 0:8] = jnp.zeros((8, size_z), F32)
            line_ref[place, size_x : size_x + 8] = jnp.zeros((8, size_z), F32)
            line_ref[place, ROW0 - 2 : ROW0] = ends[4 + 4 * line : 6 + 4 * line]
            line_ref[place, ROW0 : ROW0 + size_x] = lines[line]
            line_ref[place, ROW0 + size_x : ROW0 + size_x + 2] = ends[6 + 4 * line : 8 + 4 * line]
    inside = slice(8, 8 + size_y)
    for x in range(-2, size_x + 2):
        if x < 0:
            zone = low_x[x + 2]
        elif x >= size_x:
            zone = high_x[x - size_x]
        else:
            zone = zones_ref[x].astype(F32)
        for field in range(2):
            half_ref[field, x + 2, inside] = looked_up(halves_of[field], zone)
        if -1 <= x <= size_x:
            for which in range(3):
                mass_ref[which, x + 1] = looked_up(masses[which], zone)
    for field in range(2):
        for outer in (0, 1):
            half_ref[field, outer, inside] = chosen(
                flags, LOW_X, half_ref[field, outer, inside], half_ref[field, 2, inside]
            )
            place = size_x + 2 + outer
            half_ref[field, place, inside] = chosen(
                flags, HIGH_X, half_ref[field, place, inside], half_ref[field, size_x + 1, inside]
            )
    count = half_rows_ref.shape[2]
    position = lax.broadcasted_iota(jnp.int32, (count, size_z), 0)
    for line, flag in enumerate((LOW_Y, LOW_Y, HIGH_Y, HIGH_Y)):
        zone = line_ref[line]
        for field in range(2):
            value = looked_up(halves_of[field], zone)
            below = value[ROW0 : ROW0 + 1]
            above = value[ROW0 + size_x - 1 : ROW0 + size_x]
            value = jnp.where((position < ROW0) & (flags[LOW_X] == 0), below, value)
            value = jnp.where((position >= ROW0 + size_x) & (flags[HIGH_X] == 0), above, value)
            near = half_ref[field, :, 8 if flag == LOW_Y else 8 + size_y - 1]
            half_rows_ref[field, line] = value
            half_rows_ref[field, line, ROW0 - 2 : ROW0 + size_x + 2] = chosen(
                flags, flag, half_rows_ref[field, line, ROW0 - 2 : ROW0 + size_x + 2], near
            )
            if line in (1, 2):
                row = 7 if line == 1 else 8 + size_y
                half_ref[field, :, row] = half_rows_ref[field, line, ROW0 - 2 : ROW0 + size_x + 2]
        if line in (1, 2):
            for which in range(3):
                mass_rows_ref[which, line - 1] = looked_up(masses[which], zone)
    for field in range(2):
        for x in range(0, size_x + 2, 2):
            faces = faces_z(half_ref[field, x + 1 : x + 3, inside])
            for way in range(2):
                face_ref[field, way, x : x + 2] = faces[way]
        for side in range(2):
            faces = faces_z(half_rows_ref[field, side + 1])
            for way in range(2):
                face_rows_ref[field, way, side] = faces[way]
        for line, row in ((4, 8), (5, 8 + size_y - 1)):
            half_rows_ref[field, line] = jnp.zeros((count, size_z), F32)
            half_rows_ref[field, line, ROW0 - 2 : ROW0 + size_x + 2] = half_ref[field, :, row]


def first_solve_kernel(
    mesh, load_ref, first_x, second_x, first_y, second_y, inverse_ref, c0, c1, c2, c3,
    part_ref, part_rows_ref, even_ref, odd_ref, even_lines, odd_lines, field_ref, rows_ref, before_ref, after_ref,
):
    flags = standing(mesh)
    size_x = load_ref.shape[1]
    for field in range(2):
        field_ref[field, 1 : 1 + size_x] = load_ref[field]
        field_ref[field, 0] = keep(flags, LOW_X, chosen(flags, EVEN_X, second_x[field], first_x[field]))
        field_ref[field, 1 + size_x] = keep(flags, HIGH_X, chosen(flags, EVEN_X, first_x[field], second_x[field]))
        for side, flag, even, odd in ((0, LOW_Y, second_y, first_y), (1, HIGH_Y, first_y, second_y)):
            place, after = slice(field * size_x, (field + 1) * size_x), slice(4 * size_x, 4 * size_x + 8)
            line = keep(flags, flag, chosen(flags, EVEN_Y, even[place], odd[place]))
            ends = keep(flags, flag, chosen(flags, EVEN_Y, even[after], odd[after]))
            rows_ref[field, side, 0:8] = jnp.zeros((8, line.shape[1]), F32)
            rows_ref[field, side, size_x : size_x + 8] = jnp.zeros((8, line.shape[1]), F32)
            rows_ref[field, side, ROW0 - 1 : ROW0] = ends[2 * field : 2 * field + 1]
            rows_ref[field, side, ROW0 : ROW0 + size_x] = line
            rows_ref[field, side, ROW0 + size_x : ROW0 + size_x + 1] = ends[2 * field + 1 : 2 * field + 2]
    solve(field_ref, rows_ref, inverse_ref, (c0, c1, c2, c3), before_ref, after_ref, part_ref, part_rows_ref)
    pack_x(flags, part_ref, part_rows_ref, even_ref, odd_ref)
    pack_lines(flags, part_ref, part_rows_ref, even_lines, odd_lines)


def merge_x_kernel(mesh, part_ref, part_rows_ref, first_ref, second_ref, whole_ref, whole_rows_ref, even_ref, odd_ref):
    flags = standing(mesh)
    size_x = part_ref.shape[1] - 2
    size_y, size_z = part_ref.shape[2:]
    depth = first_ref.shape[1]
    end = ROW0 + size_x
    for field in range(2):
        low = keep(flags, LOW_X, chosen(flags, EVEN_X, second_ref[field], first_ref[field]))
        high = keep(flags, HIGH_X, chosen(flags, EVEN_X, first_ref[field], second_ref[field]))
        whole_ref[field, 1] = keep(flags, LOW_X, part_ref[field, 0]) + low[depth - 2, :size_y]
        whole_ref[field, 2] = part_ref[field, 1] + low[depth - 1, :size_y]
        whole_ref[field, 3 : size_x + 1] = part_ref[field, 2:size_x]
        whole_ref[field, size_x + 1] = part_ref[field, size_x] + high[0, :size_y]
        whole_ref[field, size_x + 2] = keep(flags, HIGH_X, part_ref[field, size_x + 1]) + high[1, :size_y]
        whole_ref[field, 0] = low[0, :size_y] if depth == 3 else jnp.zeros((size_y, size_z), F32)
        whole_ref[field, size_x + 3] = high[2, :size_y] if depth == 3 else jnp.zeros((size_y, size_z), F32)
        for side in range(2):
            row = slice(size_y + side, size_y + side + 1)
            edge = ROW0 - 1
            whole_rows_ref[field, side] = part_rows_ref[field, side]
            whole_rows_ref[field, side, edge : edge + 1] = (
                keep(flags, LOW_X, part_rows_ref[field, side, edge : edge + 1]) + low[depth - 2, row]
            )
            whole_rows_ref[field, side, edge + 1 : edge + 2] = (
                part_rows_ref[field, side, edge + 1 : edge + 2] + low[depth - 1, row]
            )
            whole_rows_ref[field, side, end - 1 : end] = part_rows_ref[field, side, end - 1 : end] + high[0, row]
            whole_rows_ref[field, side, end : end + 1] = (
                keep(flags, HIGH_X, part_rows_ref[field, side, end : end + 1]) + high[1, row]
            )
            if depth == 3:
                whole_rows_ref[field, side, edge - 1 : edge] = low[0, row]
                whole_rows_ref[field, side, end + 1 : end + 2] = high[2, row]

        for line in range(depth):
            for ref in (even_ref, odd_ref):
                ref[field, 8 * line : 8 * line + 8] = jnp.zeros((8, size_z), F32)
        for start, x in ((0, -2), (3, size_x - 1)):
            layers, rows = slice(x + 2, x + 5), slice(x + ROW0, x + ROW0 + 3)
            pairs = line_pairs(whole_ref, whole_rows_ref, field, layers, rows, depth)
            for line, (to_low, to_high) in enumerate(pairs):
                place = slice(8 * line + start, 8 * line + start + 3)
                even_ref[field, place] = chosen(flags, EVEN_Y, to_high, to_low)
                odd_ref[field, place] = chosen(flags, EVEN_Y, to_low, to_high)


def assemble(flags, whole_ref, whole_rows_ref, lines_refs, ends_refs, came_ref, field_ref, lines):
    size_x = whole_ref.shape[1] - 4
    size_y = whole_ref.shape[2]
    spread = slice(ROW0 - 2, ROW0 + size_x + 2)
    for field in range(2):
        unpack_lines(flags, lines_refs, ends_refs, came_ref, field)
        low, high = came_ref[0], came_ref[1]
        below = keep(flags, LOW_Y, whole_rows_ref[field, 0]) + low[1]
        above = keep(flags, HIGH_Y, whole_rows_ref[field, 1]) + high[1]
        lines[field, 0] = low[0]
        lines[field, 1] = below
        lines[field, 2] = above
        lines[field, 3] = high[2]
        lines[field, 4] = low[2]
        lines[field, 5] = high[0]
        field_ref[field, :, 8 : 8 + size_y] = whole_ref[field]
        field_ref[field, :, 7] = lines[field, 1, spread]
        field_ref[field, :, 8 + size_y] = lines[field, 2, spread]
        field_ref[field, :, 8] = field_ref[field, :, 8] + lines[field, 4, spread]
        field_ref[field, :, 7 + size_y] = field_ref[field, :, 7 + size_y] + lines[field, 5, spread]


def faces_z(half):
    size_z, axis = half.shape[-1], half.ndim - 1
    lane = lax.broadcasted_iota(jnp.int32, half.shape, axis)
    upper = half + jnp.where(lane == size_z - 1, half, pltpu.roll(half, size_z - 1, axis))
    lower = half + jnp.where(lane == 0, half, pltpu.roll(half, 1, axis))
    return upper, lower


def along_z(value, upper, lower):
    size_z, axis = value.shape[-1], value.ndim - 1
    lane = lax.broadcasted_iota(jnp.int32, value.shape, axis)
    above = jnp.where(lane == size_z - 1, 0.0, pltpu.roll(value, size_z - 1, axis))
    below = jnp.where(lane == 0, 0.0, pltpu.roll(value, 1, axis))
    return upper * (value - above) + lower * (value - below)


def operate(field_ref, half_ref, mass_ref, face_ref, x, count):
    size_y = mass_ref.shape[2]
    inside = slice(8, 8 + size_y)
    masses = slice(x + 1, x + 1 + count)
    here = slice(x + 2, x + 2 + count)
    values, images = [], []
    for field in range(2):
        value = field_ref[field, here, inside]
        half = half_ref[field, here, inside]
        flux = along_z(value, face_ref[field, 0, masses], face_ref[field, 1, masses])
        for start in (x + 1, x + 3):
            place = slice(start, start + count)
            flux = flux + (half + half_ref[field, place, inside]) * (value - field_ref[field, place, inside])
        for shift in (-1, 1):
            moved = slice(8 + shift, 8 + shift + size_y)
            flux = flux + (half + half_ref[field, here, moved]) * (value - field_ref[field, here, moved])
        values.append(value)
        images.append(flux)
    first = mass_ref[0, masses] * values[0] + mass_ref[2, masses] * values[1] + images[0]
    second = mass_ref[2, masses] * values[0] + mass_ref[1, masses] * values[1] + images[1]
    return values, (first, second)


def operate_line(lines, half_lines, mass_lines, face_lines, side, near):
    outer, center, inner = (0, 1, 4) if side == 0 else (3, 2, 5)
    values, images = [], []
    for field in range(2):
        value = lines[field, center]
        half = half_lines[field, center]
        count = value.shape[0]
        flux = along_z(value, face_lines[field, 0, side], face_lines[field, 1, side])
        for turn in (1, count - 1):
            flux = flux + (half + pltpu.roll(half, turn, 0)) * (value - pltpu.roll(value, turn, 0))
        flux = flux + (half + half_lines[field, outer]) * (value - lines[field, outer])
        flux = flux + (half + half_lines[field, inner]) * (value - near[field, side])
        values.append(value)
        images.append(flux)
    first = mass_lines[0, side] * values[0] + mass_lines[2, side] * values[1] + images[0]
    second = mass_lines[2, side] * values[0] + mass_lines[1, side] * values[1] + images[1]
    return first, second


def second_solve_kernel(
    mesh, whole_ref, whole_rows_ref, first_lines, second_lines, first_ends, second_ends,
    half_ref, mass_ref, face_ref, half_lines, mass_lines, face_lines, load_ref, inverse_ref, c0, c1, c2, c3,
    precond_ref, image_ref, sums_ref, part_ref, part_rows_ref, even_ref, odd_ref, even_lines, odd_lines,
    came_ref, value_ref, lines, near, field_ref, rows_ref, before_ref, after_ref,
):
    flags = standing(mesh)
    size_x, size_y, size_z = load_ref.shape[1:]
    lines_refs, ends_refs = (first_lines, second_lines), (first_ends, second_ends)
    assemble(flags, whole_ref, whole_rows_ref, lines_refs, ends_refs, came_ref, value_ref, lines)
    for x, flag in ((-1, LOW_X), (size_x, HIGH_X)):
        _, images = operate(value_ref, half_ref, mass_ref, face_ref, x, 1)
        for field in range(2):
            field_ref[field, x + 1 : x + 2] = keep(flags, flag, images[field])
    total_a = total_b = jnp.zeros((CHUNK, size_y, size_z), F32)
    for x in range(0, size_x, CHUNK):
        chunk = slice(x, x + CHUNK)
        values, images = operate(value_ref, half_ref, mass_ref, face_ref, x, CHUNK)
        for field in range(2):
            precond_ref[field, chunk] = values[field]
            image_ref[field, chunk] = images[field]
            field_ref[field, x + 1 : x + 1 + CHUNK] = images[field]
            total_a = total_a + load_ref[field, chunk] * values[field]
            total_b = total_b + images[field] * values[field]
    sums_ref[0:1] = jnp.sum(jnp.sum(total_a, axis=0), axis=0, keepdims=True)
    sums_ref[1:2] = jnp.sum(jnp.sum(total_b, axis=0), axis=0, keepdims=True)
    sums_ref[2:8] = jnp.zeros((6, size_z), F32)
    count = rows_ref.shape[2]
    position = lax.broadcasted_iota(jnp.int32, (count, size_z), 0)
    begin = jnp.where(flags[LOW_X] > 0, ROW0 - 1, ROW0)
    end = jnp.where(flags[HIGH_X] > 0, ROW0 + size_x + 1, ROW0 + size_x)
    valid = (position >= begin) & (position < end)
    for field in range(2):
        for side, row in ((0, 8), (1, 7 + size_y)):
            near[field, side] = jnp.zeros((count, size_z), F32)
            near[field, side, ROW0 - 2 : ROW0 + size_x + 2] = value_ref[field, :, row]
    for side, flag in ((0, LOW_Y), (1, HIGH_Y)):
        images = operate_line(lines, half_lines, mass_lines, face_lines, side, near)
        for field in range(2):
            rows_ref[field, side] = keep(flags, flag, jnp.where(valid, images[field], 0.0))
    solve(field_ref, rows_ref, inverse_ref, (c0, c1, c2, c3), before_ref, after_ref, part_ref, part_rows_ref)
    pack_x(flags, part_ref, part_rows_ref, even_ref, odd_ref)
    pack_lines(flags, part_ref, part_rows_ref, even_lines, odd_lines)


def second_image_kernel(
    mesh, whole_ref, whole_rows_ref, first_lines, second_lines, first_ends, second_ends,
    half_ref, mass_ref, face_ref, old_image_ref, old_sums_ref,
    precond_ref, image_ref, sums_ref, came_ref, value_ref,
):
    flags = standing(mesh)
    size_x, size_y, size_z = old_image_ref.shape[1:]
    own, wide = slice(2, size_x + 2), slice(1, size_x + 3)
    rows, margins = slice(ROW0, ROW0 + size_x), slice(ROW0 - 1, ROW0 + size_x + 1)
    for field in range(2):
        unpack_lines(flags, (first_lines, second_lines), (first_ends, second_ends), came_ref, field)
        value_ref[field, wide, 8 : 8 + size_y] = whole_ref[field, wide]
        value_ref[field, own, 7] = keep(flags, LOW_Y, whole_rows_ref[field, 0, rows]) + came_ref[0, 0, rows]
        value_ref[field, wide, 8] = whole_ref[field, wide, 0] + came_ref[0, 1, margins]
        value_ref[field, wide, 7 + size_y] = whole_ref[field, wide, size_y - 1] + came_ref[1, 1, margins]
        value_ref[field, own, 8 + size_y] = keep(flags, HIGH_Y, whole_rows_ref[field, 1, rows]) + came_ref[1, 0, rows]
    total_c = total_d = jnp.zeros((CHUNK, size_y, size_z), F32)
    for x in range(0, size_x, CHUNK):
        chunk = slice(x, x + CHUNK)
        values, images = operate(value_ref, half_ref, mass_ref, face_ref, x, CHUNK)
        for field in range(2):
            precond_ref[field, chunk] = values[field]
            image_ref[field, chunk] = images[field]
            total_c = total_c + old_image_ref[field, chunk] * values[field]
            total_d = total_d + images[field] * values[field]
    total_c, total_d = jnp.sum(total_c, axis=0), jnp.sum(total_d, axis=0)
    totals = [
        jnp.sum(old_sums_ref[0:1], axis=1, keepdims=True),
        jnp.sum(old_sums_ref[1:2], axis=1, keepdims=True),
        jnp.sum(jnp.sum(total_c, axis=0, keepdims=True), axis=1, keepdims=True),
        jnp.sum(jnp.sum(total_d, axis=0, keepdims=True), axis=1, keepdims=True),
    ]
    lane = lax.broadcasted_iota(jnp.int32, sums_ref.shape, 1)
    spread = jnp.zeros(sums_ref.shape, F32)
    for place, total in enumerate(totals):
        spread = jnp.where(lane == place, total, spread)
    sums_ref[...] = spread


def finish_kernel(
    sums_ref, load_ref, z_ref, q_ref, w_ref, s_ref, solution_hbm, residual_hbm, solution_ref, residual_ref, sems
):
    line = jnp.sum(sums_ref[...], axis=0, keepdims=True)
    lane = lax.broadcasted_iota(jnp.int32, line.shape, 1)
    rz, zq, qw, ws = [jnp.sum(jnp.where(lane == place, line, 0.0), axis=1, keepdims=True) for place in range(4)]
    alpha = rz / zq
    rz_next = rz - alpha * (2.0 * zq) + alpha * alpha * qw
    grown = 1.0 + rz_next / rz
    curvature = grown * grown * zq - 2.0 * grown * alpha * qw + alpha * alpha * ws
    alpha_next = rz_next / curvature
    along = alpha + alpha_next * grown
    against = alpha_next * alpha
    copies = []
    step = load_ref.shape[1] // 2
    for field in range(2):
        for start in range(0, 2 * step, step):
            part = pl.ds(start, step)
            for x in range(start, start + step):
                solution_ref[field, x] = along * z_ref[field, x] - against * w_ref[field, x]
                residual_ref[field, x] = load_ref[field, x] - along * q_ref[field, x] + against * s_ref[field, x]
            for here, there in ((solution_ref, solution_hbm), (residual_ref, residual_hbm)):
                copies.append(
                    pltpu.make_async_copy(here.at[field, part], there.at[field, part], sems.at[len(copies)])
                )
                copies[-1].start()
    for copy in copies:
        copy.wait()


SMEM = pl.BlockSpec(memory_space=pltpu.SMEM)
VMEM = pl.BlockSpec(memory_space=pltpu.VMEM)
HBM = pl.BlockSpec(memory_space=pltpu.HBM)


def call(mesh, kernel, scalars, arrays, outs, scratch=(), flops=0, limit=24, in_hbm=False, outs_in_hbm=False):
    moved = sum(math.prod(a.shape) * a.dtype.itemsize for a in list(arrays) + list(outs))
    return pl.pallas_call(
        kernel if mesh is None else functools.partial(kernel, mesh),
        out_shape=tuple(outs),
        in_specs=[SMEM] * len(scalars) + [HBM if in_hbm else VMEM] * len(arrays),
        out_specs=tuple([HBM if outs_in_hbm else VMEM] * len(outs)),
        scratch_shapes=list(scratch),
        compiler_params=pltpu.CompilerParams(vmem_limit_bytes=limit * 1024 * 1024),
        cost_estimate=pl.CostEstimate(flops=flops, bytes_accessed=moved, transcendentals=0),
    )(*scalars, *arrays)


def shards(mesh, load, zones, conductance, capacity, coupling):
    size_x, size_y, size_z = zones.shape
    assert size_x % BOX == 0 and size_y == BOX and size_z % BOX == 0
    boxes = size_x // BOX
    count = size_x + 8
    sds = lambda *shape: jax.ShapeDtypeStruct(shape, F32)
    consts = [jnp.asarray(c) for c in constants(size_z)]
    modes, lanes = consts[0].shape[0], size_z // BOX * SPAN
    assert size_z == 128
    load, zones, *packed = call(
        mesh,
        edge_layers_kernel,
        [],
        [load, zones],
        [sds(*load.shape), jax.ShapeDtypeStruct(zones.shape, zones.dtype)] + [sds(4, size_y, size_z)] * 2,
        [pltpu.SemaphoreType.DMA((3,))],
        in_hbm=True,
    )
    x_halo = swap(mesh, "gx", *packed)
    (inverse,) = call(
        None,
        divisor_kernel,
        [conductance, capacity],
        [zones],
        [sds(2 * boxes, modes, lanes)],
        flops=40_000_000,
    )
    packed = call(mesh, edge_lines_kernel, [], [load, zones, *x_halo], [sds(4 * size_x + 16, size_z)] * 2)
    y_halo = swap(mesh, "gy", *packed)
    half, mass, face, half_lines, mass_lines, face_lines = call(
        mesh,
        coefficient_kernel,
        [conductance, capacity, coupling],
        [zones, *x_halo, *y_halo],
        [
            sds(2, size_x + 4, size_y + 16, size_z),
            sds(3, size_x + 2, size_y, size_z),
            sds(2, 2, size_x + 2, size_y, size_z),
            sds(2, 6, count, size_z),
            sds(3, 2, count, size_z),
            sds(2, 2, 2, count, size_z),
        ],
        [pltpu.VMEM((4, count, size_z), F32)],
        flops=20_000_000,
    )
    parts = [sds(2, size_x + 2, size_y, size_z), sds(2, 2, count, size_z)]
    packed_x = [[sds(2, depth, size_y + 8, size_z)] * 2 for depth in (3, 2)]
    wholes = [sds(2, size_x + 4, size_y, size_z), sds(2, 2, count, size_z)]
    packed_lines = [[sds(2, depth * size_x, size_z)] * 2 for depth in (3, 2)]
    packed_ends = [[sds(2, depth * 8, size_z)] * 2 for depth in (3, 2)]
    rows = SPAN * size_y + 48
    work = [
        pltpu.VMEM((2, size_x + 2, size_y, size_z), F32),
        pltpu.VMEM((2, 2, count, size_z), F32),
        pltpu.VMEM((2, 3 * rows, boxes * size_z), BF16),
        pltpu.VMEM((2, 3 * rows, boxes * size_z), BF16),
    ]
    padded = [
        pltpu.VMEM((2, size_x + 4, size_y + 16, size_z), F32),
        pltpu.VMEM((2, 6, count, size_z), F32),
    ]
    own = sds(2, size_x, size_y, size_z)

    part, part_rows, *packed = call(
        mesh,
        first_solve_kernel,
        [],
        [load, *x_halo, *y_halo, inverse, *consts],
        parts + packed_x[0] + packed_lines[0],
        work,
        3_000_000_000,
    )
    lines = swap(mesh, "gy", *packed[2:])
    received = swap(mesh, "gx", *packed[:2])
    whole, whole_rows, *packed = call(mesh, merge_x_kernel, [], [part, part_rows, *received], wholes + packed_ends[0])
    ends = swap(mesh, "gy", *packed)
    precond, image, sums, part, part_rows, *packed = call(
        mesh,
        second_solve_kernel,
        [],
        [whole, whole_rows, *lines, *ends, half, mass, face, half_lines, mass_lines, face_lines, load, inverse, *consts],
        [own, own, sds(8, size_z)] + parts + packed_x[1] + packed_lines[1],
        [pltpu.VMEM((2, 3, count, size_z), F32)] + padded + [pltpu.VMEM((2, 2, count, size_z), F32)] + work,
        3_000_000_000,
    )
    lines = swap(mesh, "gy", *packed[2:])
    received = swap(mesh, "gx", *packed[:2])
    whole, whole_rows, *packed = call(mesh, merge_x_kernel, [], [part, part_rows, *received], wholes + packed_ends[1])
    ends = swap(mesh, "gy", *packed)
    devices = mesh.shape["gx"] * mesh.shape["gy"]
    last_precond, last_image, sums = call(
        mesh,
        second_image_kernel,
        [],
        [whole, whole_rows, *lines, *ends, half, mass, face, image, sums],
        [own, own, sds(devices, size_z)],
        [pltpu.VMEM((2, 2, count, size_z), F32), padded[0]],
        10_000_000,
    )
    sums = lax.all_to_all(sums, AXES, 0, 0, tiled=True)
    whole_block = pltpu.VMEM((2, size_x, size_y, size_z), F32)
    return call(
        None,
        finish_kernel,
        [],
        [sums, load, precond, image, last_precond, last_image],
        [own, own],
        [whole_block, whole_block, pltpu.SemaphoreType.DMA((8,))],
        outs_in_hbm=True,
    )


def solution(mesh):
    in_specs = (P(None, "gx", "gy", None), P("gx", "gy", None), P(), P(), P())
    out_specs = (P(None, "gx", "gy", None), P(None, "gx", "gy", None))
    return jax.shard_map(
        functools.partial(shards, mesh), mesh=mesh, in_specs=in_specs, out_specs=out_specs, check_vma=False
    )
```

```python
import functools
import math

import jax
import jax.numpy as jnp
import ml_dtypes
import numpy as np
from jax import lax
from jax.experimental import pallas as pl
from jax.experimental.pallas import tpu as pltpu
from jax.sharding import PartitionSpec as P

BOX = 16
SPAN = BOX + 2
F32 = jnp.float32
BF16 = jnp.bfloat16
AXES = ("gx", "gy")
ROW0 = 4
CHUNK = 4


def split(matrix):
    high = matrix.astype(ml_dtypes.bfloat16)
    low = (matrix - high.astype(np.float64)).astype(ml_dtypes.bfloat16)
    return high, low


def round_up(value, step):
    return (value + step - 1) // step * step


def sine_basis():
    index = np.arange(SPAN)
    angle = np.pi * np.outer(index + 1, index + 1) / (SPAN + 1)
    return np.sqrt(2.0 / (SPAN + 1)) * np.sin(angle)


def eigenvalues():
    return 4.0 * np.sin(np.pi * (np.arange(SPAN) + 1) / (2 * (SPAN + 1))) ** 2


def line_places(y):
    return [(x, y) if 0 <= x < SPAN else None for x in range(1 - ROW0, 25 - ROW0)]


def layer_places(x):
    return [(x, y + 1) for y in range(BOX)]


def plane_matrix(places):
    basis = sine_basis()
    modes = SPAN * SPAN
    plane = np.zeros((round_up(modes, 16), len(places)))
    for column, place in enumerate(places):
        if place is not None:
            plane[:modes, column] = np.outer(basis[:, place[0]], basis[:, place[1]]).reshape(-1)
    return plane


def three_products(matrix):
    high, low = split(matrix)
    return np.concatenate([high, high, low], axis=1)


def constants(size_z):
    basis = sine_basis()
    outer = line_places(0) + line_places(SPAN - 1)
    plane = plane_matrix(sum([layer_places(x) for x in range(SPAN)], []) + outer)
    ends = plane_matrix(layer_places(0) + layer_places(SPAN - 1) + outer)
    lines = plane_matrix(sum([line_places(y) for y in (1, 2, BOX - 1, BOX)], []) + outer)
    boxes = size_z // BOX
    line = np.zeros((size_z, boxes * SPAN))
    for box in range(boxes):
        for mode in range(SPAN):
            for offset in range(SPAN):
                cell = box * BOX + offset - 1
                if 0 <= cell < size_z:
                    line[cell, box * SPAN + mode] = basis[mode, offset]
    high, low = split(line)
    line_forward = np.concatenate([high, high, low], axis=0)
    high, low = split(line.T)
    line_inverse = np.concatenate([high, low], axis=1)
    return three_products(plane), three_products(plane.T), line_forward, line_inverse, three_products(ends), three_products(lines)


def swap_pairs(mesh, axis, odd):
    sizes = [mesh.shape[name] for name in AXES]
    along = AXES.index(axis)
    pairs = []
    for i in range(sizes[0]):
        for j in range(sizes[1]):
            here = [i, j]
            there = [i, j]
            place = here[along]
            target = place ^ 1 if not odd else (place + 1 if place % 2 else place - 1)
            if 0 <= target < sizes[along]:
                there[along] = target
            elif along == 0:
                there[0] = sizes[0] - 1 - place
            else:
                there[0] = i ^ 1
            pairs.append((here[0] * sizes[1] + here[1], there[0] * sizes[1] + there[1]))
    return pairs


def swap(mesh, axis, even_part, odd_part):
    if axis == "gx":
        first = lax.ppermute(even_part, AXES, swap_pairs(mesh, axis, False))
        second = lax.ppermute(odd_part, AXES, swap_pairs(mesh, axis, True))
    else:
        second = lax.ppermute(odd_part, AXES, swap_pairs(mesh, axis, True))
        first = lax.ppermute(even_part, AXES, swap_pairs(mesh, axis, False))
    return first, second


EVEN_X, EVEN_Y, LOW_X, HIGH_X, LOW_Y, HIGH_Y = range(6)


def standing(mesh):
    here_x, here_y = lax.axis_index("gx"), lax.axis_index("gy")
    facts = (
        lax.rem(here_x, 2) == 0,
        lax.rem(here_y, 2) == 0,
        here_x > 0,
        here_x < mesh.shape["gx"] - 1,
        here_y > 0,
        here_y < mesh.shape["gy"] - 1,
    )
    return [fact.astype(jnp.int32) for fact in facts]


def chosen(flags, which, yes, no):
    return jnp.where(flags[which] > 0, yes, no)


def keep(flags, which, value):
    return jnp.where(flags[which] > 0, value, jnp.zeros_like(value))


def halves(value):
    high = value.astype(BF16)
    low = (value - high.astype(F32)).astype(BF16)
    return high, low


def dot(left, right):
    return jnp.dot(left, right, preferred_element_type=F32)


def store_split(stack_ref, lanes, value):
    rows = value.shape[0]
    high, low = halves(value)
    stack_ref[0:rows, lanes] = high
    stack_ref[rows : 2 * rows, lanes] = low
    stack_ref[2 * rows : 3 * rows, lanes] = high


def stacked(before_ref, lanes, parts):
    store_split(before_ref, lanes, jnp.concatenate(parts, axis=0))


def forward_own(field_ref, forward_ref, before_ref, spectral_ref):
    boxes = (field_ref.shape[1] - 2) // BOX
    size_y, size_z = field_ref.shape[2:]
    blank = jnp.zeros((48, size_z), F32)
    for field in range(2):
        for box in range(boxes):
            main = field_ref[field, box * BOX : box * BOX + SPAN].reshape(SPAN * size_y, size_z)
            stacked(before_ref.at[field], slice(box * size_z, (box + 1) * size_z), [main, blank])
    for field in range(2):
        spectral_ref[field] = dot(forward_ref[...], before_ref[field])


def solve(spectral, inverse_ref, consts, after_ref, out_ref, out_rows_ref):
    back_ref, line_forward_ref, line_back_ref = consts
    boxes = (out_ref.shape[1] - 2) // BOX
    size_y, size_z = out_ref.shape[2:]
    inner = SPAN * size_y
    line_rows = line_forward_ref.shape[0] // 3
    lanes = [slice(box * size_z, (box + 1) * size_z) for box in range(boxes)]
    for field in range(2):
        for box in range(boxes):
            high, low = halves(spectral[field][:, lanes[box]])
            both = jnp.concatenate([high, low], axis=1)
            modes = dot(both, line_forward_ref[0 : 2 * line_rows]) + dot(high, line_forward_ref[2 * line_rows :])
            modes = modes * inverse_ref[field * boxes + box]
            high, low = halves(modes)
            cells = dot(high, line_back_ref[...])
            cells = cells[:, :size_z] + (cells[:, size_z:] + dot(low, line_back_ref[:, :size_z]))
            store_split(after_ref.at[field], lanes[box], cells)
    for field in range(2):
        result = dot(back_ref[...], after_ref[field])
        for box in range(boxes):
            start = box * BOX
            main = result[:inner, lanes[box]].reshape(SPAN, size_y, size_z)
            if box == 0:
                out_ref[field, 0:SPAN] = main
            else:
                out_ref[field, start : start + 2] = out_ref[field, start : start + 2] + main[0:2]
                out_ref[field, start + 2 : start + SPAN] = main[2:]
            for side in range(2):
                strip = result[inner + 24 * side : inner + 24 * side + 24, lanes[box]]
                if box == 0:
                    out_rows_ref[field, side, 0:24] = strip
                else:
                    out_rows_ref[field, side, start : start + 8] = (
                        out_rows_ref[field, side, start : start + 8] + strip[0:8]
                    )
                    out_rows_ref[field, side, start + 8 : start + 24] = strip[8:]


def pack_x(flags, part_ref, part_rows_ref, even_ref, odd_ref):
    last = part_ref.shape[1] - 1
    depth = even_ref.shape[1]
    size_y = part_ref.shape[2]
    for field in range(2):
        for layer in range(depth):
            low, high = layer, last + 1 - depth + layer
            for side, place in ((None, slice(0, size_y)), (0, slice(size_y, size_y + 1)), (1, slice(size_y + 1, size_y + 2))):
                if side is None:
                    to_low, to_high = part_ref[field, low], part_ref[field, high]
                else:
                    shift = ROW0 - 1
                    to_low = part_rows_ref[field, side, low + shift : low + shift + 1]
                    to_high = part_rows_ref[field, side, high + shift : high + shift + 1]
                even_ref[field, layer, place] = chosen(flags, EVEN_X, to_high, to_low)
                odd_ref[field, layer, place] = chosen(flags, EVEN_X, to_low, to_high)
            rest = even_ref.shape[2] - size_y - 2
            blank = jnp.zeros((rest, even_ref.shape[3]), F32)
            even_ref[field, layer, size_y + 2 :] = blank
            odd_ref[field, layer, size_y + 2 :] = blank


def line_pairs(whole_ref, whole_rows_ref, field, layers, rows, depth):
    size_y = whole_ref.shape[2]
    if depth == 3:
        return (
            (whole_rows_ref[field, 0, rows], whole_ref[field, layers, size_y - 2]),
            (whole_ref[field, layers, 0], whole_ref[field, layers, size_y - 1]),
            (whole_ref[field, layers, 1], whole_rows_ref[field, 1, rows]),
        )
    return (
        (whole_ref[field, layers, 0], whole_ref[field, layers, size_y - 1]),
        (whole_rows_ref[field, 0, rows], whole_rows_ref[field, 1, rows]),
    )


def pack_lines(flags, part_ref, part_rows_ref, even_ref, odd_ref):
    size_x = part_ref.shape[1] - 2
    depth = even_ref.shape[1] // size_x
    for field in range(2):
        pairs = line_pairs(
            part_ref, part_rows_ref, field, slice(1, size_x + 1), slice(ROW0, ROW0 + size_x), depth
        )
        for line, (to_low, to_high) in enumerate(pairs):
            place = slice(line * size_x, (line + 1) * size_x)
            even_ref[field, place] = chosen(flags, EVEN_Y, to_high, to_low)
            odd_ref[field, place] = chosen(flags, EVEN_Y, to_low, to_high)


def unpack_lines(flags, lines_refs, ends_refs, out_ref, field):
    size_x = out_ref.shape[2] - 8
    depth = lines_refs[0].shape[1] // size_x
    blank = jnp.zeros((8, out_ref.shape[3]), F32)
    for side, flag, (even, odd) in ((0, LOW_Y, (1, 0)), (1, HIGH_Y, (0, 1))):
        lines = keep(flags, flag, chosen(flags, EVEN_Y, lines_refs[even][field], lines_refs[odd][field]))
        ends = keep(flags, flag, chosen(flags, EVEN_Y, ends_refs[even][field], ends_refs[odd][field]))
        for line in range(depth):
            out_ref[side, line, 0:8] = blank
            out_ref[side, line, size_x : size_x + 8] = blank
            out_ref[side, line, ROW0 : ROW0 + size_x] = lines[line * size_x : (line + 1) * size_x]
            out_ref[side, line, ROW0 - 2 : ROW0 + 1] = ends[8 * line : 8 * line + 3]
            out_ref[side, line, ROW0 + size_x - 1 : ROW0 + size_x + 2] = ends[8 * line + 3 : 8 * line + 6]


def divisor_kernel(conductance_ref, capacity_ref, zones_ref, inverse_ref):
    size_x, size_y, size_z = zones_ref.shape
    boxes = size_x // BOX
    lines = []
    for table_ref, which in ((capacity_ref, 0), (capacity_ref, 1), (conductance_ref, 0), (conductance_ref, 1)):
        for box in range(boxes):
            total = jnp.zeros((size_y, size_z), F32)
            for x in range(box * BOX, (box + 1) * BOX):
                zone = zones_ref[x]
                value = jnp.full((size_y, size_z), table_ref[which, 0], F32)
                for label in range(1, table_ref.shape[1]):
                    value = jnp.where(zone == label, table_ref[which, label], value)
                total = total + value
            lines.append(jnp.sum(total, axis=0, keepdims=True))
    sums = jnp.concatenate(lines, axis=0)
    modes, lanes = inverse_ref.shape[1:]
    cell = lax.broadcasted_iota(jnp.int32, (size_z, lanes), 0)
    lane = lax.broadcasted_iota(jnp.int32, (size_z, lanes), 1)
    spread = jnp.zeros((size_z, lanes), F32)
    for box in range(size_z // BOX):
        here = (cell >= box * BOX) & (cell < (box + 1) * BOX) & (lane >= box * SPAN) & (lane < (box + 1) * SPAN)
        spread = jnp.where(here, 1.0 / BOX**3, spread)
    means = jnp.dot(sums, spread, preferred_element_type=F32, precision=lax.Precision.HIGHEST)
    eigen = [float(value) for value in eigenvalues()]
    row = lax.broadcasted_iota(jnp.int32, (modes, 128), 0)
    first = jnp.zeros(row.shape, jnp.int32)
    for mode in range(1, SPAN):
        first = first + (row >= mode * SPAN).astype(jnp.int32)
    second = row - SPAN * first
    pair = jnp.zeros(row.shape, F32)
    for mode in range(SPAN):
        pair = pair + jnp.where(first == mode, eigen[mode], 0.0) + jnp.where(second == mode, eigen[mode], 0.0)
    lane = lax.broadcasted_iota(jnp.int32, (8, lanes), 1)
    for box in range(1, size_z // BOX):
        lane = lane - SPAN * (lax.broadcasted_iota(jnp.int32, (8, lanes), 1) >= box * SPAN).astype(jnp.int32)
    third = jnp.zeros(lane.shape, F32)
    for mode in range(SPAN):
        third = jnp.where(lane == mode, eigen[mode], third)
    summed = jnp.concatenate([pair, pair[:, : lanes - 128]], axis=1) + third[0:1]
    half = 2 * boxes
    for combo in range(half):
        cbar = means[combo : combo + 1]
        kbar = means[half + combo : half + combo + 1]
        inverse_ref[combo] = 1.0 / (cbar + kbar * summed)


def edge_layers_kernel(mesh, load_hbm, zones_hbm, even_ref, odd_ref, load_ref, zones_ref, sems):
    last = zones_hbm.shape[0] - 1
    copies = [
        pltpu.make_async_copy(load_hbm.at[:, 0], load_ref.at[0], sems.at[0]),
        pltpu.make_async_copy(load_hbm.at[:, last], load_ref.at[1], sems.at[1]),
        pltpu.make_async_copy(zones_hbm.at[pl.ds(0, 2)], zones_ref.at[0], sems.at[2]),
        pltpu.make_async_copy(zones_hbm.at[pl.ds(last - 1, 2)], zones_ref.at[1], sems.at[3]),
    ]
    for copy in copies:
        copy.start()
    flags = standing(mesh)
    for copy in copies:
        copy.wait()
    for channel in range(4):
        if channel < 2:
            low, high = load_ref[0, channel], load_ref[1, channel]
        else:
            low, high = zones_ref[0, channel - 2].astype(F32), zones_ref[1, channel - 2].astype(F32)
        even_ref[channel] = chosen(flags, EVEN_X, high, low)
        odd_ref[channel] = chosen(flags, EVEN_X, low, high)


def fetched_kernel(load_ref, zones_ref, token_ref):
    token_ref[...] = load_ref[0, 0, 0:8] + zones_ref[0, 0:8].astype(F32)


def edge_lines_kernel(mesh, load_ref, zones_ref, token_ref, first_ref, second_ref, even_ref, odd_ref):
    flags = standing(mesh)
    size_x, size_y = zones_ref.shape[:2]
    from_low = chosen(flags, EVEN_X, second_ref[...], first_ref[...])
    from_high = chosen(flags, EVEN_X, first_ref[...], second_ref[...])

    def put(row, to_low, to_high):
        place = slice(row, row + to_low.shape[0])
        even_ref[place] = chosen(flags, EVEN_Y, to_high, to_low)
        odd_ref[place] = chosen(flags, EVEN_Y, to_low, to_high)

    def put_end(row, layer, near, far):
        put(4 * size_x + row, layer[near : near + 1], layer[far : far + 1])

    blank = jnp.zeros((8, even_ref.shape[1]), F32)
    put(4 * size_x + 8, blank, blank)
    for field in range(2):
        put(field * size_x, load_ref[field, :, 0], load_ref[field, :, size_y - 1])
        put_end(2 * field, keep(flags, LOW_X, from_low[field]), 0, size_y - 1)
        put_end(2 * field + 1, keep(flags, HIGH_X, from_high[field]), 0, size_y - 1)
    for line in range(2):
        far = size_y - 2 + line
        put((2 + line) * size_x, zones_ref[:, line].astype(F32), zones_ref[:, far].astype(F32))
        for depth in range(2):
            put_end(4 + 4 * line + depth, from_low[2 + depth], line, far)
            put_end(6 + 4 * line + depth, from_high[2 + depth], line, far)


def tables(conductance_ref, capacity_ref, coupling_ref, size_z):
    labels = range(coupling_ref.shape[0])
    halves_of = [[0.5 * conductance_ref[field, label] for label in labels] for field in range(2)]
    masses = [[capacity_ref[field, label] for label in labels] for field in range(2)]
    products = [jnp.full((8, size_z), capacity_ref[0, label] * capacity_ref[1, label], F32) for label in labels]
    masses.append([coupling_ref[label] * jnp.sqrt(products[label])[0:1] for label in labels])
    return halves_of, masses


def looked_up(entries, zone):
    value = jnp.full(zone.shape, entries[0], F32)
    for label in range(1, len(entries)):
        value = jnp.where(zone == float(label), entries[label], value)
    return value


def coefficient_kernel(
    mesh, conductance_ref, capacity_ref, coupling_ref, zones_ref, first_x, second_x, half_ref, mass_ref, face_ref
):
    flags = standing(mesh)
    size_x, size_y, size_z = zones_ref.shape
    halves_of, masses = tables(conductance_ref, capacity_ref, coupling_ref, size_z)
    low_x = chosen(flags, EVEN_X, second_x[2:4], first_x[2:4])
    high_x = chosen(flags, EVEN_X, first_x[2:4], second_x[2:4])
    inside = slice(8, 8 + size_y)
    for x in range(-2, size_x + 2):
        if x < 0:
            zone = low_x[x + 2]
        elif x >= size_x:
            zone = high_x[x - size_x]
        else:
            zone = zones_ref[x].astype(F32)
        for field in range(2):
            half_ref[field, x + 2, inside] = looked_up(halves_of[field], zone)
        if -1 <= x <= size_x:
            for which in range(3):
                mass_ref[which, x + 1] = looked_up(masses[which], zone)
    for field in range(2):
        for outer in (0, 1):
            half_ref[field, outer, inside] = chosen(
                flags, LOW_X, half_ref[field, outer, inside], half_ref[field, 2, inside]
            )
            place = size_x + 2 + outer
            half_ref[field, place, inside] = chosen(
                flags, HIGH_X, half_ref[field, place, inside], half_ref[field, size_x + 1, inside]
            )
    for field in range(2):
        for x in range(0, size_x + 2, 2):
            faces = faces_z(half_ref[field, x + 1 : x + 3, inside])
            for way in range(2):
                face_ref[field, way, x : x + 2] = faces[way]


def coefficient_lines_kernel(
    mesh, conductance_ref, capacity_ref, coupling_ref, old_half_ref, mass_ref, face_ref, first_y, second_y,
    half_ref, half_rows_ref, mass_rows_ref, face_rows_ref, line_ref,
):
    flags = standing(mesh)
    size_x, size_y, size_z = mass_ref.shape[1] - 2, mass_ref.shape[2], mass_ref.shape[3]
    halves_of, masses = tables(conductance_ref, capacity_ref, coupling_ref, size_z)
    for side, (even, odd) in enumerate(((second_y, first_y), (first_y, second_y))):
        came = chosen(flags, EVEN_Y, even[2 * size_x :], odd[2 * size_x :])
        lines, ends = (came[:size_x], came[size_x : 2 * size_x]), came[2 * size_x :]
        for line in range(2):
            place = 2 * side + line
            line_ref[place, 0:8] = jnp.zeros((8, size_z), F32)
            line_ref[place, size_x : size_x + 8] = jnp.zeros((8, size_z), F32)
            line_ref[place, ROW0 - 2 : ROW0] = ends[4 + 4 * line : 6 + 4 * line]
            line_ref[place, ROW0 : ROW0 + size_x] = lines[line]
            line_ref[place, ROW0 + size_x : ROW0 + size_x + 2] = ends[6 + 4 * line : 8 + 4 * line]
    count = half_rows_ref.shape[2]
    position = lax.broadcasted_iota(jnp.int32, (count, size_z), 0)
    for line, flag in enumerate((LOW_Y, LOW_Y, HIGH_Y, HIGH_Y)):
        zone = line_ref[line]
        for field in range(2):
            value = looked_up(halves_of[field], zone)
            below = value[ROW0 : ROW0 + 1]
            above = value[ROW0 + size_x - 1 : ROW0 + size_x]
            value = jnp.where((position < ROW0) & (flags[LOW_X] == 0), below, value)
            value = jnp.where((position >= ROW0 + size_x) & (flags[HIGH_X] == 0), above, value)
            near = old_half_ref[field, :, 8 if flag == LOW_Y else 8 + size_y - 1]
            half_rows_ref[field, line] = value
            half_rows_ref[field, line, ROW0 - 2 : ROW0 + size_x + 2] = chosen(
                flags, flag, half_rows_ref[field, line, ROW0 - 2 : ROW0 + size_x + 2], near
            )
            if line in (1, 2):
                row = 7 if line == 1 else 8 + size_y
                half_ref[field, :, row] = half_rows_ref[field, line, ROW0 - 2 : ROW0 + size_x + 2]
        if line in (1, 2):
            for which in range(3):
                mass_rows_ref[which, line - 1] = looked_up(masses[which], zone)
    for field in range(2):
        for side in range(2):
            faces = faces_z(half_rows_ref[field, side + 1])
            for way in range(2):
                face_rows_ref[field, way, side] = faces[way]
        for line, row in ((4, 0), (5, size_y - 1), (6, 1), (7, size_y - 2)):
            half_rows_ref[field, line] = jnp.zeros((count, size_z), F32)
            half_rows_ref[field, line, ROW0 - 2 : ROW0 + size_x + 2] = old_half_ref[field, :, 8 + row]
    for line, row in ((2, 0), (3, size_y - 1)):
        spread = slice(ROW0 - 1, ROW0 + size_x + 1)
        for which in range(3):
            mass_rows_ref[which, line] = jnp.zeros((count, size_z), F32)
            mass_rows_ref[which, line, spread] = mass_ref[which, :, row]
        for field in range(2):
            for way in range(2):
                face_rows_ref[field, way, line] = jnp.zeros((count, size_z), F32)
                face_rows_ref[field, way, line, spread] = face_ref[field, way, :, row]


def own_transform_kernel(load_ref, forward_ref, spectral_ref, field_ref, before_ref):
    size_x = load_ref.shape[1]
    for field in range(2):
        field_ref[field, 0] = jnp.zeros(load_ref.shape[2:], F32)
        field_ref[field, 1 : 1 + size_x] = load_ref[field]
        field_ref[field, 1 + size_x] = jnp.zeros(load_ref.shape[2:], F32)
    forward_own(field_ref, forward_ref, before_ref, spectral_ref)


def first_solve_kernel(
    mesh, spectral_ref, mass_ref, first_x, second_x, first_y, second_y, inverse_ref, c1, c2, c3, ends_ref,
    part_ref, part_rows_ref, even_ref, odd_ref, even_lines, odd_lines, rows_ref, before_ref, after_ref,
):
    flags = standing(mesh)
    size_x, size_y, size_z = part_ref.shape[1] - 2, part_ref.shape[2], part_ref.shape[3]
    boxes = size_x // BOX
    blank = jnp.zeros((size_y, size_z), F32)
    spectral = []
    for field in range(2):
        low = keep(flags, LOW_X, chosen(flags, EVEN_X, second_x[field], first_x[field]))
        high = keep(flags, HIGH_X, chosen(flags, EVEN_X, first_x[field], second_x[field]))
        for side, flag, even, odd in ((0, LOW_Y, second_y, first_y), (1, HIGH_Y, first_y, second_y)):
            place, after = slice(field * size_x, (field + 1) * size_x), slice(4 * size_x, 4 * size_x + 8)
            line = keep(flags, flag, chosen(flags, EVEN_Y, even[place], odd[place]))
            ends = keep(flags, flag, chosen(flags, EVEN_Y, even[after], odd[after]))
            rows_ref[field, side, 0:8] = blank[0:8]
            rows_ref[field, side, size_x : size_x + 8] = blank[0:8]
            rows_ref[field, side, ROW0 - 1 : ROW0] = ends[2 * field : 2 * field + 1]
            rows_ref[field, side, ROW0 : ROW0 + size_x] = line
            rows_ref[field, side, ROW0 + size_x : ROW0 + size_x + 1] = ends[2 * field + 1 : 2 * field + 2]
        for box in range(boxes):
            parts = [low if box == 0 else blank, high if box == boxes - 1 else blank]
            parts += [rows_ref[field, side, box * BOX : box * BOX + 24] for side in range(2)]
            stacked(before_ref.at[field], slice(box * size_z, (box + 1) * size_z), parts)
    for field in range(2):
        spectral.append(spectral_ref[field] + dot(ends_ref[...], before_ref[field]))
    solve(spectral, inverse_ref, (c1, c2, c3), after_ref, part_ref, part_rows_ref)
    pack_x(flags, part_ref, part_rows_ref, even_ref, odd_ref)
    pack_lines(flags, part_ref, part_rows_ref, even_lines, odd_lines)


def merge_x_kernel(mesh, part_ref, part_rows_ref, first_ref, second_ref, whole_ref, whole_rows_ref, even_ref, odd_ref):
    flags = standing(mesh)
    size_x = part_ref.shape[1] - 2
    size_y, size_z = part_ref.shape[2:]
    depth = first_ref.shape[1]
    end = ROW0 + size_x
    for field in range(2):
        low = keep(flags, LOW_X, chosen(flags, EVEN_X, second_ref[field], first_ref[field]))
        high = keep(flags, HIGH_X, chosen(flags, EVEN_X, first_ref[field], second_ref[field]))
        whole_ref[field, 1] = keep(flags, LOW_X, part_ref[field, 0]) + low[depth - 2, :size_y]
        whole_ref[field, 2] = part_ref[field, 1] + low[depth - 1, :size_y]
        whole_ref[field, 3 : size_x + 1] = part_ref[field, 2:size_x]
        whole_ref[field, size_x + 1] = part_ref[field, size_x] + high[0, :size_y]
        whole_ref[field, size_x + 2] = keep(flags, HIGH_X, part_ref[field, size_x + 1]) + high[1, :size_y]
        whole_ref[field, 0] = low[0, :size_y] if depth == 3 else jnp.zeros((size_y, size_z), F32)
        whole_ref[field, size_x + 3] = high[2, :size_y] if depth == 3 else jnp.zeros((size_y, size_z), F32)
        for side in range(2):
            row = slice(size_y + side, size_y + side + 1)
            edge = ROW0 - 1
            whole_rows_ref[field, side] = part_rows_ref[field, side]
            whole_rows_ref[field, side, edge : edge + 1] = (
                keep(flags, LOW_X, part_rows_ref[field, side, edge : edge + 1]) + low[depth - 2, row]
            )
            whole_rows_ref[field, side, edge + 1 : edge + 2] = (
                part_rows_ref[field, side, edge + 1 : edge + 2] + low[depth - 1, row]
            )
            whole_rows_ref[field, side, end - 1 : end] = part_rows_ref[field, side, end - 1 : end] + high[0, row]
            whole_rows_ref[field, side, end : end + 1] = (
                keep(flags, HIGH_X, part_rows_ref[field, side, end : end + 1]) + high[1, row]
            )
            if depth == 3:
                whole_rows_ref[field, side, edge - 1 : edge] = low[0, row]
                whole_rows_ref[field, side, end + 1 : end + 2] = high[2, row]

        for line in range(depth):
            for ref in (even_ref, odd_ref):
                ref[field, 8 * line : 8 * line + 8] = jnp.zeros((8, size_z), F32)
        for start, x in ((0, -2), (3, size_x - 1)):
            layers, rows = slice(x + 2, x + 5), slice(x + ROW0, x + ROW0 + 3)
            pairs = line_pairs(whole_ref, whole_rows_ref, field, layers, rows, depth)
            for line, (to_low, to_high) in enumerate(pairs):
                place = slice(8 * line + start, 8 * line + start + 3)
                even_ref[field, place] = chosen(flags, EVEN_Y, to_high, to_low)
                odd_ref[field, place] = chosen(flags, EVEN_Y, to_low, to_high)


def faces_z(half):
    size_z, axis = half.shape[-1], half.ndim - 1
    lane = lax.broadcasted_iota(jnp.int32, half.shape, axis)
    upper = half + jnp.where(lane == size_z - 1, half, pltpu.roll(half, size_z - 1, axis))
    lower = half + jnp.where(lane == 0, half, pltpu.roll(half, 1, axis))
    return upper, lower


def along_z(value, upper, lower):
    size_z, axis = value.shape[-1], value.ndim - 1
    lane = lax.broadcasted_iota(jnp.int32, value.shape, axis)
    above = jnp.where(lane == size_z - 1, 0.0, pltpu.roll(value, size_z - 1, axis))
    below = jnp.where(lane == 0, 0.0, pltpu.roll(value, 1, axis))
    return upper * (value - above) + lower * (value - below)


def operate(field_ref, half_ref, mass_ref, face_ref, x, count):
    size_y = mass_ref.shape[2]
    inside = slice(8, 8 + size_y)
    masses = slice(x + 1, x + 1 + count)
    here = slice(x + 2, x + 2 + count)
    values, images = [], []
    for field in range(2):
        value = field_ref[field, here, inside]
        half = half_ref[field, here, inside]
        flux = along_z(value, face_ref[field, 0, masses], face_ref[field, 1, masses])
        for start in (x + 1, x + 3):
            place = slice(start, start + count)
            flux = flux + (half + half_ref[field, place, inside]) * (value - field_ref[field, place, inside])
        for shift in (-1, 1):
            moved = slice(8 + shift, 8 + shift + size_y)
            flux = flux + (half + half_ref[field, here, moved]) * (value - field_ref[field, here, moved])
        values.append(value)
        images.append(flux)
    first = mass_ref[0, masses] * values[0] + mass_ref[2, masses] * values[1] + images[0]
    second = mass_ref[2, masses] * values[0] + mass_ref[1, masses] * values[1] + images[1]
    return values, (first, second)


def fill(flags, whole_ref, whole_rows_ref, value_ref):
    size_x, size_y = whole_ref.shape[1] - 4, whole_ref.shape[2]
    spread = slice(ROW0 - 2, ROW0 + size_x + 2)
    for field in range(2):
        value_ref[field, :, 8 : 8 + size_y] = whole_ref[field]
        value_ref[field, :, 7] = keep(flags, LOW_Y, whole_rows_ref[field, 0, spread])
        value_ref[field, :, 8 + size_y] = keep(flags, HIGH_Y, whole_rows_ref[field, 1, spread])


def line_image(values, outers, inners, half_lines, places, mass_lines, face_lines, place):
    center, outer, inner = places
    images = []
    for field in range(2):
        value, half = values[field], half_lines[field, center]
        count = value.shape[0]
        flux = along_z(value, face_lines[field, 0, place], face_lines[field, 1, place])
        for turn in (1, count - 1):
            flux = flux + (half + pltpu.roll(half, turn, 0)) * (value - pltpu.roll(value, turn, 0))
        flux = flux + (half + half_lines[field, outer]) * (value - outers[field])
        flux = flux + (half + half_lines[field, inner]) * (value - inners[field])
        images.append(flux)
    first = mass_lines[0, place] * values[0] + mass_lines[2, place] * values[1] + images[0]
    second = mass_lines[2, place] * values[0] + mass_lines[1, place] * values[1] + images[1]
    return first, second


SIDES = (((4, 1, 6, 0), (2, 0)), ((5, 2, 7, 3), (3, 1)))


def line_changes(delta, outer, half_lines, mass_lines, face_lines, side):
    (edge, out, inner, _), (place, _) = SIDES[side]
    nothing = [jnp.zeros_like(line) for line in delta]
    at_edge = line_image(delta, outer, nothing, half_lines, (edge, out, inner), mass_lines, face_lines, place)
    at_next = [-(half_lines[field, edge] + half_lines[field, inner]) * delta[field] for field in range(2)]
    return at_edge, at_next


def own_image_kernel(
    mesh, whole_ref, whole_rows_ref, half_ref, mass_ref, face_ref, forward_ref, image_ref, spectral_ref,
    value_ref, before_ref,
):
    flags = standing(mesh)
    size_x = whole_ref.shape[1] - 4
    fill(flags, whole_ref, whole_rows_ref, value_ref)
    for x, flag in ((-1, LOW_X), (size_x, HIGH_X)):
        _, images = operate(value_ref, half_ref, mass_ref, face_ref, x, 1)
        for field in range(2):
            image_ref[field, x + 1 : x + 2] = keep(flags, flag, images[field])
    for x in range(0, size_x, CHUNK):
        _, images = operate(value_ref, half_ref, mass_ref, face_ref, x, CHUNK)
        for field in range(2):
            image_ref[field, x + 1 : x + 1 + CHUNK] = images[field]
    forward_own(image_ref, forward_ref, before_ref, spectral_ref)


def second_solve_kernel(
    mesh, whole_ref, whole_rows_ref, first_lines, second_lines, first_ends, second_ends,
    half_lines, mass_lines, face_lines, spectral_ref, inverse_ref, c1, c2, c3, lines_ref,
    deltas_ref, changes_ref, part_ref, part_rows_ref, even_ref, odd_ref, even_lines, odd_lines,
    came_ref, near, before_ref, after_ref,
):
    flags = standing(mesh)
    size_x, size_y, size_z = part_ref.shape[1] - 2, part_ref.shape[2], part_ref.shape[3]
    boxes = size_x // BOX
    count = near.shape[2]
    position = lax.broadcasted_iota(jnp.int32, (count, size_z), 0)
    begin = jnp.where(flags[LOW_X] > 0, ROW0 - 1, ROW0)
    end = jnp.where(flags[HIGH_X] > 0, ROW0 + size_x + 1, ROW0 + size_x)
    valid = (position >= begin) & (position < end)
    for field in range(2):
        unpack_lines(flags, (first_lines, second_lines), (first_ends, second_ends), came_ref.at[field], field)
        for side, row in ((0, 0), (1, size_y - 1)):
            near[field, side] = jnp.zeros((count, size_z), F32)
            near[field, side, ROW0 - 2 : ROW0 + size_x + 2] = whole_ref[field, :, row]
    for side, flag, order in ((0, LOW_Y, (2, 1, 0)), (1, HIGH_Y, (0, 1, 2))):
        delta, outer, far = [[came_ref[field, side, line] for field in range(2)] for line in order]
        at_edge, at_next = line_changes(delta, outer, half_lines, mass_lines, face_lines, side)
        (edge, out, _, beyond), (_, place) = SIDES[side]
        at_outer = line_image(
            [keep(flags, flag, whole_rows_ref[field, side]) + outer[field] for field in range(2)],
            far,
            [near[field, side] + delta[field] for field in range(2)],
            half_lines,
            (out, beyond, edge),
            mass_lines,
            face_lines,
            place,
        )
        for field in range(2):
            deltas_ref[field, side] = delta[field]
            changes_ref[field, 3 * side] = jnp.where(valid, at_edge[field], 0.0)
            changes_ref[field, 1 + side] = jnp.where(valid, at_next[field], 0.0)
            changes_ref[field, 4 + side] = keep(flags, flag, jnp.where(valid, at_outer[field], 0.0))
    spectral = []
    for field in range(2):
        for box in range(boxes):
            parts = [changes_ref[field, line, box * BOX : box * BOX + 24] for line in range(6)]
            stacked(before_ref.at[field], slice(box * size_z, (box + 1) * size_z), parts)
    for field in range(2):
        spectral.append(spectral_ref[field] + dot(lines_ref[...], before_ref[field]))
    solve(spectral, inverse_ref, (c1, c2, c3), after_ref, part_ref, part_rows_ref)
    pack_x(flags, part_ref, part_rows_ref, even_ref, odd_ref)
    pack_lines(flags, part_ref, part_rows_ref, even_lines, odd_lines)


def first_sums_kernel(load_ref, whole_ref, image_ref, deltas_ref, changes_ref, precond_ref, out_ref, sums_ref):
    size_x, size_y, size_z = load_ref.shape[1:]
    rows = slice(ROW0, ROW0 + size_x)
    total_a = total_b = jnp.zeros((size_y, size_z), F32)
    for field in range(2):
        precond_ref[field] = whole_ref[field, 2 : size_x + 2]
        out_ref[field] = image_ref[field, 1 : size_x + 1]
        for side, row in ((0, 0), (1, size_y - 1)):
            precond_ref[field, :, row] = precond_ref[field, :, row] + deltas_ref[field, side, rows]
        for line, row in enumerate((0, 1, size_y - 2, size_y - 1)):
            out_ref[field, :, row] = out_ref[field, :, row] + changes_ref[field, line, rows]
        for x in range(size_x):
            total_a = total_a + load_ref[field, x] * precond_ref[field, x]
            total_b = total_b + out_ref[field, x] * precond_ref[field, x]
    sums_ref[0:1] = jnp.sum(total_a, axis=0, keepdims=True)
    sums_ref[1:2] = jnp.sum(total_b, axis=0, keepdims=True)
    sums_ref[2:8] = jnp.zeros((6, size_z), F32)


def own_second_image_kernel(
    mesh, whole_ref, whole_rows_ref, half_ref, mass_ref, face_ref, old_image_ref, image_ref, sums_ref, value_ref
):
    flags = standing(mesh)
    size_x, size_y, size_z = old_image_ref.shape[1:]
    fill(flags, whole_ref, whole_rows_ref, value_ref)
    total_c = total_d = jnp.zeros((CHUNK, size_y, size_z), F32)
    for x in range(0, size_x, CHUNK):
        chunk = slice(x, x + CHUNK)
        values, images = operate(value_ref, half_ref, mass_ref, face_ref, x, CHUNK)
        for field in range(2):
            image_ref[field, chunk] = images[field]
            total_c = total_c + old_image_ref[field, chunk] * values[field]
            total_d = total_d + images[field] * values[field]
    sums_ref[0:1] = jnp.sum(jnp.sum(total_c, axis=0), axis=0, keepdims=True)
    sums_ref[1:2] = jnp.sum(jnp.sum(total_d, axis=0), axis=0, keepdims=True)
    sums_ref[2:8] = jnp.zeros((6, size_z), F32)


def second_image_kernel(
    mesh, whole_ref, image_ref, first_lines, second_lines, first_ends, second_ends,
    half_lines, mass_lines, face_lines, old_image_ref, old_sums_ref, own_sums_ref,
    deltas_ref, changes_ref, sums_ref, came_ref,
):
    flags = standing(mesh)
    size_x, size_y, size_z = old_image_ref.shape[1:]
    own = slice(2, size_x + 2)
    rows = slice(ROW0, ROW0 + size_x)
    total_c = total_d = jnp.zeros((size_x, size_z), F32)
    for field in range(2):
        unpack_lines(flags, (first_lines, second_lines), (first_ends, second_ends), came_ref.at[field], field)
    for side, row, beside in ((0, 0, 1), (1, size_y - 1, size_y - 2)):
        outer, delta = [[came_ref[field, side, line] for field in range(2)] for line in range(2)]
        at_edge, at_next = line_changes(delta, outer, half_lines, mass_lines, face_lines, side)
        for field in range(2):
            changed, edge, inner = delta[field][rows], at_edge[field][rows], at_next[field][rows]
            deltas_ref[field, side] = changed
            changes_ref[field, 3 * side] = edge
            changes_ref[field, 1 + side] = inner
            total_c = total_c + old_image_ref[field, :, row] * changed
            total_d = total_d + (image_ref[field, :, row] + edge) * changed
            total_d = total_d + whole_ref[field, own, row] * edge + whole_ref[field, own, beside] * inner
    totals = [
        jnp.sum(old_sums_ref[0:1], axis=1, keepdims=True),
        jnp.sum(old_sums_ref[1:2], axis=1, keepdims=True),
        jnp.sum(jnp.sum(total_c, axis=0, keepdims=True) + own_sums_ref[0:1], axis=1, keepdims=True),
        jnp.sum(jnp.sum(total_d, axis=0, keepdims=True) + own_sums_ref[1:2], axis=1, keepdims=True),
    ]
    lane = lax.broadcasted_iota(jnp.int32, sums_ref.shape, 1)
    spread = jnp.zeros(sums_ref.shape, F32)
    for place, total in enumerate(totals):
        spread = jnp.where(lane == place, total, spread)
    sums_ref[...] = spread


def finish_kernel(
    sums_ref, load_ref, z_ref, q_ref, w_ref, s_ref, deltas_ref, changes_ref,
    solution_hbm, residual_hbm, solution_ref, residual_ref, sems,
):
    line = jnp.sum(sums_ref[...], axis=0, keepdims=True)
    lane = lax.broadcasted_iota(jnp.int32, line.shape, 1)
    rz, zq, qw, ws = [jnp.sum(jnp.where(lane == place, line, 0.0), axis=1, keepdims=True) for place in range(4)]
    alpha = rz / zq
    rz_next = rz - alpha * (2.0 * zq) + alpha * alpha * qw
    grown = 1.0 + rz_next / rz
    curvature = grown * grown * zq - 2.0 * grown * alpha * qw + alpha * alpha * ws
    alpha_next = rz_next / curvature
    along = alpha + alpha_next * grown
    against = alpha_next * alpha
    copies = []
    step = load_ref.shape[1] // 2
    for field in range(2):
        for start in range(0, 2 * step, step):
            part = pl.ds(start, step)
            for x in range(start, start + step):
                solution_ref[field, x] = along * z_ref[field, x] - against * w_ref[field, x + 2]
                residual_ref[field, x] = load_ref[field, x] - along * q_ref[field, x] + against * s_ref[field, x]
            size_y = load_ref.shape[2]
            chunk = slice(start, start + step)
            for side, row in ((0, 0), (1, size_y - 1)):
                solution_ref[field, chunk, row] = (
                    solution_ref[field, chunk, row] - against * deltas_ref[field, side, chunk]
                )
            for line, row in enumerate((0, 1, size_y - 2, size_y - 1)):
                residual_ref[field, chunk, row] = (
                    residual_ref[field, chunk, row] + against * changes_ref[field, line, chunk]
                )
            for here, there in ((solution_ref, solution_hbm), (residual_ref, residual_hbm)):
                copies.append(
                    pltpu.make_async_copy(here.at[field, part], there.at[field, part], sems.at[len(copies)])
                )
                copies[-1].start()
    for copy in copies:
        copy.wait()


SMEM = pl.BlockSpec(memory_space=pltpu.SMEM)
VMEM = pl.BlockSpec(memory_space=pltpu.VMEM)
HBM = pl.BlockSpec(memory_space=pltpu.HBM)


def call(mesh, kernel, scalars, arrays, outs, scratch=(), flops=0, limit=24, in_hbm=False, outs_in_hbm=False, aliases=()):
    moved = sum(math.prod(a.shape) * a.dtype.itemsize for a in list(arrays) + list(outs))
    return pl.pallas_call(
        kernel if mesh is None else functools.partial(kernel, mesh),
        out_shape=tuple(outs),
        in_specs=[SMEM] * len(scalars) + [HBM if in_hbm else VMEM] * len(arrays),
        out_specs=tuple([HBM if outs_in_hbm else VMEM] * len(outs)),
        scratch_shapes=list(scratch),
        input_output_aliases=dict(aliases),
        compiler_params=pltpu.CompilerParams(vmem_limit_bytes=limit * 1024 * 1024),
        cost_estimate=pl.CostEstimate(flops=flops, bytes_accessed=moved, transcendentals=0),
    )(*scalars, *arrays)


def shards(mesh, load, zones, conductance, capacity, coupling):
    size_x, size_y, size_z = zones.shape
    assert size_x % BOX == 0 and size_y == BOX and size_z % BOX == 0
    boxes = size_x // BOX
    count = size_x + 8
    sds = lambda *shape: jax.ShapeDtypeStruct(shape, F32)
    forward, back, line_forward, line_back, ends_forward, lines_forward = [jnp.asarray(c) for c in constants(size_z)]
    consts = (back, line_forward, line_back)
    modes, lanes = forward.shape[0], size_z // BOX * SPAN
    assert size_z == 128
    packed = call(
        mesh,
        edge_layers_kernel,
        [],
        [load, zones],
        [sds(4, size_y, size_z)] * 2,
        [
            pltpu.VMEM((2, 2, size_y, size_z), F32),
            pltpu.VMEM((2, 2, size_y, size_z), zones.dtype),
            pltpu.SemaphoreType.DMA((4,)),
        ],
        in_hbm=True,
        limit=56,
    )
    (token,) = call(None, fetched_kernel, [], [load, zones], [sds(8, size_z)])
    x_halo = swap(mesh, "gx", *packed)
    (inverse,) = call(
        None,
        divisor_kernel,
        [conductance, capacity],
        [zones],
        [sds(2 * boxes, modes, lanes)],
        flops=40_000_000,
    )
    packed = call(mesh, edge_lines_kernel, [], [load, zones, token, *x_halo], [sds(4 * size_x + 16, size_z)] * 2)
    y_halo = swap(mesh, "gy", *packed)
    laws = [conductance, capacity, coupling]
    padded_shape = sds(2, size_x + 4, size_y + 16, size_z)
    half, mass, face = call(
        mesh,
        coefficient_kernel,
        laws,
        [zones, *x_halo],
        [padded_shape, sds(3, size_x + 2, size_y, size_z), sds(2, 2, size_x + 2, size_y, size_z)],
        flops=20_000_000,
    )
    half, half_lines, mass_lines, face_lines = call(
        mesh,
        coefficient_lines_kernel,
        laws,
        [half, mass, face, *y_halo],
        [padded_shape, sds(2, 8, count, size_z), sds(3, 4, count, size_z), sds(2, 2, 4, count, size_z)],
        [pltpu.VMEM((4, count, size_z), F32)],
        flops=2_000_000,
        aliases={3: 0},
    )
    parts = [sds(2, size_x + 2, size_y, size_z), sds(2, 2, count, size_z)]
    packed_x = [[sds(2, depth, size_y + 8, size_z)] * 2 for depth in (3, 2)]
    wholes = [sds(2, size_x + 4, size_y, size_z), sds(2, 2, count, size_z)]
    packed_lines = [[sds(2, depth * size_x, size_z)] * 2 for depth in (3, 2)]
    packed_ends = [[sds(2, depth * 8, size_z)] * 2 for depth in (3, 2)]
    rows = SPAN * size_y + 48
    wide = boxes * size_z
    spectrum = sds(2, modes, wide)
    stack = lambda depth: pltpu.VMEM((2, depth, wide), BF16)
    halo = pltpu.VMEM((2, size_x + 2, size_y, size_z), F32)
    padded = pltpu.VMEM((2, size_x + 4, size_y + 16, size_z), F32)
    own = sds(2, size_x, size_y, size_z)

    (spectral,) = call(None, own_transform_kernel, [], [load, forward], [spectrum], [halo, stack(3 * rows)], 700_000_000)
    part, part_rows, *packed = call(
        mesh,
        first_solve_kernel,
        [],
        [spectral, mass, *x_halo, *y_halo, inverse, *consts, ends_forward],
        parts + packed_x[0] + packed_lines[0],
        [pltpu.VMEM((2, 2, count, size_z), F32), stack(ends_forward.shape[1]), stack(3 * rows)],
        2_000_000_000,
    )
    lines = swap(mesh, "gy", *packed[2:])
    received = swap(mesh, "gx", *packed[:2])
    whole, whole_rows, *packed = call(mesh, merge_x_kernel, [], [part, part_rows, *received], wholes + packed_ends[0])
    ends = swap(mesh, "gy", *packed)
    own_image, spectral = call(
        mesh,
        own_image_kernel,
        [],
        [whole, whole_rows, half, mass, face, forward],
        [sds(2, size_x + 2, size_y, size_z), spectrum],
        [padded, stack(3 * rows)],
        700_000_000,
    )
    deltas, changes, part, part_rows, *packed = call(
        mesh,
        second_solve_kernel,
        [],
        [whole, whole_rows, *lines, *ends, half_lines, mass_lines, face_lines, spectral, inverse, *consts, lines_forward],
        [sds(2, 2, count, size_z), sds(2, 6, count, size_z)] + parts + packed_x[1] + packed_lines[1],
        [
            pltpu.VMEM((2, 2, 3, count, size_z), F32),
            pltpu.VMEM((2, 2, count, size_z), F32),
            stack(lines_forward.shape[1]),
            stack(3 * rows),
        ],
        2_000_000_000,
    )
    lines = swap(mesh, "gy", *packed[2:])
    received = swap(mesh, "gx", *packed[:2])
    precond, image, sums = call(
        None, first_sums_kernel, [], [load, whole, own_image, deltas, changes], [own, own, sds(8, size_z)], flops=1_000_000
    )
    whole, whole_rows, *packed = call(mesh, merge_x_kernel, [], [part, part_rows, *received], wholes + packed_ends[1])
    ends = swap(mesh, "gy", *packed)
    last_image, own_sums = call(
        mesh,
        own_second_image_kernel,
        [],
        [whole, whole_rows, half, mass, face, image],
        [own, sds(8, size_z)],
        [padded],
        10_000_000,
    )
    devices = mesh.shape["gx"] * mesh.shape["gy"]
    deltas, changes, sums = call(
        mesh,
        second_image_kernel,
        [],
        [whole, last_image, *lines, *ends, half_lines, mass_lines, face_lines, image, sums, own_sums],
        [sds(2, 2, size_x, size_z), sds(2, 4, size_x, size_z), sds(devices, size_z)],
        [pltpu.VMEM((2, 2, 2, count, size_z), F32)],
        1_000_000,
    )
    sums = lax.all_to_all(sums, AXES, 0, 0, tiled=True)
    whole_block = pltpu.VMEM((2, size_x, size_y, size_z), F32)
    return call(
        None,
        finish_kernel,
        [],
        [sums, load, precond, image, whole, last_image, deltas, changes],
        [own, own],
        [whole_block, whole_block, pltpu.SemaphoreType.DMA((8,))],
        outs_in_hbm=True,
    )


def solution(mesh):
    in_specs = (P(None, "gx", "gy", None), P("gx", "gy", None), P(), P(), P())
    out_specs = (P(None, "gx", "gy", None), P(None, "gx", "gy", None))
    return jax.shard_map(
        functools.partial(shards, mesh), mesh=mesh, in_specs=in_specs, out_specs=out_specs, check_vma=False
    )
```

```python
import functools
import math

import jax
import jax.numpy as jnp
import ml_dtypes
import numpy as np
from jax import lax
from jax.experimental import pallas as pl
from jax.experimental.pallas import tpu as pltpu
from jax.sharding import PartitionSpec as P

BOX = 16
SPAN = BOX + 2
F32 = jnp.float32
BF16 = jnp.bfloat16
AXES = ("gx", "gy")
ROW0 = 4
EDGE_LAYERS = (0, 1, 2, SPAN - 3, SPAN - 2, SPAN - 1)
CHUNK = 4


def split(matrix):
    high = matrix.astype(ml_dtypes.bfloat16)
    low = (matrix - high.astype(np.float64)).astype(ml_dtypes.bfloat16)
    return high, low


def round_up(value, step):
    return (value + step - 1) // step * step


def sine_basis():
    index = np.arange(SPAN)
    angle = np.pi * np.outer(index + 1, index + 1) / (SPAN + 1)
    return np.sqrt(2.0 / (SPAN + 1)) * np.sin(angle)


def eigenvalues():
    return 4.0 * np.sin(np.pi * (np.arange(SPAN) + 1) / (2 * (SPAN + 1))) ** 2


def line_places(y):
    return [(x, y) if 0 <= x < SPAN else None for x in range(1 - ROW0, 25 - ROW0)]


def layer_places(x):
    return [(x, y + 1) for y in range(BOX)]


def plane_matrix(places):
    basis = sine_basis()
    modes = SPAN * SPAN
    plane = np.zeros((round_up(modes, 16), len(places)))
    for column, place in enumerate(places):
        if place is not None:
            plane[:modes, column] = np.outer(basis[:, place[0]], basis[:, place[1]]).reshape(-1)
    return plane


def three_products(matrix):
    high, low = split(matrix)
    return np.concatenate([high, high, low], axis=1)


def constants(size_z):
    basis = sine_basis()
    outer = line_places(0) + line_places(SPAN - 1)
    plane = plane_matrix(sum([layer_places(x) for x in range(SPAN)], []) + outer)
    ends = plane_matrix(layer_places(0) + layer_places(SPAN - 1) + outer)
    lines = plane_matrix(sum([line_places(y) for y in (1, 2, BOX - 1, BOX)], []) + outer)
    boxes = size_z // BOX
    line = np.zeros((size_z, boxes * SPAN))
    for box in range(boxes):
        for mode in range(SPAN):
            for offset in range(SPAN):
                cell = box * BOX + offset - 1
                if 0 <= cell < size_z:
                    line[cell, box * SPAN + mode] = basis[mode, offset]
    high, low = split(line)
    line_forward = np.concatenate([high, high, low], axis=0)
    high, low = split(line.T)
    line_inverse = np.concatenate([high, low], axis=1)
    edges = plane_matrix(sum([layer_places(x) for x in EDGE_LAYERS], []) + outer)
    return (
        three_products(plane),
        three_products(plane.T),
        line_forward,
        line_inverse,
        three_products(ends),
        three_products(lines),
        three_products(edges.T),
    )


def swap_pairs(mesh, axis, odd):
    sizes = [mesh.shape[name] for name in AXES]
    along = AXES.index(axis)
    pairs = []
    for i in range(sizes[0]):
        for j in range(sizes[1]):
            here = [i, j]
            there = [i, j]
            place = here[along]
            target = place ^ 1 if not odd else (place + 1 if place % 2 else place - 1)
            if 0 <= target < sizes[along]:
                there[along] = target
            elif along == 0:
                there[0] = sizes[0] - 1 - place
            else:
                there[0] = i ^ 1
            pairs.append((here[0] * sizes[1] + here[1], there[0] * sizes[1] + there[1]))
    return pairs


def swap(mesh, axis, even_part, odd_part):
    if axis == "gx":
        first = lax.ppermute(even_part, AXES, swap_pairs(mesh, axis, False))
        second = lax.ppermute(odd_part, AXES, swap_pairs(mesh, axis, True))
    else:
        second = lax.ppermute(odd_part, AXES, swap_pairs(mesh, axis, True))
        first = lax.ppermute(even_part, AXES, swap_pairs(mesh, axis, False))
    return first, second


EVEN_X, EVEN_Y, LOW_X, HIGH_X, LOW_Y, HIGH_Y = range(6)


def standing(mesh):
    here_x, here_y = lax.axis_index("gx"), lax.axis_index("gy")
    facts = (
        lax.rem(here_x, 2) == 0,
        lax.rem(here_y, 2) == 0,
        here_x > 0,
        here_x < mesh.shape["gx"] - 1,
        here_y > 0,
        here_y < mesh.shape["gy"] - 1,
    )
    return [fact.astype(jnp.int32) for fact in facts]


def chosen(flags, which, yes, no):
    return jnp.where(flags[which] > 0, yes, no)


def keep(flags, which, value):
    return jnp.where(flags[which] > 0, value, jnp.zeros_like(value))


def halves(value):
    high = value.astype(BF16)
    low = (value - high.astype(F32)).astype(BF16)
    return high, low


def dot(left, right):
    return jnp.dot(left, right, preferred_element_type=F32)


def store_split(stack_ref, lanes, value):
    rows = value.shape[0]
    high, low = halves(value)
    stack_ref[0:rows, lanes] = high
    stack_ref[rows : 2 * rows, lanes] = low
    stack_ref[2 * rows : 3 * rows, lanes] = high


def stacked(before_ref, lanes, parts):
    store_split(before_ref, lanes, jnp.concatenate(parts, axis=0))


def forward_own(field_ref, forward_ref, before_ref, spectral_ref):
    boxes = (field_ref.shape[1] - 2) // BOX
    size_y, size_z = field_ref.shape[2:]
    blank = jnp.zeros((48, size_z), F32)
    for field in range(2):
        for box in range(boxes):
            main = field_ref[field, box * BOX : box * BOX + SPAN].reshape(SPAN * size_y, size_z)
            stacked(before_ref.at[field], slice(box * size_z, (box + 1) * size_z), [main, blank])
    for field in range(2):
        spectral_ref[field] = dot(forward_ref[...], before_ref[field])


def solve(spectral, inverse_ref, consts, after_ref):
    line_forward_ref, line_back_ref = consts
    line_rows = line_forward_ref.shape[0] // 3
    size_z = line_rows
    boxes = spectral[0].shape[1] // size_z
    lanes = [slice(box * size_z, (box + 1) * size_z) for box in range(boxes)]
    for field in range(2):
        for box in range(boxes):
            high, low = halves(spectral[field][:, lanes[box]])
            both = jnp.concatenate([high, low], axis=1)
            modes = dot(both, line_forward_ref[0 : 2 * line_rows]) + dot(high, line_forward_ref[2 * line_rows :])
            modes = modes * inverse_ref[field * boxes + box]
            high, low = halves(modes)
            cells = dot(high, line_back_ref[...])
            cells = cells[:, :size_z] + (cells[:, size_z:] + dot(low, line_back_ref[:, :size_z]))
            store_split(after_ref.at[field], lanes[box], cells)

def solved_kernel(mesh, after_ref, back_ref, out_ref, out_rows_ref, *lines_refs):
    boxes = (out_ref.shape[1] - 2) // BOX
    size_y, size_z = out_ref.shape[2:]
    inner = SPAN * size_y
    lanes = [slice(box * size_z, (box + 1) * size_z) for box in range(boxes)]
    for field in range(2):
        result = dot(back_ref[...], after_ref[field])
        for box in range(boxes):
            start = box * BOX
            main = result[:inner, lanes[box]].reshape(SPAN, size_y, size_z)
            if box == 0:
                out_ref[field, 0:SPAN] = main
            else:
                out_ref[field, start : start + 2] = out_ref[field, start : start + 2] + main[0:2]
                out_ref[field, start + 2 : start + SPAN] = main[2:]
            for side in range(2):
                strip = result[inner + 24 * side : inner + 24 * side + 24, lanes[box]]
                if box == 0:
                    out_rows_ref[field, side, 0:24] = strip
                else:
                    out_rows_ref[field, side, start : start + 8] = (
                        out_rows_ref[field, side, start : start + 8] + strip[0:8]
                    )
                    out_rows_ref[field, side, start + 8 : start + 24] = strip[8:]
    if lines_refs:
        pack_lines(standing(mesh), out_ref, out_rows_ref, *lines_refs)


def pack_x(flags, after_ref, edges_ref, even_ref, odd_ref):
    depth, size_z = even_ref.shape[1], even_ref.shape[3]
    size_y = BOX
    after = len(EDGE_LAYERS) * size_y
    for field in range(2):
        result = dot(edges_ref[...], after_ref[field])
        low, high = result[:, :size_z], result[:, result.shape[1] - size_z :]
        for layer in range(depth):
            far = len(EDGE_LAYERS) - depth + layer
            pairs = [(slice(0, size_y), low[layer * size_y : (layer + 1) * size_y], high[far * size_y : (far + 1) * size_y])]
            for side in range(2):
                near_row = after + 24 * side + ROW0 - 1 + layer
                far_row = after + 24 * side + ROW0 - 1 + SPAN - depth + layer
                pairs.append(
                    (slice(size_y + side, size_y + side + 1), low[near_row : near_row + 1], high[far_row : far_row + 1])
                )
            for place, to_low, to_high in pairs:
                even_ref[field, layer, place] = chosen(flags, EVEN_X, to_high, to_low)
                odd_ref[field, layer, place] = chosen(flags, EVEN_X, to_low, to_high)
            blank = jnp.zeros((even_ref.shape[2] - size_y - 2, size_z), F32)
            even_ref[field, layer, size_y + 2 :] = blank
            odd_ref[field, layer, size_y + 2 :] = blank


def line_pairs(whole_ref, whole_rows_ref, field, layers, rows, depth):
    size_y = whole_ref.shape[2]
    if depth == 3:
        return (
            (whole_rows_ref[field, 0, rows], whole_ref[field, layers, size_y - 2]),
            (whole_ref[field, layers, 0], whole_ref[field, layers, size_y - 1]),
            (whole_ref[field, layers, 1], whole_rows_ref[field, 1, rows]),
        )
    return (
        (whole_ref[field, layers, 0], whole_ref[field, layers, size_y - 1]),
        (whole_rows_ref[field, 0, rows], whole_rows_ref[field, 1, rows]),
    )


def pack_lines(flags, part_ref, part_rows_ref, even_ref, odd_ref):
    size_x = part_ref.shape[1] - 2
    depth = even_ref.shape[1] // size_x
    for field in range(2):
        pairs = line_pairs(
            part_ref, part_rows_ref, field, slice(1, size_x + 1), slice(ROW0, ROW0 + size_x), depth
        )
        for line, (to_low, to_high) in enumerate(pairs):
            place = slice(line * size_x, (line + 1) * size_x)
            even_ref[field, place] = chosen(flags, EVEN_Y, to_high, to_low)
            odd_ref[field, place] = chosen(flags, EVEN_Y, to_low, to_high)


def unpack_lines(flags, lines_refs, ends_refs, out_ref, field):
    size_x = out_ref.shape[2] - 8
    depth = lines_refs[0].shape[1] // size_x
    blank = jnp.zeros((8, out_ref.shape[3]), F32)
    for side, flag, (even, odd) in ((0, LOW_Y, (1, 0)), (1, HIGH_Y, (0, 1))):
        lines = keep(flags, flag, chosen(flags, EVEN_Y, lines_refs[even][field], lines_refs[odd][field]))
        ends = keep(flags, flag, chosen(flags, EVEN_Y, ends_refs[even][field], ends_refs[odd][field]))
        for line in range(depth):
            out_ref[side, line, 0:8] = blank
            out_ref[side, line, size_x : size_x + 8] = blank
            out_ref[side, line, ROW0 : ROW0 + size_x] = lines[line * size_x : (line + 1) * size_x]
            if depth == 3:
                out_ref[side, line, ROW0 - 2 : ROW0 + 1] = ends[8 * line : 8 * line + 3]
                out_ref[side, line, ROW0 + size_x - 1 : ROW0 + size_x + 2] = ends[8 * line + 3 : 8 * line + 6]
            elif line == 1:
                out_ref[side, line, ROW0 - 1 : ROW0] = ends[0:1]
                out_ref[side, line, ROW0 + size_x : ROW0 + size_x + 1] = ends[1:2]


def divisor_kernel(conductance_ref, capacity_ref, zones_ref, inverse_ref):
    size_x, size_y, size_z = zones_ref.shape
    boxes = size_x // BOX
    lines = []
    for table_ref, which in ((capacity_ref, 0), (capacity_ref, 1), (conductance_ref, 0), (conductance_ref, 1)):
        for box in range(boxes):
            total = jnp.zeros((size_y, size_z), F32)
            for x in range(box * BOX, (box + 1) * BOX):
                zone = zones_ref[x]
                value = jnp.full((size_y, size_z), table_ref[which, 0], F32)
                for label in range(1, table_ref.shape[1]):
                    value = jnp.where(zone == label, table_ref[which, label], value)
                total = total + value
            lines.append(jnp.sum(total, axis=0, keepdims=True))
    sums = jnp.concatenate(lines, axis=0)
    modes, lanes = inverse_ref.shape[1:]
    cell = lax.broadcasted_iota(jnp.int32, (size_z, lanes), 0)
    lane = lax.broadcasted_iota(jnp.int32, (size_z, lanes), 1)
    spread = jnp.zeros((size_z, lanes), F32)
    for box in range(size_z // BOX):
        here = (cell >= box * BOX) & (cell < (box + 1) * BOX) & (lane >= box * SPAN) & (lane < (box + 1) * SPAN)
        spread = jnp.where(here, 1.0 / BOX**3, spread)
    means = jnp.dot(sums, spread, preferred_element_type=F32, precision=lax.Precision.HIGHEST)
    eigen = [float(value) for value in eigenvalues()]
    row = lax.broadcasted_iota(jnp.int32, (modes, 128), 0)
    first = jnp.zeros(row.shape, jnp.int32)
    for mode in range(1, SPAN):
        first = first + (row >= mode * SPAN).astype(jnp.int32)
    second = row - SPAN * first
    pair = jnp.zeros(row.shape, F32)
    for mode in range(SPAN):
        pair = pair + jnp.where(first == mode, eigen[mode], 0.0) + jnp.where(second == mode, eigen[mode], 0.0)
    lane = lax.broadcasted_iota(jnp.int32, (8, lanes), 1)
    for box in range(1, size_z // BOX):
        lane = lane - SPAN * (lax.broadcasted_iota(jnp.int32, (8, lanes), 1) >= box * SPAN).astype(jnp.int32)
    third = jnp.zeros(lane.shape, F32)
    for mode in range(SPAN):
        third = jnp.where(lane == mode, eigen[mode], third)
    summed = jnp.concatenate([pair, pair[:, : lanes - 128]], axis=1) + third[0:1]
    half = 2 * boxes
    for combo in range(half):
        cbar = means[combo : combo + 1]
        kbar = means[half + combo : half + combo + 1]
        inverse_ref[combo] = 1.0 / (cbar + kbar * summed)


def edge_layers_kernel(mesh, load_hbm, zones_hbm, even_ref, odd_ref, load_ref, zones_ref, sems):
    last = zones_hbm.shape[0] - 1
    copies = [
        pltpu.make_async_copy(load_hbm.at[:, 0], load_ref.at[0], sems.at[0]),
        pltpu.make_async_copy(load_hbm.at[:, last], load_ref.at[1], sems.at[1]),
        pltpu.make_async_copy(zones_hbm.at[pl.ds(0, 2)], zones_ref.at[0], sems.at[2]),
        pltpu.make_async_copy(zones_hbm.at[pl.ds(last - 1, 2)], zones_ref.at[1], sems.at[3]),
    ]
    for copy in copies:
        copy.start()
    flags = standing(mesh)
    for copy in copies:
        copy.wait()
    for channel in range(4):
        if channel < 2:
            low, high = load_ref[0, channel], load_ref[1, channel]
        else:
            low, high = zones_ref[0, channel - 2].astype(F32), zones_ref[1, channel - 2].astype(F32)
        even_ref[channel] = chosen(flags, EVEN_X, high, low)
        odd_ref[channel] = chosen(flags, EVEN_X, low, high)


def fetched_kernel(load_ref, zones_ref, token_ref):
    token_ref[...] = load_ref[0, 0, 0:8] + zones_ref[0, 0:8].astype(F32)


def edge_lines_kernel(mesh, load_ref, zones_ref, token_ref, first_ref, second_ref, even_ref, odd_ref):
    flags = standing(mesh)
    size_x, size_y = zones_ref.shape[:2]
    from_low = chosen(flags, EVEN_X, second_ref[...], first_ref[...])
    from_high = chosen(flags, EVEN_X, first_ref[...], second_ref[...])

    def put(row, to_low, to_high):
        place = slice(row, row + to_low.shape[0])
        even_ref[place] = chosen(flags, EVEN_Y, to_high, to_low)
        odd_ref[place] = chosen(flags, EVEN_Y, to_low, to_high)

    def put_end(row, layer, near, far):
        put(4 * size_x + row, layer[near : near + 1], layer[far : far + 1])

    blank = jnp.zeros((8, even_ref.shape[1]), F32)
    put(4 * size_x + 8, blank, blank)
    for field in range(2):
        put(field * size_x, load_ref[field, :, 0], load_ref[field, :, size_y - 1])
        put_end(2 * field, keep(flags, LOW_X, from_low[field]), 0, size_y - 1)
        put_end(2 * field + 1, keep(flags, HIGH_X, from_high[field]), 0, size_y - 1)
    for line in range(2):
        far = size_y - 2 + line
        put((2 + line) * size_x, zones_ref[:, line].astype(F32), zones_ref[:, far].astype(F32))
        for depth in range(2):
            put_end(4 + 4 * line + depth, from_low[2 + depth], line, far)
            put_end(6 + 4 * line + depth, from_high[2 + depth], line, far)


def tables(conductance_ref, capacity_ref, coupling_ref, size_z):
    labels = range(coupling_ref.shape[0])
    halves_of = [[0.5 * conductance_ref[field, label] for label in labels] for field in range(2)]
    masses = [[capacity_ref[field, label] for label in labels] for field in range(2)]
    products = [jnp.full((8, size_z), capacity_ref[0, label] * capacity_ref[1, label], F32) for label in labels]
    masses.append([coupling_ref[label] * jnp.sqrt(products[label])[0:1] for label in labels])
    return halves_of, masses


def looked_up(entries, zone):
    value = jnp.broadcast_to(entries[0], zone.shape)
    for label in range(1, len(entries)):
        value = jnp.where(zone == float(label), entries[label], value)
    return value


def coefficient_kernel(
    mesh, conductance_ref, capacity_ref, coupling_ref, zones_ref, first_x, second_x,
    half_ref, mass_ref, face_ref, table_ref,
):
    flags = standing(mesh)
    size_x, size_y, size_z = zones_ref.shape
    halves_of, masses = tables(conductance_ref, capacity_ref, coupling_ref, size_z)
    for which, entries in enumerate(halves_of + masses):
        for label, entry in enumerate(entries):
            table_ref[which, label : label + 1] = jnp.broadcast_to(entry, (1, size_z))
    low_x = chosen(flags, EVEN_X, second_x[2:4], first_x[2:4])
    high_x = chosen(flags, EVEN_X, first_x[2:4], second_x[2:4])
    inside = slice(8, 8 + size_y)
    for x in range(-2, size_x + 2):
        if x < 0:
            zone = low_x[x + 2]
        elif x >= size_x:
            zone = high_x[x - size_x]
        else:
            zone = zones_ref[x].astype(F32)
        for field in range(2):
            half_ref[field, x + 2, inside] = looked_up(halves_of[field], zone)
        if -1 <= x <= size_x:
            for which in range(3):
                mass_ref[which, x + 1] = looked_up(masses[which], zone)
    for field in range(2):
        for outer in (0, 1):
            half_ref[field, outer, inside] = chosen(
                flags, LOW_X, half_ref[field, outer, inside], half_ref[field, 2, inside]
            )
            place = size_x + 2 + outer
            half_ref[field, place, inside] = chosen(
                flags, HIGH_X, half_ref[field, place, inside], half_ref[field, size_x + 1, inside]
            )
    for field in range(2):
        for x in range(0, size_x + 2, 2):
            faces = faces_z(half_ref[field, x + 1 : x + 3, inside])
            for way in range(2):
                face_ref[field, way, x : x + 2] = faces[way]


def coefficient_lines_kernel(
    mesh, old_half_ref, mass_ref, face_ref, table_ref, first_y, second_y, after_ref,
    half_ref, half_rows_ref, mass_rows_ref, face_rows_ref, line_ref,
):
    flags = standing(mesh)
    size_x, size_y, size_z = mass_ref.shape[1] - 2, mass_ref.shape[2], mass_ref.shape[3]
    rows_of = [[table_ref[which, label : label + 1] for label in range(table_ref.shape[1])] for which in range(5)]
    halves_of, masses = rows_of[:2], rows_of[2:]
    for side, (even, odd) in enumerate(((second_y, first_y), (first_y, second_y))):
        came = chosen(flags, EVEN_Y, even[2 * size_x :], odd[2 * size_x :])
        lines, ends = (came[:size_x], came[size_x : 2 * size_x]), came[2 * size_x :]
        for line in range(2):
            place = 2 * side + line
            line_ref[place, 0:8] = jnp.zeros((8, size_z), F32)
            line_ref[place, size_x : size_x + 8] = jnp.zeros((8, size_z), F32)
            line_ref[place, ROW0 - 2 : ROW0] = ends[4 + 4 * line : 6 + 4 * line]
            line_ref[place, ROW0 : ROW0 + size_x] = lines[line]
            line_ref[place, ROW0 + size_x : ROW0 + size_x + 2] = ends[6 + 4 * line : 8 + 4 * line]
    count = half_rows_ref.shape[2]
    position = lax.broadcasted_iota(jnp.int32, (count, size_z), 0)
    for line, flag in enumerate((LOW_Y, LOW_Y, HIGH_Y, HIGH_Y)):
        zone = line_ref[line]
        for field in range(2):
            value = looked_up(halves_of[field], zone)
            below = value[ROW0 : ROW0 + 1]
            above = value[ROW0 + size_x - 1 : ROW0 + size_x]
            value = jnp.where((position < ROW0) & (flags[LOW_X] == 0), below, value)
            value = jnp.where((position >= ROW0 + size_x) & (flags[HIGH_X] == 0), above, value)
            near = old_half_ref[field, :, 8 if flag == LOW_Y else 8 + size_y - 1]
            half_rows_ref[field, line] = value
            half_rows_ref[field, line, ROW0 - 2 : ROW0 + size_x + 2] = chosen(
                flags, flag, half_rows_ref[field, line, ROW0 - 2 : ROW0 + size_x + 2], near
            )
            if line in (1, 2):
                row = 7 if line == 1 else 8 + size_y
                half_ref[field, :, row] = half_rows_ref[field, line, ROW0 - 2 : ROW0 + size_x + 2]
        if line in (1, 2):
            for which in range(3):
                mass_rows_ref[which, line - 1] = looked_up(masses[which], zone)
    for field in range(2):
        for side in range(2):
            faces = faces_z(half_rows_ref[field, side + 1])
            for way in range(2):
                face_rows_ref[field, way, side] = faces[way]
        for line, row in ((4, 0), (5, size_y - 1), (6, 1), (7, size_y - 2)):
            half_rows_ref[field, line] = jnp.zeros((count, size_z), F32)
            half_rows_ref[field, line, ROW0 - 2 : ROW0 + size_x + 2] = old_half_ref[field, :, 8 + row]
    for line, row in ((2, 0), (3, size_y - 1)):
        spread = slice(ROW0 - 1, ROW0 + size_x + 1)
        for which in range(3):
            mass_rows_ref[which, line] = jnp.zeros((count, size_z), F32)
            mass_rows_ref[which, line, spread] = mass_ref[which, :, row]
        for field in range(2):
            for way in range(2):
                face_rows_ref[field, way, line] = jnp.zeros((count, size_z), F32)
                face_rows_ref[field, way, line, spread] = face_ref[field, way, :, row]


def own_transform_kernel(load_ref, forward_ref, spectral_ref, field_ref, before_ref):
    size_x = load_ref.shape[1]
    for field in range(2):
        field_ref[field, 0] = jnp.zeros(load_ref.shape[2:], F32)
        field_ref[field, 1 : 1 + size_x] = load_ref[field]
        field_ref[field, 1 + size_x] = jnp.zeros(load_ref.shape[2:], F32)
    forward_own(field_ref, forward_ref, before_ref, spectral_ref)


def first_solve_kernel(
    mesh, spectral_ref, mass_ref, first_x, second_x, first_y, second_y, inverse_ref, c2, c3, ends_ref, edges_ref,
    after_ref, even_ref, odd_ref, rows_ref, before_ref,
):
    flags = standing(mesh)
    size_x, size_y, size_z = mass_ref.shape[1] - 2, mass_ref.shape[2], mass_ref.shape[3]
    boxes = size_x // BOX
    blank = jnp.zeros((size_y, size_z), F32)
    spectral = []
    for field in range(2):
        low = keep(flags, LOW_X, chosen(flags, EVEN_X, second_x[field], first_x[field]))
        high = keep(flags, HIGH_X, chosen(flags, EVEN_X, first_x[field], second_x[field]))
        for side, flag, even, odd in ((0, LOW_Y, second_y, first_y), (1, HIGH_Y, first_y, second_y)):
            place, after = slice(field * size_x, (field + 1) * size_x), slice(4 * size_x, 4 * size_x + 8)
            line = keep(flags, flag, chosen(flags, EVEN_Y, even[place], odd[place]))
            ends = keep(flags, flag, chosen(flags, EVEN_Y, even[after], odd[after]))
            rows_ref[field, side, 0:8] = blank[0:8]
            rows_ref[field, side, size_x : size_x + 8] = blank[0:8]
            rows_ref[field, side, ROW0 - 1 : ROW0] = ends[2 * field : 2 * field + 1]
            rows_ref[field, side, ROW0 : ROW0 + size_x] = line
            rows_ref[field, side, ROW0 + size_x : ROW0 + size_x + 1] = ends[2 * field + 1 : 2 * field + 2]
        for box in range(boxes):
            parts = [low if box == 0 else blank, high if box == boxes - 1 else blank]
            parts += [rows_ref[field, side, box * BOX : box * BOX + 24] for side in range(2)]
            stacked(before_ref.at[field], slice(box * size_z, (box + 1) * size_z), parts)
    for field in range(2):
        spectral.append(spectral_ref[field] + dot(ends_ref[...], before_ref[field]))
    solve(spectral, inverse_ref, (c2, c3), after_ref)
    pack_x(flags, after_ref, edges_ref, even_ref, odd_ref)


def merge_x_kernel(mesh, part_ref, part_rows_ref, first_ref, second_ref, whole_ref, whole_rows_ref, even_ref, odd_ref):
    flags = standing(mesh)
    size_x = part_ref.shape[1] - 2
    size_y, size_z = part_ref.shape[2:]
    depth = first_ref.shape[1]
    end = ROW0 + size_x
    for field in range(2):
        low = keep(flags, LOW_X, chosen(flags, EVEN_X, second_ref[field], first_ref[field]))
        high = keep(flags, HIGH_X, chosen(flags, EVEN_X, first_ref[field], second_ref[field]))
        whole_ref[field, 1] = keep(flags, LOW_X, part_ref[field, 0]) + low[depth - 2, :size_y]
        whole_ref[field, 2] = part_ref[field, 1] + low[depth - 1, :size_y]
        whole_ref[field, 3 : size_x + 1] = part_ref[field, 2:size_x]
        whole_ref[field, size_x + 1] = part_ref[field, size_x] + high[0, :size_y]
        whole_ref[field, size_x + 2] = keep(flags, HIGH_X, part_ref[field, size_x + 1]) + high[1, :size_y]
        whole_ref[field, 0] = low[0, :size_y] if depth == 3 else jnp.zeros((size_y, size_z), F32)
        whole_ref[field, size_x + 3] = high[2, :size_y] if depth == 3 else jnp.zeros((size_y, size_z), F32)
        for side in range(2):
            row = slice(size_y + side, size_y + side + 1)
            edge = ROW0 - 1
            whole_rows_ref[field, side] = part_rows_ref[field, side]
            whole_rows_ref[field, side, edge : edge + 1] = (
                keep(flags, LOW_X, part_rows_ref[field, side, edge : edge + 1]) + low[depth - 2, row]
            )
            whole_rows_ref[field, side, edge + 1 : edge + 2] = (
                part_rows_ref[field, side, edge + 1 : edge + 2] + low[depth - 1, row]
            )
            whole_rows_ref[field, side, end - 1 : end] = part_rows_ref[field, side, end - 1 : end] + high[0, row]
            whole_rows_ref[field, side, end : end + 1] = (
                keep(flags, HIGH_X, part_rows_ref[field, side, end : end + 1]) + high[1, row]
            )
            if depth == 3:
                whole_rows_ref[field, side, edge - 1 : edge] = low[0, row]
                whole_rows_ref[field, side, end + 1 : end + 2] = high[2, row]

        base = 2 * size_x if depth == 2 else 0
        for ref in (even_ref, odd_ref):
            ref[field, base:] = jnp.zeros((ref.shape[1] - base, size_z), F32)
        if base:
            own, rows = slice(2, size_x + 2), slice(ROW0, ROW0 + size_x)
            pairs = line_pairs(whole_ref, whole_rows_ref, field, own, rows, depth)
            for line, (to_low, to_high) in enumerate(pairs):
                place = slice(line * size_x, (line + 1) * size_x)
                even_ref[field, place] = chosen(flags, EVEN_Y, to_high, to_low)
                odd_ref[field, place] = chosen(flags, EVEN_Y, to_low, to_high)
            for row, x in ((base, -1), (base + 1, size_x)):
                pairs = line_pairs(
                    whole_ref, whole_rows_ref, field, slice(x + 2, x + 3), slice(x + ROW0, x + ROW0 + 1), depth
                )
                even_ref[field, row : row + 1] = chosen(flags, EVEN_Y, pairs[1][1], pairs[1][0])
                odd_ref[field, row : row + 1] = chosen(flags, EVEN_Y, pairs[1][0], pairs[1][1])
            continue
        for start, x in ((base, -2), (base + 3, size_x - 1)):
            layers, rows = slice(x + 2, x + 5), slice(x + ROW0, x + ROW0 + 3)
            pairs = line_pairs(whole_ref, whole_rows_ref, field, layers, rows, depth)
            for line, (to_low, to_high) in enumerate(pairs):
                place = slice(8 * line + start, 8 * line + start + 3)
                even_ref[field, place] = chosen(flags, EVEN_Y, to_high, to_low)
                odd_ref[field, place] = chosen(flags, EVEN_Y, to_low, to_high)


def faces_z(half):
    size_z, axis = half.shape[-1], half.ndim - 1
    lane = lax.broadcasted_iota(jnp.int32, half.shape, axis)
    upper = half + jnp.where(lane == size_z - 1, half, pltpu.roll(half, size_z - 1, axis))
    lower = half + jnp.where(lane == 0, half, pltpu.roll(half, 1, axis))
    return upper, lower


def along_z(value, upper, lower):
    size_z, axis = value.shape[-1], value.ndim - 1
    lane = lax.broadcasted_iota(jnp.int32, value.shape, axis)
    above = jnp.where(lane == size_z - 1, 0.0, pltpu.roll(value, size_z - 1, axis))
    below = jnp.where(lane == 0, 0.0, pltpu.roll(value, 1, axis))
    return upper * (value - above) + lower * (value - below)


def operate(field_ref, half_ref, mass_ref, face_ref, x, count):
    size_y = mass_ref.shape[2]
    inside = slice(8, 8 + size_y)
    masses = slice(x + 1, x + 1 + count)
    here = slice(x + 2, x + 2 + count)
    values, images = [], []
    for field in range(2):
        value = field_ref[field, here, inside]
        half = half_ref[field, here, inside]
        flux = along_z(value, face_ref[field, 0, masses], face_ref[field, 1, masses])
        for start in (x + 1, x + 3):
            place = slice(start, start + count)
            flux = flux + (half + half_ref[field, place, inside]) * (value - field_ref[field, place, inside])
        for shift in (-1, 1):
            moved = slice(8 + shift, 8 + shift + size_y)
            flux = flux + (half + half_ref[field, here, moved]) * (value - field_ref[field, here, moved])
        values.append(value)
        images.append(flux)
    first = mass_ref[0, masses] * values[0] + mass_ref[2, masses] * values[1] + images[0]
    second = mass_ref[2, masses] * values[0] + mass_ref[1, masses] * values[1] + images[1]
    return values, (first, second)


def fill(flags, whole_ref, whole_rows_ref, value_ref):
    size_x, size_y = whole_ref.shape[1] - 4, whole_ref.shape[2]
    spread = slice(ROW0 - 2, ROW0 + size_x + 2)
    for field in range(2):
        value_ref[field, :, 8 : 8 + size_y] = whole_ref[field]
        value_ref[field, :, 7] = keep(flags, LOW_Y, whole_rows_ref[field, 0, spread])
        value_ref[field, :, 8 + size_y] = keep(flags, HIGH_Y, whole_rows_ref[field, 1, spread])


def line_image(values, outers, inners, half_lines, places, mass_lines, face_lines, place):
    center, outer, inner = places
    images = []
    for field in range(2):
        value, half = values[field], half_lines[field, center]
        count = value.shape[0]
        flux = along_z(value, face_lines[field, 0, place], face_lines[field, 1, place])
        for turn in (1, count - 1):
            flux = flux + (half + pltpu.roll(half, turn, 0)) * (value - pltpu.roll(value, turn, 0))
        flux = flux + (half + half_lines[field, outer]) * (value - outers[field])
        flux = flux + (half + half_lines[field, inner]) * (value - inners[field])
        images.append(flux)
    first = mass_lines[0, place] * values[0] + mass_lines[2, place] * values[1] + images[0]
    second = mass_lines[2, place] * values[0] + mass_lines[1, place] * values[1] + images[1]
    return first, second


SIDES = (((4, 1, 6, 0), (2, 0)), ((5, 2, 7, 3), (3, 1)))


def line_changes(delta, outer, half_lines, mass_lines, face_lines, side):
    (edge, out, inner, _), (place, _) = SIDES[side]
    nothing = [jnp.zeros_like(line) for line in delta]
    at_edge = line_image(delta, outer, nothing, half_lines, (edge, out, inner), mass_lines, face_lines, place)
    at_next = [-(half_lines[field, edge] + half_lines[field, inner]) * delta[field] for field in range(2)]
    return at_edge, at_next


def own_image_kernel(
    mesh, whole_ref, whole_rows_ref, half_ref, mass_ref, face_ref, forward_ref, image_ref, spectral_ref,
    value_ref, before_ref,
):
    flags = standing(mesh)
    size_x = whole_ref.shape[1] - 4
    fill(flags, whole_ref, whole_rows_ref, value_ref)
    for x, flag in ((-1, LOW_X), (size_x, HIGH_X)):
        _, images = operate(value_ref, half_ref, mass_ref, face_ref, x, 1)
        for field in range(2):
            image_ref[field, x + 1 : x + 2] = keep(flags, flag, images[field])
    for x in range(0, size_x, CHUNK):
        _, images = operate(value_ref, half_ref, mass_ref, face_ref, x, CHUNK)
        for field in range(2):
            image_ref[field, x + 1 : x + 1 + CHUNK] = images[field]
    forward_own(image_ref, forward_ref, before_ref, spectral_ref)


def second_solve_kernel(
    mesh, whole_ref, whole_rows_ref, first_lines, second_lines, first_ends, second_ends,
    half_lines, mass_lines, face_lines, spectral_ref, inverse_ref, c2, c3, lines_ref, edges_ref,
    deltas_ref, changes_ref, after_ref, even_ref, odd_ref, came_ref, near, before_ref,
):
    flags = standing(mesh)
    size_x, size_y, size_z = whole_ref.shape[1] - 4, whole_ref.shape[2], whole_ref.shape[3]
    boxes = size_x // BOX
    count = near.shape[2]
    position = lax.broadcasted_iota(jnp.int32, (count, size_z), 0)
    begin = jnp.where(flags[LOW_X] > 0, ROW0 - 1, ROW0)
    end = jnp.where(flags[HIGH_X] > 0, ROW0 + size_x + 1, ROW0 + size_x)
    valid = (position >= begin) & (position < end)
    for field in range(2):
        unpack_lines(flags, (first_lines, second_lines), (first_ends, second_ends), came_ref.at[field], field)
        for side, row in ((0, 0), (1, size_y - 1)):
            near[field, side] = jnp.zeros((count, size_z), F32)
            near[field, side, ROW0 - 2 : ROW0 + size_x + 2] = whole_ref[field, :, row]
    for side, flag, order in ((0, LOW_Y, (2, 1, 0)), (1, HIGH_Y, (0, 1, 2))):
        delta, outer, far = [[came_ref[field, side, line] for field in range(2)] for line in order]
        at_edge, at_next = line_changes(delta, outer, half_lines, mass_lines, face_lines, side)
        (edge, out, _, beyond), (_, place) = SIDES[side]
        at_outer = line_image(
            [keep(flags, flag, whole_rows_ref[field, side]) + outer[field] for field in range(2)],
            far,
            [near[field, side] + delta[field] for field in range(2)],
            half_lines,
            (out, beyond, edge),
            mass_lines,
            face_lines,
            place,
        )
        for field in range(2):
            deltas_ref[field, side] = delta[field]
            changes_ref[field, 3 * side] = jnp.where(valid, at_edge[field], 0.0)
            changes_ref[field, 1 + side] = jnp.where(valid, at_next[field], 0.0)
            changes_ref[field, 4 + side] = keep(flags, flag, jnp.where(valid, at_outer[field], 0.0))
    spectral = []
    for field in range(2):
        for box in range(boxes):
            parts = [changes_ref[field, line, box * BOX : box * BOX + 24] for line in range(6)]
            stacked(before_ref.at[field], slice(box * size_z, (box + 1) * size_z), parts)
    for field in range(2):
        spectral.append(spectral_ref[field] + dot(lines_ref[...], before_ref[field]))
    solve(spectral, inverse_ref, (c2, c3), after_ref)
    pack_x(flags, after_ref, edges_ref, even_ref, odd_ref)


def first_sums_kernel(load_ref, whole_ref, image_ref, deltas_ref, changes_ref, precond_ref, out_ref, sums_ref):
    size_x, size_y, size_z = load_ref.shape[1:]
    rows = slice(ROW0, ROW0 + size_x)
    total_a = total_b = jnp.zeros((size_y, size_z), F32)
    for field in range(2):
        precond_ref[field] = whole_ref[field, 2 : size_x + 2]
        out_ref[field] = image_ref[field, 1 : size_x + 1]
        for side, row in ((0, 0), (1, size_y - 1)):
            precond_ref[field, :, row] = precond_ref[field, :, row] + deltas_ref[field, side, rows]
        for line, row in enumerate((0, 1, size_y - 2, size_y - 1)):
            out_ref[field, :, row] = out_ref[field, :, row] + changes_ref[field, line, rows]
        for x in range(size_x):
            total_a = total_a + load_ref[field, x] * precond_ref[field, x]
            total_b = total_b + out_ref[field, x] * precond_ref[field, x]
    sums_ref[0:1] = jnp.sum(total_a, axis=0, keepdims=True)
    sums_ref[1:2] = jnp.sum(total_b, axis=0, keepdims=True)
    sums_ref[2:8] = jnp.zeros((6, size_z), F32)


def own_second_image_kernel(
    mesh, whole_ref, whole_rows_ref, half_ref, mass_ref, face_ref, old_image_ref, image_ref, sums_ref, value_ref
):
    flags = standing(mesh)
    size_x, size_y, size_z = old_image_ref.shape[1:]
    fill(flags, whole_ref, whole_rows_ref, value_ref)
    total_c = total_d = jnp.zeros((CHUNK, size_y, size_z), F32)
    for x in range(0, size_x, CHUNK):
        chunk = slice(x, x + CHUNK)
        values, images = operate(value_ref, half_ref, mass_ref, face_ref, x, CHUNK)
        for field in range(2):
            image_ref[field, chunk] = images[field]
            total_c = total_c + old_image_ref[field, chunk] * values[field]
            total_d = total_d + images[field] * values[field]
    sums_ref[0:1] = jnp.sum(jnp.sum(total_c, axis=0), axis=0, keepdims=True)
    sums_ref[1:2] = jnp.sum(jnp.sum(total_d, axis=0), axis=0, keepdims=True)
    sums_ref[2:8] = jnp.zeros((6, size_z), F32)


def second_image_kernel(
    mesh, whole_ref, image_ref, first_ref, second_ref,
    half_lines, mass_lines, face_lines, old_image_ref, old_sums_ref, own_sums_ref,
    deltas_ref, changes_ref, sums_ref, came_ref,
):
    flags = standing(mesh)
    size_x, size_y, size_z = old_image_ref.shape[1:]
    own = slice(2, size_x + 2)
    rows = slice(ROW0, ROW0 + size_x)
    total_c = total_d = jnp.zeros((size_x, size_z), F32)
    lines_refs = [ref.at[:, pl.ds(0, 2 * size_x)] for ref in (first_ref, second_ref)]
    ends_refs = [ref.at[:, pl.ds(2 * size_x, 8)] for ref in (first_ref, second_ref)]
    for field in range(2):
        unpack_lines(flags, lines_refs, ends_refs, came_ref.at[field], field)
    for side, row, beside in ((0, 0, 1), (1, size_y - 1, size_y - 2)):
        outer, delta = [[came_ref[field, side, line] for field in range(2)] for line in range(2)]
        at_edge, at_next = line_changes(delta, outer, half_lines, mass_lines, face_lines, side)
        for field in range(2):
            changed, edge, inner = delta[field][rows], at_edge[field][rows], at_next[field][rows]
            deltas_ref[field, side] = changed
            changes_ref[field, 3 * side] = edge
            changes_ref[field, 1 + side] = inner
            total_c = total_c + old_image_ref[field, :, row] * changed
            total_d = total_d + (image_ref[field, :, row] + edge) * changed
            total_d = total_d + whole_ref[field, own, row] * edge + whole_ref[field, own, beside] * inner
    totals = [
        jnp.sum(old_sums_ref[0:1], axis=1, keepdims=True),
        jnp.sum(old_sums_ref[1:2], axis=1, keepdims=True),
        jnp.sum(jnp.sum(total_c, axis=0, keepdims=True) + own_sums_ref[0:1], axis=1, keepdims=True),
        jnp.sum(jnp.sum(total_d, axis=0, keepdims=True) + own_sums_ref[1:2], axis=1, keepdims=True),
    ]
    lane = lax.broadcasted_iota(jnp.int32, sums_ref.shape, 1)
    spread = jnp.zeros(sums_ref.shape, F32)
    for place, total in enumerate(totals):
        spread = jnp.where(lane == place, total, spread)
    sums_ref[...] = spread


def finish_kernel(
    sums_ref, load_ref, z_ref, q_ref, w_ref, s_ref, deltas_ref, changes_ref,
    solution_hbm, residual_hbm, solution_ref, residual_ref, sems,
):
    line = jnp.sum(sums_ref[...], axis=0, keepdims=True)
    lane = lax.broadcasted_iota(jnp.int32, line.shape, 1)
    rz, zq, qw, ws = [jnp.sum(jnp.where(lane == place, line, 0.0), axis=1, keepdims=True) for place in range(4)]
    alpha = rz / zq
    rz_next = rz - alpha * (2.0 * zq) + alpha * alpha * qw
    grown = 1.0 + rz_next / rz
    curvature = grown * grown * zq - 2.0 * grown * alpha * qw + alpha * alpha * ws
    alpha_next = rz_next / curvature
    along = alpha + alpha_next * grown
    against = alpha_next * alpha
    copies = []
    step = load_ref.shape[1] // 2
    for field in range(2):
        for start in range(0, 2 * step, step):
            part = pl.ds(start, step)
            for x in range(start, start + step):
                solution_ref[field, x] = along * z_ref[field, x] - against * w_ref[field, x + 2]
                residual_ref[field, x] = load_ref[field, x] - along * q_ref[field, x] + against * s_ref[field, x]
            size_y = load_ref.shape[2]
            chunk = slice(start, start + step)
            for side, row in ((0, 0), (1, size_y - 1)):
                solution_ref[field, chunk, row] = (
                    solution_ref[field, chunk, row] - against * deltas_ref[field, side, chunk]
                )
            for line, row in enumerate((0, 1, size_y - 2, size_y - 1)):
                residual_ref[field, chunk, row] = (
                    residual_ref[field, chunk, row] + against * changes_ref[field, line, chunk]
                )
            for here, there in ((solution_ref, solution_hbm), (residual_ref, residual_hbm)):
                copies.append(
                    pltpu.make_async_copy(here.at[field, part], there.at[field, part], sems.at[len(copies)])
                )
                copies[-1].start()
    for copy in copies:
        copy.wait()


SMEM = pl.BlockSpec(memory_space=pltpu.SMEM)
VMEM = pl.BlockSpec(memory_space=pltpu.VMEM)
HBM = pl.BlockSpec(memory_space=pltpu.HBM)


def call(mesh, kernel, scalars, arrays, outs, scratch=(), flops=0, limit=24, in_hbm=False, outs_in_hbm=False, aliases=()):
    moved = sum(math.prod(a.shape) * a.dtype.itemsize for a in list(arrays) + list(outs))
    return pl.pallas_call(
        kernel if mesh is None else functools.partial(kernel, mesh),
        out_shape=tuple(outs),
        in_specs=[SMEM] * len(scalars) + [HBM if in_hbm else VMEM] * len(arrays),
        out_specs=tuple([HBM if outs_in_hbm else VMEM] * len(outs)),
        scratch_shapes=list(scratch),
        input_output_aliases=dict(aliases),
        compiler_params=pltpu.CompilerParams(vmem_limit_bytes=limit * 1024 * 1024),
        cost_estimate=pl.CostEstimate(flops=flops, bytes_accessed=moved, transcendentals=0),
    )(*scalars, *arrays)


def shards(mesh, load, zones, conductance, capacity, coupling):
    size_x, size_y, size_z = zones.shape
    assert size_x % BOX == 0 and size_y == BOX and size_z % BOX == 0
    boxes = size_x // BOX
    count = size_x + 8
    sds = lambda *shape: jax.ShapeDtypeStruct(shape, F32)
    forward, back, line_forward, line_back, ends_forward, lines_forward, edges_back = [
        jnp.asarray(c) for c in constants(size_z)
    ]
    consts = (line_forward, line_back)
    modes, lanes = forward.shape[0], size_z // BOX * SPAN
    assert size_z == 128
    packed = call(
        mesh,
        edge_layers_kernel,
        [],
        [load, zones],
        [sds(4, size_y, size_z)] * 2,
        [
            pltpu.VMEM((2, 2, size_y, size_z), F32),
            pltpu.VMEM((2, 2, size_y, size_z), zones.dtype),
            pltpu.SemaphoreType.DMA((4,)),
        ],
        in_hbm=True,
        limit=56,
    )
    (token,) = call(None, fetched_kernel, [], [load, zones], [sds(8, size_z)])
    x_halo = swap(mesh, "gx", *packed)
    (inverse,) = call(
        None,
        divisor_kernel,
        [conductance, capacity],
        [zones],
        [sds(2 * boxes, modes, lanes)],
        flops=40_000_000,
    )
    packed = call(mesh, edge_lines_kernel, [], [load, zones, token, *x_halo], [sds(4 * size_x + 16, size_z)] * 2)
    y_halo = swap(mesh, "gy", *packed)
    laws = [conductance, capacity, coupling]
    padded_shape = sds(2, size_x + 4, size_y + 16, size_z)
    half, mass, face, table = call(
        mesh,
        coefficient_kernel,
        laws,
        [zones, *x_halo],
        [padded_shape, sds(3, size_x + 2, size_y, size_z), sds(2, 2, size_x + 2, size_y, size_z)]
        + [sds(5, coupling.shape[0], size_z)],
        flops=20_000_000,
    )
    parts = [sds(2, size_x + 2, size_y, size_z), sds(2, 2, count, size_z)]
    packed_x = [[sds(2, depth, size_y + 8, size_z)] * 2 for depth in (3, 2)]
    wholes = [sds(2, size_x + 4, size_y, size_z), sds(2, 2, count, size_z)]
    packed_lines = [sds(2, 3 * size_x, size_z)] * 2
    packed_ends = [sds(2, 3 * 8, size_z)] * 2
    packed_y = [sds(2, 2 * size_x + 8, size_z)] * 2
    rows = SPAN * size_y + 48
    wide = boxes * size_z
    spectrum = sds(2, modes, wide)
    stack = lambda depth: pltpu.VMEM((2, depth, wide), BF16)
    halo = pltpu.VMEM((2, size_x + 2, size_y, size_z), F32)
    padded = pltpu.VMEM((2, size_x + 4, size_y + 16, size_z), F32)
    own = sds(2, size_x, size_y, size_z)

    (spectral,) = call(None, own_transform_kernel, [], [load, forward], [spectrum], [halo, stack(3 * rows)], 700_000_000)
    stacked_cells = jax.ShapeDtypeStruct((2, 3 * rows, wide), BF16)
    after, *packed = call(
        mesh,
        first_solve_kernel,
        [],
        [spectral, mass, *x_halo, *y_halo, inverse, *consts, ends_forward, edges_back],
        [stacked_cells] + packed_x[0],
        [pltpu.VMEM((2, 2, count, size_z), F32), stack(ends_forward.shape[1])],
        2_000_000_000,
    )
    received = swap(mesh, "gx", *packed)
    part, part_rows, *packed = call(mesh, solved_kernel, [], [after, back], parts + packed_lines, (), 700_000_000)
    lines = swap(mesh, "gy", *packed)
    whole, whole_rows, *packed = call(mesh, merge_x_kernel, [], [part, part_rows, *received], wholes + packed_ends)
    ends = swap(mesh, "gy", *packed)
    half, half_lines, mass_lines, face_lines = call(
        mesh,
        coefficient_lines_kernel,
        [],
        [half, mass, face, table, *y_halo, whole_rows],
        [padded_shape, sds(2, 8, count, size_z), sds(3, 4, count, size_z), sds(2, 2, 4, count, size_z)],
        [pltpu.VMEM((4, count, size_z), F32)],
        flops=2_000_000,
        aliases={0: 0},
    )
    own_image, spectral = call(
        mesh,
        own_image_kernel,
        [],
        [whole, whole_rows, half, mass, face, forward],
        [sds(2, size_x + 2, size_y, size_z), spectrum],
        [padded, stack(3 * rows)],
        700_000_000,
    )
    deltas, changes, after, *packed = call(
        mesh,
        second_solve_kernel,
        [],
        [whole, whole_rows, *lines, *ends, half_lines, mass_lines, face_lines, spectral, inverse, *consts]
        + [lines_forward, edges_back],
        [sds(2, 2, count, size_z), sds(2, 6, count, size_z), stacked_cells] + packed_x[1],
        [
            pltpu.VMEM((2, 2, 3, count, size_z), F32),
            pltpu.VMEM((2, 2, count, size_z), F32),
            stack(lines_forward.shape[1]),
        ],
        2_000_000_000,
    )
    received = swap(mesh, "gx", *packed)
    part, part_rows = call(mesh, solved_kernel, [], [after, back], parts, (), 700_000_000)
    precond, image, sums = call(
        None, first_sums_kernel, [], [load, whole, own_image, deltas, changes], [own, own, sds(8, size_z)], flops=1_000_000
    )
    whole, whole_rows, *packed = call(mesh, merge_x_kernel, [], [part, part_rows, *received], wholes + packed_y)
    received = swap(mesh, "gy", *packed)
    last_image, own_sums = call(
        mesh,
        own_second_image_kernel,
        [],
        [whole, whole_rows, half, mass, face, image],
        [own, sds(8, size_z)],
        [padded],
        10_000_000,
    )
    devices = mesh.shape["gx"] * mesh.shape["gy"]
    deltas, changes, sums = call(
        mesh,
        second_image_kernel,
        [],
        [whole, last_image, *received, half_lines, mass_lines, face_lines, image, sums, own_sums],
        [sds(2, 2, size_x, size_z), sds(2, 4, size_x, size_z), sds(devices, size_z)],
        [pltpu.VMEM((2, 2, 2, count, size_z), F32)],
        1_000_000,
    )
    sums = lax.all_to_all(sums, AXES, 0, 0, tiled=True)
    whole_block = pltpu.VMEM((2, size_x, size_y, size_z), F32)
    return call(
        None,
        finish_kernel,
        [],
        [sums, load, precond, image, whole, last_image, deltas, changes],
        [own, own],
        [whole_block, whole_block, pltpu.SemaphoreType.DMA((8,))],
        outs_in_hbm=True,
    )


def solution(mesh):
    in_specs = (P(None, "gx", "gy", None), P("gx", "gy", None), P(), P(), P())
    out_specs = (P(None, "gx", "gy", None), P(None, "gx", "gy", None))
    return jax.shard_map(
        functools.partial(shards, mesh), mesh=mesh, in_specs=in_specs, out_specs=out_specs, check_vma=False
    )
```

```python
import functools
import math

import jax
import jax.numpy as jnp
import ml_dtypes
import numpy as np
from jax import lax
from jax.experimental import pallas as pl
from jax.experimental.pallas import tpu as pltpu
from jax.sharding import PartitionSpec as P

BOX = 16
SPAN = BOX + 2
F32 = jnp.float32
BF16 = jnp.bfloat16
AXES = ("gx", "gy")
ROW0 = 4
EDGE_LAYERS = (0, 1, 2, SPAN - 3, SPAN - 2, SPAN - 1)
CHUNK = 4


def split(matrix):
    high = matrix.astype(ml_dtypes.bfloat16)
    low = (matrix - high.astype(np.float64)).astype(ml_dtypes.bfloat16)
    return high, low


def round_up(value, step):
    return (value + step - 1) // step * step


def sine_basis():
    index = np.arange(SPAN)
    angle = np.pi * np.outer(index + 1, index + 1) / (SPAN + 1)
    return np.sqrt(2.0 / (SPAN + 1)) * np.sin(angle)


def eigenvalues():
    return 4.0 * np.sin(np.pi * (np.arange(SPAN) + 1) / (2 * (SPAN + 1))) ** 2


def line_places(y):
    return [(x, y) if 0 <= x < SPAN else None for x in range(1 - ROW0, 25 - ROW0)]


def layer_places(x):
    return [(x, y + 1) for y in range(BOX)]


def plane_matrix(places):
    basis = sine_basis()
    modes = SPAN * SPAN
    plane = np.zeros((round_up(modes, 16), len(places)))
    for column, place in enumerate(places):
        if place is not None:
            plane[:modes, column] = np.outer(basis[:, place[0]], basis[:, place[1]]).reshape(-1)
    return plane


def three_products(matrix):
    high, low = split(matrix)
    return np.concatenate([high, high, low], axis=1)


def constants(size_z):
    basis = sine_basis()
    outer = line_places(0) + line_places(SPAN - 1)
    plane = plane_matrix(sum([layer_places(x) for x in range(SPAN)], []) + outer)
    ends = plane_matrix(layer_places(0) + layer_places(SPAN - 1) + outer)
    lines = plane_matrix(sum([line_places(y) for y in (1, 2, BOX - 1, BOX)], []) + outer)
    boxes = size_z // BOX
    line = np.zeros((size_z, boxes * SPAN))
    for box in range(boxes):
        for mode in range(SPAN):
            for offset in range(SPAN):
                cell = box * BOX + offset - 1
                if 0 <= cell < size_z:
                    line[cell, box * SPAN + mode] = basis[mode, offset]
    high, low = split(line)
    line_forward = np.concatenate([high, high, low], axis=0)
    high, low = split(line.T)
    line_inverse = np.concatenate([high, low], axis=1)
    edges = plane_matrix(sum([layer_places(x) for x in EDGE_LAYERS], []) + outer)
    return (
        three_products(plane),
        three_products(plane.T),
        line_forward,
        line_inverse,
        three_products(ends),
        three_products(lines),
        three_products(edges.T),
    )


def swap_pairs(mesh, axis, odd):
    sizes = [mesh.shape[name] for name in AXES]
    along = AXES.index(axis)
    pairs = []
    for i in range(sizes[0]):
        for j in range(sizes[1]):
            here = [i, j]
            there = [i, j]
            place = here[along]
            target = place ^ 1 if not odd else (place + 1 if place % 2 else place - 1)
            if 0 <= target < sizes[along]:
                there[along] = target
            elif along == 0:
                there[0] = sizes[0] - 1 - place
            else:
                there[0] = i ^ 1
            pairs.append((here[0] * sizes[1] + here[1], there[0] * sizes[1] + there[1]))
    return pairs


def swap(mesh, axis, even_part, odd_part):
    if axis == "gx":
        first = lax.ppermute(even_part, AXES, swap_pairs(mesh, axis, False))
        second = lax.ppermute(odd_part, AXES, swap_pairs(mesh, axis, True))
    else:
        second = lax.ppermute(odd_part, AXES, swap_pairs(mesh, axis, True))
        first = lax.ppermute(even_part, AXES, swap_pairs(mesh, axis, False))
    return first, second


EVEN_X, EVEN_Y, LOW_X, HIGH_X, LOW_Y, HIGH_Y = range(6)


def standing(mesh):
    here_x, here_y = lax.axis_index("gx"), lax.axis_index("gy")
    facts = (
        lax.rem(here_x, 2) == 0,
        lax.rem(here_y, 2) == 0,
        here_x > 0,
        here_x < mesh.shape["gx"] - 1,
        here_y > 0,
        here_y < mesh.shape["gy"] - 1,
    )
    return [fact.astype(jnp.int32) for fact in facts]


def chosen(flags, which, yes, no):
    return jnp.where(flags[which] > 0, yes, no)


def keep(flags, which, value):
    return jnp.where(flags[which] > 0, value, jnp.zeros_like(value))


def halves(value):
    high = value.astype(BF16)
    low = (value - high.astype(F32)).astype(BF16)
    return high, low


def dot(left, right):
    return jnp.dot(left, right, preferred_element_type=F32)


def store_split(stack_ref, lanes, value):
    rows = value.shape[0]
    high, low = halves(value)
    stack_ref[0:rows, lanes] = high
    stack_ref[rows : 2 * rows, lanes] = low
    stack_ref[2 * rows : 3 * rows, lanes] = high


def stacked(before_ref, lanes, parts):
    store_split(before_ref, lanes, jnp.concatenate(parts, axis=0))


def forward_own(field_ref, forward_ref, before_ref, spectral_ref):
    boxes = (field_ref.shape[1] - 2) // BOX
    size_y, size_z = field_ref.shape[2:]
    blank = jnp.zeros((48, size_z), F32)
    for field in range(2):
        for box in range(boxes):
            main = field_ref[field, box * BOX : box * BOX + SPAN].reshape(SPAN * size_y, size_z)
            stacked(before_ref.at[field], slice(box * size_z, (box + 1) * size_z), [main, blank])
    for field in range(2):
        spectral_ref[field] = dot(forward_ref[...], before_ref[field])


def solve(spectral, inverse_ref, consts, after_ref):
    line_forward_ref, line_back_ref = consts
    line_rows = line_forward_ref.shape[0] // 3
    size_z = line_rows
    boxes = spectral[0].shape[1] // size_z
    lanes = [slice(box * size_z, (box + 1) * size_z) for box in range(boxes)]
    for field in range(2):
        for box in range(boxes):
            high, low = halves(spectral[field][:, lanes[box]])
            both = jnp.concatenate([high, low], axis=1)
            modes = dot(both, line_forward_ref[0 : 2 * line_rows]) + dot(high, line_forward_ref[2 * line_rows :])
            modes = modes * inverse_ref[field * boxes + box]
            high, low = halves(modes)
            cells = dot(high, line_back_ref[...])
            cells = cells[:, :size_z] + (cells[:, size_z:] + dot(low, line_back_ref[:, :size_z]))
            store_split(after_ref.at[field], lanes[box], cells)

def solved_kernel(mesh, after_ref, back_ref, out_ref, out_rows_ref, *lines_refs):
    boxes = (out_ref.shape[1] - 2) // BOX
    size_y, size_z = out_ref.shape[2:]
    inner = SPAN * size_y
    lanes = [slice(box * size_z, (box + 1) * size_z) for box in range(boxes)]
    for field in range(2):
        result = dot(back_ref[...], after_ref[field])
        for box in range(boxes):
            start = box * BOX
            main = result[:inner, lanes[box]].reshape(SPAN, size_y, size_z)
            if box == 0:
                out_ref[field, 0:SPAN] = main
            else:
                out_ref[field, start : start + 2] = out_ref[field, start : start + 2] + main[0:2]
                out_ref[field, start + 2 : start + SPAN] = main[2:]
            for side in range(2):
                strip = result[inner + 24 * side : inner + 24 * side + 24, lanes[box]]
                if box == 0:
                    out_rows_ref[field, side, 0:24] = strip
                else:
                    out_rows_ref[field, side, start : start + 8] = (
                        out_rows_ref[field, side, start : start + 8] + strip[0:8]
                    )
                    out_rows_ref[field, side, start + 8 : start + 24] = strip[8:]
    if lines_refs:
        pack_lines(standing(mesh), out_ref, out_rows_ref, *lines_refs)


def x_depth(message_ref):
    return message_ref.shape[1] // SPAN


def pack_x(flags, after_ref, edges_ref, even_ref, odd_ref):
    depth, size_z = x_depth(even_ref), even_ref.shape[2]
    layers = depth * BOX
    after = len(EDGE_LAYERS) * BOX
    for field in range(2):
        result = dot(edges_ref[...], after_ref[field])
        low, high = result[:, :size_z], result[:, result.shape[1] - size_z :]
        pairs = [(0, low[:layers], high[after - layers : after])]
        for side in range(2):
            near = after + 24 * side + ROW0 - 1
            far = near + SPAN - depth
            pairs.append((layers + depth * side, low[near : near + depth], high[far : far + depth]))
        blank = jnp.zeros((even_ref.shape[1] - SPAN * depth, size_z), F32)
        pairs.append((SPAN * depth, blank, blank))
        for start, to_low, to_high in pairs:
            place = slice(start, start + to_low.shape[0])
            even_ref[field, place] = chosen(flags, EVEN_X, to_high, to_low)
            odd_ref[field, place] = chosen(flags, EVEN_X, to_low, to_high)


def line_pairs(whole_ref, whole_rows_ref, field, layers, rows, depth):
    size_y = whole_ref.shape[2]
    if depth == 3:
        return (
            (whole_rows_ref[field, 0, rows], whole_ref[field, layers, size_y - 2]),
            (whole_ref[field, layers, 0], whole_ref[field, layers, size_y - 1]),
            (whole_ref[field, layers, 1], whole_rows_ref[field, 1, rows]),
        )
    return (
        (whole_ref[field, layers, 0], whole_ref[field, layers, size_y - 1]),
        (whole_rows_ref[field, 0, rows], whole_rows_ref[field, 1, rows]),
    )


def pack_lines(flags, part_ref, part_rows_ref, even_ref, odd_ref):
    size_x = part_ref.shape[1] - 2
    depth = even_ref.shape[1] // size_x
    for field in range(2):
        pairs = line_pairs(
            part_ref, part_rows_ref, field, slice(1, size_x + 1), slice(ROW0, ROW0 + size_x), depth
        )
        for line, (to_low, to_high) in enumerate(pairs):
            place = slice(line * size_x, (line + 1) * size_x)
            even_ref[field, place] = chosen(flags, EVEN_Y, to_high, to_low)
            odd_ref[field, place] = chosen(flags, EVEN_Y, to_low, to_high)


def unpack_lines(flags, lines_refs, ends_refs, out_ref, field):
    size_x = out_ref.shape[2] - 8
    depth = lines_refs[0].shape[1] // size_x
    blank = jnp.zeros((8, out_ref.shape[3]), F32)
    for side, flag, (even, odd) in ((0, LOW_Y, (1, 0)), (1, HIGH_Y, (0, 1))):
        lines = keep(flags, flag, chosen(flags, EVEN_Y, lines_refs[even][field], lines_refs[odd][field]))
        ends = keep(flags, flag, chosen(flags, EVEN_Y, ends_refs[even][field], ends_refs[odd][field]))
        for line in range(depth):
            out_ref[side, line, 0:8] = blank
            out_ref[side, line, size_x : size_x + 8] = blank
            out_ref[side, line, ROW0 : ROW0 + size_x] = lines[line * size_x : (line + 1) * size_x]
            if depth == 3:
                out_ref[side, line, ROW0 - 2 : ROW0 + 1] = ends[8 * line : 8 * line + 3]
                out_ref[side, line, ROW0 + size_x - 1 : ROW0 + size_x + 2] = ends[8 * line + 3 : 8 * line + 6]
            elif line == 1:
                out_ref[side, line, ROW0 - 1 : ROW0] = ends[0:1]
                out_ref[side, line, ROW0 + size_x : ROW0 + size_x + 1] = ends[1:2]


def divisor_kernel(conductance_ref, capacity_ref, zones_ref, inverse_ref):
    size_x, size_y, size_z = zones_ref.shape
    boxes = size_x // BOX
    lines = []
    for table_ref, which in ((capacity_ref, 0), (capacity_ref, 1), (conductance_ref, 0), (conductance_ref, 1)):
        for box in range(boxes):
            total = jnp.zeros((size_y, size_z), F32)
            for x in range(box * BOX, (box + 1) * BOX):
                zone = zones_ref[x]
                value = jnp.full((size_y, size_z), table_ref[which, 0], F32)
                for label in range(1, table_ref.shape[1]):
                    value = jnp.where(zone == label, table_ref[which, label], value)
                total = total + value
            lines.append(jnp.sum(total, axis=0, keepdims=True))
    sums = jnp.concatenate(lines, axis=0)
    modes, lanes = inverse_ref.shape[1:]
    cell = lax.broadcasted_iota(jnp.int32, (size_z, lanes), 0)
    lane = lax.broadcasted_iota(jnp.int32, (size_z, lanes), 1)
    spread = jnp.zeros((size_z, lanes), F32)
    for box in range(size_z // BOX):
        here = (cell >= box * BOX) & (cell < (box + 1) * BOX) & (lane >= box * SPAN) & (lane < (box + 1) * SPAN)
        spread = jnp.where(here, 1.0 / BOX**3, spread)
    means = jnp.dot(sums, spread, preferred_element_type=F32, precision=lax.Precision.HIGHEST)
    eigen = [float(value) for value in eigenvalues()]
    row = lax.broadcasted_iota(jnp.int32, (modes, 128), 0)
    first = jnp.zeros(row.shape, jnp.int32)
    for mode in range(1, SPAN):
        first = first + (row >= mode * SPAN).astype(jnp.int32)
    second = row - SPAN * first
    pair = jnp.zeros(row.shape, F32)
    for mode in range(SPAN):
        pair = pair + jnp.where(first == mode, eigen[mode], 0.0) + jnp.where(second == mode, eigen[mode], 0.0)
    lane = lax.broadcasted_iota(jnp.int32, (8, lanes), 1)
    for box in range(1, size_z // BOX):
        lane = lane - SPAN * (lax.broadcasted_iota(jnp.int32, (8, lanes), 1) >= box * SPAN).astype(jnp.int32)
    third = jnp.zeros(lane.shape, F32)
    for mode in range(SPAN):
        third = jnp.where(lane == mode, eigen[mode], third)
    summed = jnp.concatenate([pair, pair[:, : lanes - 128]], axis=1) + third[0:1]
    half = 2 * boxes
    for combo in range(half):
        cbar = means[combo : combo + 1]
        kbar = means[half + combo : half + combo + 1]
        inverse_ref[combo] = 1.0 / (cbar + kbar * summed)


def edge_layers_kernel(mesh, load_hbm, zones_hbm, even_ref, odd_ref, load_ref, zones_ref, sems):
    last = zones_hbm.shape[0] - 1
    copies = [
        pltpu.make_async_copy(load_hbm.at[:, 0], load_ref.at[0], sems.at[0]),
        pltpu.make_async_copy(load_hbm.at[:, last], load_ref.at[1], sems.at[1]),
        pltpu.make_async_copy(zones_hbm.at[pl.ds(0, 2)], zones_ref.at[0], sems.at[2]),
        pltpu.make_async_copy(zones_hbm.at[pl.ds(last - 1, 2)], zones_ref.at[1], sems.at[3]),
    ]
    for copy in copies:
        copy.start()
    flags = standing(mesh)
    for copy in copies:
        copy.wait()
    for channel in range(4):
        if channel < 2:
            low, high = load_ref[0, channel], load_ref[1, channel]
        else:
            low, high = zones_ref[0, channel - 2].astype(F32), zones_ref[1, channel - 2].astype(F32)
        even_ref[channel] = chosen(flags, EVEN_X, high, low)
        odd_ref[channel] = chosen(flags, EVEN_X, low, high)


def fetched_kernel(load_ref, zones_ref, token_ref):
    token_ref[...] = load_ref[0, 0, 0:8] + zones_ref[0, 0:8].astype(F32)


def edge_lines_kernel(mesh, load_ref, zones_ref, token_ref, first_ref, second_ref, even_ref, odd_ref):
    flags = standing(mesh)
    size_x, size_y = zones_ref.shape[:2]
    from_low = chosen(flags, EVEN_X, second_ref[...], first_ref[...])
    from_high = chosen(flags, EVEN_X, first_ref[...], second_ref[...])

    def put(row, to_low, to_high):
        place = slice(row, row + to_low.shape[0])
        even_ref[place] = chosen(flags, EVEN_Y, to_high, to_low)
        odd_ref[place] = chosen(flags, EVEN_Y, to_low, to_high)

    def put_end(row, layer, near, far):
        put(4 * size_x + row, layer[near : near + 1], layer[far : far + 1])

    blank = jnp.zeros((8, even_ref.shape[1]), F32)
    put(4 * size_x + 8, blank, blank)
    for field in range(2):
        put(field * size_x, load_ref[field, :, 0], load_ref[field, :, size_y - 1])
        put_end(2 * field, keep(flags, LOW_X, from_low[field]), 0, size_y - 1)
        put_end(2 * field + 1, keep(flags, HIGH_X, from_high[field]), 0, size_y - 1)
    for line in range(2):
        far = size_y - 2 + line
        put((2 + line) * size_x, zones_ref[:, line].astype(F32), zones_ref[:, far].astype(F32))
        for depth in range(2):
            put_end(4 + 4 * line + depth, from_low[2 + depth], line, far)
            put_end(6 + 4 * line + depth, from_high[2 + depth], line, far)


def tables(conductance_ref, capacity_ref, coupling_ref, size_z):
    labels = range(coupling_ref.shape[0])
    halves_of = [[0.5 * conductance_ref[field, label] for label in labels] for field in range(2)]
    masses = [[capacity_ref[field, label] for label in labels] for field in range(2)]
    products = [jnp.full((8, size_z), capacity_ref[0, label] * capacity_ref[1, label], F32) for label in labels]
    masses.append([coupling_ref[label] * jnp.sqrt(products[label])[0:1] for label in labels])
    return halves_of, masses


def looked_up(entries, zone):
    value = jnp.broadcast_to(entries[0], zone.shape)
    for label in range(1, len(entries)):
        value = jnp.where(zone == float(label), entries[label], value)
    return value


def coefficient_kernel(
    mesh, conductance_ref, capacity_ref, coupling_ref, zones_ref, first_x, second_x,
    half_ref, mass_ref, face_ref, table_ref,
):
    flags = standing(mesh)
    size_x, size_y, size_z = zones_ref.shape
    halves_of, masses = tables(conductance_ref, capacity_ref, coupling_ref, size_z)
    for which, entries in enumerate(halves_of + masses):
        for label, entry in enumerate(entries):
            table_ref[which, label : label + 1] = jnp.broadcast_to(entry, (1, size_z))
    low_x = chosen(flags, EVEN_X, second_x[2:4], first_x[2:4])
    high_x = chosen(flags, EVEN_X, first_x[2:4], second_x[2:4])
    inside = slice(8, 8 + size_y)
    for x in range(-2, size_x + 2):
        if x < 0:
            zone = low_x[x + 2]
        elif x >= size_x:
            zone = high_x[x - size_x]
        else:
            zone = zones_ref[x].astype(F32)
        for field in range(2):
            half_ref[field, x + 2, inside] = looked_up(halves_of[field], zone)
        if -1 <= x <= size_x:
            for which in range(3):
                mass_ref[which, x + 1] = looked_up(masses[which], zone)
    for field in range(2):
        for outer in (0, 1):
            half_ref[field, outer, inside] = chosen(
                flags, LOW_X, half_ref[field, outer, inside], half_ref[field, 2, inside]
            )
            place = size_x + 2 + outer
            half_ref[field, place, inside] = chosen(
                flags, HIGH_X, half_ref[field, place, inside], half_ref[field, size_x + 1, inside]
            )
    for field in range(2):
        for x in range(0, size_x + 2, 2):
            faces = faces_z(half_ref[field, x + 1 : x + 3, inside])
            for way in range(2):
                face_ref[field, way, x : x + 2] = faces[way]


def coefficient_lines_kernel(
    mesh, old_half_ref, mass_ref, face_ref, table_ref, first_y, second_y, after_ref,
    half_ref, half_rows_ref, mass_rows_ref, face_rows_ref, line_ref,
):
    flags = standing(mesh)
    size_x, size_y, size_z = mass_ref.shape[1] - 2, mass_ref.shape[2], mass_ref.shape[3]
    rows_of = [[table_ref[which, label : label + 1] for label in range(table_ref.shape[1])] for which in range(5)]
    halves_of, masses = rows_of[:2], rows_of[2:]
    for side, (even, odd) in enumerate(((second_y, first_y), (first_y, second_y))):
        came = chosen(flags, EVEN_Y, even[2 * size_x :], odd[2 * size_x :])
        lines, ends = (came[:size_x], came[size_x : 2 * size_x]), came[2 * size_x :]
        for line in range(2):
            place = 2 * side + line
            line_ref[place, 0:8] = jnp.zeros((8, size_z), F32)
            line_ref[place, size_x : size_x + 8] = jnp.zeros((8, size_z), F32)
            line_ref[place, ROW0 - 2 : ROW0] = ends[4 + 4 * line : 6 + 4 * line]
            line_ref[place, ROW0 : ROW0 + size_x] = lines[line]
            line_ref[place, ROW0 + size_x : ROW0 + size_x + 2] = ends[6 + 4 * line : 8 + 4 * line]
    count = half_rows_ref.shape[2]
    position = lax.broadcasted_iota(jnp.int32, (count, size_z), 0)
    for line, flag in enumerate((LOW_Y, LOW_Y, HIGH_Y, HIGH_Y)):
        zone = line_ref[line]
        for field in range(2):
            value = looked_up(halves_of[field], zone)
            below = value[ROW0 : ROW0 + 1]
            above = value[ROW0 + size_x - 1 : ROW0 + size_x]
            value = jnp.where((position < ROW0) & (flags[LOW_X] == 0), below, value)
            value = jnp.where((position >= ROW0 + size_x) & (flags[HIGH_X] == 0), above, value)
            near = old_half_ref[field, :, 8 if flag == LOW_Y else 8 + size_y - 1]
            half_rows_ref[field, line] = value
            half_rows_ref[field, line, ROW0 - 2 : ROW0 + size_x + 2] = chosen(
                flags, flag, half_rows_ref[field, line, ROW0 - 2 : ROW0 + size_x + 2], near
            )
            if line in (1, 2):
                row = 7 if line == 1 else 8 + size_y
                half_ref[field, :, row] = half_rows_ref[field, line, ROW0 - 2 : ROW0 + size_x + 2]
        if line in (1, 2):
            for which in range(3):
                mass_rows_ref[which, line - 1] = looked_up(masses[which], zone)
    for field in range(2):
        for side in range(2):
            faces = faces_z(half_rows_ref[field, side + 1])
            for way in range(2):
                face_rows_ref[field, way, side] = faces[way]
        for line, row in ((4, 0), (5, size_y - 1), (6, 1), (7, size_y - 2)):
            half_rows_ref[field, line] = jnp.zeros((count, size_z), F32)
            half_rows_ref[field, line, ROW0 - 2 : ROW0 + size_x + 2] = old_half_ref[field, :, 8 + row]
    for line, row in ((2, 0), (3, size_y - 1)):
        spread = slice(ROW0 - 1, ROW0 + size_x + 1)
        for which in range(3):
            mass_rows_ref[which, line] = jnp.zeros((count, size_z), F32)
            mass_rows_ref[which, line, spread] = mass_ref[which, :, row]
        for field in range(2):
            for way in range(2):
                face_rows_ref[field, way, line] = jnp.zeros((count, size_z), F32)
                face_rows_ref[field, way, line, spread] = face_ref[field, way, :, row]


def own_transform_kernel(load_ref, forward_ref, spectral_ref, field_ref, before_ref):
    size_x = load_ref.shape[1]
    for field in range(2):
        field_ref[field, 0] = jnp.zeros(load_ref.shape[2:], F32)
        field_ref[field, 1 : 1 + size_x] = load_ref[field]
        field_ref[field, 1 + size_x] = jnp.zeros(load_ref.shape[2:], F32)
    forward_own(field_ref, forward_ref, before_ref, spectral_ref)


def first_solve_kernel(
    mesh, spectral_ref, mass_ref, first_x, second_x, first_y, second_y, inverse_ref, c2, c3, ends_ref, edges_ref,
    after_ref, even_ref, odd_ref, rows_ref, before_ref,
):
    flags = standing(mesh)
    size_x, size_y, size_z = mass_ref.shape[1] - 2, mass_ref.shape[2], mass_ref.shape[3]
    boxes = size_x // BOX
    blank = jnp.zeros((size_y, size_z), F32)
    spectral = []
    for field in range(2):
        low = keep(flags, LOW_X, chosen(flags, EVEN_X, second_x[field], first_x[field]))
        high = keep(flags, HIGH_X, chosen(flags, EVEN_X, first_x[field], second_x[field]))
        for side, flag, even, odd in ((0, LOW_Y, second_y, first_y), (1, HIGH_Y, first_y, second_y)):
            place, after = slice(field * size_x, (field + 1) * size_x), slice(4 * size_x, 4 * size_x + 8)
            line = keep(flags, flag, chosen(flags, EVEN_Y, even[place], odd[place]))
            ends = keep(flags, flag, chosen(flags, EVEN_Y, even[after], odd[after]))
            rows_ref[field, side, 0:8] = blank[0:8]
            rows_ref[field, side, size_x : size_x + 8] = blank[0:8]
            rows_ref[field, side, ROW0 - 1 : ROW0] = ends[2 * field : 2 * field + 1]
            rows_ref[field, side, ROW0 : ROW0 + size_x] = line
            rows_ref[field, side, ROW0 + size_x : ROW0 + size_x + 1] = ends[2 * field + 1 : 2 * field + 2]
        for box in range(boxes):
            parts = [low if box == 0 else blank, high if box == boxes - 1 else blank]
            parts += [rows_ref[field, side, box * BOX : box * BOX + 24] for side in range(2)]
            stacked(before_ref.at[field], slice(box * size_z, (box + 1) * size_z), parts)
    for field in range(2):
        spectral.append(spectral_ref[field] + dot(ends_ref[...], before_ref[field]))
    solve(spectral, inverse_ref, (c2, c3), after_ref)
    pack_x(flags, after_ref, edges_ref, even_ref, odd_ref)


def merge_x_kernel(mesh, part_ref, part_rows_ref, first_ref, second_ref, whole_ref, whole_rows_ref, even_ref, odd_ref):
    flags = standing(mesh)
    size_x = part_ref.shape[1] - 2
    size_y, size_z = part_ref.shape[2:]
    depth = x_depth(first_ref)
    end = ROW0 + size_x
    for field in range(2):
        low = keep(flags, LOW_X, chosen(flags, EVEN_X, second_ref[field], first_ref[field]))
        high = keep(flags, HIGH_X, chosen(flags, EVEN_X, first_ref[field], second_ref[field]))
        low_layers, high_layers = [
            [came[layer * size_y : (layer + 1) * size_y] for layer in range(depth)] for came in (low, high)
        ]
        whole_ref[field, 1] = keep(flags, LOW_X, part_ref[field, 0]) + low_layers[depth - 2]
        whole_ref[field, 2] = part_ref[field, 1] + low_layers[depth - 1]
        whole_ref[field, 3 : size_x + 1] = part_ref[field, 2:size_x]
        whole_ref[field, size_x + 1] = part_ref[field, size_x] + high_layers[0]
        whole_ref[field, size_x + 2] = keep(flags, HIGH_X, part_ref[field, size_x + 1]) + high_layers[1]
        whole_ref[field, 0] = low_layers[0] if depth == 3 else jnp.zeros((size_y, size_z), F32)
        whole_ref[field, size_x + 3] = high_layers[2] if depth == 3 else jnp.zeros((size_y, size_z), F32)
        for side in range(2):
            start = depth * (size_y + side)
            low_row, high_row = [
                [came[start + layer : start + layer + 1] for layer in range(depth)] for came in (low, high)
            ]
            edge = ROW0 - 1
            whole_rows_ref[field, side] = part_rows_ref[field, side]
            whole_rows_ref[field, side, edge : edge + 1] = (
                keep(flags, LOW_X, part_rows_ref[field, side, edge : edge + 1]) + low_row[depth - 2]
            )
            whole_rows_ref[field, side, edge + 1 : edge + 2] = (
                part_rows_ref[field, side, edge + 1 : edge + 2] + low_row[depth - 1]
            )
            whole_rows_ref[field, side, end - 1 : end] = part_rows_ref[field, side, end - 1 : end] + high_row[0]
            whole_rows_ref[field, side, end : end + 1] = (
                keep(flags, HIGH_X, part_rows_ref[field, side, end : end + 1]) + high_row[1]
            )
            if depth == 3:
                whole_rows_ref[field, side, edge - 1 : edge] = low_row[0]
                whole_rows_ref[field, side, end + 1 : end + 2] = high_row[2]

        base = 2 * size_x if depth == 2 else 0
        for ref in (even_ref, odd_ref):
            ref[field, base:] = jnp.zeros((ref.shape[1] - base, size_z), F32)
        if base:
            own, rows = slice(2, size_x + 2), slice(ROW0, ROW0 + size_x)
            pairs = line_pairs(whole_ref, whole_rows_ref, field, own, rows, depth)
            for line, (to_low, to_high) in enumerate(pairs):
                place = slice(line * size_x, (line + 1) * size_x)
                even_ref[field, place] = chosen(flags, EVEN_Y, to_high, to_low)
                odd_ref[field, place] = chosen(flags, EVEN_Y, to_low, to_high)
            for row, x in ((base, -1), (base + 1, size_x)):
                pairs = line_pairs(
                    whole_ref, whole_rows_ref, field, slice(x + 2, x + 3), slice(x + ROW0, x + ROW0 + 1), depth
                )
                even_ref[field, row : row + 1] = chosen(flags, EVEN_Y, pairs[1][1], pairs[1][0])
                odd_ref[field, row : row + 1] = chosen(flags, EVEN_Y, pairs[1][0], pairs[1][1])
            continue
        for start, x in ((base, -2), (base + 3, size_x - 1)):
            layers, rows = slice(x + 2, x + 5), slice(x + ROW0, x + ROW0 + 3)
            pairs = line_pairs(whole_ref, whole_rows_ref, field, layers, rows, depth)
            for line, (to_low, to_high) in enumerate(pairs):
                place = slice(8 * line + start, 8 * line + start + 3)
                even_ref[field, place] = chosen(flags, EVEN_Y, to_high, to_low)
                odd_ref[field, place] = chosen(flags, EVEN_Y, to_low, to_high)


def faces_z(half):
    size_z, axis = half.shape[-1], half.ndim - 1
    lane = lax.broadcasted_iota(jnp.int32, half.shape, axis)
    upper = half + jnp.where(lane == size_z - 1, half, pltpu.roll(half, size_z - 1, axis))
    lower = half + jnp.where(lane == 0, half, pltpu.roll(half, 1, axis))
    return upper, lower


def along_z(value, upper, lower):
    size_z, axis = value.shape[-1], value.ndim - 1
    lane = lax.broadcasted_iota(jnp.int32, value.shape, axis)
    above = jnp.where(lane == size_z - 1, 0.0, pltpu.roll(value, size_z - 1, axis))
    below = jnp.where(lane == 0, 0.0, pltpu.roll(value, 1, axis))
    return upper * (value - above) + lower * (value - below)


def operate(field_ref, half_ref, mass_ref, face_ref, x, count):
    size_y = mass_ref.shape[2]
    inside = slice(8, 8 + size_y)
    masses = slice(x + 1, x + 1 + count)
    here = slice(x + 2, x + 2 + count)
    values, images = [], []
    for field in range(2):
        value = field_ref[field, here, inside]
        half = half_ref[field, here, inside]
        flux = along_z(value, face_ref[field, 0, masses], face_ref[field, 1, masses])
        for start in (x + 1, x + 3):
            place = slice(start, start + count)
            flux = flux + (half + half_ref[field, place, inside]) * (value - field_ref[field, place, inside])
        for shift in (-1, 1):
            moved = slice(8 + shift, 8 + shift + size_y)
            flux = flux + (half + half_ref[field, here, moved]) * (value - field_ref[field, here, moved])
        values.append(value)
        images.append(flux)
    first = mass_ref[0, masses] * values[0] + mass_ref[2, masses] * values[1] + images[0]
    second = mass_ref[2, masses] * values[0] + mass_ref[1, masses] * values[1] + images[1]
    return values, (first, second)


def merge_x_after_kernel(mesh, part_ref, part_rows_ref, first_ref, second_ref, sums_ref, *outs):
    merge_x_kernel(mesh, part_ref, part_rows_ref, first_ref, second_ref, *outs)


def fill(flags, whole_ref, whole_rows_ref, value_ref):
    size_x, size_y = whole_ref.shape[1] - 4, whole_ref.shape[2]
    spread = slice(ROW0 - 2, ROW0 + size_x + 2)
    for field in range(2):
        value_ref[field, :, 8 : 8 + size_y] = whole_ref[field]
        value_ref[field, :, 7] = keep(flags, LOW_Y, whole_rows_ref[field, 0, spread])
        value_ref[field, :, 8 + size_y] = keep(flags, HIGH_Y, whole_rows_ref[field, 1, spread])


def line_image(values, outers, inners, half_lines, places, mass_lines, face_lines, place):
    center, outer, inner = places
    images = []
    for field in range(2):
        value, half = values[field], half_lines[field, center]
        count = value.shape[0]
        flux = along_z(value, face_lines[field, 0, place], face_lines[field, 1, place])
        for turn in (1, count - 1):
            flux = flux + (half + pltpu.roll(half, turn, 0)) * (value - pltpu.roll(value, turn, 0))
        flux = flux + (half + half_lines[field, outer]) * (value - outers[field])
        flux = flux + (half + half_lines[field, inner]) * (value - inners[field])
        images.append(flux)
    first = mass_lines[0, place] * values[0] + mass_lines[2, place] * values[1] + images[0]
    second = mass_lines[2, place] * values[0] + mass_lines[1, place] * values[1] + images[1]
    return first, second


SIDES = (((4, 1, 6, 0), (2, 0)), ((5, 2, 7, 3), (3, 1)))


def line_changes(delta, outer, half_lines, mass_lines, face_lines, side):
    (edge, out, inner, _), (place, _) = SIDES[side]
    nothing = [jnp.zeros_like(line) for line in delta]
    at_edge = line_image(delta, outer, nothing, half_lines, (edge, out, inner), mass_lines, face_lines, place)
    at_next = [-(half_lines[field, edge] + half_lines[field, inner]) * delta[field] for field in range(2)]
    return at_edge, at_next


def own_image_kernel(
    mesh, whole_ref, whole_rows_ref, half_ref, mass_ref, face_ref, forward_ref, image_ref, spectral_ref,
    value_ref, before_ref,
):
    flags = standing(mesh)
    size_x = whole_ref.shape[1] - 4
    fill(flags, whole_ref, whole_rows_ref, value_ref)
    for x, flag in ((-1, LOW_X), (size_x, HIGH_X)):
        _, images = operate(value_ref, half_ref, mass_ref, face_ref, x, 1)
        for field in range(2):
            image_ref[field, x + 1 : x + 2] = keep(flags, flag, images[field])
    for x in range(0, size_x, CHUNK):
        _, images = operate(value_ref, half_ref, mass_ref, face_ref, x, CHUNK)
        for field in range(2):
            image_ref[field, x + 1 : x + 1 + CHUNK] = images[field]
    forward_own(image_ref, forward_ref, before_ref, spectral_ref)


def second_solve_kernel(
    mesh, whole_ref, whole_rows_ref, first_lines, second_lines, first_ends, second_ends,
    half_lines, mass_lines, face_lines, spectral_ref, inverse_ref, c2, c3, lines_ref, edges_ref,
    deltas_ref, changes_ref, after_ref, even_ref, odd_ref, came_ref, near, before_ref,
):
    flags = standing(mesh)
    size_x, size_y, size_z = whole_ref.shape[1] - 4, whole_ref.shape[2], whole_ref.shape[3]
    boxes = size_x // BOX
    count = near.shape[2]
    position = lax.broadcasted_iota(jnp.int32, (count, size_z), 0)
    begin = jnp.where(flags[LOW_X] > 0, ROW0 - 1, ROW0)
    end = jnp.where(flags[HIGH_X] > 0, ROW0 + size_x + 1, ROW0 + size_x)
    valid = (position >= begin) & (position < end)
    for field in range(2):
        unpack_lines(flags, (first_lines, second_lines), (first_ends, second_ends), came_ref.at[field], field)
        for side, row in ((0, 0), (1, size_y - 1)):
            near[field, side] = jnp.zeros((count, size_z), F32)
            near[field, side, ROW0 - 2 : ROW0 + size_x + 2] = whole_ref[field, :, row]
    for side, flag, order in ((0, LOW_Y, (2, 1, 0)), (1, HIGH_Y, (0, 1, 2))):
        delta, outer, far = [[came_ref[field, side, line] for field in range(2)] for line in order]
        at_edge, at_next = line_changes(delta, outer, half_lines, mass_lines, face_lines, side)
        (edge, out, _, beyond), (_, place) = SIDES[side]
        at_outer = line_image(
            [keep(flags, flag, whole_rows_ref[field, side]) + outer[field] for field in range(2)],
            far,
            [near[field, side] + delta[field] for field in range(2)],
            half_lines,
            (out, beyond, edge),
            mass_lines,
            face_lines,
            place,
        )
        for field in range(2):
            deltas_ref[field, side] = delta[field]
            changes_ref[field, 3 * side] = jnp.where(valid, at_edge[field], 0.0)
            changes_ref[field, 1 + side] = jnp.where(valid, at_next[field], 0.0)
            changes_ref[field, 4 + side] = keep(flags, flag, jnp.where(valid, at_outer[field], 0.0))
    spectral = []
    for field in range(2):
        for box in range(boxes):
            parts = [changes_ref[field, line, box * BOX : box * BOX + 24] for line in range(6)]
            stacked(before_ref.at[field], slice(box * size_z, (box + 1) * size_z), parts)
    for field in range(2):
        spectral.append(spectral_ref[field] + dot(lines_ref[...], before_ref[field]))
    solve(spectral, inverse_ref, (c2, c3), after_ref)
    pack_x(flags, after_ref, edges_ref, even_ref, odd_ref)


def first_sums_kernel(load_ref, whole_ref, image_ref, deltas_ref, changes_ref, precond_ref, out_ref, sums_ref):
    size_x, size_y, size_z = load_ref.shape[1:]
    rows = slice(ROW0, ROW0 + size_x)
    total_a = total_b = jnp.zeros((size_y, size_z), F32)
    for field in range(2):
        precond_ref[field] = whole_ref[field, 2 : size_x + 2]
        out_ref[field] = image_ref[field, 1 : size_x + 1]
        for side, row in ((0, 0), (1, size_y - 1)):
            precond_ref[field, :, row] = precond_ref[field, :, row] + deltas_ref[field, side, rows]
        for line, row in enumerate((0, 1, size_y - 2, size_y - 1)):
            out_ref[field, :, row] = out_ref[field, :, row] + changes_ref[field, line, rows]
        for x in range(size_x):
            total_a = total_a + load_ref[field, x] * precond_ref[field, x]
            total_b = total_b + out_ref[field, x] * precond_ref[field, x]
    sums_ref[0:1] = jnp.sum(total_a, axis=0, keepdims=True)
    sums_ref[1:2] = jnp.sum(total_b, axis=0, keepdims=True)
    sums_ref[2:8] = jnp.zeros((6, size_z), F32)


def own_second_image_kernel(
    mesh, whole_ref, whole_rows_ref, half_ref, mass_ref, face_ref, old_image_ref, image_ref, sums_ref, value_ref
):
    flags = standing(mesh)
    size_x, size_y, size_z = old_image_ref.shape[1:]
    fill(flags, whole_ref, whole_rows_ref, value_ref)
    total_c = total_d = jnp.zeros((CHUNK, size_y, size_z), F32)
    for x in range(0, size_x, CHUNK):
        chunk = slice(x, x + CHUNK)
        values, images = operate(value_ref, half_ref, mass_ref, face_ref, x, CHUNK)
        for field in range(2):
            image_ref[field, chunk] = images[field]
            total_c = total_c + old_image_ref[field, chunk] * values[field]
            total_d = total_d + images[field] * values[field]
    sums_ref[0:1] = jnp.sum(jnp.sum(total_c, axis=0), axis=0, keepdims=True)
    sums_ref[1:2] = jnp.sum(jnp.sum(total_d, axis=0), axis=0, keepdims=True)
    sums_ref[2:8] = jnp.zeros((6, size_z), F32)


def second_image_kernel(
    mesh, whole_ref, image_ref, first_ref, second_ref,
    half_lines, mass_lines, face_lines, old_image_ref, old_sums_ref, own_sums_ref,
    deltas_ref, changes_ref, sums_ref, came_ref,
):
    flags = standing(mesh)
    size_x, size_y, size_z = old_image_ref.shape[1:]
    own = slice(2, size_x + 2)
    rows = slice(ROW0, ROW0 + size_x)
    total_c = total_d = jnp.zeros((size_x, size_z), F32)
    lines_refs = [ref.at[:, pl.ds(0, 2 * size_x)] for ref in (first_ref, second_ref)]
    ends_refs = [ref.at[:, pl.ds(2 * size_x, 8)] for ref in (first_ref, second_ref)]
    for field in range(2):
        unpack_lines(flags, lines_refs, ends_refs, came_ref.at[field], field)
    for side, row, beside in ((0, 0, 1), (1, size_y - 1, size_y - 2)):
        outer, delta = [[came_ref[field, side, line] for field in range(2)] for line in range(2)]
        at_edge, at_next = line_changes(delta, outer, half_lines, mass_lines, face_lines, side)
        for field in range(2):
            changed, edge, inner = delta[field][rows], at_edge[field][rows], at_next[field][rows]
            deltas_ref[field, side] = changed
            changes_ref[field, 3 * side] = edge
            changes_ref[field, 1 + side] = inner
            total_c = total_c + old_image_ref[field, :, row] * changed
            total_d = total_d + (image_ref[field, :, row] + edge) * changed
            total_d = total_d + whole_ref[field, own, row] * edge + whole_ref[field, own, beside] * inner
    totals = [
        jnp.sum(old_sums_ref[0:1], axis=1, keepdims=True),
        jnp.sum(old_sums_ref[1:2], axis=1, keepdims=True),
        jnp.sum(jnp.sum(total_c, axis=0, keepdims=True) + own_sums_ref[0:1], axis=1, keepdims=True),
        jnp.sum(jnp.sum(total_d, axis=0, keepdims=True) + own_sums_ref[1:2], axis=1, keepdims=True),
    ]
    lane = lax.broadcasted_iota(jnp.int32, sums_ref.shape, 1)
    spread = jnp.zeros(sums_ref.shape, F32)
    for place, total in enumerate(totals):
        spread = jnp.where(lane == place, total, spread)
    sums_ref[...] = spread


def finish_kernel(
    sums_ref, load_ref, z_ref, q_ref, w_ref, s_ref, deltas_ref, changes_ref,
    solution_hbm, residual_hbm, solution_ref, residual_ref, sems,
):
    line = jnp.sum(sums_ref[...], axis=0, keepdims=True)
    lane = lax.broadcasted_iota(jnp.int32, line.shape, 1)
    rz, zq, qw, ws = [jnp.sum(jnp.where(lane == place, line, 0.0), axis=1, keepdims=True) for place in range(4)]
    alpha = rz / zq
    rz_next = rz - alpha * (2.0 * zq) + alpha * alpha * qw
    grown = 1.0 + rz_next / rz
    curvature = grown * grown * zq - 2.0 * grown * alpha * qw + alpha * alpha * ws
    alpha_next = rz_next / curvature
    along = alpha + alpha_next * grown
    against = alpha_next * alpha
    copies = []
    step = load_ref.shape[1] // 2
    for field in range(2):
        for start in range(0, 2 * step, step):
            part = pl.ds(start, step)
            for x in range(start, start + step):
                solution_ref[field, x] = along * z_ref[field, x] - against * w_ref[field, x + 2]
                residual_ref[field, x] = load_ref[field, x] - along * q_ref[field, x] + against * s_ref[field, x]
            size_y = load_ref.shape[2]
            chunk = slice(start, start + step)
            for side, row in ((0, 0), (1, size_y - 1)):
                solution_ref[field, chunk, row] = (
                    solution_ref[field, chunk, row] - against * deltas_ref[field, side, chunk]
                )
            for line, row in enumerate((0, 1, size_y - 2, size_y - 1)):
                residual_ref[field, chunk, row] = (
                    residual_ref[field, chunk, row] + against * changes_ref[field, line, chunk]
                )
            for here, there in ((solution_ref, solution_hbm), (residual_ref, residual_hbm)):
                copies.append(
                    pltpu.make_async_copy(here.at[field, part], there.at[field, part], sems.at[len(copies)])
                )
                copies[-1].start()
    for copy in copies:
        copy.wait()


SMEM = pl.BlockSpec(memory_space=pltpu.SMEM)
VMEM = pl.BlockSpec(memory_space=pltpu.VMEM)
HBM = pl.BlockSpec(memory_space=pltpu.HBM)


def call(mesh, kernel, scalars, arrays, outs, scratch=(), flops=0, limit=24, in_hbm=False, outs_in_hbm=False, aliases=()):
    moved = sum(math.prod(a.shape) * a.dtype.itemsize for a in list(arrays) + list(outs))
    return pl.pallas_call(
        kernel if mesh is None else functools.partial(kernel, mesh),
        out_shape=tuple(outs),
        in_specs=[SMEM] * len(scalars) + [HBM if in_hbm else VMEM] * len(arrays),
        out_specs=tuple([HBM if outs_in_hbm else VMEM] * len(outs)),
        scratch_shapes=list(scratch),
        input_output_aliases=dict(aliases),
        compiler_params=pltpu.CompilerParams(vmem_limit_bytes=int(limit * 1024 * 1024)),
        cost_estimate=pl.CostEstimate(flops=flops, bytes_accessed=moved, transcendentals=0),
    )(*scalars, *arrays)


def shards(mesh, load, zones, conductance, capacity, coupling):
    size_x, size_y, size_z = zones.shape
    assert size_x % BOX == 0 and size_y == BOX and size_z % BOX == 0
    boxes = size_x // BOX
    count = size_x + 8
    sds = lambda *shape: jax.ShapeDtypeStruct(shape, F32)
    forward, back, line_forward, line_back, ends_forward, lines_forward, edges_back = [
        jnp.asarray(c) for c in constants(size_z)
    ]
    consts = (line_forward, line_back)
    modes, lanes = forward.shape[0], size_z // BOX * SPAN
    assert size_z == 128
    packed = call(
        mesh,
        edge_layers_kernel,
        [],
        [load, zones],
        [sds(4, size_y, size_z)] * 2,
        [
            pltpu.VMEM((2, 2, size_y, size_z), F32),
            pltpu.VMEM((2, 2, size_y, size_z), zones.dtype),
            pltpu.SemaphoreType.DMA((4,)),
        ],
        in_hbm=True,
        limit=53.75,
    )
    (token,) = call(None, fetched_kernel, [], [load, zones], [sds(8, size_z)])
    x_halo = swap(mesh, "gx", *packed)
    (inverse,) = call(
        None,
        divisor_kernel,
        [conductance, capacity],
        [zones],
        [sds(2 * boxes, modes, lanes)],
        flops=40_000_000,
    )
    packed = call(mesh, edge_lines_kernel, [], [load, zones, token, *x_halo], [sds(4 * size_x + 16, size_z)] * 2)
    y_halo = swap(mesh, "gy", *packed)
    laws = [conductance, capacity, coupling]
    padded_shape = sds(2, size_x + 4, size_y + 16, size_z)
    half, mass, face, table = call(
        mesh,
        coefficient_kernel,
        laws,
        [zones, *x_halo],
        [padded_shape, sds(3, size_x + 2, size_y, size_z), sds(2, 2, size_x + 2, size_y, size_z)]
        + [sds(5, coupling.shape[0], size_z)],
        flops=20_000_000,
    )
    parts = [sds(2, size_x + 2, size_y, size_z), sds(2, 2, count, size_z)]
    packed_x = [[sds(2, round_up(depth * SPAN, 8), size_z)] * 2 for depth in (3, 2)]
    wholes = [sds(2, size_x + 4, size_y, size_z), sds(2, 2, count, size_z)]
    packed_lines = [sds(2, 3 * size_x, size_z)] * 2
    packed_ends = [sds(2, 3 * 8, size_z)] * 2
    packed_y = [sds(2, 2 * size_x + 8, size_z)] * 2
    rows = SPAN * size_y + 48
    wide = boxes * size_z
    spectrum = sds(2, modes, wide)
    stack = lambda depth: pltpu.VMEM((2, depth, wide), BF16)
    halo = pltpu.VMEM((2, size_x + 2, size_y, size_z), F32)
    padded = pltpu.VMEM((2, size_x + 4, size_y + 16, size_z), F32)
    own = sds(2, size_x, size_y, size_z)

    (spectral,) = call(None, own_transform_kernel, [], [load, forward], [spectrum], [halo, stack(3 * rows)], 700_000_000)
    stacked_cells = jax.ShapeDtypeStruct((2, 3 * rows, wide), BF16)
    after, *packed = call(
        mesh,
        first_solve_kernel,
        [],
        [spectral, mass, *x_halo, *y_halo, inverse, *consts, ends_forward, edges_back],
        [stacked_cells] + packed_x[0],
        [pltpu.VMEM((2, 2, count, size_z), F32), stack(ends_forward.shape[1])],
        2_000_000_000,
    )
    received = swap(mesh, "gx", *packed)
    part, part_rows, *packed = call(mesh, solved_kernel, [], [after, back], parts + packed_lines, (), 700_000_000)
    lines = swap(mesh, "gy", *packed)
    whole, whole_rows, *packed = call(mesh, merge_x_kernel, [], [part, part_rows, *received], wholes + packed_ends)
    ends = swap(mesh, "gy", *packed)
    half, half_lines, mass_lines, face_lines = call(
        mesh,
        coefficient_lines_kernel,
        [],
        [half, mass, face, table, *y_halo, whole_rows],
        [padded_shape, sds(2, 8, count, size_z), sds(3, 4, count, size_z), sds(2, 2, 4, count, size_z)],
        [pltpu.VMEM((4, count, size_z), F32)],
        flops=2_000_000,
        aliases={0: 0},
    )
    own_image, spectral = call(
        mesh,
        own_image_kernel,
        [],
        [whole, whole_rows, half, mass, face, forward],
        [sds(2, size_x + 2, size_y, size_z), spectrum],
        [padded, stack(3 * rows)],
        700_000_000,
    )
    deltas, changes, after, *packed = call(
        mesh,
        second_solve_kernel,
        [],
        [whole, whole_rows, *lines, *ends, half_lines, mass_lines, face_lines, spectral, inverse, *consts]
        + [lines_forward, edges_back],
        [sds(2, 2, count, size_z), sds(2, 6, count, size_z), stacked_cells] + packed_x[1],
        [
            pltpu.VMEM((2, 2, 3, count, size_z), F32),
            pltpu.VMEM((2, 2, count, size_z), F32),
            stack(lines_forward.shape[1]),
        ],
        2_000_000_000,
    )
    received = swap(mesh, "gx", *packed)
    part, part_rows = call(mesh, solved_kernel, [], [after, back], parts, (), 700_000_000)
    precond, image, sums = call(
        None, first_sums_kernel, [], [load, whole, own_image, deltas, changes], [own, own, sds(8, size_z)], flops=1_000_000
    )
    whole, whole_rows, *packed = call(
        mesh, merge_x_after_kernel, [], [part, part_rows, *received, sums], wholes + packed_y
    )
    received = swap(mesh, "gy", *packed)
    last_image, own_sums = call(
        mesh,
        own_second_image_kernel,
        [],
        [whole, whole_rows, half, mass, face, image],
        [own, sds(8, size_z)],
        [padded],
        10_000_000,
    )
    devices = mesh.shape["gx"] * mesh.shape["gy"]
    deltas, changes, sums = call(
        mesh,
        second_image_kernel,
        [],
        [whole, last_image, *received, half_lines, mass_lines, face_lines, image, sums, own_sums],
        [sds(2, 2, size_x, size_z), sds(2, 4, size_x, size_z), sds(devices, size_z)],
        [pltpu.VMEM((2, 2, 2, count, size_z), F32)],
        1_000_000,
    )
    sums = lax.all_to_all(sums, AXES, 0, 0, tiled=True)
    whole_block = pltpu.VMEM((2, size_x, size_y, size_z), F32)
    return call(
        None,
        finish_kernel,
        [],
        [sums, load, precond, image, whole, last_image, deltas, changes],
        [own, own],
        [whole_block, whole_block, pltpu.SemaphoreType.DMA((8,))],
        outs_in_hbm=True,
    )


def solution(mesh):
    in_specs = (P(None, "gx", "gy", None), P("gx", "gy", None), P(), P(), P())
    out_specs = (P(None, "gx", "gy", None), P(None, "gx", "gy", None))
    return jax.shard_map(
        functools.partial(shards, mesh), mesh=mesh, in_specs=in_specs, out_specs=out_specs, check_vma=False
    )
```

```python
import functools
import math

import jax
import jax.numpy as jnp
import ml_dtypes
import numpy as np
from jax import lax
from jax.experimental import pallas as pl
from jax.experimental.pallas import tpu as pltpu
from jax.sharding import PartitionSpec as P

BOX = 16
SPAN = BOX + 2
F32 = jnp.float32
BF16 = jnp.bfloat16
AXES = ("gx", "gy")
ROW0 = 4
EDGE_LAYERS = (0, 1, 2, SPAN - 3, SPAN - 2, SPAN - 1)
CHUNK = 4


def split(matrix):
    high = matrix.astype(ml_dtypes.bfloat16)
    low = (matrix - high.astype(np.float64)).astype(ml_dtypes.bfloat16)
    return high, low


def round_up(value, step):
    return (value + step - 1) // step * step


def sine_basis():
    index = np.arange(SPAN)
    angle = np.pi * np.outer(index + 1, index + 1) / (SPAN + 1)
    return np.sqrt(2.0 / (SPAN + 1)) * np.sin(angle)


def eigenvalues():
    return 4.0 * np.sin(np.pi * (np.arange(SPAN) + 1) / (2 * (SPAN + 1))) ** 2


def line_places(y):
    return [(x, y) if 0 <= x < SPAN else None for x in range(1 - ROW0, 25 - ROW0)]


def layer_places(x):
    return [(x, y + 1) for y in range(BOX)]


def plane_matrix(places):
    basis = sine_basis()
    modes = SPAN * SPAN
    plane = np.zeros((round_up(modes, 16), len(places)))
    for column, place in enumerate(places):
        if place is not None:
            plane[:modes, column] = np.outer(basis[:, place[0]], basis[:, place[1]]).reshape(-1)
    return plane


def three_products(matrix):
    high, low = split(matrix)
    return np.concatenate([high, high, low], axis=1)


def constants(size_z):
    basis = sine_basis()
    outer = line_places(0) + line_places(SPAN - 1)
    plane = plane_matrix(sum([layer_places(x) for x in range(SPAN)], []) + outer)
    ends = plane_matrix(layer_places(0) + layer_places(SPAN - 1) + outer)
    lines = plane_matrix(sum([line_places(y) for y in (1, 2, BOX - 1, BOX)], []) + outer)
    boxes = size_z // BOX
    line = np.zeros((size_z, boxes * SPAN))
    for box in range(boxes):
        for mode in range(SPAN):
            for offset in range(SPAN):
                cell = box * BOX + offset - 1
                if 0 <= cell < size_z:
                    line[cell, box * SPAN + mode] = basis[mode, offset]
    high, low = split(line)
    line_forward = np.concatenate([high, high, low], axis=0)
    high, low = split(line.T)
    line_inverse = np.concatenate([high, low], axis=1)
    edges = plane_matrix(sum([layer_places(x) for x in EDGE_LAYERS], []) + outer)
    return (
        three_products(plane),
        three_products(plane.T),
        line_forward,
        line_inverse,
        three_products(ends),
        three_products(lines),
        three_products(edges.T),
    )


def swap_pairs(mesh, axis, odd):
    sizes = [mesh.shape[name] for name in AXES]
    along = AXES.index(axis)
    pairs = []
    for i in range(sizes[0]):
        for j in range(sizes[1]):
            here = [i, j]
            there = [i, j]
            place = here[along]
            target = place ^ 1 if not odd else (place + 1 if place % 2 else place - 1)
            if 0 <= target < sizes[along]:
                there[along] = target
            elif along == 0:
                there[0] = sizes[0] - 1 - place
            else:
                there[0] = i ^ 1
            pairs.append((here[0] * sizes[1] + here[1], there[0] * sizes[1] + there[1]))
    return pairs


def swap(mesh, axis, even_part, odd_part):
    if axis == "gx":
        first = lax.ppermute(even_part, AXES, swap_pairs(mesh, axis, False))
        second = lax.ppermute(odd_part, AXES, swap_pairs(mesh, axis, True))
    else:
        second = lax.ppermute(odd_part, AXES, swap_pairs(mesh, axis, True))
        first = lax.ppermute(even_part, AXES, swap_pairs(mesh, axis, False))
    return first, second


EVEN_X, EVEN_Y, LOW_X, HIGH_X, LOW_Y, HIGH_Y = range(6)


def standing(mesh):
    here_x, here_y = lax.axis_index("gx"), lax.axis_index("gy")
    facts = (
        lax.rem(here_x, 2) == 0,
        lax.rem(here_y, 2) == 0,
        here_x > 0,
        here_x < mesh.shape["gx"] - 1,
        here_y > 0,
        here_y < mesh.shape["gy"] - 1,
    )
    return [fact.astype(jnp.int32) for fact in facts]


def chosen(flags, which, yes, no):
    return jnp.where(flags[which] > 0, yes, no)


def keep(flags, which, value):
    return jnp.where(flags[which] > 0, value, jnp.zeros_like(value))


def halves(value):
    high = value.astype(BF16)
    low = (value - high.astype(F32)).astype(BF16)
    return high, low


def dot(left, right):
    return jnp.dot(left, right, preferred_element_type=F32)


def store_split(stack_ref, lanes, value):
    rows = value.shape[0]
    high, low = halves(value)
    stack_ref[0:rows, lanes] = high
    stack_ref[rows : 2 * rows, lanes] = low
    stack_ref[2 * rows : 3 * rows, lanes] = high


def stacked(before_ref, lanes, parts):
    store_split(before_ref, lanes, jnp.concatenate(parts, axis=0))


def forward_own(field_ref, forward_ref, before_ref, spectral_ref):
    boxes = (field_ref.shape[1] - 2) // BOX
    size_y, size_z = field_ref.shape[2:]
    blank = jnp.zeros((48, size_z), F32)
    for field in range(2):
        for box in range(boxes):
            main = field_ref[field, box * BOX : box * BOX + SPAN].reshape(SPAN * size_y, size_z)
            stacked(before_ref.at[field], slice(box * size_z, (box + 1) * size_z), [main, blank])
    for field in range(2):
        spectral_ref[field] = dot(forward_ref[...], before_ref[field])


def solve(spectral, inverse_ref, consts, after_ref):
    line_forward_ref, line_back_ref = consts
    line_rows = line_forward_ref.shape[0] // 3
    size_z = line_rows
    boxes = spectral[0].shape[1] // size_z
    lanes = [slice(box * size_z, (box + 1) * size_z) for box in range(boxes)]
    for field in range(2):
        for box in range(boxes):
            high, low = halves(spectral[field][:, lanes[box]])
            both = jnp.concatenate([high, low], axis=1)
            modes = dot(both, line_forward_ref[0 : 2 * line_rows]) + dot(high, line_forward_ref[2 * line_rows :])
            modes = modes * inverse_ref[field * boxes + box]
            high, low = halves(modes)
            cells = dot(high, line_back_ref[...])
            cells = cells[:, :size_z] + (cells[:, size_z:] + dot(low, line_back_ref[:, :size_z]))
            store_split(after_ref.at[field], lanes[box], cells)

def solved_kernel(mesh, after_ref, back_ref, out_ref, out_rows_ref, *lines_refs):
    boxes = (out_ref.shape[1] - 2) // BOX
    size_y, size_z = out_ref.shape[2:]
    inner = SPAN * size_y
    lanes = [slice(box * size_z, (box + 1) * size_z) for box in range(boxes)]
    for field in range(2):
        result = dot(back_ref[...], after_ref[field])
        for box in range(boxes):
            start = box * BOX
            main = result[:inner, lanes[box]].reshape(SPAN, size_y, size_z)
            if box == 0:
                out_ref[field, 0:SPAN] = main
            else:
                out_ref[field, start : start + 2] = out_ref[field, start : start + 2] + main[0:2]
                out_ref[field, start + 2 : start + SPAN] = main[2:]
            for side in range(2):
                strip = result[inner + 24 * side : inner + 24 * side + 24, lanes[box]]
                if box == 0:
                    out_rows_ref[field, side, 0:24] = strip
                else:
                    out_rows_ref[field, side, start : start + 8] = (
                        out_rows_ref[field, side, start : start + 8] + strip[0:8]
                    )
                    out_rows_ref[field, side, start + 8 : start + 24] = strip[8:]
    if lines_refs:
        pack_lines(standing(mesh), out_ref, out_rows_ref, *lines_refs)


def x_depth(message_ref):
    return message_ref.shape[1] // SPAN


def pack_x(flags, after_ref, edges_ref, even_ref, odd_ref):
    depth, size_z = x_depth(even_ref), even_ref.shape[2]
    layers = depth * BOX
    after = len(EDGE_LAYERS) * BOX
    for field in range(2):
        result = dot(edges_ref[...], after_ref[field])
        low, high = result[:, :size_z], result[:, result.shape[1] - size_z :]
        pairs = [(0, low[:layers], high[after - layers : after])]
        for side in range(2):
            near = after + 24 * side + ROW0 - 1
            far = near + SPAN - depth
            pairs.append((layers + depth * side, low[near : near + depth], high[far : far + depth]))
        blank = jnp.zeros((even_ref.shape[1] - SPAN * depth, size_z), F32)
        pairs.append((SPAN * depth, blank, blank))
        for start, to_low, to_high in pairs:
            place = slice(start, start + to_low.shape[0])
            even_ref[field, place] = chosen(flags, EVEN_X, to_high, to_low)
            odd_ref[field, place] = chosen(flags, EVEN_X, to_low, to_high)


def line_pairs(whole_ref, whole_rows_ref, field, layers, rows, depth):
    size_y = whole_ref.shape[2]
    if depth == 3:
        return (
            (whole_rows_ref[field, 0, rows], whole_ref[field, layers, size_y - 2]),
            (whole_ref[field, layers, 0], whole_ref[field, layers, size_y - 1]),
            (whole_ref[field, layers, 1], whole_rows_ref[field, 1, rows]),
        )
    return (
        (whole_ref[field, layers, 0], whole_ref[field, layers, size_y - 1]),
        (whole_rows_ref[field, 0, rows], whole_rows_ref[field, 1, rows]),
    )


def pack_lines(flags, part_ref, part_rows_ref, even_ref, odd_ref):
    size_x = part_ref.shape[1] - 2
    depth = even_ref.shape[1] // size_x
    for field in range(2):
        pairs = line_pairs(
            part_ref, part_rows_ref, field, slice(1, size_x + 1), slice(ROW0, ROW0 + size_x), depth
        )
        for line, (to_low, to_high) in enumerate(pairs):
            place = slice(line * size_x, (line + 1) * size_x)
            even_ref[field, place] = chosen(flags, EVEN_Y, to_high, to_low)
            odd_ref[field, place] = chosen(flags, EVEN_Y, to_low, to_high)


def unpack_lines(flags, lines_refs, ends_refs, out_ref, field):
    size_x = out_ref.shape[2] - 8
    depth = lines_refs[0].shape[1] // size_x
    blank = jnp.zeros((8, out_ref.shape[3]), F32)
    for side, flag, (even, odd) in ((0, LOW_Y, (1, 0)), (1, HIGH_Y, (0, 1))):
        lines = keep(flags, flag, chosen(flags, EVEN_Y, lines_refs[even][field], lines_refs[odd][field]))
        ends = keep(flags, flag, chosen(flags, EVEN_Y, ends_refs[even][field], ends_refs[odd][field]))
        for line in range(depth):
            out_ref[side, line, 0:8] = blank
            out_ref[side, line, size_x : size_x + 8] = blank
            out_ref[side, line, ROW0 : ROW0 + size_x] = lines[line * size_x : (line + 1) * size_x]
            if depth == 3:
                out_ref[side, line, ROW0 - 2 : ROW0 + 1] = ends[8 * line : 8 * line + 3]
                out_ref[side, line, ROW0 + size_x - 1 : ROW0 + size_x + 2] = ends[8 * line + 3 : 8 * line + 6]
            elif line == 1:
                out_ref[side, line, ROW0 - 1 : ROW0] = ends[0:1]
                out_ref[side, line, ROW0 + size_x : ROW0 + size_x + 1] = ends[1:2]


def divisor_kernel(conductance_ref, capacity_ref, zones_ref, inverse_ref):
    size_x, size_y, size_z = zones_ref.shape
    boxes = size_x // BOX
    lines = []
    for table_ref, which in ((capacity_ref, 0), (capacity_ref, 1), (conductance_ref, 0), (conductance_ref, 1)):
        entries = entries_of(table_ref, which, size_z)
        for box in range(boxes):
            total = jnp.zeros((size_y, size_z), F32)
            for x in range(box * BOX, (box + 1) * BOX):
                zone = zones_ref[x]
                value = jnp.broadcast_to(entries[0], zone.shape)
                for label in range(1, len(entries)):
                    value = jnp.where(zone == label, entries[label], value)
                total = total + value
            lines.append(jnp.sum(total, axis=0, keepdims=True))
    sums = jnp.concatenate(lines, axis=0)
    modes, lanes = inverse_ref.shape[1:]
    cell = lax.broadcasted_iota(jnp.int32, (size_z, lanes), 0)
    lane = lax.broadcasted_iota(jnp.int32, (size_z, lanes), 1)
    spread = jnp.zeros((size_z, lanes), F32)
    for box in range(size_z // BOX):
        here = (cell >= box * BOX) & (cell < (box + 1) * BOX) & (lane >= box * SPAN) & (lane < (box + 1) * SPAN)
        spread = jnp.where(here, 1.0 / BOX**3, spread)
    means = jnp.dot(sums, spread, preferred_element_type=F32, precision=lax.Precision.HIGHEST)
    eigen = [float(value) for value in eigenvalues()]
    row = lax.broadcasted_iota(jnp.int32, (modes, 128), 0)
    first = jnp.zeros(row.shape, jnp.int32)
    for mode in range(1, SPAN):
        first = first + (row >= mode * SPAN).astype(jnp.int32)
    second = row - SPAN * first
    pair = jnp.zeros(row.shape, F32)
    for mode in range(SPAN):
        pair = pair + jnp.where(first == mode, eigen[mode], 0.0) + jnp.where(second == mode, eigen[mode], 0.0)
    lane = lax.broadcasted_iota(jnp.int32, (8, lanes), 1)
    for box in range(1, size_z // BOX):
        lane = lane - SPAN * (lax.broadcasted_iota(jnp.int32, (8, lanes), 1) >= box * SPAN).astype(jnp.int32)
    third = jnp.zeros(lane.shape, F32)
    for mode in range(SPAN):
        third = jnp.where(lane == mode, eigen[mode], third)
    summed = jnp.concatenate([pair, pair[:, : lanes - 128]], axis=1) + third[0:1]
    half = 2 * boxes
    for combo in range(half):
        cbar = means[combo : combo + 1]
        kbar = means[half + combo : half + combo + 1]
        inverse_ref[combo] = 1.0 / (cbar + kbar * summed)


def edge_layers_kernel(mesh, load_hbm, zones_hbm, even_ref, odd_ref, load_ref, zones_ref, sems):
    last = zones_hbm.shape[0] - 1
    copies = [
        pltpu.make_async_copy(load_hbm.at[:, 0], load_ref.at[0], sems.at[0]),
        pltpu.make_async_copy(load_hbm.at[:, last], load_ref.at[1], sems.at[1]),
        pltpu.make_async_copy(zones_hbm.at[pl.ds(0, 2)], zones_ref.at[0], sems.at[2]),
        pltpu.make_async_copy(zones_hbm.at[pl.ds(last - 1, 2)], zones_ref.at[1], sems.at[3]),
    ]
    for copy in copies:
        copy.start()
    flags = standing(mesh)
    for copy in copies:
        copy.wait()
    for channel in range(4):
        if channel < 2:
            low, high = load_ref[0, channel], load_ref[1, channel]
        else:
            low, high = zones_ref[0, channel - 2].astype(F32), zones_ref[1, channel - 2].astype(F32)
        even_ref[channel] = chosen(flags, EVEN_X, high, low)
        odd_ref[channel] = chosen(flags, EVEN_X, low, high)


def fetched_kernel(load_ref, zones_ref, token_ref):
    token_ref[...] = load_ref[0, 0, 0:8] + zones_ref[0, 0:8].astype(F32)


def edge_lines_kernel(mesh, load_ref, zones_ref, token_ref, first_ref, second_ref, even_ref, odd_ref):
    flags = standing(mesh)
    size_x, size_y = zones_ref.shape[:2]
    from_low = chosen(flags, EVEN_X, second_ref[...], first_ref[...])
    from_high = chosen(flags, EVEN_X, first_ref[...], second_ref[...])

    def put(row, to_low, to_high):
        place = slice(row, row + to_low.shape[0])
        even_ref[place] = chosen(flags, EVEN_Y, to_high, to_low)
        odd_ref[place] = chosen(flags, EVEN_Y, to_low, to_high)

    def put_end(row, layer, near, far):
        put(4 * size_x + row, layer[near : near + 1], layer[far : far + 1])

    blank = jnp.zeros((8, even_ref.shape[1]), F32)
    put(4 * size_x + 8, blank, blank)
    for field in range(2):
        put(field * size_x, load_ref[field, :, 0], load_ref[field, :, size_y - 1])
        put_end(2 * field, keep(flags, LOW_X, from_low[field]), 0, size_y - 1)
        put_end(2 * field + 1, keep(flags, HIGH_X, from_high[field]), 0, size_y - 1)
    for line in range(2):
        far = size_y - 2 + line
        put((2 + line) * size_x, zones_ref[:, line].astype(F32), zones_ref[:, far].astype(F32))
        for depth in range(2):
            put_end(4 + 4 * line + depth, from_low[2 + depth], line, far)
            put_end(6 + 4 * line + depth, from_high[2 + depth], line, far)


def entries_of(ref, row, size_z):
    return [
        jnp.broadcast_to(ref[row : row + 1, label : label + 1], (1, size_z)) for label in range(ref.shape[1])
    ]


def tables(conductance_ref, capacity_ref, coupling_ref, size_z):
    halves_of = [[0.5 * entry for entry in entries_of(conductance_ref, field, size_z)] for field in range(2)]
    masses = [entries_of(capacity_ref, field, size_z) for field in range(2)]
    shares = entries_of(coupling_ref, 0, size_z)
    masses.append([share * jnp.sqrt(one * two) for share, one, two in zip(shares, *masses)])
    return halves_of, masses


def looked_up(entries, zone):
    value = jnp.broadcast_to(entries[0], zone.shape)
    for label in range(1, len(entries)):
        value = jnp.where(zone == float(label), entries[label], value)
    return value


def coefficient_kernel(
    mesh, conductance_ref, capacity_ref, coupling_ref, zones_ref, first_x, second_x,
    half_ref, mass_ref, face_ref, table_ref,
):
    flags = standing(mesh)
    size_x, size_y, size_z = zones_ref.shape
    halves_of, masses = tables(conductance_ref, capacity_ref, coupling_ref, size_z)
    for which, entries in enumerate(halves_of + masses):
        for label, entry in enumerate(entries):
            table_ref[which, label : label + 1] = jnp.broadcast_to(entry, (1, size_z))
    low_x = chosen(flags, EVEN_X, second_x[2:4], first_x[2:4])
    high_x = chosen(flags, EVEN_X, first_x[2:4], second_x[2:4])
    inside = slice(8, 8 + size_y)
    for x in range(-2, size_x + 2):
        if x < 0:
            zone = low_x[x + 2]
        elif x >= size_x:
            zone = high_x[x - size_x]
        else:
            zone = zones_ref[x].astype(F32)
        for field in range(2):
            half_ref[field, x + 2, inside] = looked_up(halves_of[field], zone)
        if -1 <= x <= size_x:
            for which in range(3):
                mass_ref[which, x + 1] = looked_up(masses[which], zone)
    for field in range(2):
        for outer in (0, 1):
            half_ref[field, outer, inside] = chosen(
                flags, LOW_X, half_ref[field, outer, inside], half_ref[field, 2, inside]
            )
            place = size_x + 2 + outer
            half_ref[field, place, inside] = chosen(
                flags, HIGH_X, half_ref[field, place, inside], half_ref[field, size_x + 1, inside]
            )
    for field in range(2):
        for x in range(0, size_x + 2, 2):
            faces = faces_z(half_ref[field, x + 1 : x + 3, inside])
            for way in range(2):
                face_ref[field, way, x : x + 2] = faces[way]


def coefficient_lines_kernel(
    mesh, old_half_ref, mass_ref, face_ref, table_ref, first_y, second_y, after_ref,
    half_ref, half_rows_ref, mass_rows_ref, face_rows_ref, line_ref,
):
    flags = standing(mesh)
    size_x, size_y, size_z = mass_ref.shape[1] - 2, mass_ref.shape[2], mass_ref.shape[3]
    rows_of = [[table_ref[which, label : label + 1] for label in range(table_ref.shape[1])] for which in range(5)]
    halves_of, masses = rows_of[:2], rows_of[2:]
    for side, (even, odd) in enumerate(((second_y, first_y), (first_y, second_y))):
        came = chosen(flags, EVEN_Y, even[2 * size_x :], odd[2 * size_x :])
        lines, ends = (came[:size_x], came[size_x : 2 * size_x]), came[2 * size_x :]
        for line in range(2):
            place = 2 * side + line
            line_ref[place, 0:8] = jnp.zeros((8, size_z), F32)
            line_ref[place, size_x : size_x + 8] = jnp.zeros((8, size_z), F32)
            line_ref[place, ROW0 - 2 : ROW0] = ends[4 + 4 * line : 6 + 4 * line]
            line_ref[place, ROW0 : ROW0 + size_x] = lines[line]
            line_ref[place, ROW0 + size_x : ROW0 + size_x + 2] = ends[6 + 4 * line : 8 + 4 * line]
    count = half_rows_ref.shape[2]
    position = lax.broadcasted_iota(jnp.int32, (count, size_z), 0)
    for line, flag in enumerate((LOW_Y, LOW_Y, HIGH_Y, HIGH_Y)):
        zone = line_ref[line]
        for field in range(2):
            value = looked_up(halves_of[field], zone)
            below = value[ROW0 : ROW0 + 1]
            above = value[ROW0 + size_x - 1 : ROW0 + size_x]
            value = jnp.where((position < ROW0) & (flags[LOW_X] == 0), below, value)
            value = jnp.where((position >= ROW0 + size_x) & (flags[HIGH_X] == 0), above, value)
            near = old_half_ref[field, :, 8 if flag == LOW_Y else 8 + size_y - 1]
            half_rows_ref[field, line] = value
            half_rows_ref[field, line, ROW0 - 2 : ROW0 + size_x + 2] = chosen(
                flags, flag, half_rows_ref[field, line, ROW0 - 2 : ROW0 + size_x + 2], near
            )
            if line in (1, 2):
                row = 7 if line == 1 else 8 + size_y
                half_ref[field, :, row] = half_rows_ref[field, line, ROW0 - 2 : ROW0 + size_x + 2]
        if line in (1, 2):
            for which in range(3):
                mass_rows_ref[which, line - 1] = looked_up(masses[which], zone)
    for field in range(2):
        for side in range(2):
            faces = faces_z(half_rows_ref[field, side + 1])
            for way in range(2):
                face_rows_ref[field, way, side] = faces[way]
        for line, row in ((4, 0), (5, size_y - 1), (6, 1), (7, size_y - 2)):
            half_rows_ref[field, line] = jnp.zeros((count, size_z), F32)
            half_rows_ref[field, line, ROW0 - 2 : ROW0 + size_x + 2] = old_half_ref[field, :, 8 + row]
    for line, row in ((2, 0), (3, size_y - 1)):
        spread = slice(ROW0 - 1, ROW0 + size_x + 1)
        for which in range(3):
            mass_rows_ref[which, line] = jnp.zeros((count, size_z), F32)
            mass_rows_ref[which, line, spread] = mass_ref[which, :, row]
        for field in range(2):
            for way in range(2):
                face_rows_ref[field, way, line] = jnp.zeros((count, size_z), F32)
                face_rows_ref[field, way, line, spread] = face_ref[field, way, :, row]


def own_transform_kernel(load_ref, forward_ref, spectral_ref, field_ref, before_ref):
    size_x = load_ref.shape[1]
    for field in range(2):
        field_ref[field, 0] = jnp.zeros(load_ref.shape[2:], F32)
        field_ref[field, 1 : 1 + size_x] = load_ref[field]
        field_ref[field, 1 + size_x] = jnp.zeros(load_ref.shape[2:], F32)
    forward_own(field_ref, forward_ref, before_ref, spectral_ref)


def first_solve_kernel(
    mesh, spectral_ref, mass_ref, first_x, second_x, first_y, second_y, inverse_ref, c2, c3, ends_ref, edges_ref,
    after_ref, even_ref, odd_ref, rows_ref, before_ref,
):
    flags = standing(mesh)
    size_x, size_y, size_z = mass_ref.shape[1] - 2, mass_ref.shape[2], mass_ref.shape[3]
    boxes = size_x // BOX
    blank = jnp.zeros((size_y, size_z), F32)
    spectral = []
    for field in range(2):
        low = keep(flags, LOW_X, chosen(flags, EVEN_X, second_x[field], first_x[field]))
        high = keep(flags, HIGH_X, chosen(flags, EVEN_X, first_x[field], second_x[field]))
        for side, flag, even, odd in ((0, LOW_Y, second_y, first_y), (1, HIGH_Y, first_y, second_y)):
            place, after = slice(field * size_x, (field + 1) * size_x), slice(4 * size_x, 4 * size_x + 8)
            line = keep(flags, flag, chosen(flags, EVEN_Y, even[place], odd[place]))
            ends = keep(flags, flag, chosen(flags, EVEN_Y, even[after], odd[after]))
            rows_ref[field, side, 0:8] = blank[0:8]
            rows_ref[field, side, size_x : size_x + 8] = blank[0:8]
            rows_ref[field, side, ROW0 - 1 : ROW0] = ends[2 * field : 2 * field + 1]
            rows_ref[field, side, ROW0 : ROW0 + size_x] = line
            rows_ref[field, side, ROW0 + size_x : ROW0 + size_x + 1] = ends[2 * field + 1 : 2 * field + 2]
        for box in range(boxes):
            parts = [low if box == 0 else blank, high if box == boxes - 1 else blank]
            parts += [rows_ref[field, side, box * BOX : box * BOX + 24] for side in range(2)]
            stacked(before_ref.at[field], slice(box * size_z, (box + 1) * size_z), parts)
    for field in range(2):
        spectral.append(spectral_ref[field] + dot(ends_ref[...], before_ref[field]))
    solve(spectral, inverse_ref, (c2, c3), after_ref)
    pack_x(flags, after_ref, edges_ref, even_ref, odd_ref)


def merge_x_kernel(mesh, part_ref, part_rows_ref, first_ref, second_ref, whole_ref, whole_rows_ref, even_ref, odd_ref):
    flags = standing(mesh)
    size_x = part_ref.shape[1] - 2
    size_y, size_z = part_ref.shape[2:]
    depth = x_depth(first_ref)
    end = ROW0 + size_x
    for field in range(2):
        low = keep(flags, LOW_X, chosen(flags, EVEN_X, second_ref[field], first_ref[field]))
        high = keep(flags, HIGH_X, chosen(flags, EVEN_X, first_ref[field], second_ref[field]))
        low_layers, high_layers = [
            [came[layer * size_y : (layer + 1) * size_y] for layer in range(depth)] for came in (low, high)
        ]
        whole_ref[field, 1] = keep(flags, LOW_X, part_ref[field, 0]) + low_layers[depth - 2]
        whole_ref[field, 2] = part_ref[field, 1] + low_layers[depth - 1]
        whole_ref[field, 3 : size_x + 1] = part_ref[field, 2:size_x]
        whole_ref[field, size_x + 1] = part_ref[field, size_x] + high_layers[0]
        whole_ref[field, size_x + 2] = keep(flags, HIGH_X, part_ref[field, size_x + 1]) + high_layers[1]
        whole_ref[field, 0] = low_layers[0] if depth == 3 else jnp.zeros((size_y, size_z), F32)
        whole_ref[field, size_x + 3] = high_layers[2] if depth == 3 else jnp.zeros((size_y, size_z), F32)
        for side in range(2):
            start = depth * (size_y + side)
            low_row, high_row = [
                [came[start + layer : start + layer + 1] for layer in range(depth)] for came in (low, high)
            ]
            edge = ROW0 - 1
            whole_rows_ref[field, side] = part_rows_ref[field, side]
            whole_rows_ref[field, side, edge : edge + 1] = (
                keep(flags, LOW_X, part_rows_ref[field, side, edge : edge + 1]) + low_row[depth - 2]
            )
            whole_rows_ref[field, side, edge + 1 : edge + 2] = (
                part_rows_ref[field, side, edge + 1 : edge + 2] + low_row[depth - 1]
            )
            whole_rows_ref[field, side, end - 1 : end] = part_rows_ref[field, side, end - 1 : end] + high_row[0]
            whole_rows_ref[field, side, end : end + 1] = (
                keep(flags, HIGH_X, part_rows_ref[field, side, end : end + 1]) + high_row[1]
            )
            if depth == 3:
                whole_rows_ref[field, side, edge - 1 : edge] = low_row[0]
                whole_rows_ref[field, side, end + 1 : end + 2] = high_row[2]

        base = 2 * size_x if depth == 2 else 0
        for ref in (even_ref, odd_ref):
            ref[field, base:] = jnp.zeros((ref.shape[1] - base, size_z), F32)
        if base:
            own, rows = slice(2, size_x + 2), slice(ROW0, ROW0 + size_x)
            pairs = line_pairs(whole_ref, whole_rows_ref, field, own, rows, depth)
            for line, (to_low, to_high) in enumerate(pairs):
                place = slice(line * size_x, (line + 1) * size_x)
                even_ref[field, place] = chosen(flags, EVEN_Y, to_high, to_low)
                odd_ref[field, place] = chosen(flags, EVEN_Y, to_low, to_high)
            for row, x in ((base, -1), (base + 1, size_x)):
                pairs = line_pairs(
                    whole_ref, whole_rows_ref, field, slice(x + 2, x + 3), slice(x + ROW0, x + ROW0 + 1), depth
                )
                even_ref[field, row : row + 1] = chosen(flags, EVEN_Y, pairs[1][1], pairs[1][0])
                odd_ref[field, row : row + 1] = chosen(flags, EVEN_Y, pairs[1][0], pairs[1][1])
            continue
        for start, x in ((base, -2), (base + 3, size_x - 1)):
            layers, rows = slice(x + 2, x + 5), slice(x + ROW0, x + ROW0 + 3)
            pairs = line_pairs(whole_ref, whole_rows_ref, field, layers, rows, depth)
            for line, (to_low, to_high) in enumerate(pairs):
                place = slice(8 * line + start, 8 * line + start + 3)
                even_ref[field, place] = chosen(flags, EVEN_Y, to_high, to_low)
                odd_ref[field, place] = chosen(flags, EVEN_Y, to_low, to_high)


def faces_z(half):
    size_z, axis = half.shape[-1], half.ndim - 1
    lane = lax.broadcasted_iota(jnp.int32, half.shape, axis)
    upper = half + jnp.where(lane == size_z - 1, half, pltpu.roll(half, size_z - 1, axis))
    lower = half + jnp.where(lane == 0, half, pltpu.roll(half, 1, axis))
    return upper, lower


def along_z(value, upper, lower):
    size_z, axis = value.shape[-1], value.ndim - 1
    lane = lax.broadcasted_iota(jnp.int32, value.shape, axis)
    above = jnp.where(lane == size_z - 1, 0.0, pltpu.roll(value, size_z - 1, axis))
    below = jnp.where(lane == 0, 0.0, pltpu.roll(value, 1, axis))
    return upper * (value - above) + lower * (value - below)


def operate(field_ref, half_ref, mass_ref, face_ref, x, count):
    size_y = mass_ref.shape[2]
    inside = slice(8, 8 + size_y)
    masses = slice(x + 1, x + 1 + count)
    here = slice(x + 2, x + 2 + count)
    values, images = [], []
    for field in range(2):
        value = field_ref[field, here, inside]
        half = half_ref[field, here, inside]
        flux = along_z(value, face_ref[field, 0, masses], face_ref[field, 1, masses])
        for start in (x + 1, x + 3):
            place = slice(start, start + count)
            flux = flux + (half + half_ref[field, place, inside]) * (value - field_ref[field, place, inside])
        for shift in (-1, 1):
            moved = slice(8 + shift, 8 + shift + size_y)
            flux = flux + (half + half_ref[field, here, moved]) * (value - field_ref[field, here, moved])
        values.append(value)
        images.append(flux)
    first = mass_ref[0, masses] * values[0] + mass_ref[2, masses] * values[1] + images[0]
    second = mass_ref[2, masses] * values[0] + mass_ref[1, masses] * values[1] + images[1]
    return values, (first, second)


def merge_x_after_kernel(mesh, part_ref, part_rows_ref, first_ref, second_ref, sums_ref, *outs):
    merge_x_kernel(mesh, part_ref, part_rows_ref, first_ref, second_ref, *outs)


def fill(flags, whole_ref, whole_rows_ref, value_ref):
    size_x, size_y = whole_ref.shape[1] - 4, whole_ref.shape[2]
    spread = slice(ROW0 - 2, ROW0 + size_x + 2)
    for field in range(2):
        value_ref[field, :, 8 : 8 + size_y] = whole_ref[field]
        value_ref[field, :, 7] = keep(flags, LOW_Y, whole_rows_ref[field, 0, spread])
        value_ref[field, :, 8 + size_y] = keep(flags, HIGH_Y, whole_rows_ref[field, 1, spread])


def line_image(values, outers, inners, half_lines, places, mass_lines, face_lines, place):
    center, outer, inner = places
    images = []
    for field in range(2):
        value, half = values[field], half_lines[field, center]
        count = value.shape[0]
        flux = along_z(value, face_lines[field, 0, place], face_lines[field, 1, place])
        for turn in (1, count - 1):
            flux = flux + (half + pltpu.roll(half, turn, 0)) * (value - pltpu.roll(value, turn, 0))
        flux = flux + (half + half_lines[field, outer]) * (value - outers[field])
        flux = flux + (half + half_lines[field, inner]) * (value - inners[field])
        images.append(flux)
    first = mass_lines[0, place] * values[0] + mass_lines[2, place] * values[1] + images[0]
    second = mass_lines[2, place] * values[0] + mass_lines[1, place] * values[1] + images[1]
    return first, second


SIDES = (((4, 1, 6, 0), (2, 0)), ((5, 2, 7, 3), (3, 1)))


def line_changes(delta, outer, half_lines, mass_lines, face_lines, side):
    (edge, out, inner, _), (place, _) = SIDES[side]
    nothing = [jnp.zeros_like(line) for line in delta]
    at_edge = line_image(delta, outer, nothing, half_lines, (edge, out, inner), mass_lines, face_lines, place)
    at_next = [-(half_lines[field, edge] + half_lines[field, inner]) * delta[field] for field in range(2)]
    return at_edge, at_next


def own_image_kernel(
    mesh, whole_ref, whole_rows_ref, half_ref, mass_ref, face_ref, forward_ref, image_ref, spectral_ref,
    value_ref, before_ref,
):
    flags = standing(mesh)
    size_x = whole_ref.shape[1] - 4
    fill(flags, whole_ref, whole_rows_ref, value_ref)
    for x, flag in ((-1, LOW_X), (size_x, HIGH_X)):
        _, images = operate(value_ref, half_ref, mass_ref, face_ref, x, 1)
        for field in range(2):
            image_ref[field, x + 1 : x + 2] = keep(flags, flag, images[field])
    for x in range(0, size_x, CHUNK):
        _, images = operate(value_ref, half_ref, mass_ref, face_ref, x, CHUNK)
        for field in range(2):
            image_ref[field, x + 1 : x + 1 + CHUNK] = images[field]
    forward_own(image_ref, forward_ref, before_ref, spectral_ref)


def second_solve_kernel(
    mesh, whole_ref, whole_rows_ref, first_lines, second_lines, first_ends, second_ends,
    half_lines, mass_lines, face_lines, spectral_ref, inverse_ref, c2, c3, lines_ref, edges_ref,
    deltas_ref, changes_ref, after_ref, even_ref, odd_ref, came_ref, near, before_ref,
):
    flags = standing(mesh)
    size_x, size_y, size_z = whole_ref.shape[1] - 4, whole_ref.shape[2], whole_ref.shape[3]
    boxes = size_x // BOX
    count = near.shape[2]
    position = lax.broadcasted_iota(jnp.int32, (count, size_z), 0)
    begin = jnp.where(flags[LOW_X] > 0, ROW0 - 1, ROW0)
    end = jnp.where(flags[HIGH_X] > 0, ROW0 + size_x + 1, ROW0 + size_x)
    valid = (position >= begin) & (position < end)
    for field in range(2):
        unpack_lines(flags, (first_lines, second_lines), (first_ends, second_ends), came_ref.at[field], field)
        for side, row in ((0, 0), (1, size_y - 1)):
            near[field, side] = jnp.zeros((count, size_z), F32)
            near[field, side, ROW0 - 2 : ROW0 + size_x + 2] = whole_ref[field, :, row]
    for side, flag, order in ((0, LOW_Y, (2, 1, 0)), (1, HIGH_Y, (0, 1, 2))):
        delta, outer, far = [[came_ref[field, side, line] for field in range(2)] for line in order]
        at_edge, at_next = line_changes(delta, outer, half_lines, mass_lines, face_lines, side)
        (edge, out, _, beyond), (_, place) = SIDES[side]
        at_outer = line_image(
            [keep(flags, flag, whole_rows_ref[field, side]) + outer[field] for field in range(2)],
            far,
            [near[field, side] + delta[field] for field in range(2)],
            half_lines,
            (out, beyond, edge),
            mass_lines,
            face_lines,
            place,
        )
        for field in range(2):
            deltas_ref[field, side] = delta[field]
            changes_ref[field, 3 * side] = jnp.where(valid, at_edge[field], 0.0)
            changes_ref[field, 1 + side] = jnp.where(valid, at_next[field], 0.0)
            changes_ref[field, 4 + side] = keep(flags, flag, jnp.where(valid, at_outer[field], 0.0))
    spectral = []
    for field in range(2):
        for box in range(boxes):
            parts = [changes_ref[field, line, box * BOX : box * BOX + 24] for line in range(6)]
            stacked(before_ref.at[field], slice(box * size_z, (box + 1) * size_z), parts)
    for field in range(2):
        spectral.append(spectral_ref[field] + dot(lines_ref[...], before_ref[field]))
    solve(spectral, inverse_ref, (c2, c3), after_ref)
    pack_x(flags, after_ref, edges_ref, even_ref, odd_ref)


def first_sums_kernel(load_ref, whole_ref, image_ref, deltas_ref, changes_ref, precond_ref, out_ref, sums_ref):
    size_x, size_y, size_z = load_ref.shape[1:]
    rows = slice(ROW0, ROW0 + size_x)
    total_a = total_b = jnp.zeros((size_y, size_z), F32)
    for field in range(2):
        precond_ref[field] = whole_ref[field, 2 : size_x + 2]
        out_ref[field] = image_ref[field, 1 : size_x + 1]
        for side, row in ((0, 0), (1, size_y - 1)):
            precond_ref[field, :, row] = precond_ref[field, :, row] + deltas_ref[field, side, rows]
        for line, row in enumerate((0, 1, size_y - 2, size_y - 1)):
            out_ref[field, :, row] = out_ref[field, :, row] + changes_ref[field, line, rows]
        for x in range(size_x):
            total_a = total_a + load_ref[field, x] * precond_ref[field, x]
            total_b = total_b + out_ref[field, x] * precond_ref[field, x]
    sums_ref[0:1] = jnp.sum(total_a, axis=0, keepdims=True)
    sums_ref[1:2] = jnp.sum(total_b, axis=0, keepdims=True)
    sums_ref[2:8] = jnp.zeros((6, size_z), F32)


def own_second_image_kernel(
    mesh, whole_ref, whole_rows_ref, half_ref, mass_ref, face_ref, old_image_ref, image_ref, sums_ref, value_ref
):
    flags = standing(mesh)
    size_x, size_y, size_z = old_image_ref.shape[1:]
    fill(flags, whole_ref, whole_rows_ref, value_ref)
    total_c = total_d = jnp.zeros((CHUNK, size_y, size_z), F32)
    for x in range(0, size_x, CHUNK):
        chunk = slice(x, x + CHUNK)
        values, images = operate(value_ref, half_ref, mass_ref, face_ref, x, CHUNK)
        for field in range(2):
            image_ref[field, chunk] = images[field]
            total_c = total_c + old_image_ref[field, chunk] * values[field]
            total_d = total_d + images[field] * values[field]
    sums_ref[0:1] = jnp.sum(jnp.sum(total_c, axis=0), axis=0, keepdims=True)
    sums_ref[1:2] = jnp.sum(jnp.sum(total_d, axis=0), axis=0, keepdims=True)
    sums_ref[2:8] = jnp.zeros((6, size_z), F32)


def second_image_kernel(
    mesh, whole_ref, image_ref, first_ref, second_ref,
    half_lines, mass_lines, face_lines, old_image_ref, old_sums_ref, own_sums_ref,
    deltas_ref, changes_ref, sums_ref, came_ref,
):
    flags = standing(mesh)
    size_x, size_y, size_z = old_image_ref.shape[1:]
    own = slice(2, size_x + 2)
    rows = slice(ROW0, ROW0 + size_x)
    total_c = total_d = jnp.zeros((size_x, size_z), F32)
    lines_refs = [ref.at[:, pl.ds(0, 2 * size_x)] for ref in (first_ref, second_ref)]
    ends_refs = [ref.at[:, pl.ds(2 * size_x, 8)] for ref in (first_ref, second_ref)]
    for field in range(2):
        unpack_lines(flags, lines_refs, ends_refs, came_ref.at[field], field)
    for side, row, beside in ((0, 0, 1), (1, size_y - 1, size_y - 2)):
        outer, delta = [[came_ref[field, side, line] for field in range(2)] for line in range(2)]
        at_edge, at_next = line_changes(delta, outer, half_lines, mass_lines, face_lines, side)
        for field in range(2):
            changed, edge, inner = delta[field][rows], at_edge[field][rows], at_next[field][rows]
            deltas_ref[field, side] = changed
            changes_ref[field, 3 * side] = edge
            changes_ref[field, 1 + side] = inner
            total_c = total_c + old_image_ref[field, :, row] * changed
            total_d = total_d + (image_ref[field, :, row] + edge) * changed
            total_d = total_d + whole_ref[field, own, row] * edge + whole_ref[field, own, beside] * inner
    totals = [
        jnp.sum(old_sums_ref[0:1], axis=1, keepdims=True),
        jnp.sum(old_sums_ref[1:2], axis=1, keepdims=True),
        jnp.sum(jnp.sum(total_c, axis=0, keepdims=True) + own_sums_ref[0:1], axis=1, keepdims=True),
        jnp.sum(jnp.sum(total_d, axis=0, keepdims=True) + own_sums_ref[1:2], axis=1, keepdims=True),
    ]
    lane = lax.broadcasted_iota(jnp.int32, sums_ref.shape, 1)
    spread = jnp.zeros(sums_ref.shape, F32)
    for place, total in enumerate(totals):
        spread = jnp.where(lane == place, total, spread)
    sums_ref[...] = spread


def finish_kernel(
    sums_ref, load_ref, z_ref, q_ref, w_ref, s_ref, deltas_ref, changes_ref,
    solution_hbm, residual_hbm, solution_ref, residual_ref, sems,
):
    line = jnp.sum(sums_ref[...], axis=0, keepdims=True)
    lane = lax.broadcasted_iota(jnp.int32, line.shape, 1)
    rz, zq, qw, ws = [jnp.sum(jnp.where(lane == place, line, 0.0), axis=1, keepdims=True) for place in range(4)]
    alpha = rz / zq
    rz_next = rz - alpha * (2.0 * zq) + alpha * alpha * qw
    grown = 1.0 + rz_next / rz
    curvature = grown * grown * zq - 2.0 * grown * alpha * qw + alpha * alpha * ws
    alpha_next = rz_next / curvature
    along = alpha + alpha_next * grown
    against = alpha_next * alpha
    copies = []
    step = load_ref.shape[1] // 2
    for field in range(2):
        for start in range(0, 2 * step, step):
            part = pl.ds(start, step)
            for x in range(start, start + step):
                solution_ref[field, x] = along * z_ref[field, x] - against * w_ref[field, x + 2]
                residual_ref[field, x] = load_ref[field, x] - along * q_ref[field, x] + against * s_ref[field, x]
            size_y = load_ref.shape[2]
            chunk = slice(start, start + step)
            for side, row in ((0, 0), (1, size_y - 1)):
                solution_ref[field, chunk, row] = (
                    solution_ref[field, chunk, row] - against * deltas_ref[field, side, chunk]
                )
            for line, row in enumerate((0, 1, size_y - 2, size_y - 1)):
                residual_ref[field, chunk, row] = (
                    residual_ref[field, chunk, row] + against * changes_ref[field, line, chunk]
                )
            for here, there in ((solution_ref, solution_hbm), (residual_ref, residual_hbm)):
                copies.append(
                    pltpu.make_async_copy(here.at[field, part], there.at[field, part], sems.at[len(copies)])
                )
                copies[-1].start()
    for copy in copies:
        copy.wait()


VMEM = pl.BlockSpec(memory_space=pltpu.VMEM)
HBM = pl.BlockSpec(memory_space=pltpu.HBM)


def call(mesh, kernel, scalars, arrays, outs, scratch=(), flops=0, limit=24, in_hbm=False, outs_in_hbm=False, aliases=()):
    moved = sum(math.prod(a.shape) * a.dtype.itemsize for a in list(arrays) + list(outs))
    return pl.pallas_call(
        kernel if mesh is None else functools.partial(kernel, mesh),
        out_shape=tuple(outs),
        in_specs=[VMEM] * len(scalars) + [HBM if in_hbm else VMEM] * len(arrays),
        out_specs=tuple([HBM if outs_in_hbm else VMEM] * len(outs)),
        scratch_shapes=list(scratch),
        input_output_aliases=dict(aliases),
        compiler_params=pltpu.CompilerParams(vmem_limit_bytes=int(limit * 1024 * 1024)),
        cost_estimate=pl.CostEstimate(flops=flops, bytes_accessed=moved, transcendentals=0),
    )(*scalars, *arrays)


def shards(mesh, load, zones, conductance, capacity, coupling):
    size_x, size_y, size_z = zones.shape
    assert size_x % BOX == 0 and size_y == BOX and size_z % BOX == 0
    boxes = size_x // BOX
    count = size_x + 8
    sds = lambda *shape: jax.ShapeDtypeStruct(shape, F32)
    forward, back, line_forward, line_back, ends_forward, lines_forward, edges_back = [
        jnp.asarray(c) for c in constants(size_z)
    ]
    consts = (line_forward, line_back)
    modes, lanes = forward.shape[0], size_z // BOX * SPAN
    assert size_z == 128
    packed = call(
        mesh,
        edge_layers_kernel,
        [],
        [load, zones],
        [sds(4, size_y, size_z)] * 2,
        [
            pltpu.VMEM((2, 2, size_y, size_z), F32),
            pltpu.VMEM((2, 2, size_y, size_z), zones.dtype),
            pltpu.SemaphoreType.DMA((4,)),
        ],
        in_hbm=True,
        limit=53.75,
    )
    (token,) = call(None, fetched_kernel, [], [load, zones], [sds(8, size_z)])
    x_halo = swap(mesh, "gx", *packed)
    (inverse,) = call(
        None,
        divisor_kernel,
        [conductance, capacity],
        [zones],
        [sds(2 * boxes, modes, lanes)],
        flops=40_000_000,
    )
    packed = call(mesh, edge_lines_kernel, [], [load, zones, token, *x_halo], [sds(4 * size_x + 16, size_z)] * 2)
    y_halo = swap(mesh, "gy", *packed)
    laws = [conductance, capacity, coupling[None]]
    padded_shape = sds(2, size_x + 4, size_y + 16, size_z)
    half, mass, face, table = call(
        mesh,
        coefficient_kernel,
        laws,
        [zones, *x_halo],
        [padded_shape, sds(3, size_x + 2, size_y, size_z), sds(2, 2, size_x + 2, size_y, size_z)]
        + [sds(5, coupling.shape[0], size_z)],
        flops=20_000_000,
    )
    parts = [sds(2, size_x + 2, size_y, size_z), sds(2, 2, count, size_z)]
    packed_x = [[sds(2, round_up(depth * SPAN, 8), size_z)] * 2 for depth in (3, 2)]
    wholes = [sds(2, size_x + 4, size_y, size_z), sds(2, 2, count, size_z)]
    packed_lines = [sds(2, 3 * size_x, size_z)] * 2
    packed_ends = [sds(2, 3 * 8, size_z)] * 2
    packed_y = [sds(2, 2 * size_x + 8, size_z)] * 2
    rows = SPAN * size_y + 48
    wide = boxes * size_z
    spectrum = sds(2, modes, wide)
    stack = lambda depth: pltpu.VMEM((2, depth, wide), BF16)
    halo = pltpu.VMEM((2, size_x + 2, size_y, size_z), F32)
    padded = pltpu.VMEM((2, size_x + 4, size_y + 16, size_z), F32)
    own = sds(2, size_x, size_y, size_z)

    (spectral,) = call(None, own_transform_kernel, [], [load, forward], [spectrum], [halo, stack(3 * rows)], 700_000_000)
    stacked_cells = jax.ShapeDtypeStruct((2, 3 * rows, wide), BF16)
    after, *packed = call(
        mesh,
        first_solve_kernel,
        [],
        [spectral, mass, *x_halo, *y_halo, inverse, *consts, ends_forward, edges_back],
        [stacked_cells] + packed_x[0],
        [pltpu.VMEM((2, 2, count, size_z), F32), stack(ends_forward.shape[1])],
        2_000_000_000,
    )
    received = swap(mesh, "gx", *packed)
    part, part_rows, *packed = call(mesh, solved_kernel, [], [after, back], parts + packed_lines, (), 700_000_000)
    lines = swap(mesh, "gy", *packed)
    whole, whole_rows, *packed = call(mesh, merge_x_kernel, [], [part, part_rows, *received], wholes + packed_ends)
    ends = swap(mesh, "gy", *packed)
    half, half_lines, mass_lines, face_lines = call(
        mesh,
        coefficient_lines_kernel,
        [],
        [half, mass, face, table, *y_halo, whole_rows],
        [padded_shape, sds(2, 8, count, size_z), sds(3, 4, count, size_z), sds(2, 2, 4, count, size_z)],
        [pltpu.VMEM((4, count, size_z), F32)],
        flops=2_000_000,
        aliases={0: 0},
    )
    own_image, spectral = call(
        mesh,
        own_image_kernel,
        [],
        [whole, whole_rows, half, mass, face, forward],
        [sds(2, size_x + 2, size_y, size_z), spectrum],
        [padded, stack(3 * rows)],
        700_000_000,
    )
    deltas, changes, after, *packed = call(
        mesh,
        second_solve_kernel,
        [],
        [whole, whole_rows, *lines, *ends, half_lines, mass_lines, face_lines, spectral, inverse, *consts]
        + [lines_forward, edges_back],
        [sds(2, 2, count, size_z), sds(2, 6, count, size_z), stacked_cells] + packed_x[1],
        [
            pltpu.VMEM((2, 2, 3, count, size_z), F32),
            pltpu.VMEM((2, 2, count, size_z), F32),
            stack(lines_forward.shape[1]),
        ],
        2_000_000_000,
    )
    received = swap(mesh, "gx", *packed)
    part, part_rows = call(mesh, solved_kernel, [], [after, back], parts, (), 700_000_000)
    precond, image, sums = call(
        None, first_sums_kernel, [], [load, whole, own_image, deltas, changes], [own, own, sds(8, size_z)], flops=1_000_000
    )
    whole, whole_rows, *packed = call(
        mesh, merge_x_after_kernel, [], [part, part_rows, *received, sums], wholes + packed_y
    )
    received = swap(mesh, "gy", *packed)
    last_image, own_sums = call(
        mesh,
        own_second_image_kernel,
        [],
        [whole, whole_rows, half, mass, face, image],
        [own, sds(8, size_z)],
        [padded],
        10_000_000,
    )
    devices = mesh.shape["gx"] * mesh.shape["gy"]
    deltas, changes, sums = call(
        mesh,
        second_image_kernel,
        [],
        [whole, last_image, *received, half_lines, mass_lines, face_lines, image, sums, own_sums],
        [sds(2, 2, size_x, size_z), sds(2, 4, size_x, size_z), sds(devices, size_z)],
        [pltpu.VMEM((2, 2, 2, count, size_z), F32)],
        1_000_000,
    )
    sums = lax.all_to_all(sums, AXES, 0, 0, tiled=True)
    whole_block = pltpu.VMEM((2, size_x, size_y, size_z), F32)
    return call(
        None,
        finish_kernel,
        [],
        [sums, load, precond, image, whole, last_image, deltas, changes],
        [own, own],
        [whole_block, whole_block, pltpu.SemaphoreType.DMA((8,))],
        outs_in_hbm=True,
    )


def solution(mesh):
    in_specs = (P(None, "gx", "gy", None), P("gx", "gy", None), P(), P(), P())
    out_specs = (P(None, "gx", "gy", None), P(None, "gx", "gy", None))
    return jax.shard_map(
        functools.partial(shards, mesh), mesh=mesh, in_specs=in_specs, out_specs=out_specs, check_vma=False
    )
```

```python
import functools
import math

import jax
import jax.numpy as jnp
import ml_dtypes
import numpy as np
from jax import lax
from jax.experimental import pallas as pl
from jax.experimental.pallas import tpu as pltpu
from jax.sharding import PartitionSpec as P

BOX = 16
SPAN = BOX + 2
F32 = jnp.float32
BF16 = jnp.bfloat16
AXES = ("gx", "gy")
ROW0 = 4
EDGE_LAYERS = (0, 1, 2, SPAN - 3, SPAN - 2, SPAN - 1)
CHUNK = 4


def split(matrix):
    high = matrix.astype(ml_dtypes.bfloat16)
    low = (matrix - high.astype(np.float64)).astype(ml_dtypes.bfloat16)
    return high, low


def round_up(value, step):
    return (value + step - 1) // step * step


def sine_basis():
    index = np.arange(SPAN)
    angle = np.pi * np.outer(index + 1, index + 1) / (SPAN + 1)
    return np.sqrt(2.0 / (SPAN + 1)) * np.sin(angle)


def eigenvalues():
    return 4.0 * np.sin(np.pi * (np.arange(SPAN) + 1) / (2 * (SPAN + 1))) ** 2


def line_places(y):
    return [(x, y) if 0 <= x < SPAN else None for x in range(1 - ROW0, 25 - ROW0)]


def layer_places(x):
    return [(x, y + 1) for y in range(BOX)]


def plane_matrix(places):
    basis = sine_basis()
    modes = SPAN * SPAN
    plane = np.zeros((round_up(modes, 16), len(places)))
    for column, place in enumerate(places):
        if place is not None:
            plane[:modes, column] = np.outer(basis[:, place[0]], basis[:, place[1]]).reshape(-1)
    return plane


def three_products(matrix):
    high, low = split(matrix)
    return np.concatenate([high, high, low], axis=1)


def constants(size_z):
    basis = sine_basis()
    outer = line_places(0) + line_places(SPAN - 1)
    plane = plane_matrix(sum([layer_places(x) for x in range(SPAN)], []) + outer)
    ends = plane_matrix(layer_places(0) + layer_places(SPAN - 1) + outer)
    lines = plane_matrix(sum([line_places(y) for y in (1, 2, BOX - 1, BOX)], []) + outer)
    boxes = size_z // BOX
    line = np.zeros((size_z, boxes * SPAN))
    for box in range(boxes):
        for mode in range(SPAN):
            for offset in range(SPAN):
                cell = box * BOX + offset - 1
                if 0 <= cell < size_z:
                    line[cell, box * SPAN + mode] = basis[mode, offset]
    high, low = split(line)
    line_forward = np.concatenate([high, high, low], axis=0)
    high, low = split(line.T)
    line_inverse = np.concatenate([high, low], axis=1)
    edges = plane_matrix(sum([layer_places(x) for x in EDGE_LAYERS], []) + outer)
    return (
        three_products(plane),
        three_products(plane.T),
        line_forward,
        line_inverse,
        three_products(ends),
        three_products(lines),
        three_products(edges.T),
    )


def swap_pairs(mesh, axis, odd):
    sizes = [mesh.shape[name] for name in AXES]
    along = AXES.index(axis)
    pairs = []
    for i in range(sizes[0]):
        for j in range(sizes[1]):
            here = [i, j]
            there = [i, j]
            place = here[along]
            target = place ^ 1 if not odd else (place + 1 if place % 2 else place - 1)
            if 0 <= target < sizes[along]:
                there[along] = target
            elif along == 0:
                there[0] = sizes[0] - 1 - place
            else:
                there[0] = i ^ 1
            pairs.append((here[0] * sizes[1] + here[1], there[0] * sizes[1] + there[1]))
    return pairs


def swap(mesh, axis, even_part, odd_part):
    if axis == "gx":
        first = lax.ppermute(even_part, AXES, swap_pairs(mesh, axis, False))
        second = lax.ppermute(odd_part, AXES, swap_pairs(mesh, axis, True))
    else:
        second = lax.ppermute(odd_part, AXES, swap_pairs(mesh, axis, True))
        first = lax.ppermute(even_part, AXES, swap_pairs(mesh, axis, False))
    return first, second


EVEN_X, EVEN_Y, LOW_X, HIGH_X, LOW_Y, HIGH_Y = range(6)


def standing(mesh):
    here_x, here_y = lax.axis_index("gx"), lax.axis_index("gy")
    facts = (
        lax.rem(here_x, 2) == 0,
        lax.rem(here_y, 2) == 0,
        here_x > 0,
        here_x < mesh.shape["gx"] - 1,
        here_y > 0,
        here_y < mesh.shape["gy"] - 1,
    )
    return [fact.astype(jnp.int32) for fact in facts]


def chosen(flags, which, yes, no):
    return jnp.where(flags[which] > 0, yes, no)


def keep(flags, which, value):
    return jnp.where(flags[which] > 0, value, jnp.zeros_like(value))


def halves(value):
    high = value.astype(BF16)
    low = (value - high.astype(F32)).astype(BF16)
    return high, low


def dot(left, right):
    return jnp.dot(left, right, preferred_element_type=F32)


def store_split(stack_ref, lanes, value):
    rows = value.shape[0]
    high, low = halves(value)
    stack_ref[0:rows, lanes] = high
    stack_ref[rows : 2 * rows, lanes] = low
    stack_ref[2 * rows : 3 * rows, lanes] = high


def stacked(before_ref, lanes, parts):
    store_split(before_ref, lanes, jnp.concatenate(parts, axis=0))


def forward_own(field_ref, forward_ref, before_ref, spectral_ref):
    boxes = (field_ref.shape[1] - 2) // BOX
    size_y, size_z = field_ref.shape[2:]
    blank = jnp.zeros((48, size_z), F32)
    for field in range(2):
        for box in range(boxes):
            main = field_ref[field, box * BOX : box * BOX + SPAN].reshape(SPAN * size_y, size_z)
            stacked(before_ref.at[field], slice(box * size_z, (box + 1) * size_z), [main, blank])
    for field in range(2):
        spectral_ref[field] = dot(forward_ref[...], before_ref[field])


def solve(spectral, inverse_ref, consts, after_ref):
    line_forward_ref, line_back_ref = consts
    line_rows = line_forward_ref.shape[0] // 3
    size_z = line_rows
    boxes = spectral[0].shape[1] // size_z
    lanes = [slice(box * size_z, (box + 1) * size_z) for box in range(boxes)]
    for field in range(2):
        for box in range(boxes):
            high, low = halves(spectral[field][:, lanes[box]])
            both = jnp.concatenate([high, low], axis=1)
            modes = dot(both, line_forward_ref[0 : 2 * line_rows]) + dot(high, line_forward_ref[2 * line_rows :])
            modes = modes * inverse_ref[field * boxes + box]
            high, low = halves(modes)
            cells = dot(high, line_back_ref[...])
            cells = cells[:, :size_z] + (cells[:, size_z:] + dot(low, line_back_ref[:, :size_z]))
            store_split(after_ref.at[field], lanes[box], cells)

def solved_kernel(mesh, after_ref, back_ref, out_ref, out_rows_ref, *lines_refs):
    boxes = (out_ref.shape[1] - 2) // BOX
    size_y, size_z = out_ref.shape[2:]
    inner = SPAN * size_y
    lanes = [slice(box * size_z, (box + 1) * size_z) for box in range(boxes)]
    for field in range(2):
        result = dot(back_ref[...], after_ref[field])
        for box in range(boxes):
            start = box * BOX
            main = result[:inner, lanes[box]].reshape(SPAN, size_y, size_z)
            if box == 0:
                out_ref[field, 0:SPAN] = main
            else:
                out_ref[field, start : start + 2] = out_ref[field, start : start + 2] + main[0:2]
                out_ref[field, start + 2 : start + SPAN] = main[2:]
            for side in range(2):
                strip = result[inner + 24 * side : inner + 24 * side + 24, lanes[box]]
                if box == 0:
                    out_rows_ref[field, side, 0:24] = strip
                else:
                    out_rows_ref[field, side, start : start + 8] = (
                        out_rows_ref[field, side, start : start + 8] + strip[0:8]
                    )
                    out_rows_ref[field, side, start + 8 : start + 24] = strip[8:]
    if lines_refs:
        pack_lines(standing(mesh), out_ref, out_rows_ref, *lines_refs)


def x_depth(message_ref):
    return message_ref.shape[1] // SPAN


def pack_x(flags, after_ref, edges_ref, even_ref, odd_ref):
    depth, size_z = x_depth(even_ref), even_ref.shape[2]
    layers = depth * BOX
    after = len(EDGE_LAYERS) * BOX
    for field in range(2):
        result = dot(edges_ref[...], after_ref[field])
        low, high = result[:, :size_z], result[:, result.shape[1] - size_z :]
        pairs = [(0, low[:layers], high[after - layers : after])]
        for side in range(2):
            near = after + 24 * side + ROW0 - 1
            far = near + SPAN - depth
            pairs.append((layers + depth * side, low[near : near + depth], high[far : far + depth]))
        blank = jnp.zeros((even_ref.shape[1] - SPAN * depth, size_z), F32)
        pairs.append((SPAN * depth, blank, blank))
        for start, to_low, to_high in pairs:
            place = slice(start, start + to_low.shape[0])
            even_ref[field, place] = chosen(flags, EVEN_X, to_high, to_low)
            odd_ref[field, place] = chosen(flags, EVEN_X, to_low, to_high)


def line_pairs(whole_ref, whole_rows_ref, field, layers, rows, depth):
    size_y = whole_ref.shape[2]
    if depth == 3:
        return (
            (whole_rows_ref[field, 0, rows], whole_ref[field, layers, size_y - 2]),
            (whole_ref[field, layers, 0], whole_ref[field, layers, size_y - 1]),
            (whole_ref[field, layers, 1], whole_rows_ref[field, 1, rows]),
        )
    return (
        (whole_ref[field, layers, 0], whole_ref[field, layers, size_y - 1]),
        (whole_rows_ref[field, 0, rows], whole_rows_ref[field, 1, rows]),
    )


def pack_lines(flags, part_ref, part_rows_ref, even_ref, odd_ref):
    size_x = part_ref.shape[1] - 2
    depth = even_ref.shape[1] // size_x
    for field in range(2):
        pairs = line_pairs(
            part_ref, part_rows_ref, field, slice(1, size_x + 1), slice(ROW0, ROW0 + size_x), depth
        )
        for line, (to_low, to_high) in enumerate(pairs):
            place = slice(line * size_x, (line + 1) * size_x)
            even_ref[field, place] = chosen(flags, EVEN_Y, to_high, to_low)
            odd_ref[field, place] = chosen(flags, EVEN_Y, to_low, to_high)


def unpack_lines(flags, lines_refs, ends_refs, out_ref, field):
    size_x = out_ref.shape[2] - 8
    depth = lines_refs[0].shape[1] // size_x
    blank = jnp.zeros((8, out_ref.shape[3]), F32)
    for side, flag, (even, odd) in ((0, LOW_Y, (1, 0)), (1, HIGH_Y, (0, 1))):
        lines = keep(flags, flag, chosen(flags, EVEN_Y, lines_refs[even][field], lines_refs[odd][field]))
        ends = keep(flags, flag, chosen(flags, EVEN_Y, ends_refs[even][field], ends_refs[odd][field]))
        for line in range(depth):
            out_ref[side, line, 0:8] = blank
            out_ref[side, line, size_x : size_x + 8] = blank
            out_ref[side, line, ROW0 : ROW0 + size_x] = lines[line * size_x : (line + 1) * size_x]
            if depth == 3:
                out_ref[side, line, ROW0 - 2 : ROW0 + 1] = ends[8 * line : 8 * line + 3]
                out_ref[side, line, ROW0 + size_x - 1 : ROW0 + size_x + 2] = ends[8 * line + 3 : 8 * line + 6]
            elif line == 1:
                out_ref[side, line, ROW0 - 1 : ROW0] = ends[0:1]
                out_ref[side, line, ROW0 + size_x : ROW0 + size_x + 1] = ends[1:2]


def divisor_kernel(conductance_ref, capacity_ref, zones_ref, inverse_ref):
    size_x, size_y, size_z = zones_ref.shape
    boxes = size_x // BOX
    lines = []
    for table_ref, which in ((capacity_ref, 0), (capacity_ref, 1), (conductance_ref, 0), (conductance_ref, 1)):
        for box in range(boxes):
            total = jnp.zeros((size_y, size_z), F32)
            for x in range(box * BOX, (box + 1) * BOX):
                zone = zones_ref[x]
                value = jnp.full((size_y, size_z), table_ref[which, 0], F32)
                for label in range(1, table_ref.shape[1]):
                    value = jnp.where(zone == label, table_ref[which, label], value)
                total = total + value
            lines.append(jnp.sum(total, axis=0, keepdims=True))
    sums = jnp.concatenate(lines, axis=0)
    modes, lanes = inverse_ref.shape[1:]
    cell = lax.broadcasted_iota(jnp.int32, (size_z, lanes), 0)
    lane = lax.broadcasted_iota(jnp.int32, (size_z, lanes), 1)
    spread = jnp.zeros((size_z, lanes), F32)
    for box in range(size_z // BOX):
        here = (cell >= box * BOX) & (cell < (box + 1) * BOX) & (lane >= box * SPAN) & (lane < (box + 1) * SPAN)
        spread = jnp.where(here, 1.0 / BOX**3, spread)
    means = jnp.dot(sums, spread, preferred_element_type=F32, precision=lax.Precision.HIGHEST)
    eigen = [float(value) for value in eigenvalues()]
    row = lax.broadcasted_iota(jnp.int32, (modes, 128), 0)
    first = jnp.zeros(row.shape, jnp.int32)
    for mode in range(1, SPAN):
        first = first + (row >= mode * SPAN).astype(jnp.int32)
    second = row - SPAN * first
    pair = jnp.zeros(row.shape, F32)
    for mode in range(SPAN):
        pair = pair + jnp.where(first == mode, eigen[mode], 0.0) + jnp.where(second == mode, eigen[mode], 0.0)
    lane = lax.broadcasted_iota(jnp.int32, (8, lanes), 1)
    for box in range(1, size_z // BOX):
        lane = lane - SPAN * (lax.broadcasted_iota(jnp.int32, (8, lanes), 1) >= box * SPAN).astype(jnp.int32)
    third = jnp.zeros(lane.shape, F32)
    for mode in range(SPAN):
        third = jnp.where(lane == mode, eigen[mode], third)
    summed = jnp.concatenate([pair, pair[:, : lanes - 128]], axis=1) + third[0:1]
    half = 2 * boxes
    for combo in range(half):
        cbar = means[combo : combo + 1]
        kbar = means[half + combo : half + combo + 1]
        inverse_ref[combo] = 1.0 / (cbar + kbar * summed)


def edge_layers_kernel(mesh, load_hbm, zones_hbm, even_ref, odd_ref, load_ref, zones_ref, sems):
    last = zones_hbm.shape[0] - 1
    copies = [
        pltpu.make_async_copy(load_hbm.at[:, 0], load_ref.at[0], sems.at[0]),
        pltpu.make_async_copy(load_hbm.at[:, last], load_ref.at[1], sems.at[1]),
        pltpu.make_async_copy(zones_hbm.at[pl.ds(0, 2)], zones_ref.at[0], sems.at[2]),
        pltpu.make_async_copy(zones_hbm.at[pl.ds(last - 1, 2)], zones_ref.at[1], sems.at[3]),
    ]
    for copy in copies:
        copy.start()
    flags = standing(mesh)
    for copy in copies:
        copy.wait()
    for channel in range(4):
        if channel < 2:
            low, high = load_ref[0, channel], load_ref[1, channel]
        else:
            low, high = zones_ref[0, channel - 2].astype(F32), zones_ref[1, channel - 2].astype(F32)
        even_ref[channel] = chosen(flags, EVEN_X, high, low)
        odd_ref[channel] = chosen(flags, EVEN_X, low, high)


def fetched_kernel(load_ref, zones_ref, token_ref):
    token_ref[...] = load_ref[0, 0, 0:8] + zones_ref[0, 0:8].astype(F32)


def edge_lines_kernel(mesh, load_ref, zones_ref, token_ref, first_ref, second_ref, even_ref, odd_ref):
    flags = standing(mesh)
    size_x, size_y = zones_ref.shape[:2]
    from_low = chosen(flags, EVEN_X, second_ref[...], first_ref[...])
    from_high = chosen(flags, EVEN_X, first_ref[...], second_ref[...])

    def put(row, to_low, to_high):
        place = slice(row, row + to_low.shape[0])
        even_ref[place] = chosen(flags, EVEN_Y, to_high, to_low)
        odd_ref[place] = chosen(flags, EVEN_Y, to_low, to_high)

    def put_end(row, layer, near, far):
        put(4 * size_x + row, layer[near : near + 1], layer[far : far + 1])

    blank = jnp.zeros((8, even_ref.shape[1]), F32)
    put(4 * size_x + 8, blank, blank)
    for field in range(2):
        put(field * size_x, load_ref[field, :, 0], load_ref[field, :, size_y - 1])
        put_end(2 * field, keep(flags, LOW_X, from_low[field]), 0, size_y - 1)
        put_end(2 * field + 1, keep(flags, HIGH_X, from_high[field]), 0, size_y - 1)
    for line in range(2):
        far = size_y - 2 + line
        put((2 + line) * size_x, zones_ref[:, line].astype(F32), zones_ref[:, far].astype(F32))
        for depth in range(2):
            put_end(4 + 4 * line + depth, from_low[2 + depth], line, far)
            put_end(6 + 4 * line + depth, from_high[2 + depth], line, far)


def tables(conductance_ref, capacity_ref, coupling_ref, size_z):
    labels = range(coupling_ref.shape[0])
    halves_of = [[0.5 * conductance_ref[field, label] for label in labels] for field in range(2)]
    masses = [[capacity_ref[field, label] for label in labels] for field in range(2)]
    products = [jnp.full((8, size_z), capacity_ref[0, label] * capacity_ref[1, label], F32) for label in labels]
    masses.append([coupling_ref[label] * jnp.sqrt(products[label])[0:1] for label in labels])
    return halves_of, masses


def looked_up(entries, zone):
    value = jnp.broadcast_to(entries[0], zone.shape)
    for label in range(1, len(entries)):
        value = jnp.where(zone == float(label), entries[label], value)
    return value


def coefficient_kernel(
    mesh, conductance_ref, capacity_ref, coupling_ref, zones_ref, first_x, second_x,
    half_ref, mass_ref, face_ref, table_ref,
):
    flags = standing(mesh)
    size_x, size_y, size_z = zones_ref.shape
    halves_of, masses = tables(conductance_ref, capacity_ref, coupling_ref, size_z)
    for which, entries in enumerate(halves_of + masses):
        for label, entry in enumerate(entries):
            table_ref[which, label : label + 1] = jnp.broadcast_to(entry, (1, size_z))
    low_x = chosen(flags, EVEN_X, second_x[2:4], first_x[2:4])
    high_x = chosen(flags, EVEN_X, first_x[2:4], second_x[2:4])
    inside = slice(8, 8 + size_y)
    for x in range(-2, size_x + 2):
        if x < 0:
            zone = low_x[x + 2]
        elif x >= size_x:
            zone = high_x[x - size_x]
        else:
            zone = zones_ref[x].astype(F32)
        for field in range(2):
            half_ref[field, x + 2, inside] = looked_up(halves_of[field], zone)
        if -1 <= x <= size_x:
            for which in range(3):
                mass_ref[which, x + 1] = looked_up(masses[which], zone)
    for field in range(2):
        for outer in (0, 1):
            half_ref[field, outer, inside] = chosen(
                flags, LOW_X, half_ref[field, outer, inside], half_ref[field, 2, inside]
            )
            place = size_x + 2 + outer
            half_ref[field, place, inside] = chosen(
                flags, HIGH_X, half_ref[field, place, inside], half_ref[field, size_x + 1, inside]
            )
    for field in range(2):
        for x in range(0, size_x + 2, 2):
            faces = faces_z(half_ref[field, x + 1 : x + 3, inside])
            for way in range(2):
                face_ref[field, way, x : x + 2] = faces[way]


def coefficient_lines_kernel(
    mesh, old_half_ref, mass_ref, face_ref, table_ref, first_y, second_y, after_ref,
    half_ref, half_rows_ref, mass_rows_ref, face_rows_ref, line_ref,
):
    flags = standing(mesh)
    size_x, size_y, size_z = mass_ref.shape[1] - 2, mass_ref.shape[2], mass_ref.shape[3]
    rows_of = [[table_ref[which, label : label + 1] for label in range(table_ref.shape[1])] for which in range(5)]
    halves_of, masses = rows_of[:2], rows_of[2:]
    for side, (even, odd) in enumerate(((second_y, first_y), (first_y, second_y))):
        came = chosen(flags, EVEN_Y, even[2 * size_x :], odd[2 * size_x :])
        lines, ends = (came[:size_x], came[size_x : 2 * size_x]), came[2 * size_x :]
        for line in range(2):
            place = 2 * side + line
            line_ref[place, 0:8] = jnp.zeros((8, size_z), F32)
            line_ref[place, size_x : size_x + 8] = jnp.zeros((8, size_z), F32)
            line_ref[place, ROW0 - 2 : ROW0] = ends[4 + 4 * line : 6 + 4 * line]
            line_ref[place, ROW0 : ROW0 + size_x] = lines[line]
            line_ref[place, ROW0 + size_x : ROW0 + size_x + 2] = ends[6 + 4 * line : 8 + 4 * line]
    count = half_rows_ref.shape[2]
    position = lax.broadcasted_iota(jnp.int32, (count, size_z), 0)
    for line, flag in enumerate((LOW_Y, LOW_Y, HIGH_Y, HIGH_Y)):
        zone = line_ref[line]
        for field in range(2):
            value = looked_up(halves_of[field], zone)
            below = value[ROW0 : ROW0 + 1]
            above = value[ROW0 + size_x - 1 : ROW0 + size_x]
            value = jnp.where((position < ROW0) & (flags[LOW_X] == 0), below, value)
            value = jnp.where((position >= ROW0 + size_x) & (flags[HIGH_X] == 0), above, value)
            near = old_half_ref[field, :, 8 if flag == LOW_Y else 8 + size_y - 1]
            half_rows_ref[field, line] = value
            half_rows_ref[field, line, ROW0 - 2 : ROW0 + size_x + 2] = chosen(
                flags, flag, half_rows_ref[field, line, ROW0 - 2 : ROW0 + size_x + 2], near
            )
            if line in (1, 2):
                row = 7 if line == 1 else 8 + size_y
                half_ref[field, :, row] = half_rows_ref[field, line, ROW0 - 2 : ROW0 + size_x + 2]
        if line in (1, 2):
            for which in range(3):
                mass_rows_ref[which, line - 1] = looked_up(masses[which], zone)
    for field in range(2):
        for side in range(2):
            faces = faces_z(half_rows_ref[field, side + 1])
            for way in range(2):
                face_rows_ref[field, way, side] = faces[way]
        for line, row in ((4, 0), (5, size_y - 1), (6, 1), (7, size_y - 2)):
            half_rows_ref[field, line] = jnp.zeros((count, size_z), F32)
            half_rows_ref[field, line, ROW0 - 2 : ROW0 + size_x + 2] = old_half_ref[field, :, 8 + row]
    for line, row in ((2, 0), (3, size_y - 1)):
        spread = slice(ROW0 - 1, ROW0 + size_x + 1)
        for which in range(3):
            mass_rows_ref[which, line] = jnp.zeros((count, size_z), F32)
            mass_rows_ref[which, line, spread] = mass_ref[which, :, row]
        for field in range(2):
            for way in range(2):
                face_rows_ref[field, way, line] = jnp.zeros((count, size_z), F32)
                face_rows_ref[field, way, line, spread] = face_ref[field, way, :, row]


def own_transform_kernel(load_ref, forward_ref, spectral_ref, field_ref, before_ref):
    size_x = load_ref.shape[1]
    for field in range(2):
        field_ref[field, 0] = jnp.zeros(load_ref.shape[2:], F32)
        field_ref[field, 1 : 1 + size_x] = load_ref[field]
        field_ref[field, 1 + size_x] = jnp.zeros(load_ref.shape[2:], F32)
    forward_own(field_ref, forward_ref, before_ref, spectral_ref)


def first_solve_kernel(
    mesh, spectral_ref, mass_ref, first_x, second_x, first_y, second_y, inverse_ref, c2, c3, ends_ref, edges_ref,
    after_ref, even_ref, odd_ref, rows_ref, before_ref,
):
    flags = standing(mesh)
    size_x, size_y, size_z = mass_ref.shape[1] - 2, mass_ref.shape[2], mass_ref.shape[3]
    boxes = size_x // BOX
    blank = jnp.zeros((size_y, size_z), F32)
    spectral = []
    for field in range(2):
        low = keep(flags, LOW_X, chosen(flags, EVEN_X, second_x[field], first_x[field]))
        high = keep(flags, HIGH_X, chosen(flags, EVEN_X, first_x[field], second_x[field]))
        for side, flag, even, odd in ((0, LOW_Y, second_y, first_y), (1, HIGH_Y, first_y, second_y)):
            place, after = slice(field * size_x, (field + 1) * size_x), slice(4 * size_x, 4 * size_x + 8)
            line = keep(flags, flag, chosen(flags, EVEN_Y, even[place], odd[place]))
            ends = keep(flags, flag, chosen(flags, EVEN_Y, even[after], odd[after]))
            rows_ref[field, side, 0:8] = blank[0:8]
            rows_ref[field, side, size_x : size_x + 8] = blank[0:8]
            rows_ref[field, side, ROW0 - 1 : ROW0] = ends[2 * field : 2 * field + 1]
            rows_ref[field, side, ROW0 : ROW0 + size_x] = line
            rows_ref[field, side, ROW0 + size_x : ROW0 + size_x + 1] = ends[2 * field + 1 : 2 * field + 2]
        for box in range(boxes):
            parts = [low if box == 0 else blank, high if box == boxes - 1 else blank]
            parts += [rows_ref[field, side, box * BOX : box * BOX + 24] for side in range(2)]
            stacked(before_ref.at[field], slice(box * size_z, (box + 1) * size_z), parts)
    for field in range(2):
        spectral.append(spectral_ref[field] + dot(ends_ref[...], before_ref[field]))
    solve(spectral, inverse_ref, (c2, c3), after_ref)
    pack_x(flags, after_ref, edges_ref, even_ref, odd_ref)


def merge_x_kernel(mesh, part_ref, part_rows_ref, first_ref, second_ref, whole_ref, whole_rows_ref, even_ref, odd_ref):
    flags = standing(mesh)
    size_x = part_ref.shape[1] - 2
    size_y, size_z = part_ref.shape[2:]
    depth = x_depth(first_ref)
    end = ROW0 + size_x
    for field in range(2):
        low = keep(flags, LOW_X, chosen(flags, EVEN_X, second_ref[field], first_ref[field]))
        high = keep(flags, HIGH_X, chosen(flags, EVEN_X, first_ref[field], second_ref[field]))
        low_layers, high_layers = [
            [came[layer * size_y : (layer + 1) * size_y] for layer in range(depth)] for came in (low, high)
        ]
        whole_ref[field, 1] = keep(flags, LOW_X, part_ref[field, 0]) + low_layers[depth - 2]
        whole_ref[field, 2] = part_ref[field, 1] + low_layers[depth - 1]
        whole_ref[field, 3 : size_x + 1] = part_ref[field, 2:size_x]
        whole_ref[field, size_x + 1] = part_ref[field, size_x] + high_layers[0]
        whole_ref[field, size_x + 2] = keep(flags, HIGH_X, part_ref[field, size_x + 1]) + high_layers[1]
        whole_ref[field, 0] = low_layers[0] if depth == 3 else jnp.zeros((size_y, size_z), F32)
        whole_ref[field, size_x + 3] = high_layers[2] if depth == 3 else jnp.zeros((size_y, size_z), F32)
        for side in range(2):
            start = depth * (size_y + side)
            low_row, high_row = [
                [came[start + layer : start + layer + 1] for layer in range(depth)] for came in (low, high)
            ]
            edge = ROW0 - 1
            whole_rows_ref[field, side] = part_rows_ref[field, side]
            whole_rows_ref[field, side, edge : edge + 1] = (
                keep(flags, LOW_X, part_rows_ref[field, side, edge : edge + 1]) + low_row[depth - 2]
            )
            whole_rows_ref[field, side, edge + 1 : edge + 2] = (
                part_rows_ref[field, side, edge + 1 : edge + 2] + low_row[depth - 1]
            )
            whole_rows_ref[field, side, end - 1 : end] = part_rows_ref[field, side, end - 1 : end] + high_row[0]
            whole_rows_ref[field, side, end : end + 1] = (
                keep(flags, HIGH_X, part_rows_ref[field, side, end : end + 1]) + high_row[1]
            )
            if depth == 3:
                whole_rows_ref[field, side, edge - 1 : edge] = low_row[0]
                whole_rows_ref[field, side, end + 1 : end + 2] = high_row[2]

        base = 2 * size_x if depth == 2 else 0
        for ref in (even_ref, odd_ref):
            ref[field, base:] = jnp.zeros((ref.shape[1] - base, size_z), F32)
        if base:
            own, rows = slice(2, size_x + 2), slice(ROW0, ROW0 + size_x)
            pairs = line_pairs(whole_ref, whole_rows_ref, field, own, rows, depth)
            for line, (to_low, to_high) in enumerate(pairs):
                place = slice(line * size_x, (line + 1) * size_x)
                even_ref[field, place] = chosen(flags, EVEN_Y, to_high, to_low)
                odd_ref[field, place] = chosen(flags, EVEN_Y, to_low, to_high)
            for row, x in ((base, -1), (base + 1, size_x)):
                pairs = line_pairs(
                    whole_ref, whole_rows_ref, field, slice(x + 2, x + 3), slice(x + ROW0, x + ROW0 + 1), depth
                )
                even_ref[field, row : row + 1] = chosen(flags, EVEN_Y, pairs[1][1], pairs[1][0])
                odd_ref[field, row : row + 1] = chosen(flags, EVEN_Y, pairs[1][0], pairs[1][1])
            continue
        for start, x in ((base, -2), (base + 3, size_x - 1)):
            layers, rows = slice(x + 2, x + 5), slice(x + ROW0, x + ROW0 + 3)
            pairs = line_pairs(whole_ref, whole_rows_ref, field, layers, rows, depth)
            for line, (to_low, to_high) in enumerate(pairs):
                place = slice(8 * line + start, 8 * line + start + 3)
                even_ref[field, place] = chosen(flags, EVEN_Y, to_high, to_low)
                odd_ref[field, place] = chosen(flags, EVEN_Y, to_low, to_high)


def faces_z(half):
    size_z, axis = half.shape[-1], half.ndim - 1
    lane = lax.broadcasted_iota(jnp.int32, half.shape, axis)
    upper = half + jnp.where(lane == size_z - 1, half, pltpu.roll(half, size_z - 1, axis))
    lower = half + jnp.where(lane == 0, half, pltpu.roll(half, 1, axis))
    return upper, lower


def along_z(value, upper, lower):
    size_z, axis = value.shape[-1], value.ndim - 1
    lane = lax.broadcasted_iota(jnp.int32, value.shape, axis)
    above = jnp.where(lane == size_z - 1, 0.0, pltpu.roll(value, size_z - 1, axis))
    below = jnp.where(lane == 0, 0.0, pltpu.roll(value, 1, axis))
    return upper * (value - above) + lower * (value - below)


def operate(field_ref, half_ref, mass_ref, face_ref, x, count):
    size_y = mass_ref.shape[2]
    inside = slice(8, 8 + size_y)
    masses = slice(x + 1, x + 1 + count)
    here = slice(x + 2, x + 2 + count)
    values, images = [], []
    for field in range(2):
        value = field_ref[field, here, inside]
        half = half_ref[field, here, inside]
        flux = along_z(value, face_ref[field, 0, masses], face_ref[field, 1, masses])
        for start in (x + 1, x + 3):
            place = slice(start, start + count)
            flux = flux + (half + half_ref[field, place, inside]) * (value - field_ref[field, place, inside])
        for shift in (-1, 1):
            moved = slice(8 + shift, 8 + shift + size_y)
            flux = flux + (half + half_ref[field, here, moved]) * (value - field_ref[field, here, moved])
        values.append(value)
        images.append(flux)
    first = mass_ref[0, masses] * values[0] + mass_ref[2, masses] * values[1] + images[0]
    second = mass_ref[2, masses] * values[0] + mass_ref[1, masses] * values[1] + images[1]
    return values, (first, second)


def merge_x_after_kernel(mesh, part_ref, part_rows_ref, first_ref, second_ref, sums_ref, *outs):
    merge_x_kernel(mesh, part_ref, part_rows_ref, first_ref, second_ref, *outs)


def fill(flags, whole_ref, whole_rows_ref, value_ref):
    size_x, size_y = whole_ref.shape[1] - 4, whole_ref.shape[2]
    spread = slice(ROW0 - 2, ROW0 + size_x + 2)
    for field in range(2):
        value_ref[field, :, 8 : 8 + size_y] = whole_ref[field]
        value_ref[field, :, 7] = keep(flags, LOW_Y, whole_rows_ref[field, 0, spread])
        value_ref[field, :, 8 + size_y] = keep(flags, HIGH_Y, whole_rows_ref[field, 1, spread])


def line_image(values, outers, inners, half_lines, places, mass_lines, face_lines, place):
    center, outer, inner = places
    images = []
    for field in range(2):
        value, half = values[field], half_lines[field, center]
        count = value.shape[0]
        flux = along_z(value, face_lines[field, 0, place], face_lines[field, 1, place])
        for turn in (1, count - 1):
            flux = flux + (half + pltpu.roll(half, turn, 0)) * (value - pltpu.roll(value, turn, 0))
        flux = flux + (half + half_lines[field, outer]) * (value - outers[field])
        flux = flux + (half + half_lines[field, inner]) * (value - inners[field])
        images.append(flux)
    first = mass_lines[0, place] * values[0] + mass_lines[2, place] * values[1] + images[0]
    second = mass_lines[2, place] * values[0] + mass_lines[1, place] * values[1] + images[1]
    return first, second


SIDES = (((4, 1, 6, 0), (2, 0)), ((5, 2, 7, 3), (3, 1)))


def line_changes(delta, outer, half_lines, mass_lines, face_lines, side):
    (edge, out, inner, _), (place, _) = SIDES[side]
    nothing = [jnp.zeros_like(line) for line in delta]
    at_edge = line_image(delta, outer, nothing, half_lines, (edge, out, inner), mass_lines, face_lines, place)
    at_next = [-(half_lines[field, edge] + half_lines[field, inner]) * delta[field] for field in range(2)]
    return at_edge, at_next


def own_image_kernel(
    mesh, whole_ref, whole_rows_ref, half_ref, mass_ref, face_ref, forward_ref, image_ref, spectral_ref,
    value_ref, before_ref,
):
    flags = standing(mesh)
    size_x = whole_ref.shape[1] - 4
    fill(flags, whole_ref, whole_rows_ref, value_ref)
    for x, flag in ((-1, LOW_X), (size_x, HIGH_X)):
        _, images = operate(value_ref, half_ref, mass_ref, face_ref, x, 1)
        for field in range(2):
            image_ref[field, x + 1 : x + 2] = keep(flags, flag, images[field])
    for x in range(0, size_x, CHUNK):
        _, images = operate(value_ref, half_ref, mass_ref, face_ref, x, CHUNK)
        for field in range(2):
            image_ref[field, x + 1 : x + 1 + CHUNK] = images[field]
    forward_own(image_ref, forward_ref, before_ref, spectral_ref)


def second_solve_kernel(
    mesh, whole_ref, whole_rows_ref, first_lines, second_lines, first_ends, second_ends,
    half_lines, mass_lines, face_lines, spectral_ref, inverse_ref, c2, c3, lines_ref, edges_ref,
    deltas_ref, changes_ref, after_ref, even_ref, odd_ref, came_ref, near, before_ref,
):
    flags = standing(mesh)
    size_x, size_y, size_z = whole_ref.shape[1] - 4, whole_ref.shape[2], whole_ref.shape[3]
    boxes = size_x // BOX
    count = near.shape[2]
    position = lax.broadcasted_iota(jnp.int32, (count, size_z), 0)
    begin = jnp.where(flags[LOW_X] > 0, ROW0 - 1, ROW0)
    end = jnp.where(flags[HIGH_X] > 0, ROW0 + size_x + 1, ROW0 + size_x)
    valid = (position >= begin) & (position < end)
    for field in range(2):
        unpack_lines(flags, (first_lines, second_lines), (first_ends, second_ends), came_ref.at[field], field)
        for side, row in ((0, 0), (1, size_y - 1)):
            near[field, side] = jnp.zeros((count, size_z), F32)
            near[field, side, ROW0 - 2 : ROW0 + size_x + 2] = whole_ref[field, :, row]
    for side, flag, order in ((0, LOW_Y, (2, 1, 0)), (1, HIGH_Y, (0, 1, 2))):
        delta, outer, far = [[came_ref[field, side, line] for field in range(2)] for line in order]
        at_edge, at_next = line_changes(delta, outer, half_lines, mass_lines, face_lines, side)
        (edge, out, _, beyond), (_, place) = SIDES[side]
        at_outer = line_image(
            [keep(flags, flag, whole_rows_ref[field, side]) + outer[field] for field in range(2)],
            far,
            [near[field, side] + delta[field] for field in range(2)],
            half_lines,
            (out, beyond, edge),
            mass_lines,
            face_lines,
            place,
        )
        for field in range(2):
            deltas_ref[field, side] = delta[field]
            changes_ref[field, 3 * side] = jnp.where(valid, at_edge[field], 0.0)
            changes_ref[field, 1 + side] = jnp.where(valid, at_next[field], 0.0)
            changes_ref[field, 4 + side] = keep(flags, flag, jnp.where(valid, at_outer[field], 0.0))
    spectral = []
    for field in range(2):
        for box in range(boxes):
            parts = [changes_ref[field, line, box * BOX : box * BOX + 24] for line in range(6)]
            stacked(before_ref.at[field], slice(box * size_z, (box + 1) * size_z), parts)
    for field in range(2):
        spectral.append(spectral_ref[field] + dot(lines_ref[...], before_ref[field]))
    solve(spectral, inverse_ref, (c2, c3), after_ref)
    pack_x(flags, after_ref, edges_ref, even_ref, odd_ref)


def first_sums_kernel(load_ref, whole_ref, image_ref, deltas_ref, changes_ref, precond_ref, out_ref, sums_ref):
    size_x, size_y, size_z = load_ref.shape[1:]
    rows = slice(ROW0, ROW0 + size_x)
    total_a = total_b = jnp.zeros((size_y, size_z), F32)
    for field in range(2):
        precond_ref[field] = whole_ref[field, 2 : size_x + 2]
        out_ref[field] = image_ref[field, 1 : size_x + 1]
        for side, row in ((0, 0), (1, size_y - 1)):
            precond_ref[field, :, row] = precond_ref[field, :, row] + deltas_ref[field, side, rows]
        for line, row in enumerate((0, 1, size_y - 2, size_y - 1)):
            out_ref[field, :, row] = out_ref[field, :, row] + changes_ref[field, line, rows]
        for x in range(size_x):
            total_a = total_a + load_ref[field, x] * precond_ref[field, x]
            total_b = total_b + out_ref[field, x] * precond_ref[field, x]
    sums_ref[0:1] = jnp.sum(total_a, axis=0, keepdims=True)
    sums_ref[1:2] = jnp.sum(total_b, axis=0, keepdims=True)
    sums_ref[2:8] = jnp.zeros((6, size_z), F32)


def own_second_image_kernel(
    mesh, whole_ref, whole_rows_ref, half_ref, mass_ref, face_ref, old_image_ref, image_ref, sums_ref, value_ref
):
    flags = standing(mesh)
    size_x, size_y, size_z = old_image_ref.shape[1:]
    fill(flags, whole_ref, whole_rows_ref, value_ref)
    total_c = total_d = jnp.zeros((CHUNK, size_y, size_z), F32)
    for x in range(0, size_x, CHUNK):
        chunk = slice(x, x + CHUNK)
        values, images = operate(value_ref, half_ref, mass_ref, face_ref, x, CHUNK)
        for field in range(2):
            image_ref[field, chunk] = images[field]
            total_c = total_c + old_image_ref[field, chunk] * values[field]
            total_d = total_d + images[field] * values[field]
    sums_ref[0:1] = jnp.sum(jnp.sum(total_c, axis=0), axis=0, keepdims=True)
    sums_ref[1:2] = jnp.sum(jnp.sum(total_d, axis=0), axis=0, keepdims=True)
    sums_ref[2:8] = jnp.zeros((6, size_z), F32)


def second_image_kernel(
    mesh, whole_ref, image_ref, first_ref, second_ref,
    half_lines, mass_lines, face_lines, old_image_ref, old_sums_ref, own_sums_ref,
    deltas_ref, changes_ref, sums_ref, came_ref,
):
    flags = standing(mesh)
    size_x, size_y, size_z = old_image_ref.shape[1:]
    own = slice(2, size_x + 2)
    rows = slice(ROW0, ROW0 + size_x)
    total_c = total_d = jnp.zeros((size_x, size_z), F32)
    lines_refs = [ref.at[:, pl.ds(0, 2 * size_x)] for ref in (first_ref, second_ref)]
    ends_refs = [ref.at[:, pl.ds(2 * size_x, 8)] for ref in (first_ref, second_ref)]
    for field in range(2):
        unpack_lines(flags, lines_refs, ends_refs, came_ref.at[field], field)
    for side, row, beside in ((0, 0, 1), (1, size_y - 1, size_y - 2)):
        outer, delta = [[came_ref[field, side, line] for field in range(2)] for line in range(2)]
        at_edge, at_next = line_changes(delta, outer, half_lines, mass_lines, face_lines, side)
        for field in range(2):
            changed, edge, inner = delta[field][rows], at_edge[field][rows], at_next[field][rows]
            deltas_ref[field, side] = changed
            changes_ref[field, 3 * side] = edge
            changes_ref[field, 1 + side] = inner
            total_c = total_c + old_image_ref[field, :, row] * changed
            total_d = total_d + (image_ref[field, :, row] + edge) * changed
            total_d = total_d + whole_ref[field, own, row] * edge + whole_ref[field, own, beside] * inner
    totals = [
        jnp.sum(old_sums_ref[0:1], axis=1, keepdims=True),
        jnp.sum(old_sums_ref[1:2], axis=1, keepdims=True),
        jnp.sum(jnp.sum(total_c, axis=0, keepdims=True) + own_sums_ref[0:1], axis=1, keepdims=True),
        jnp.sum(jnp.sum(total_d, axis=0, keepdims=True) + own_sums_ref[1:2], axis=1, keepdims=True),
    ]
    lane = lax.broadcasted_iota(jnp.int32, sums_ref.shape, 1)
    spread = jnp.zeros(sums_ref.shape, F32)
    for place, total in enumerate(totals):
        spread = jnp.where(lane == place, total, spread)
    sums_ref[...] = spread


def finish_kernel(
    sums_ref, load_ref, z_ref, q_ref, w_ref, s_ref, deltas_ref, changes_ref,
    solution_hbm, residual_hbm, solution_ref, residual_ref, sems,
):
    line = jnp.sum(sums_ref[...], axis=0, keepdims=True)
    lane = lax.broadcasted_iota(jnp.int32, line.shape, 1)
    rz, zq, qw, ws = [jnp.sum(jnp.where(lane == place, line, 0.0), axis=1, keepdims=True) for place in range(4)]
    alpha = rz / zq
    ratio = qw / zq
    grown = alpha * ratio
    alpha_next = (qw - zq * (zq / rz)) / (ws - qw * ratio)
    along = alpha + alpha_next * grown
    against = alpha_next * alpha
    copies = []
    step = load_ref.shape[1] // 2
    for field in range(2):
        for start in range(0, 2 * step, step):
            part = pl.ds(start, step)
            for x in range(start, start + step):
                solution_ref[field, x] = along * z_ref[field, x] - against * w_ref[field, x + 2]
                residual_ref[field, x] = load_ref[field, x] - along * q_ref[field, x] + against * s_ref[field, x]
            size_y = load_ref.shape[2]
            chunk = slice(start, start + step)
            for side, row in ((0, 0), (1, size_y - 1)):
                solution_ref[field, chunk, row] = (
                    solution_ref[field, chunk, row] - against * deltas_ref[field, side, chunk]
                )
            for line, row in enumerate((0, 1, size_y - 2, size_y - 1)):
                residual_ref[field, chunk, row] = (
                    residual_ref[field, chunk, row] + against * changes_ref[field, line, chunk]
                )
            for here, there in ((solution_ref, solution_hbm), (residual_ref, residual_hbm)):
                copies.append(
                    pltpu.make_async_copy(here.at[field, part], there.at[field, part], sems.at[len(copies)])
                )
                copies[-1].start()
    for copy in copies:
        copy.wait()


SMEM = pl.BlockSpec(memory_space=pltpu.SMEM)
VMEM = pl.BlockSpec(memory_space=pltpu.VMEM)
HBM = pl.BlockSpec(memory_space=pltpu.HBM)


def call(mesh, kernel, scalars, arrays, outs, scratch=(), flops=0, limit=24, in_hbm=False, outs_in_hbm=False, aliases=()):
    moved = sum(math.prod(a.shape) * a.dtype.itemsize for a in list(arrays) + list(outs))
    return pl.pallas_call(
        kernel if mesh is None else functools.partial(kernel, mesh),
        out_shape=tuple(outs),
        in_specs=[SMEM] * len(scalars) + [HBM if in_hbm else VMEM] * len(arrays),
        out_specs=tuple([HBM if outs_in_hbm else VMEM] * len(outs)),
        scratch_shapes=list(scratch),
        input_output_aliases=dict(aliases),
        compiler_params=pltpu.CompilerParams(vmem_limit_bytes=int(limit * 1024 * 1024)),
        cost_estimate=pl.CostEstimate(flops=flops, bytes_accessed=moved, transcendentals=0),
    )(*scalars, *arrays)


def shards(mesh, load, zones, conductance, capacity, coupling):
    size_x, size_y, size_z = zones.shape
    assert size_x % BOX == 0 and size_y == BOX and size_z % BOX == 0
    boxes = size_x // BOX
    count = size_x + 8
    sds = lambda *shape: jax.ShapeDtypeStruct(shape, F32)
    forward, back, line_forward, line_back, ends_forward, lines_forward, edges_back = [
        jnp.asarray(c) for c in constants(size_z)
    ]
    consts = (line_forward, line_back)
    modes, lanes = forward.shape[0], size_z // BOX * SPAN
    assert size_z == 128
    packed = call(
        mesh,
        edge_layers_kernel,
        [],
        [load, zones],
        [sds(4, size_y, size_z)] * 2,
        [
            pltpu.VMEM((2, 2, size_y, size_z), F32),
            pltpu.VMEM((2, 2, size_y, size_z), zones.dtype),
            pltpu.SemaphoreType.DMA((4,)),
        ],
        in_hbm=True,
        limit=53.75,
    )
    (token,) = call(None, fetched_kernel, [], [load, zones], [sds(8, size_z)])
    x_halo = swap(mesh, "gx", *packed)
    (inverse,) = call(
        None,
        divisor_kernel,
        [conductance, capacity],
        [zones],
        [sds(2 * boxes, modes, lanes)],
        flops=40_000_000,
    )
    packed = call(mesh, edge_lines_kernel, [], [load, zones, token, *x_halo], [sds(4 * size_x + 16, size_z)] * 2)
    y_halo = swap(mesh, "gy", *packed)
    laws = [conductance, capacity, coupling]
    padded_shape = sds(2, size_x + 4, size_y + 16, size_z)
    half, mass, face, table = call(
        mesh,
        coefficient_kernel,
        laws,
        [zones, *x_halo],
        [padded_shape, sds(3, size_x + 2, size_y, size_z), sds(2, 2, size_x + 2, size_y, size_z)]
        + [sds(5, coupling.shape[0], size_z)],
        flops=20_000_000,
    )
    parts = [sds(2, size_x + 2, size_y, size_z), sds(2, 2, count, size_z)]
    packed_x = [[sds(2, round_up(depth * SPAN, 8), size_z)] * 2 for depth in (3, 2)]
    wholes = [sds(2, size_x + 4, size_y, size_z), sds(2, 2, count, size_z)]
    packed_lines = [sds(2, 3 * size_x, size_z)] * 2
    packed_ends = [sds(2, 3 * 8, size_z)] * 2
    packed_y = [sds(2, 2 * size_x + 8, size_z)] * 2
    rows = SPAN * size_y + 48
    wide = boxes * size_z
    spectrum = sds(2, modes, wide)
    stack = lambda depth: pltpu.VMEM((2, depth, wide), BF16)
    halo = pltpu.VMEM((2, size_x + 2, size_y, size_z), F32)
    padded = pltpu.VMEM((2, size_x + 4, size_y + 16, size_z), F32)
    own = sds(2, size_x, size_y, size_z)

    (spectral,) = call(None, own_transform_kernel, [], [load, forward], [spectrum], [halo, stack(3 * rows)], 700_000_000)
    stacked_cells = jax.ShapeDtypeStruct((2, 3 * rows, wide), BF16)
    after, *packed = call(
        mesh,
        first_solve_kernel,
        [],
        [spectral, mass, *x_halo, *y_halo, inverse, *consts, ends_forward, edges_back],
        [stacked_cells] + packed_x[0],
        [pltpu.VMEM((2, 2, count, size_z), F32), stack(ends_forward.shape[1])],
        2_000_000_000,
    )
    received = swap(mesh, "gx", *packed)
    part, part_rows, *packed = call(mesh, solved_kernel, [], [after, back], parts + packed_lines, (), 700_000_000)
    lines = swap(mesh, "gy", *packed)
    whole, whole_rows, *packed = call(mesh, merge_x_kernel, [], [part, part_rows, *received], wholes + packed_ends)
    ends = swap(mesh, "gy", *packed)
    half, half_lines, mass_lines, face_lines = call(
        mesh,
        coefficient_lines_kernel,
        [],
        [half, mass, face, table, *y_halo, whole_rows],
        [padded_shape, sds(2, 8, count, size_z), sds(3, 4, count, size_z), sds(2, 2, 4, count, size_z)],
        [pltpu.VMEM((4, count, size_z), F32)],
        flops=2_000_000,
        aliases={0: 0},
    )
    own_image, spectral = call(
        mesh,
        own_image_kernel,
        [],
        [whole, whole_rows, half, mass, face, forward],
        [sds(2, size_x + 2, size_y, size_z), spectrum],
        [padded, stack(3 * rows)],
        700_000_000,
    )
    deltas, changes, after, *packed = call(
        mesh,
        second_solve_kernel,
        [],
        [whole, whole_rows, *lines, *ends, half_lines, mass_lines, face_lines, spectral, inverse, *consts]
        + [lines_forward, edges_back],
        [sds(2, 2, count, size_z), sds(2, 6, count, size_z), stacked_cells] + packed_x[1],
        [
            pltpu.VMEM((2, 2, 3, count, size_z), F32),
            pltpu.VMEM((2, 2, count, size_z), F32),
            stack(lines_forward.shape[1]),
        ],
        2_000_000_000,
    )
    received = swap(mesh, "gx", *packed)
    part, part_rows = call(mesh, solved_kernel, [], [after, back], parts, (), 700_000_000)
    precond, image, sums = call(
        None, first_sums_kernel, [], [load, whole, own_image, deltas, changes], [own, own, sds(8, size_z)], flops=1_000_000
    )
    whole, whole_rows, *packed = call(
        mesh, merge_x_after_kernel, [], [part, part_rows, *received, sums], wholes + packed_y
    )
    received = swap(mesh, "gy", *packed)
    last_image, own_sums = call(
        mesh,
        own_second_image_kernel,
        [],
        [whole, whole_rows, half, mass, face, image],
        [own, sds(8, size_z)],
        [padded],
        10_000_000,
    )
    devices = mesh.shape["gx"] * mesh.shape["gy"]
    deltas, changes, sums = call(
        mesh,
        second_image_kernel,
        [],
        [whole, last_image, *received, half_lines, mass_lines, face_lines, image, sums, own_sums],
        [sds(2, 2, size_x, size_z), sds(2, 4, size_x, size_z), sds(devices, size_z)],
        [pltpu.VMEM((2, 2, 2, count, size_z), F32)],
        1_000_000,
    )
    sums = lax.all_to_all(sums, AXES, 0, 0, tiled=True)
    whole_block = pltpu.VMEM((2, size_x, size_y, size_z), F32)
    return call(
        None,
        finish_kernel,
        [],
        [sums, load, precond, image, whole, last_image, deltas, changes],
        [own, own],
        [whole_block, whole_block, pltpu.SemaphoreType.DMA((8,))],
        outs_in_hbm=True,
    )


def solution(mesh):
    in_specs = (P(None, "gx", "gy", None), P("gx", "gy", None), P(), P(), P())
    out_specs = (P(None, "gx", "gy", None), P(None, "gx", "gy", None))
    return jax.shard_map(
        functools.partial(shards, mesh), mesh=mesh, in_specs=in_specs, out_specs=out_specs, check_vma=False
    )
```
